32 devices in a mesh: wide: 16 (over z, y, core), tensor: 2 (over x).
Axes of the slice: x: 2, y: 2, z: 4, core: 2. Of those that a mesh axis runs over, the one named last changes fastest.
Arguments:
- block_in: bfloat16 [2, 2048, 2560], P(None, 'wide'), may hold values from -6 to 6
- segment_ids: int32 [2, 2048], P(None, 'wide'), may hold values from 0 to 6, as said below
- cotangent: bfloat16 [2, 2048, 2560], P(None, 'wide'), may hold values from -6 to 6
- first_gain: bfloat16 [2560], P('wide'), may hold values from 0.5 to 1.5
- gelu_weight: bfloat16 [2560, 10, 256], P('wide', 'tensor'), may hold values from -0.125 to 0.125
- gelu_bias: bfloat16 [10, 256], P('tensor', 'wide'), may hold values from -3 to 3
- input_weight: bfloat16 [2560, 10, 256], P('wide', 'tensor'), may hold values from -0.125 to 0.125
- input_bias: bfloat16 [10, 256], P('tensor', 'wide'), may hold values from -3 to 3
- conv_weight: bfloat16 [4, 10, 256], P(None, 'tensor', 'wide'), may hold values from -3 to 3
- conv_bias: bfloat16 [10, 256], P('tensor', 'wide'), may hold values from -2 to 2
- inlet_weight: bfloat16 [10, 256, 256], P('tensor', 'wide'), may hold values from -0.375 to 0.375
- inlet_bias: bfloat16 [10, 256], P('tensor', 'wide'), may hold values from -3 to 3
- forget_weight: bfloat16 [10, 256, 256], P('tensor', 'wide'), may hold values from -0.375 to 0.375
- forget_bias: bfloat16 [10, 256], P('tensor', 'wide'), may hold values from -3 to 3
- decay_rate: bfloat16 [10, 256], P('tensor', 'wide'), may hold values from -11.5 to -4
- out_weight: bfloat16 [10, 256, 2560], P('tensor', None, 'wide'), may hold values from -0.25 to 0.25
- out_bias: bfloat16 [2560], P('wide'), may hold values from -3 to 3
- second_gain: bfloat16 [2560], P('wide'), may hold values from 0.5 to 1.5
- mlp_gate: bfloat16 [2560, 7680], P('wide', 'tensor'), may hold values from -0.125 to 0.125
- mlp_up: bfloat16 [2560, 7680], P('wide', 'tensor'), may hold values from -0.125 to 0.125
- mlp_down: bfloat16 [7680, 2560], P('tensor', 'wide'), may hold values from -0.125 to 0.125
Outputs:
- block_out: bfloat16 [2, 2048, 2560], P(None, 'wide')
- input_grad: float32 [2, 2048, 2560], P(None, 'wide')
- first_gain_grad: float32 [2560], P('wide')
- gelu_weight_grad: float32 [2560, 10, 256], P('wide', 'tensor')
- gelu_bias_grad: float32 [10, 256], P('tensor', 'wide')
- input_weight_grad: float32 [2560, 10, 256], P('wide', 'tensor')
- input_bias_grad: float32 [10, 256], P('tensor', 'wide')
- conv_weight_grad: float32 [4, 10, 256], P(None, 'tensor', 'wide')
- conv_bias_grad: float32 [10, 256], P('tensor', 'wide')
- inlet_weight_grad: float32 [10, 256, 256], P('tensor', 'wide')
- inlet_bias_grad: float32 [10, 256], P('tensor', 'wide')
- forget_weight_grad: float32 [10, 256, 256], P('tensor', 'wide')
- forget_bias_grad: float32 [10, 256], P('tensor', 'wide')
- decay_rate_grad: float32 [10, 256], P('tensor', 'wide')
- out_weight_grad: float32 [10, 256, 2560], P('tensor', None, 'wide')
- out_bias_grad: float32 [2560], P('wide')
- second_gain_grad: float32 [2560], P('wide')
- mlp_gate_grad: float32 [2560, 7680], P('wide', 'tensor')
- mlp_up_grad: float32 [2560, 7680], P('wide', 'tensor')
- mlp_down_grad: float32 [7680, 2560], P('tensor', 'wide')
The draws below stay inside these ranges and needn't reach their ends.
Inputs may be any that keep to these rules, and one draw needn't show every extreme that they name: `segment_ids`: along each sequence the ids start at 0 and rise by one at each of exactly 6 document starts. In one sequence, drawn from the seed, all starts lie within its first 128 or its last 128 tokens.
All inputs are finite; a program needn't handle non-finite values.
Results may differ from the reference program's by a relative error of at most 0.012.
Values may be sent and summed in bfloat16 or wider, within the bound.
A program may use at most 384 MiB of HBM per device.

```python
import jax
import jax.numpy as jnp
from jax import lax

D = 2560
FF = 7680
H = 10
BW = 256
CONV = 4
TOK_DEV = 128
SEQS = 2
BOUNDS = 6
LENGTH = 2048
N_WIDE = 16


def draw_segment_ids(key, part):
    key = jax.random.fold_in(key, 11)
    long_row = jax.random.randint(jax.random.fold_in(key, 1), (), 0, SEQS)
    columns = []
    for row in range(SEQS):
        row_draw = jax.random.fold_in(key, 100 + row)
        spread = jax.random.choice(row_draw, LENGTH - 1, (BOUNDS,), replace=False) + 1
        edges = jax.random.choice(jax.random.fold_in(row_draw, 7), 2 * TOK_DEV - 1, (BOUNDS,), replace=False)
        edge_pos = jnp.where(edges < TOK_DEV - 1, edges + 1, LENGTH - 2 * TOK_DEV + 1 + edges)
        starts = jnp.where(long_row == row, edge_pos, spread)
        flags = jnp.zeros((LENGTH,), jnp.int32).at[starts].set(1)
        columns.append(jnp.cumsum(flags).astype(jnp.int32))
    return jnp.stack(columns)


def draw_decay_rate(key, part):
    key = jax.random.fold_in(key, 23)
    slow = jax.random.uniform(jax.random.fold_in(key, 1), (H, BW), minval=-11.7, maxval=-10.0)
    fast = jax.random.uniform(jax.random.fold_in(key, 2), (H, BW), minval=-10.0, maxval=-3.8)
    share = 0.5
    pick = jax.random.uniform(jax.random.fold_in(key, 3), (H, BW)) < share
    return jnp.clip(jnp.where(pick, slow, fast), -11.5, -4.0).astype(jnp.bfloat16)


def block_scale(stream_key, extent, split, low, high):
    level, own = 1.0, jax.random.fold_in(stream_key, 6)
    for position, shards_of in split:
        heights = jnp.exp(jax.random.uniform(jax.random.fold_in(own, position), (shards_of,), jnp.float32, low / len(split), high / len(split)))
        level = level * jnp.repeat(heights, extent[position] // shards_of).reshape([-1 if axis == position else 1 for axis in range(len(extent))])
    return level


def bell_draw(own_key, shape, scale, reach, shards=(), kind=jnp.bfloat16):
    factor_of = block_scale(own_key, shape, shards, -0.22, 0.18) if shards else 1.0
    array = jax.random.normal(own_key, shape, jnp.float32) * scale * factor_of
    return jnp.minimum(jnp.maximum(array, -reach), reach).astype(kind)


def setup_inputs(seed: int = 0) -> dict:
    key_of = jax.random.split(jax.random.key(seed), 22)
    return {
        "block_in": bell_draw(key_of[0], (SEQS, LENGTH, D), 1.0, 6.0, ((1, 16),)),
        "segment_ids": draw_segment_ids(jax.random.fold_in(key_of[21], 71), 0),
        "cotangent": bell_draw(key_of[2], (SEQS, LENGTH, D), 1.0, 6.0, ((1, 16),)),
        "first_gain": jnp.clip(1.0 + 0.1 * jax.random.normal(key_of[3], (D,), jnp.float32), 0.5, 1.5).astype(jnp.bfloat16),
        "gelu_weight": bell_draw(key_of[4], (D, H, BW), D ** -0.5, 0.125, ((0, 16), (1, 2))),
        "gelu_bias": bell_draw(key_of[5], (H, BW), 0.5, 3.0, ((0, 2), (1, 16))),
        "input_weight": bell_draw(key_of[6], (D, H, BW), D ** -0.5, 0.125, ((0, 16), (1, 2))),
        "input_bias": bell_draw(key_of[7], (H, BW), 0.5, 3.0, ((0, 2), (1, 16))),
        "conv_weight": bell_draw(key_of[8], (CONV, H, BW), 0.5, 3.0, ((1, 2), (2, 16))),
        "conv_bias": bell_draw(key_of[9], (H, BW), 0.3, 2.0, ((0, 2), (1, 16))),
        "inlet_weight": bell_draw(key_of[10], (H, BW, BW), BW ** -0.5, 0.375, ((0, 2), (1, 16))),
        "inlet_bias": bell_draw(key_of[11], (H, BW), 0.5, 3.0, ((0, 2), (1, 16))),
        "forget_weight": bell_draw(key_of[12], (H, BW, BW), BW ** -0.5, 0.375, ((0, 2), (1, 16))),
        "forget_bias": bell_draw(key_of[13], (H, BW), 0.5, 3.0, ((0, 2), (1, 16))),
        "decay_rate": draw_decay_rate(jax.random.fold_in(key_of[21], 71), 0),
        "out_weight": bell_draw(key_of[15], (H, BW, D), (D // 4) ** -0.5, 0.25, ((0, 2), (2, 16))),
        "out_bias": bell_draw(key_of[16], (D,), 0.5, 3.0, ((0, 16),)),
        "second_gain": jnp.clip(1.0 + 0.1 * jax.random.normal(key_of[17], (D,), jnp.float32), 0.5, 1.5).astype(jnp.bfloat16),
        "mlp_gate": bell_draw(key_of[18], (D, FF), D ** -0.5, 0.125, ((0, 16), (1, 2))),
        "mlp_up": bell_draw(key_of[19], (D, FF), D ** -0.5, 0.125, ((0, 16), (1, 2))),
        "mlp_down": bell_draw(key_of[20], (FF, D), (FF // 4) ** -0.5, 0.125, ((0, 2), (1, 16))),
    }


@jax.custom_vjp
def low(v):
    return lax.optimization_barrier(v.astype(jnp.bfloat16)).astype(jnp.float32)

@jax.custom_vjp
def low_back(v):
    return v

def low_keep(v):
    return (low(v), None)

def low_pass(kept, grad):
    return (grad,)

def back_keep(v):
    return (v, None)

def back_low(kept, grad):
    return (low(grad),)
low.defvjp(low_keep, low_pass)
low_back.defvjp(back_keep, back_low)

def matmul(left, right):
    return jnp.dot(left, right, precision=lax.Precision.HIGHEST)

def rms_norm(values, gain):
    scale = lax.rsqrt(lax.optimization_barrier(jnp.mean(values * values, axis=-1, keepdims=True)) + 1e-06)
    return values * scale * gain

def causal_conv(values, segments, weight, bias):
    total = bias + weight[0] * values
    for offset in range(1, CONV):
        moved = jnp.pad(values, ((0, 0), (offset, 0), (0, 0)))[:, :-offset]
        moved_seg = jnp.pad(segments, ((0, 0), (offset, 0)), constant_values=-1)[:, :-offset]
        same = (moved_seg == segments)[..., None]
        total = total + jnp.where(same, weight[offset] * moved, 0.0)
    return total

def lru_terms(inlet_pre, forget_pre, conv_vals, rate, starts):
    inlet = jax.nn.sigmoid(inlet_pre)
    forget = jax.nn.sigmoid(forget_pre)
    log_decay = -8.0 * forget * jax.nn.softplus(rate)
    decay = jnp.where(starts, 0.0, jnp.exp(log_decay))
    scaler = jnp.where(starts, 1.0, jnp.sqrt(-jnp.expm1(2.0 * log_decay)))
    return (decay, scaler * inlet * conv_vals)

def recurrence(decay, drive):

    def step(carry, pair):
        carry = pair[0] * carry + pair[1]
        return (carry, carry)
    start = jnp.zeros_like(drive[:, 0])
    _, states = lax.scan(step, start, (jnp.moveaxis(decay, 1, 0), jnp.moveaxis(drive, 1, 0)))
    return jnp.moveaxis(states, 0, 1)

def forward(inputs, segments, first_gain, gelu_weight, gelu_bias, input_weight, input_bias, conv_weight, conv_bias, inlet_weight, inlet_bias, forget_weight, forget_bias, decay_rate, out_weight, out_bias, second_gain, mlp_gate, mlp_up, mlp_down):
    seq_count, length, width = inputs.shape
    channels = H * BW
    normed = low(rms_norm(inputs, first_gain))
    flat = normed.reshape(seq_count * length, width)
    gelu_pre = low_back(matmul(flat, gelu_weight.reshape(width, channels)) + gelu_bias.reshape(channels))
    gelu_branch = jax.nn.gelu(gelu_pre).reshape(seq_count, length, H, BW)
    input_branch = low(low_back(matmul(flat, input_weight.reshape(width, channels)) + input_bias.reshape(channels)))
    conv_out = low(causal_conv(input_branch.reshape(seq_count, length, channels), segments, conv_weight.reshape(CONV, channels), conv_bias.reshape(channels)))
    blocks = conv_out.reshape(seq_count, length, H, BW)
    inlet_pre = low_back(jnp.einsum('slhc,hcd->slhd', blocks, inlet_weight, precision=lax.Precision.HIGHEST) + inlet_bias)
    forget_pre = low_back(jnp.einsum('slhc,hcd->slhd', blocks, forget_weight, precision=lax.Precision.HIGHEST) + forget_bias)
    starts = jnp.concatenate([jnp.ones((seq_count, 1), bool), segments[:, 1:] != segments[:, :-1]], axis=1)
    decay, drive = lru_terms(inlet_pre, forget_pre, blocks, decay_rate, starts[:, :, None, None])
    state = recurrence(decay, drive)
    mixed = low(state * gelu_branch)
    branch = low_back(matmul(mixed.reshape(seq_count * length, channels), out_weight.reshape(channels, width)) + out_bias)
    resid = inputs + branch.reshape(seq_count, length, width)

    def feed(rows):
        second = low(rms_norm(rows, second_gain))
        gate_pre = low_back(matmul(second, mlp_gate))
        up_pre = low_back(matmul(second, mlp_up))
        hidden = low(jax.nn.gelu(gate_pre) * up_pre)
        return rows + low_back(matmul(hidden, mlp_down))
    pieces = resid.reshape(seq_count * N_WIDE, TOK_DEV, width)
    result = lax.map(jax.checkpoint(feed), pieces)
    return result.reshape(seq_count, length, width)

def reference(block_in, segment_ids, cotangent, first_gain, gelu_weight, gelu_bias, input_weight, input_bias, conv_weight, conv_bias, inlet_weight, inlet_bias, forget_weight, forget_bias, decay_rate, out_weight, out_bias, second_gain, mlp_gate, mlp_up, mlp_down):
    params = (first_gain, gelu_weight, gelu_bias, input_weight, input_bias, conv_weight, conv_bias, inlet_weight, inlet_bias, forget_weight, forget_bias, decay_rate, out_weight, out_bias, second_gain, mlp_gate, mlp_up, mlp_down)
    widened = tuple((value.astype(jnp.float32) for value in params))

    def run(inputs, *weights):
        return forward(inputs, segment_ids, *weights)
    result, pull = jax.vjp(run, block_in.astype(jnp.float32), *widened)
    grads = pull(cotangent.astype(jnp.float32))
    return (result.astype(jnp.bfloat16), grads[0], grads[1], grads[2], grads[3], grads[4], grads[5], grads[6], grads[7], grads[8], grads[9], grads[10], grads[11], grads[12], grads[13], grads[14], grads[15], grads[16], grads[17], grads[18])
```

```python
import functools

import jax
import jax.numpy as jnp
from jax import lax
from jax.experimental import pallas as pl
from jax.experimental.pallas import tpu as pltpu
from jax.sharding import PartitionSpec as P

CONV = 4
LANE = 128
GRANT = 60 * 1024 * 1024
F32 = jnp.float32
BF16 = jnp.bfloat16

LINE = 4


class Grid:
    def __init__(self):
        self.n = lax.axis_size("wide")
        self.hi = LINE
        self.inner_size = self.n // LINE
        self.tensor = lax.axis_size("tensor")
        self.w = lax.axis_index("wide")
        self.t = lax.axis_index("tensor")
        self.z = self.w // self.inner_size
        self.inner = lax.rem(self.w, self.inner_size)

    def flip(self, value, bit):
        return lax.ppermute(value, "wide", [(i, i ^ bit) for i in range(self.n)])

    def swap(self, value):
        size = self.tensor
        pairs = [(i, (i + 1) % size) for i in range(size)]
        return lax.ppermute(value, "tensor", pairs)


def shifted(shard, axis, by):
    size = lax.axis_size(axis)
    place = lax.axis_index(axis) - by
    there = jnp.logical_and(place >= 0, place < size)
    pairs = [(i, (i + by) % size) for i in range(size)]
    moved = lax.ppermute(shard, axis, pairs)
    return jax.tree.map(lambda a: jnp.where(there, a, jnp.zeros_like(a)), moved)


def pick(values, index, axis=0):
    return lax.dynamic_index_in_dim(values, index, axis, keepdims=False)


def reduce_small(grid, values):
    bit = grid.n // 2
    while bit:
        halves = values.reshape(2, bit, -1)
        mine = jnp.bitwise_and(lax.div(grid.w, bit), 1)
        got = grid.flip(pick(halves, 1 - mine), bit)
        values = pick(halves, mine) + got
        bit //= 2
    return values.reshape(-1)


def prefix_wide(grid, part, reverse):
    total = part
    entering = jnp.stack([jnp.ones_like(part[0]), jnp.zeros_like(part[1])])

    def joined(earlier, later):
        return jnp.stack([later[0] * earlier[0], later[0] * earlier[1] + later[1]])

    bit = 1
    while bit < grid.n:
        got = grid.flip(total, bit)
        set_here = jnp.bitwise_and(lax.div(grid.w, bit), 1) == 1
        after = jnp.logical_not(set_here) if reverse else set_here
        entering = jnp.where(after, joined(got, entering), entering)
        total = jnp.where(after, joined(got, total), joined(total, got))
        bit *= 2
    return entering[1]


def scan_kernel(reverse, a_ref, b_ref, cum_ref, out_ref):
    rows, width = a_ref.shape[1:]
    place = lax.broadcasted_iota(jnp.int32, (8, width), 0)
    tiles = rows // 8

    def one(i, carry):
        decay_in, state_in = carry
        tile = tiles - 1 - i if reverse else i
        at = pl.ds(pl.multiple_of(tile * 8, 8), 8)
        a = a_ref[0, at, :]
        b = b_ref[0, at, :]
        for by in (1, 2, 4):
            if reverse:
                moved_a = pltpu.roll(a, 8 - by, 0)
                moved_b = pltpu.roll(b, 8 - by, 0)
                ok = place < 8 - by
            else:
                moved_a = pltpu.roll(a, by, 0)
                moved_b = pltpu.roll(b, by, 0)
                ok = place >= by
            b = jnp.where(ok, a * moved_b + b, b)
            a = jnp.where(ok, a * moved_a, a)
        b = b + a * state_in
        a = a * decay_in
        cum_ref[0, at, :] = a
        out_ref[0, at, :] = b
        last = 0 if reverse else 7
        return (
            jnp.broadcast_to(a[last : last + 1], (8, width)),
            jnp.broadcast_to(b[last : last + 1], (8, width)),
        )

    start = (jnp.ones((8, width), F32), jnp.zeros((8, width), F32))
    lax.fori_loop(0, tiles, one, start)


def local_scan(decay, drive, reverse):
    seqs, rows, channels = decay.shape
    width = 256
    spec = pl.BlockSpec((1, rows, width), lambda s, c: (s, 0, c))
    shape = jax.ShapeDtypeStruct(decay.shape, F32)
    return pl.pallas_call(
        functools.partial(scan_kernel, reverse),
        grid=(seqs, channels // width),
        in_specs=[spec, spec],
        out_specs=[spec, spec],
        out_shape=[shape, shape],
        cost_estimate=pl.CostEstimate(
            flops=20 * decay.size, bytes_accessed=16 * decay.size, transcendentals=0
        ),
    )(decay, drive)


MESH = pl.DeviceIdType.MESH


class Spot:
    def __init__(self, n, tensor):
        self.n = n
        self.hi = LINE
        self.inner_size = n // LINE
        self.bits = [1 << i for i in range(self.inner_size.bit_length() - 1)]
        self.tensor = tensor
        self.w = lax.axis_index("wide")
        self.t = lax.axis_index("tensor")
        self.z = self.w // self.inner_size
        self.inner = lax.rem(self.w, self.inner_size)
        self.cross = {"tensor": lax.rem(self.t + 1, tensor)}

    def bit(self, which):
        return lax.rem(self.inner // which, 2)

    def flip(self, which):
        return {"wide": self.w + which - 2 * which * self.bit(which)}

    def line(self, place):
        return {"wide": place * self.inner_size + self.inner}

    def away(self, distance):
        return lax.rem(self.z + distance, self.hi)

    def greet(self, *sides):
        barrier = pltpu.get_barrier_semaphore()
        for side in sides:
            pl.semaphore_signal(barrier, inc=1, device_id=side, device_id_type=MESH)
        for distance in range(1, self.hi):
            pl.semaphore_signal(
                barrier, inc=1, device_id=self.line(self.away(distance)), device_id_type=MESH
            )
        pl.semaphore_wait(barrier, len(sides) + self.hi - 1)


def remote(src, dst, sems, index, side):
    return pltpu.make_async_remote_copy(
        src_ref=src,
        dst_ref=dst,
        send_sem=sems.at[0, index],
        recv_sem=sems.at[1, index],
        device_id=side,
        device_id_type=MESH,
    )


class Fans:
    def __init__(self, spot, at, sems, base, sides):
        self.spot, self.at, self.sems, self.base, self.sides = spot, at, sems, base, sides
        self.kinds = sorted(range(1 << len(sides)), key=lambda k: (bin(k).count("1"), -k))

    def onto(self, k):
        low = (k & -k) if k else 1 << len(self.sides)
        return [i for i in reversed(range(len(self.sides))) if (1 << i) < low]

    def copy(self, place, k, i, here=False):
        spot, hi = self.spot, self.spot.hi
        landed = k if here else k | (1 << i)
        index = self.base + (landed - 1) * hi + lax.rem(place - spot.z + hi, hi)
        ref = self.at(place, k)
        return remote(ref, ref, self.sems, index, self.sides[i])

    def hand_on(self, place, k):
        for i in self.onto(k):
            self.copy(place, k, i).start()

    def arrive(self, place, k):
        low = (k & -k).bit_length() - 1
        self.copy(place, k, low, here=True).wait_recv()

    def pass_on(self, place):
        for k in self.kinds:
            if k and self.onto(k):
                self.arrive(place, k)
                self.hand_on(place, k)

    def finish(self, place):
        for k in self.kinds:
            if k and not self.onto(k):
                self.arrive(place, k)
            for i in self.onto(k):
                self.copy(place, k, i).wait_send()

    def count(sides, hi):
        return ((1 << sides) - 1) * hi


class Chain:
    def __init__(self, spot, at, sems, sides):
        self.spot, self.at, self.sems = spot, at, sems
        self.fans = Fans(spot, at, sems, 2 * (spot.hi - 1), sides)

    def line_copy(self, s, up):
        spot, hi = self.spot, self.spot.hi
        owner = spot.z - (s - 1) if up else spot.z + (s - 1)
        other = spot.z + 1 if up else spot.z - 1
        ref = self.at(owner, 0)
        return remote(ref, ref, self.sems, (s - 1) if up else hi + s - 2, spot.line(other))

    def line_here(self, s, up):
        spot, hi = self.spot, self.spot.hi
        owner = spot.z - s if up else spot.z + s
        other = spot.z - 1 if up else spot.z + 1
        ref = self.at(owner, 0)
        return remote(ref, ref, self.sems, (s - 1) if up else hi + s - 2, spot.line(other))

    def first(self):
        spot, hi = self.spot, self.spot.hi

        @pl.when(spot.z < hi - 1)
        def _():
            self.line_copy(1, True).start()

        @pl.when(spot.z > 0)
        def _():
            self.line_copy(1, False).start()

        self.fans.hand_on(spot.z, 0)

    def onward(self, s):
        spot, hi = self.spot, self.spot.hi

        @pl.when(spot.z >= s)
        def _():
            self.line_here(s, True).wait_recv()

        if s < hi - 1:

            @pl.when(jnp.logical_and(spot.z >= s, spot.z < hi - 1))
            def _():
                self.line_copy(s + 1, True).start()

        @pl.when(spot.z >= s)
        def _():
            self.fans.hand_on(spot.z - s, 0)

        @pl.when(spot.z <= hi - 1 - s)
        def _():
            self.line_here(s, False).wait_recv()

        if s < hi - 1:

            @pl.when(jnp.logical_and(spot.z <= hi - 1 - s, spot.z > 0))
            def _():
                self.line_copy(s + 1, False).start()

        @pl.when(spot.z <= hi - 1 - s)
        def _():
            self.fans.hand_on(spot.z + s, 0)

    def places(self, s, act):
        spot = self.spot
        if s == 0:
            act(spot.z)
            return

        @pl.when(spot.z >= s)
        def _():
            act(spot.z - s)

        @pl.when(spot.z <= spot.hi - 1 - s)
        def _():
            act(spot.z + s)

    def second(self, s):
        self.places(s, self.fans.pass_on)

    def finish(self):
        spot, hi = self.spot, self.spot.hi
        for s in range(hi):
            self.places(s, self.fans.finish)
        for s in range(1, hi):

            @pl.when(jnp.logical_and(spot.z >= s - 1, spot.z < hi - 1))
            def _():
                self.line_copy(s, True).wait_send()

            @pl.when(jnp.logical_and(spot.z <= hi - s, spot.z > 0))
            def _():
                self.line_copy(s, False).wait_send()


def chain_sems(sides):
    return pltpu.SemaphoreType.DMA((2, 2 * (LINE - 1) + ((1 << sides) - 1) * LINE))


class Turns:
    def __init__(self, spot, window_of, at, sems, sides):
        self.spot, self.window_of, self.at, self.sems = spot, window_of, at, sems
        self.fans = Fans(spot, at, sems, spot.hi, sides)

    def line_copy(self, distance):
        spot = self.spot
        place = spot.away(distance)
        return remote(self.window_of(place), self.at(spot.z, 0), self.sems, distance, spot.line(place))

    def back(self, distance):
        return lax.rem(self.spot.z - distance + self.spot.hi, self.spot.hi)

    def line_here(self, distance):
        place = self.back(distance)
        ref = self.at(place, 0)
        return remote(ref, ref, self.sems, distance, self.spot.line(place))

    def first(self):
        for distance in range(1, self.spot.hi):
            self.line_copy(distance).start()
        self.fans.hand_on(self.spot.z, 0)

    def onward(self, distance):
        self.line_here(distance).wait_recv()
        self.fans.hand_on(self.back(distance), 0)

    def second(self, distance):
        self.fans.pass_on(self.back(distance))

    def finish(self):
        for distance in range(self.spot.hi):
            self.fans.finish(self.back(distance))
            if distance:
                self.line_copy(distance).wait_send()


def weights_kernel(
    n, tensor, rec, gates, feed, cot, rec_all, gates_all, feed_all, cot_all,
    rec_sems, gates_sems, feed_sems, cot_sems,
):
    del rec, gates, feed, cot
    spot = Spot(n, tensor)
    hi = spot.hi

    def index(place, k):
        return place * spot.inner_size + jnp.bitwise_xor(spot.inner, k)

    cube = [spot.flip(bit) for bit in spot.bits]
    moves = [
        Chain(spot, lambda place, k: gates_all.at[index(place, k)], gates_sems, cube),
        Chain(spot, lambda place, k: rec_all.at[:, index(place, k)], rec_sems, cube),
        Turns(
            spot,
            lambda place: feed_all.at[:, n + place],
            lambda place, k: feed_all.at[:, index(place, k)],
            feed_sems,
            cube,
        ),
        Chain(
            spot,
            lambda place, k: cot_all.at[place, lax.rem(spot.t + k, tensor)],
            cot_sems,
            [spot.cross],
        ),
    ]
    spot.greet(*cube, spot.cross)
    for move in moves:
        move.first()
    for s in range(1, hi):
        for move in moves:
            move.onward(s)
        for move in moves:
            move.second(s - 1)
    for move in moves:
        move.second(hi - 1)
    for move in moves:
        move.finish()


def blank(*shapes):
    return pl.pallas_call(
        lambda *refs: None,
        out_shape=[jax.ShapeDtypeStruct(shape, BF16) for shape in shapes],
        out_specs=[pl.BlockSpec(memory_space=pl.ANY)] * len(shapes),
        compiler_params=pltpu.CompilerParams(vmem_limit_bytes=GRANT),
        name="blank",
    )()


def bring_weights(grid, rec, gates, feed, cot):
    n, hi, tensor = grid.n, grid.hi, grid.tensor
    far = pl.BlockSpec(memory_space=pl.ANY)
    arrays = (rec, gates, feed, cot)
    cube = grid.inner_size.bit_length() - 1
    return pl.pallas_call(
        functools.partial(weights_kernel, n, tensor),
        out_shape=[jax.ShapeDtypeStruct(a.shape, a.dtype) for a in arrays],
        in_specs=[far] * 4,
        out_specs=[far] * 4,
        input_output_aliases={i: i for i in range(4)},
        scratch_shapes=[
            chain_sems(cube),
            chain_sems(cube),
            pltpu.SemaphoreType.DMA((2, grid.inner_size * hi)),
            chain_sems(1),
        ],
        compiler_params=pltpu.CompilerParams(
            collective_id=0, has_side_effects=True, vmem_limit_bytes=GRANT
        ),
        name="bring_weights",
    )(*arrays)


def by_rows(rows, step, act):
    def one(i, carry):
        act(pl.ds(pl.multiple_of(i * step, step), step))
        return carry

    lax.fori_loop(0, rows // step, one, 0)


STEP = 16


def second_kernel(n, tensor, part, inputs, shift, gain, resid, whole, held, out, got, swap_sems, sems):
    spot = Spot(n, tensor)
    rows = inputs.shape[0]

    def put(at):
        out[at, :] = part[1 - spot.t, at, :].astype(BF16)

    by_rows(rows, STEP, put)
    spot.greet(spot.cross)
    copy = remote(out, got, swap_sems, 0, spot.cross)
    copy.start()
    copy.wait()

    def norm(at):
        value = inputs[at, :] + (part[spot.t, at, :] + got[at, :].astype(F32) + shift[...])
        resid[at, :] = value
        scale = lax.rsqrt(jnp.mean(value * value, axis=-1, keepdims=True) + 1e-06)
        held[spot.z, spot.t, at, :] = (value * scale * gain[...]).astype(BF16)

    by_rows(rows, STEP, norm)
    chain = Chain(
        spot, lambda place, k: held.at[place, lax.rem(spot.t + k, tensor)], sems, [spot.cross]
    )
    chain.first()
    for s in range(1, spot.hi):
        chain.onward(s)
        chain.second(s - 1)
    chain.second(spot.hi - 1)
    chain.finish()
    for place in range(spot.hi):
        for side in range(tensor):

            def give(at, place=place, side=side):
                whole[place, side, at, :] = held[place, side, at, :]

            by_rows(rows, STEP, give)


def bring_second(grid, part, inputs, shift, gain):
    rows, width = inputs.shape
    near = pl.BlockSpec(memory_space=pltpu.VMEM)
    whole = (grid.hi, grid.tensor, rows, width)
    return pl.pallas_call(
        functools.partial(second_kernel, grid.n, grid.tensor),
        out_shape=[jax.ShapeDtypeStruct((rows, width), F32), jax.ShapeDtypeStruct(whole, BF16)],
        in_specs=[near] * 4,
        out_specs=[near] * 2,
        scratch_shapes=[
            pltpu.VMEM(whole, BF16),
            pltpu.VMEM((rows, width), BF16),
            pltpu.VMEM((rows, width), BF16),
            pltpu.SemaphoreType.DMA((2, 1)),
            chain_sems(1),
        ],
        compiler_params=pltpu.CompilerParams(
            collective_id=1, has_side_effects=True, vmem_limit_bytes=GRANT
        ),
        name="bring_second",
    )(part, inputs, shift, gain)


class Rows:
    def __init__(self, spot, part, out, got, line, cross_sems, line_sems):
        self.spot, self.part, self.out, self.got, self.line = spot, part, out, got, line
        self.cross_sems, self.line_sems = cross_sems, line_sems
        self.rows = out.shape[1]

    def place(self, k):
        spot, hi = self.spot, self.spot.hi
        last = hi - 1
        flipped = jnp.where(spot.z * 2 < hi, 0, 1)
        z = spot.z + flipped * (last - 2 * spot.z)
        if k == last:
            place = z
        else:
            place = jnp.where(k < last - z, last - k, k - (last - z))
        return place + flipped * (last - 2 * place)

    def cross_copy(self, place):
        return remote(
            self.out.at[place], self.got.at[place], self.cross_sems, place, self.spot.cross
        )

    def start(self):
        spot = self.spot
        for k in range(spot.hi):
            place = self.place(k)

            def put(at, place=place):
                self.out[place, at, :] = self.part[place, 1 - spot.t, at, :]

            by_rows(self.rows, STEP, put)
            self.cross_copy(place).start()

    def line_copy(self, s, up, here=False):
        spot, hi = self.spot, self.spot.hi
        slot = (s - 1) if up else hi + s - 2
        step = 1 if up != here else -1
        return remote(
            self.line.at[0, slot], self.line.at[1, slot], self.line_sems, slot, spot.line(spot.z + step)
        )

    def own(self, place, at):
        return self.part[place, self.spot.t, at, :].astype(F32) + self.got[place, at, :].astype(F32)

    def send(self, s, up):
        spot, hi = self.spot, self.spot.hi
        place = spot.z + hi - s if up else spot.z - hi + s
        slot = (s - 1) if up else hi + s - 2
        self.cross_copy(place).wait_recv()
        begins = spot.z == 0 if up else spot.z == hi - 1

        @pl.when(begins)
        def _():
            def put(at):
                self.line[0, slot, at, :] = self.own(place, at).astype(BF16)

            by_rows(self.rows, STEP, put)

        if s > 1:

            @pl.when(jnp.logical_not(begins))
            def _():
                self.line_copy(s - 1, up, here=True).wait_recv()

                def put(at):
                    before = self.line[1, slot - 1, at, :].astype(F32)
                    self.line[0, slot, at, :] = (self.own(place, at) + before).astype(BF16)

                by_rows(self.rows, STEP, put)

        self.line_copy(s, up).start()

    def sends_up(self, s):
        return self.spot.z <= s - 1

    def sends_down(self, s):
        return self.spot.z >= self.spot.hi - s

    def run(self, done):
        spot, hi = self.spot, self.spot.hi
        for s in range(1, hi):

            @pl.when(jnp.logical_and(self.sends_up(s), spot.z < hi - 1))
            def _():
                self.send(s, True)

            @pl.when(jnp.logical_and(self.sends_down(s), spot.z > 0))
            def _():
                self.send(s, False)

        self.cross_copy(spot.z).wait_recv()

        @pl.when(spot.z > 0)
        def _():
            self.line_copy(hi - 1, True, here=True).wait_recv()

        @pl.when(spot.z < hi - 1)
        def _():
            self.line_copy(hi - 1, False, here=True).wait_recv()

        def total(at):
            below = self.line[1, hi - 2, at, :].astype(F32)
            above = self.line[1, 2 * hi - 3, at, :].astype(F32)
            value = self.own(spot.z, at)
            value = value + jnp.where(spot.z > 0, below, 0.0)
            done(at, value + jnp.where(spot.z < hi - 1, above, 0.0))

        by_rows(self.rows, STEP, total)

    def finish(self):
        spot, hi = self.spot, self.spot.hi
        for place in range(hi):
            self.cross_copy(place).wait_send()
        for s in range(1, hi):

            @pl.when(jnp.logical_and(self.sends_up(s), spot.z < hi - 1))
            def _():
                self.line_copy(s, True).wait_send()

            @pl.when(jnp.logical_and(self.sends_down(s), spot.z > 0))
            def _():
                self.line_copy(s, False).wait_send()


def rows_kernel(
    second, n, tensor, part, resid, cot, gain, both, gain_grad,
    out, got, line, mine, other, cross_sems, line_sems, swap_sems,
):
    spot = Spot(n, tensor)
    sums = Rows(spot, part, out, got, line, cross_sems, line_sems)
    spot.greet(spot.cross)
    sums.start()
    if second:
        gain_grad[...] = jnp.zeros_like(gain_grad)

    def done(at, total):
        value = resid[at, :]
        if second:
            scale = lax.rsqrt(jnp.mean(value * value, axis=-1, keepdims=True) + 1e-06)
            turned = total * gain[...]
            inner = jnp.mean(turned * value, axis=-1, keepdims=True)
            grad = cot[at, :].astype(F32) + scale * turned - value * (scale * scale * scale * inner)
            gained = total * value * scale
            gain_grad[...] += jnp.sum(gained.reshape(2, 8, -1), axis=0)
            mine[at, :] = grad.astype(BF16)
        else:
            mine[at, :] = (value + total).astype(BF16)

    sums.run(done)
    copy = remote(mine, other, swap_sems, 0, spot.cross)
    copy.start()
    sums.finish()

    def keep(at):
        both[spot.t, at, :] = mine[at, :]

    by_rows(mine.shape[0], STEP, keep)
    copy.wait()

    def take(at):
        both[1 - spot.t, at, :] = other[at, :]

    by_rows(mine.shape[0], STEP, take)


def sum_rows(grid, second, part, resid, cot, gain):
    rows, width = resid.shape
    near = pl.BlockSpec(memory_space=pltpu.VMEM)
    hi, tensor = grid.hi, grid.tensor
    return pl.pallas_call(
        functools.partial(rows_kernel, second, grid.n, tensor),
        out_shape=[
            jax.ShapeDtypeStruct((tensor, rows, width), BF16),
            jax.ShapeDtypeStruct((8, width), F32),
        ],
        in_specs=[near] * 4,
        out_specs=[near] * 2,
        scratch_shapes=[
            pltpu.VMEM((hi, rows, width), BF16),
            pltpu.VMEM((hi, rows, width), BF16),
            pltpu.VMEM((2, 2 * (hi - 1), rows, width), BF16),
            pltpu.VMEM((rows, width), BF16),
            pltpu.VMEM((rows, width), BF16),
            pltpu.SemaphoreType.DMA((2, hi)),
            pltpu.SemaphoreType.DMA((2, 2 * (hi - 1))),
            pltpu.SemaphoreType.DMA((2, 1)),
        ],
        compiler_params=pltpu.CompilerParams(
            collective_id=2 if second else 3, has_side_effects=True, vmem_limit_bytes=GRANT
        ),
        name="sum_second" if second else "sum_feed",
    )(part, resid, cot, gain)


RING = 4


def tile_rows(rows):
    return 16 if rows % 16 == 0 else 8


def grads_kernel(n, tensor, spans, kept, *refs):
    count = len(spans)
    parts, apart, summed = refs[:count], refs[count], refs[count + 1]
    refs = refs[count + 2 :]
    stages = (n // LINE).bit_length() - 1
    sends, keeps, gots = refs[:stages], refs[stages : 2 * stages], refs[2 * stages : 3 * stages]
    ready, got_line, cube_sems, line_sems = refs[3 * stages :]
    spot = Spot(n, tensor)
    hi = spot.hi
    all_spans = sum(spans)
    units = all_spans * hi
    step = pl.program_id(0)
    rows = ready.shape[1]
    each = tile_rows(rows)

    def cube_copy(stage, unit):
        slot = lax.rem(unit, RING)
        return remote(
            sends[stage].at[slot],
            gots[stage].at[slot],
            cube_sems.at[stage],
            slot,
            spot.flip(spot.bits[stage]),
        )

    def line_copy(span, place, sender):
        return pltpu.make_async_remote_copy(
            src_ref=ready.at[span * hi + place],
            dst_ref=got_line.at[span, sender],
            send_sem=line_sems.at[0, span * hi + place],
            recv_sem=line_sems.at[1, span * hi + sender],
            device_id=spot.line(place),
            device_id_type=MESH,
        )

    @pl.when(step == 0)
    def _():
        spot.greet(*[spot.flip(bit) for bit in spot.bits])

    begin = 0
    for part, width in zip(parts, spans):
        first, begin = begin * hi, begin + width

        @pl.when(jnp.logical_and(step >= first, step < begin * hi))
        def _(part=part):
            slot = lax.rem(step, RING)

            @pl.when(step >= RING)
            def _():
                cube_copy(0, step - RING).wait_send()

            mine = spot.bit(1)
            for k in range(sends[0].shape[1]):

                def put(at, k=k):
                    sends[0][slot, k, at, :] = part[0, 2 * k + 1 - mine, at, :]
                    keeps[0][slot, k, at, :] = part[0, 2 * k + mine, at, :]

                by_rows(rows, each, put)
            cube_copy(0, step).start()

    for stage in range(stages):
        unit = step - stage - 1

        @pl.when(jnp.logical_and(unit >= 0, unit < units))
        def _(stage=stage, unit=unit):
            slot = lax.rem(unit, RING)
            cube_copy(stage, unit).wait_recv()

            def total(k, at):
                return (
                    keeps[stage][slot, k, at, :].astype(F32) + gots[stage][slot, k, at, :].astype(F32)
                ).astype(BF16)

            if stage < stages - 1:

                @pl.when(unit >= RING)
                def _():
                    cube_copy(stage + 1, unit - RING).wait_send()

                mine = spot.bit(spot.bits[stage + 1])
                for k in range(sends[stage + 1].shape[1]):

                    def put(at, k=k):
                        sends[stage + 1][slot, k, at, :] = total(2 * k + 1 - mine, at)
                        keeps[stage + 1][slot, k, at, :] = total(2 * k + mine, at)

                    by_rows(rows, each, put)
                cube_copy(stage + 1, unit).start()
            else:
                span, place = unit // hi, lax.rem(unit, hi)

                def put(at):
                    ready[unit, at, :] = total(0, at)

                by_rows(rows, each, put)

                @pl.when(place != spot.z)
                def _():
                    line_copy(span, place, spot.z).start()

    @pl.when(step == units + stages - 1)
    def _():
        for span in range(all_spans):
            for distance in range(1, hi):
                place = spot.away(distance)
                line_copy(span, place, place).wait_recv()
                line_copy(span, place, spot.z).wait_send()

            def give(at, span=span):
                own = ready[span * hi + spot.z, at, :]
                if span < kept:
                    for distance in range(hi):
                        place = spot.away(distance)
                        apart[span, place, at, :] = got_line[span, place, at, :] if distance else own
                else:
                    value = own.astype(F32)
                    for distance in range(1, hi):
                        value = value + got_line[span, spot.away(distance), at, :].astype(F32)
                    summed[span - kept, at, :] = value

            by_rows(rows, each, give)
        for stage in range(stages):
            for unit in range(units - RING, units):
                cube_copy(stage, unit).wait_send()


def send_grads(grid, parts, width, kept):
    hi, inner = grid.hi, grid.inner_size
    rows = parts[0].shape[0] // grid.n
    spans = [part.shape[1] // width for part in parts]
    all_spans = sum(spans)
    stages = inner.bit_length() - 1

    def part_spec(first, count):
        def index(i):
            unit = jnp.clip(i - first * hi, 0, count * hi - 1)
            return (lax.rem(unit, hi), 0, 0, unit // hi)

        return pl.BlockSpec((1, inner, rows, width), index)

    firsts = [sum(spans[:i]) for i in range(len(spans))]
    apart = (kept, hi, rows, width)
    summed = (all_spans - kept, rows, width)
    halves = [
        pltpu.VMEM((RING, inner >> (stage + 1), rows, width), BF16) for stage in range(stages)
    ]
    return pl.pallas_call(
        functools.partial(grads_kernel, grid.n, grid.tensor, spans, kept),
        grid=(all_spans * hi + stages,),
        out_shape=[jax.ShapeDtypeStruct(apart, BF16), jax.ShapeDtypeStruct(summed, F32)],
        in_specs=[part_spec(first, count) for first, count in zip(firsts, spans)],
        out_specs=[
            pl.BlockSpec(apart, lambda i: (0, 0, 0, 0)),
            pl.BlockSpec(summed, lambda i: (0, 0, 0)),
        ],
        scratch_shapes=halves * 3
        + [
            pltpu.VMEM((all_spans * hi, rows, width), BF16),
            pltpu.VMEM((all_spans, hi, rows, width), BF16),
            pltpu.SemaphoreType.DMA((stages, 2, RING)),
            pltpu.SemaphoreType.DMA((2, all_spans * hi)),
        ],
        compiler_params=pltpu.CompilerParams(
            collective_id=4, has_side_effects=True, vmem_limit_bytes=GRANT
        ),
        name="send_grads",
    )(*[part.reshape(hi, inner, rows, part.shape[1]) for part in parts])


def rms_norm(values, gain):
    scale = lax.rsqrt(jnp.mean(values * values, axis=-1, keepdims=True) + 1e-06)
    return values * scale * gain


def causal_conv(extended, marks, weight, bias):
    margin = weight.shape[0] - 1
    tok_count = extended.shape[1] - margin
    current = marks[:, margin:]
    total = bias + weight[0] * extended[:, margin:]
    for offset in range(1, margin + 1):
        moved = extended[:, margin - offset : margin - offset + tok_count]
        same = (marks[:, margin - offset : margin - offset + tok_count] == current)[..., None]
        total = total + jnp.where(same, weight[offset] * moved, 0.0)
    return total


def lru_terms(inlet_pre, forget_pre, conv_vals, rate, starts):
    inlet = jax.nn.sigmoid(inlet_pre)
    forget = jax.nn.sigmoid(forget_pre)
    log_decay = -8.0 * forget * jax.nn.softplus(rate)
    decay = jnp.where(starts, 0.0, jnp.exp(log_decay))
    scaler = jnp.where(starts, 1.0, jnp.sqrt(-jnp.expm1(2.0 * log_decay)))
    return (decay, scaler * inlet * conv_vals)


def gelu_product(gate_pre, up_pre):
    return jax.nn.gelu(gate_pre) * up_pre


def dot(left, right):
    return jnp.dot(left, right, preferred_element_type=F32)


def dot_nt(left, right):
    return jnp.einsum("ik,jk->ij", left, right, preferred_element_type=F32)


def dot_tn(left, right):
    return jnp.einsum("ki,kj->ij", left, right, preferred_element_type=F32)


def local(
    block_in,
    segment_ids,
    cotangent,
    first_gain,
    gelu_weight,
    gelu_bias,
    input_weight,
    input_bias,
    conv_weight,
    conv_bias,
    inlet_weight,
    inlet_bias,
    forget_weight,
    forget_bias,
    decay_rate,
    out_weight,
    out_bias,
    second_gain,
    mlp_gate,
    mlp_up,
    mlp_down,
):
    grid = Grid()
    seq_count, tok_count, width = block_in.shape
    head_count, block_size = gelu_weight.shape[1:]
    channels = head_count * block_size
    margin = CONV - 1
    rows_all = seq_count * tok_count
    rows_half = rows_all // grid.tensor
    d_own = gelu_weight.shape[0]
    lane_own = gelu_bias.shape[1]
    units = mlp_gate.shape[1]
    unit_tiles = units // LANE
    window_tiles = -(-unit_tiles // grid.hi)
    window = window_tiles * LANE

    rec_own = jnp.stack(
        [
            input_weight.reshape(d_own, channels),
            gelu_weight.reshape(d_own, channels),
            out_weight.reshape(channels, d_own).T,
        ]
    )
    gates_own = jnp.stack([inlet_weight, forget_weight]).reshape(-1, block_size)
    thin_own = jnp.concatenate(
        [
            v.reshape(-1)
            for v in (
                first_gain,
                out_bias,
                second_gain,
                gelu_bias,
                input_bias,
                conv_weight,
                conv_bias,
                inlet_bias,
                forget_bias,
                decay_rate,
            )
        ]
    )
    gate_rows = gates_own.shape[0]
    thin_size = thin_own.size
    thin_rows = -(-thin_size // block_size)
    spare = -(gate_rows + thin_rows) % 16
    thin_own = jnp.pad(thin_own, (0, (thin_rows + spare) * block_size - thin_size))
    gates_own = jnp.concatenate([gates_own, thin_own.reshape(-1, block_size)])
    feed_own = jnp.stack([mlp_gate, mlp_up, mlp_down.T])
    feed_windows = jnp.stack(
        [
            feed_own[:, :, tile * LANE : tile * LANE + window]
            for tile in (
                min(place * window_tiles, unit_tiles - window_tiles) for place in range(grid.hi)
            )
        ],
        axis=1,
    )
    cot_rows = cotangent.reshape(grid.tensor, rows_half, width)
    cot_own = pick(cot_rows, grid.t)
    rec_all, gates_all, feed_all, cot_all = blank(
        (3, grid.n, d_own, channels),
        (grid.n,) + gates_own.shape,
        (3, grid.n + grid.hi, d_own, window),
        (grid.hi, grid.tensor, rows_half, width),
    )
    rec_all = lax.dynamic_update_slice(rec_all, rec_own[:, None], (0, grid.w, 0, 0))
    gates_all = lax.dynamic_update_slice(gates_all, gates_own[None], (grid.w, 0, 0))
    feed_all = lax.dynamic_update_slice(feed_all, feed_windows, (0, grid.n, 0, 0))
    feed_all = lax.dynamic_update_slice(
        feed_all, lax.dynamic_slice_in_dim(feed_windows, grid.z, 1, 1), (0, grid.w, 0, 0)
    )
    cot_all = lax.dynamic_update_slice(cot_all, cot_own[None, None], (grid.z, grid.t, 0, 0))
    rec_all, gates_all, feed_all, cot_all = bring_weights(
        grid, rec_all, gates_all, feed_all, cot_all
    )
    feed_all = feed_all[:, : grid.n]
    rec_all = rec_all.reshape(3, width, channels)
    input_full, gelu_full, out_turned = rec_all[0], rec_all[1], rec_all[2]
    thin_all = gates_all[:, gate_rows:].reshape(grid.n, -1)[:, :thin_size]
    gates_all = gates_all[:, :gate_rows]
    gates_all = (
        gates_all.reshape(grid.n, 2, head_count, lane_own, block_size)
        .transpose(1, 2, 0, 3, 4)
        .reshape(2, head_count, block_size, block_size)
    )
    inlet_full, forget_full = gates_all[0], gates_all[1]

    thin_all = thin_all.astype(F32)
    gain_first, out_shift, gain_second = (
        thin_all[:, i * d_own : (i + 1) * d_own].reshape(width) for i in range(3)
    )
    per = head_count * lane_own
    lane_rows = (
        thin_all[:, 3 * d_own :]
        .reshape(grid.n, CONV + 6, head_count, lane_own)
        .transpose(1, 2, 0, 3)
        .reshape(CONV + 6, channels)
    )
    gelu_shift, input_shift = lane_rows[0], lane_rows[1]
    conv_taps = lane_rows[2 : 2 + CONV]
    conv_offset, inlet_shift, forget_shift, rate_wide = (lane_rows[2 + CONV + i] for i in range(4))
    inlet_shift = inlet_shift.reshape(head_count, block_size)
    forget_shift = forget_shift.reshape(head_count, block_size)
    rate_wide = rate_wide.reshape(head_count, block_size)

    feed_all = feed_all.reshape(3, width, window)
    gate_full, up_full, down_turned = feed_all[0], feed_all[1], feed_all[2]
    first_tile = jnp.minimum(grid.z * window_tiles, unit_tiles - window_tiles)
    unit_place = lax.iota(jnp.int32, window) + first_tile * LANE
    valid = (unit_place >= grid.z * window)[None, :]

    inputs = block_in.astype(F32).reshape(rows_all, width)
    normed = rms_norm(inputs, gain_first).astype(BF16)
    input_pre = dot(normed, input_full) + input_shift
    input_branch = input_pre.astype(BF16).reshape(seq_count, tok_count, channels)
    marks = (segment_ids + 1).astype(BF16)
    rim_values, rim_marks = shifted(
        (input_branch[:, tok_count - margin :], marks[:, tok_count - margin :]), "wide", 1
    )
    extended = jnp.concatenate([rim_values, input_branch], axis=1).astype(F32)
    marks_ext = jnp.concatenate([rim_marks, marks], axis=1).astype(F32)
    conv_out = causal_conv(extended, marks_ext, conv_taps, conv_offset)
    blocks = conv_out.astype(BF16).reshape(seq_count, tok_count, head_count, block_size)
    inlet_pre = (
        jnp.einsum("sthc,hcd->sthd", blocks, inlet_full, preferred_element_type=F32) + inlet_shift
    )
    forget_pre = (
        jnp.einsum("sthc,hcd->sthd", blocks, forget_full, preferred_element_type=F32) + forget_shift
    )
    starts = (marks_ext[:, margin:] != marks_ext[:, margin - 1 : margin - 1 + tok_count])[
        :, :, None, None
    ]
    blocks_wide = blocks.astype(F32)
    decay, drive = lru_terms(inlet_pre, forget_pre, blocks_wide, rate_wide, starts)
    flat = (seq_count, tok_count, channels)
    decay_cum, local_state = local_scan(decay.reshape(flat), drive.reshape(flat), False)
    gelu_pre = dot(normed, gelu_full) + gelu_shift
    gelu_branch = jax.nn.gelu(gelu_pre).reshape(flat)
    state_in = prefix_wide(grid, jnp.stack([decay_cum[:, -1], local_state[:, -1]]), False)
    state = local_state + decay_cum * state_in[:, None]
    mixed = (state * gelu_branch).astype(BF16).reshape(rows_all, channels)
    branch_part = dot_nt(mixed, out_turned).reshape(grid.tensor, rows_half, width)
    own_inputs = pick(inputs.reshape(grid.tensor, rows_half, width), grid.t)
    resid, second_all = bring_second(
        grid, branch_part, own_inputs, out_shift[None], gain_second[None]
    )

    rows_feed = grid.hi * rows_all
    second_all = second_all.reshape(rows_feed, width)
    cot_all = cot_all.reshape(rows_feed, width)
    gate_pre = dot(second_all, gate_full)
    up_pre = dot(second_all, up_full)
    product, pull_feed = jax.vjp(gelu_product, gate_pre, up_pre)
    hidden = jnp.where(valid, product, 0.0).astype(BF16)
    hidden_grad = jnp.where(valid, dot(cot_all, down_turned), 0.0)
    gate_pre_grad, up_pre_grad = pull_feed(hidden_grad)
    gate_low = gate_pre_grad.astype(BF16)
    up_low = up_pre_grad.astype(BF16)
    second_part = dot_nt(gate_low, gate_full) + dot_nt(up_low, up_full)
    shape_rows = (grid.hi, grid.tensor, rows_half, width)
    branch_low, gain_two_grad = sum_rows(
        grid, True, second_part.astype(BF16).reshape(shape_rows), resid, cot_own, gain_second[None]
    )
    branch_low = branch_low.reshape(rows_all, width)
    gain_two_grad = jnp.sum(gain_two_grad, axis=0)
    gain_two_grad = gain_two_grad + grid.swap(gain_two_grad)
    feed_part = dot_nt(hidden, down_turned).astype(BF16)
    block_out, _ = sum_rows(
        grid, False, feed_part.reshape(shape_rows), resid, cot_own, gain_second[None]
    )
    block_out = block_out.reshape(block_in.shape)
    pair_grad = dot_tn(second_all, jnp.concatenate([gate_low, up_low], axis=1)).astype(BF16)
    down_grad = dot_tn(cot_all, hidden).astype(BF16)

    out_shift_grad = jnp.sum(branch_low.astype(F32), axis=0)
    mixed_grad = dot(branch_low, out_turned).reshape(flat)
    out_grad = dot_tn(branch_low, mixed).astype(BF16)
    state_grad = mixed_grad * gelu_branch
    _, pull_gelu = jax.vjp(jax.nn.gelu, gelu_pre)
    (gelu_pre_grad,) = pull_gelu((mixed_grad * state).reshape(rows_all, channels))
    gelu_low = gelu_pre_grad.astype(BF16)
    gelu_b_grad = jnp.sum(gelu_low.astype(F32), axis=0)
    decay_flat = decay.reshape(flat)
    next_decay = jnp.concatenate([decay_flat[:, 1:], jnp.ones_like(decay_flat[:, :1])], axis=1)
    tail_decay, local_carried = local_scan(next_decay, state_grad, True)
    head_decay = decay_flat[:, 0]
    from_right = prefix_wide(
        grid,
        jnp.stack([head_decay * tail_decay[:, 0], head_decay * local_carried[:, 0]]),
        True,
    )
    carried = (local_carried + tail_decay * from_right[:, None]).reshape(blocks.shape)
    prev_state = jnp.concatenate([state_in[:, None], state[:, :-1]], axis=1).reshape(blocks.shape)

    def lru_local(inlet_arg, forget_arg, block_arg, rate_arg):
        return lru_terms(inlet_arg, forget_arg, block_arg, rate_arg, starts)

    _, pull_lru = jax.vjp(lru_local, inlet_pre, forget_pre, blocks_wide, rate_wide)
    inlet_grad, forget_grad, block_direct, rate_grad = pull_lru((carried * prev_state, carried))
    inlet_low = inlet_grad.astype(BF16)
    forget_low = forget_grad.astype(BF16)
    inlet_b_grad = jnp.sum(inlet_low.astype(F32), axis=(0, 1))
    forget_b_grad = jnp.sum(forget_low.astype(F32), axis=(0, 1))
    gate_w_grads = jnp.stack(
        [
            jnp.einsum("sthc,sthd->hcd", blocks, low, preferred_element_type=F32)
            for low in (inlet_low, forget_low)
        ]
    )
    gate_w_grads = (
        gate_w_grads.reshape(2, head_count, grid.n, lane_own, block_size)
        .transpose(2, 0, 1, 3, 4)
        .reshape(width, block_size)
        .astype(BF16)
    )
    conv_grad = (
        block_direct
        + jnp.einsum("sthd,hcd->sthc", inlet_low, inlet_full, preferred_element_type=F32)
        + jnp.einsum("sthd,hcd->sthc", forget_low, forget_full, preferred_element_type=F32)
    )

    def conv_local(ext_arg, taps_arg, offset_arg):
        return causal_conv(ext_arg, marks_ext, taps_arg, offset_arg)

    _, pull_conv = jax.vjp(conv_local, extended, conv_taps, conv_offset)
    ext_grad, taps_grad, offset_grad = pull_conv(conv_grad.reshape(flat))
    rim_grad = shifted(ext_grad[:, :margin], "wide", -1)
    branch_input_grad = ext_grad[:, margin:] + jnp.concatenate(
        [jnp.zeros((seq_count, tok_count - margin, channels), F32), rim_grad], axis=1
    )
    input_low = branch_input_grad.astype(BF16).reshape(rows_all, channels)
    both_grad = dot_tn(normed, jnp.concatenate([gelu_low, input_low], axis=1)).astype(BF16)
    rec_grad = jnp.concatenate([both_grad, out_grad, gate_w_grads], axis=1)
    feed_grads, rec_grads = send_grads(grid, (pair_grad, down_grad, rec_grad), window, 3)
    rec_grads = jnp.concatenate(list(rec_grads), axis=1)
    gelu_w_grad = rec_grads[:, :channels]
    input_w_grad = rec_grads[:, channels : 2 * channels]
    out_grad = rec_grads[:, 2 * channels : 3 * channels]
    gate_w_grads = rec_grads[:, 3 * channels :].reshape(2, head_count, lane_own, block_size)

    def feed_weight_grad(got):
        pieces = []
        for place in range(grid.hi):
            begin = min(place * window_tiles, unit_tiles - window_tiles)
            skip = min(place * window_tiles - begin, window_tiles)
            if skip < window_tiles:
                pieces.append(got[place, :, skip * LANE :])
        return jnp.concatenate(pieces, axis=1).astype(F32)

    gate_grad, up_grad, down_grad = (feed_weight_grad(got) for got in feed_grads)
    down_grad = down_grad.T
    input_b_grad = jnp.sum(input_low.astype(F32), axis=0)
    first_part = (dot_nt(input_low, input_full) + dot_nt(gelu_low, gelu_full)).astype(BF16)
    first_grad = first_part.astype(F32) + grid.swap(first_part).astype(F32)
    _, pull_first = jax.vjp(rms_norm, inputs, gain_first)
    input_norm_grad, gain_one_grad = pull_first(first_grad)
    block_grad = (branch_low.astype(F32) + input_norm_grad).reshape(block_in.shape)

    lane_grads = jnp.stack(
        [
            v.reshape(channels)
            for v in (
                gelu_b_grad,
                input_b_grad,
                taps_grad[0],
                taps_grad[1],
                taps_grad[2],
                taps_grad[3],
                offset_grad,
                inlet_b_grad,
                forget_b_grad,
                rate_grad,
            )
        ]
    )
    lane_grads = (
        lane_grads.reshape(CONV + 6, head_count, grid.n, lane_own)
        .transpose(2, 0, 1, 3)
        .reshape(grid.n, -1)
    )
    thin_grads = jnp.concatenate(
        [v.reshape(grid.n, d_own) for v in (gain_one_grad, out_shift_grad, gain_two_grad)]
        + [lane_grads],
        axis=1,
    )
    thin = reduce_small(grid, thin_grads)
    gain_one_own, out_shift_own, gain_two_own = (
        thin[i * d_own : (i + 1) * d_own] for i in range(3)
    )
    lanes = thin[3 * d_own :].reshape(CONV + 6, head_count, lane_own)
    weight_shape = gelu_weight.shape
    return (
        block_out,
        block_grad,
        gain_one_own,
        gelu_w_grad.reshape(weight_shape),
        lanes[0],
        input_w_grad.reshape(weight_shape),
        lanes[1],
        lanes[2 : 2 + CONV],
        lanes[2 + CONV],
        gate_w_grads[0],
        lanes[3 + CONV],
        gate_w_grads[1],
        lanes[4 + CONV],
        lanes[5 + CONV],
        out_grad.T.reshape(out_weight.shape),
        out_shift_own,
        gain_two_own,
        gate_grad,
        up_grad,
        down_grad,
    )


def solution(mesh):
    in_specs = (
        P(None, "wide", None),
        P(None, "wide"),
        P(None, "wide", None),
        P("wide"),
        P("wide", "tensor", None),
        P("tensor", "wide"),
        P("wide", "tensor", None),
        P("tensor", "wide"),
        P(None, "tensor", "wide"),
        P("tensor", "wide"),
        P("tensor", "wide", None),
        P("tensor", "wide"),
        P("tensor", "wide", None),
        P("tensor", "wide"),
        P("tensor", "wide"),
        P("tensor", None, "wide"),
        P("wide"),
        P("wide"),
        P("wide", "tensor"),
        P("wide", "tensor"),
        P("tensor", "wide"),
    )
    out_specs = (
        P(None, "wide", None),
        P(None, "wide", None),
        P("wide"),
        P("wide", "tensor", None),
        P("tensor", "wide"),
        P("wide", "tensor", None),
        P("tensor", "wide"),
        P(None, "tensor", "wide"),
        P("tensor", "wide"),
        P("tensor", "wide", None),
        P("tensor", "wide"),
        P("tensor", "wide", None),
        P("tensor", "wide"),
        P("tensor", "wide"),
        P("tensor", None, "wide"),
        P("wide"),
        P("wide"),
        P("wide", "tensor"),
        P("wide", "tensor"),
        P("tensor", "wide"),
    )
    return jax.shard_map(local, mesh=mesh, in_specs=in_specs, out_specs=out_specs, check_vma=False)
```

```python
import functools

import jax
import jax.numpy as jnp
from jax import lax
from jax.experimental import pallas as pl
from jax.experimental.pallas import tpu as pltpu
from jax.sharding import PartitionSpec as P

CONV = 4
LANE = 128
GRANT = 60 * 1024 * 1024
F32 = jnp.float32
BF16 = jnp.bfloat16

LINE = 4


class Grid:
    def __init__(self):
        self.n = lax.axis_size("wide")
        self.hi = LINE
        self.inner_size = self.n // LINE
        self.tensor = lax.axis_size("tensor")
        self.w = lax.axis_index("wide")
        self.t = lax.axis_index("tensor")
        self.z = self.w // self.inner_size
        self.inner = lax.rem(self.w, self.inner_size)

    def flip(self, value, bit):
        return lax.ppermute(value, "wide", [(i, i ^ bit) for i in range(self.n)])

    def swap(self, value):
        size = self.tensor
        pairs = [(i, (i + 1) % size) for i in range(size)]
        return lax.ppermute(value, "tensor", pairs)


def shifted(shard, axis, by):
    size = lax.axis_size(axis)
    place = lax.axis_index(axis) - by
    there = jnp.logical_and(place >= 0, place < size)
    pairs = [(i, (i + by) % size) for i in range(size)]
    moved = lax.ppermute(shard, axis, pairs)
    return jax.tree.map(lambda a: jnp.where(there, a, jnp.zeros_like(a)), moved)


def pick(values, index, axis=0):
    return lax.dynamic_index_in_dim(values, index, axis, keepdims=False)


def prefix_wide(grid, part, reverse):
    total = part
    entering = jnp.stack([jnp.ones_like(part[0]), jnp.zeros_like(part[1])])

    def joined(earlier, later):
        return jnp.stack([later[0] * earlier[0], later[0] * earlier[1] + later[1]])

    bit = 1
    while bit < grid.n:
        got = grid.flip(total, bit)
        set_here = jnp.bitwise_and(lax.div(grid.w, bit), 1) == 1
        after = jnp.logical_not(set_here) if reverse else set_here
        entering = jnp.where(after, joined(got, entering), entering)
        total = jnp.where(after, joined(got, total), joined(total, got))
        bit *= 2
    return entering[1]


def scan_kernel(reverse, a_ref, b_ref, cum_ref, out_ref):
    rows, width = a_ref.shape[1:]
    place = lax.broadcasted_iota(jnp.int32, (8, width), 0)
    tiles = rows // 8

    def one(i, carry):
        decay_in, state_in = carry
        tile = tiles - 1 - i if reverse else i
        at = pl.ds(pl.multiple_of(tile * 8, 8), 8)
        a = a_ref[0, at, :]
        b = b_ref[0, at, :]
        for by in (1, 2, 4):
            if reverse:
                moved_a = pltpu.roll(a, 8 - by, 0)
                moved_b = pltpu.roll(b, 8 - by, 0)
                ok = place < 8 - by
            else:
                moved_a = pltpu.roll(a, by, 0)
                moved_b = pltpu.roll(b, by, 0)
                ok = place >= by
            b = jnp.where(ok, a * moved_b + b, b)
            a = jnp.where(ok, a * moved_a, a)
        b = b + a * state_in
        a = a * decay_in
        cum_ref[0, at, :] = a
        out_ref[0, at, :] = b
        last = 0 if reverse else 7
        return (
            jnp.broadcast_to(a[last : last + 1], (8, width)),
            jnp.broadcast_to(b[last : last + 1], (8, width)),
        )

    start = (jnp.ones((8, width), F32), jnp.zeros((8, width), F32))
    lax.fori_loop(0, tiles, one, start)


def local_scan(decay, drive, reverse):
    seqs, rows, channels = decay.shape
    width = 256
    spec = pl.BlockSpec((1, rows, width), lambda s, c: (s, 0, c))
    shape = jax.ShapeDtypeStruct(decay.shape, F32)
    return pl.pallas_call(
        functools.partial(scan_kernel, reverse),
        grid=(seqs, channels // width),
        in_specs=[spec, spec],
        out_specs=[spec, spec],
        out_shape=[shape, shape],
        cost_estimate=pl.CostEstimate(
            flops=20 * decay.size, bytes_accessed=16 * decay.size, transcendentals=0
        ),
    )(decay, drive)


MESH = pl.DeviceIdType.MESH


class Spot:
    def __init__(self, n, tensor):
        self.n = n
        self.hi = LINE
        self.inner_size = n // LINE
        self.bits = [1 << i for i in range(self.inner_size.bit_length() - 1)]
        self.tensor = tensor
        self.w = lax.axis_index("wide")
        self.t = lax.axis_index("tensor")
        self.z = self.w // self.inner_size
        self.inner = lax.rem(self.w, self.inner_size)
        self.cross = {"tensor": lax.rem(self.t + 1, tensor)}

    def bit(self, which):
        return lax.rem(self.inner // which, 2)

    def flip(self, which):
        return {"wide": self.w + which - 2 * which * self.bit(which)}

    def line(self, place):
        return {"wide": place * self.inner_size + self.inner}

    def away(self, distance):
        return lax.rem(self.z + distance, self.hi)

    def greet(self, *sides):
        barrier = pltpu.get_barrier_semaphore()
        for side in sides:
            pl.semaphore_signal(barrier, inc=1, device_id=side, device_id_type=MESH)
        for distance in range(1, self.hi):
            pl.semaphore_signal(
                barrier, inc=1, device_id=self.line(self.away(distance)), device_id_type=MESH
            )
        pl.semaphore_wait(barrier, len(sides) + self.hi - 1)


def remote(src, dst, sems, index, side):
    return pltpu.make_async_remote_copy(
        src_ref=src,
        dst_ref=dst,
        send_sem=sems.at[0, index],
        recv_sem=sems.at[1, index],
        device_id=side,
        device_id_type=MESH,
    )


class Fans:
    def __init__(self, spot, at, sems, base, sides):
        self.spot, self.at, self.sems, self.base, self.sides = spot, at, sems, base, sides
        self.kinds = sorted(range(1 << len(sides)), key=lambda k: (bin(k).count("1"), -k))

    def onto(self, k):
        low = (k & -k) if k else 1 << len(self.sides)
        return [i for i in reversed(range(len(self.sides))) if (1 << i) < low]

    def copy(self, place, k, i, here=False):
        spot, hi = self.spot, self.spot.hi
        landed = k if here else k | (1 << i)
        index = self.base + (landed - 1) * hi + lax.rem(place - spot.z + hi, hi)
        ref = self.at(place, k)
        return remote(ref, ref, self.sems, index, self.sides[i])

    def hand_on(self, place, k):
        for i in self.onto(k):
            self.copy(place, k, i).start()

    def arrive(self, place, k):
        low = (k & -k).bit_length() - 1
        self.copy(place, k, low, here=True).wait_recv()

    def pass_on(self, place):
        for k in self.kinds:
            if k and self.onto(k):
                self.arrive(place, k)
                self.hand_on(place, k)

    def finish(self, place):
        for k in self.kinds:
            if k and not self.onto(k):
                self.arrive(place, k)
            for i in self.onto(k):
                self.copy(place, k, i).wait_send()

    def count(sides, hi):
        return ((1 << sides) - 1) * hi


class Chain:
    def __init__(self, spot, at, sems, sides):
        self.spot, self.at, self.sems = spot, at, sems
        self.fans = Fans(spot, at, sems, 2 * (spot.hi - 1), sides)

    def line_copy(self, s, up):
        spot, hi = self.spot, self.spot.hi
        owner = spot.z - (s - 1) if up else spot.z + (s - 1)
        other = spot.z + 1 if up else spot.z - 1
        ref = self.at(owner, 0)
        return remote(ref, ref, self.sems, (s - 1) if up else hi + s - 2, spot.line(other))

    def line_here(self, s, up):
        spot, hi = self.spot, self.spot.hi
        owner = spot.z - s if up else spot.z + s
        other = spot.z - 1 if up else spot.z + 1
        ref = self.at(owner, 0)
        return remote(ref, ref, self.sems, (s - 1) if up else hi + s - 2, spot.line(other))

    def first(self):
        spot, hi = self.spot, self.spot.hi

        @pl.when(spot.z < hi - 1)
        def _():
            self.line_copy(1, True).start()

        @pl.when(spot.z > 0)
        def _():
            self.line_copy(1, False).start()

        self.fans.hand_on(spot.z, 0)

    def onward(self, s):
        spot, hi = self.spot, self.spot.hi

        @pl.when(spot.z >= s)
        def _():
            self.line_here(s, True).wait_recv()

        if s < hi - 1:

            @pl.when(jnp.logical_and(spot.z >= s, spot.z < hi - 1))
            def _():
                self.line_copy(s + 1, True).start()

        @pl.when(spot.z >= s)
        def _():
            self.fans.hand_on(spot.z - s, 0)

        @pl.when(spot.z <= hi - 1 - s)
        def _():
            self.line_here(s, False).wait_recv()

        if s < hi - 1:

            @pl.when(jnp.logical_and(spot.z <= hi - 1 - s, spot.z > 0))
            def _():
                self.line_copy(s + 1, False).start()

        @pl.when(spot.z <= hi - 1 - s)
        def _():
            self.fans.hand_on(spot.z + s, 0)

    def places(self, s, act):
        spot = self.spot
        if s == 0:
            act(spot.z)
            return

        @pl.when(spot.z >= s)
        def _():
            act(spot.z - s)

        @pl.when(spot.z <= spot.hi - 1 - s)
        def _():
            act(spot.z + s)

    def second(self, s):
        self.places(s, self.fans.pass_on)

    def finish(self):
        spot, hi = self.spot, self.spot.hi
        for s in range(hi):
            self.places(s, self.fans.finish)
        for s in range(1, hi):

            @pl.when(jnp.logical_and(spot.z >= s - 1, spot.z < hi - 1))
            def _():
                self.line_copy(s, True).wait_send()

            @pl.when(jnp.logical_and(spot.z <= hi - s, spot.z > 0))
            def _():
                self.line_copy(s, False).wait_send()


def chain_sems(sides):
    return pltpu.SemaphoreType.DMA((2, 2 * (LINE - 1) + ((1 << sides) - 1) * LINE))


class Turns:
    def __init__(self, spot, window_of, at, sems, sides):
        self.spot, self.window_of, self.at, self.sems = spot, window_of, at, sems
        self.fans = Fans(spot, at, sems, spot.hi, sides)

    def line_copy(self, distance):
        spot = self.spot
        place = spot.away(distance)
        return remote(self.window_of(place), self.at(spot.z, 0), self.sems, distance, spot.line(place))

    def back(self, distance):
        return lax.rem(self.spot.z - distance + self.spot.hi, self.spot.hi)

    def line_here(self, distance):
        place = self.back(distance)
        ref = self.at(place, 0)
        return remote(ref, ref, self.sems, distance, self.spot.line(place))

    def first(self):
        for distance in range(1, self.spot.hi):
            self.line_copy(distance).start()
        self.fans.hand_on(self.spot.z, 0)

    def onward(self, distance):
        self.line_here(distance).wait_recv()
        self.fans.hand_on(self.back(distance), 0)

    def second(self, distance):
        self.fans.pass_on(self.back(distance))

    def finish(self):
        for distance in range(self.spot.hi):
            self.fans.finish(self.back(distance))
            if distance:
                self.line_copy(distance).wait_send()


def weights_kernel(
    n, tensor, rec, gates, feed, cot, rec_all, gates_all, feed_all, cot_all,
    rec_sems, gates_sems, feed_sems, cot_sems,
):
    del rec, gates, feed, cot
    spot = Spot(n, tensor)
    hi = spot.hi

    def index(place, k):
        return place * spot.inner_size + jnp.bitwise_xor(spot.inner, k)

    cube = [spot.flip(bit) for bit in spot.bits]
    moves = [
        Chain(spot, lambda place, k: gates_all.at[index(place, k)], gates_sems, cube),
        Chain(spot, lambda place, k: rec_all.at[:, index(place, k)], rec_sems, cube),
        Turns(
            spot,
            lambda place: feed_all.at[:, n + place],
            lambda place, k: feed_all.at[:, index(place, k)],
            feed_sems,
            cube,
        ),
        Chain(
            spot,
            lambda place, k: cot_all.at[place, lax.rem(spot.t + k, tensor)],
            cot_sems,
            [spot.cross],
        ),
    ]
    spot.greet(*cube, spot.cross)
    for move in moves:
        move.first()
    for s in range(1, hi):
        for move in moves:
            move.onward(s)
        for move in moves:
            move.second(s - 1)
    for move in moves:
        move.second(hi - 1)
    for move in moves:
        move.finish()


def blank(*shapes):
    return pl.pallas_call(
        lambda *refs: None,
        out_shape=[jax.ShapeDtypeStruct(shape, BF16) for shape in shapes],
        out_specs=[pl.BlockSpec(memory_space=pl.ANY)] * len(shapes),
        compiler_params=pltpu.CompilerParams(vmem_limit_bytes=GRANT),
        name="blank",
    )()


def bring_weights(grid, rec, gates, feed, cot):
    n, hi, tensor = grid.n, grid.hi, grid.tensor
    far = pl.BlockSpec(memory_space=pl.ANY)
    arrays = (rec, gates, feed, cot)
    cube = grid.inner_size.bit_length() - 1
    return pl.pallas_call(
        functools.partial(weights_kernel, n, tensor),
        out_shape=[jax.ShapeDtypeStruct(a.shape, a.dtype) for a in arrays],
        in_specs=[far] * 4,
        out_specs=[far] * 4,
        input_output_aliases={i: i for i in range(4)},
        scratch_shapes=[
            chain_sems(cube),
            chain_sems(cube),
            pltpu.SemaphoreType.DMA((2, grid.inner_size * hi)),
            chain_sems(1),
        ],
        compiler_params=pltpu.CompilerParams(
            collective_id=0, has_side_effects=True, vmem_limit_bytes=GRANT
        ),
        name="bring_weights",
    )(*arrays)


def by_rows(rows, step, act):
    def one(i, carry):
        act(pl.ds(pl.multiple_of(i * step, step), step))
        return carry

    lax.fori_loop(0, rows // step, one, 0)


STEP = 16


def second_kernel(n, tensor, part, inputs, shift, gain, resid, whole, held, out, got, swap_sems, sems):
    spot = Spot(n, tensor)
    rows = inputs.shape[0]

    def put(at):
        out[at, :] = part[1 - spot.t, at, :].astype(BF16)

    by_rows(rows, STEP, put)
    spot.greet(spot.cross)
    copy = remote(out, got, swap_sems, 0, spot.cross)
    copy.start()
    copy.wait()

    def norm(at):
        value = inputs[at, :] + (part[spot.t, at, :] + got[at, :].astype(F32) + shift[...])
        resid[at, :] = value
        scale = lax.rsqrt(jnp.mean(value * value, axis=-1, keepdims=True) + 1e-06)
        held[spot.z, spot.t, at, :] = (value * scale * gain[...]).astype(BF16)

    by_rows(rows, STEP, norm)
    chain = Chain(
        spot, lambda place, k: held.at[place, lax.rem(spot.t + k, tensor)], sems, [spot.cross]
    )
    chain.first()
    for s in range(1, spot.hi):
        chain.onward(s)
        chain.second(s - 1)
    chain.second(spot.hi - 1)
    chain.finish()
    for place in range(spot.hi):
        for side in range(tensor):

            def give(at, place=place, side=side):
                whole[place, side, at, :] = held[place, side, at, :]

            by_rows(rows, STEP, give)


def bring_second(grid, part, inputs, shift, gain):
    rows, width = inputs.shape
    near = pl.BlockSpec(memory_space=pltpu.VMEM)
    whole = (grid.hi, grid.tensor, rows, width)
    return pl.pallas_call(
        functools.partial(second_kernel, grid.n, grid.tensor),
        out_shape=[jax.ShapeDtypeStruct((rows, width), F32), jax.ShapeDtypeStruct(whole, BF16)],
        in_specs=[near] * 4,
        out_specs=[near] * 2,
        scratch_shapes=[
            pltpu.VMEM(whole, BF16),
            pltpu.VMEM((rows, width), BF16),
            pltpu.VMEM((rows, width), BF16),
            pltpu.SemaphoreType.DMA((2, 1)),
            chain_sems(1),
        ],
        compiler_params=pltpu.CompilerParams(
            collective_id=1, has_side_effects=True, vmem_limit_bytes=GRANT
        ),
        name="bring_second",
    )(part, inputs, shift, gain)


class Rows:
    def __init__(self, spot, part, out, got, line, cross_sems, line_sems):
        self.spot, self.part, self.out, self.got, self.line = spot, part, out, got, line
        self.cross_sems, self.line_sems = cross_sems, line_sems
        self.rows = out.shape[1]

    def place(self, k):
        spot, hi = self.spot, self.spot.hi
        last = hi - 1
        flipped = jnp.where(spot.z * 2 < hi, 0, 1)
        z = spot.z + flipped * (last - 2 * spot.z)
        if k == last:
            place = z
        else:
            place = jnp.where(k < last - z, last - k, k - (last - z))
        return place + flipped * (last - 2 * place)

    def cross_copy(self, place):
        return remote(
            self.out.at[place], self.got.at[place], self.cross_sems, place, self.spot.cross
        )

    def start(self):
        spot = self.spot
        for k in range(spot.hi):
            place = self.place(k)

            def put(at, place=place):
                self.out[place, at, :] = self.part[place, 1 - spot.t, at, :]

            by_rows(self.rows, STEP, put)
            self.cross_copy(place).start()

    def line_copy(self, s, up, here=False):
        spot, hi = self.spot, self.spot.hi
        slot = (s - 1) if up else hi + s - 2
        step = 1 if up != here else -1
        return remote(
            self.line.at[0, slot], self.line.at[1, slot], self.line_sems, slot, spot.line(spot.z + step)
        )

    def own(self, place, at):
        return self.part[place, self.spot.t, at, :].astype(F32) + self.got[place, at, :].astype(F32)

    def send(self, s, up):
        spot, hi = self.spot, self.spot.hi
        place = spot.z + hi - s if up else spot.z - hi + s
        slot = (s - 1) if up else hi + s - 2
        self.cross_copy(place).wait_recv()
        begins = spot.z == 0 if up else spot.z == hi - 1

        @pl.when(begins)
        def _():
            def put(at):
                self.line[0, slot, at, :] = self.own(place, at).astype(BF16)

            by_rows(self.rows, STEP, put)

        if s > 1:

            @pl.when(jnp.logical_not(begins))
            def _():
                self.line_copy(s - 1, up, here=True).wait_recv()

                def put(at):
                    before = self.line[1, slot - 1, at, :].astype(F32)
                    self.line[0, slot, at, :] = (self.own(place, at) + before).astype(BF16)

                by_rows(self.rows, STEP, put)

        self.line_copy(s, up).start()

    def sends_up(self, s):
        return self.spot.z <= s - 1

    def sends_down(self, s):
        return self.spot.z >= self.spot.hi - s

    def run(self, done):
        spot, hi = self.spot, self.spot.hi
        for s in range(1, hi):

            @pl.when(jnp.logical_and(self.sends_up(s), spot.z < hi - 1))
            def _():
                self.send(s, True)

            @pl.when(jnp.logical_and(self.sends_down(s), spot.z > 0))
            def _():
                self.send(s, False)

        self.cross_copy(spot.z).wait_recv()

        @pl.when(spot.z > 0)
        def _():
            self.line_copy(hi - 1, True, here=True).wait_recv()

        @pl.when(spot.z < hi - 1)
        def _():
            self.line_copy(hi - 1, False, here=True).wait_recv()

        def total(at):
            below = self.line[1, hi - 2, at, :].astype(F32)
            above = self.line[1, 2 * hi - 3, at, :].astype(F32)
            value = self.own(spot.z, at)
            value = value + jnp.where(spot.z > 0, below, 0.0)
            done(at, value + jnp.where(spot.z < hi - 1, above, 0.0))

        by_rows(self.rows, STEP, total)

    def finish(self):
        spot, hi = self.spot, self.spot.hi
        for place in range(hi):
            self.cross_copy(place).wait_send()
        for s in range(1, hi):

            @pl.when(jnp.logical_and(self.sends_up(s), spot.z < hi - 1))
            def _():
                self.line_copy(s, True).wait_send()

            @pl.when(jnp.logical_and(self.sends_down(s), spot.z > 0))
            def _():
                self.line_copy(s, False).wait_send()


def rows_kernel(
    second, n, tensor, part, resid, cot, gain, both, gain_grad,
    out, got, line, mine, other, cross_sems, line_sems, swap_sems,
):
    spot = Spot(n, tensor)
    sums = Rows(spot, part, out, got, line, cross_sems, line_sems)
    spot.greet(spot.cross)
    sums.start()
    if second:
        gain_grad[...] = jnp.zeros_like(gain_grad)

    def done(at, total):
        value = resid[at, :]
        if second:
            scale = lax.rsqrt(jnp.mean(value * value, axis=-1, keepdims=True) + 1e-06)
            turned = total * gain[...]
            inner = jnp.mean(turned * value, axis=-1, keepdims=True)
            grad = cot[at, :].astype(F32) + scale * turned - value * (scale * scale * scale * inner)
            gained = total * value * scale
            gain_grad[...] += jnp.sum(gained.reshape(2, 8, -1), axis=0)
            mine[at, :] = grad.astype(BF16)
        else:
            mine[at, :] = (value + total).astype(BF16)

    sums.run(done)
    copy = remote(mine, other, swap_sems, 0, spot.cross)
    copy.start()
    sums.finish()

    def keep(at):
        both[spot.t, at, :] = mine[at, :]

    by_rows(mine.shape[0], STEP, keep)
    copy.wait()

    def take(at):
        both[1 - spot.t, at, :] = other[at, :]

    by_rows(mine.shape[0], STEP, take)


def sum_rows(grid, second, part, resid, cot, gain):
    rows, width = resid.shape
    near = pl.BlockSpec(memory_space=pltpu.VMEM)
    hi, tensor = grid.hi, grid.tensor
    return pl.pallas_call(
        functools.partial(rows_kernel, second, grid.n, tensor),
        out_shape=[
            jax.ShapeDtypeStruct((tensor, rows, width), BF16),
            jax.ShapeDtypeStruct((8, width), F32),
        ],
        in_specs=[near] * 4,
        out_specs=[near] * 2,
        scratch_shapes=[
            pltpu.VMEM((hi, rows, width), BF16),
            pltpu.VMEM((hi, rows, width), BF16),
            pltpu.VMEM((2, 2 * (hi - 1), rows, width), BF16),
            pltpu.VMEM((rows, width), BF16),
            pltpu.VMEM((rows, width), BF16),
            pltpu.SemaphoreType.DMA((2, hi)),
            pltpu.SemaphoreType.DMA((2, 2 * (hi - 1))),
            pltpu.SemaphoreType.DMA((2, 1)),
        ],
        compiler_params=pltpu.CompilerParams(
            collective_id=2 if second else 3, has_side_effects=True, vmem_limit_bytes=GRANT
        ),
        name="sum_second" if second else "sum_feed",
    )(part, resid, cot, gain)


RING = 4


def tile_rows(rows):
    return 16 if rows % 16 == 0 else 8


def grads_kernel(
    n, tensor, spans, kept,
    second, cot, normed, branch, gate_low, up_low, hidden, gelu_low, input_low, mixed, gates, first, thin,
    apart, summed, first_other, thin_own, *refs,
):
    stages = (n // LINE).bit_length() - 1
    lists = [refs[i * stages : (i + 1) * stages] for i in range(6)]
    sends, keeps, gots, thin_sends, thin_keeps, thin_gots = lists
    (
        made, ready, got_line, first_out, first_got, thin_ready, thin_line,
        cube_sems, line_sems, first_sems, thin_sems, thin_line_sems,
    ) = refs[6 * stages :]
    spot = Spot(n, tensor)
    hi = spot.hi
    all_spans = len(spans)
    units = all_spans * hi
    step = pl.program_id(0)
    rows = ready.shape[1]
    each = tile_rows(rows)
    last_step = units + stages - 1
    sources = {
        "gate": (second, gate_low),
        "up": (second, up_low),
        "down": (cot, hidden),
        "gelu": (normed, gelu_low),
        "input": (normed, input_low),
        "out": (branch, mixed),
    }

    def cube_copy(stage, unit):
        slot = lax.rem(unit, RING)
        return remote(
            sends[stage].at[slot],
            gots[stage].at[slot],
            cube_sems.at[stage],
            slot,
            spot.flip(spot.bits[stage]),
        )

    def line_copy(span, place, sender):
        return pltpu.make_async_remote_copy(
            src_ref=ready.at[span * hi + place],
            dst_ref=got_line.at[span, sender],
            send_sem=line_sems.at[0, span * hi + place],
            recv_sem=line_sems.at[1, span * hi + sender],
            device_id=spot.line(place),
            device_id_type=MESH,
        )

    def thin_copy(stage):
        return remote(
            thin_sends[stage], thin_gots[stage], thin_sems, stage, spot.flip(spot.bits[stage])
        )

    def thin_line_copy(place, sender):
        return pltpu.make_async_remote_copy(
            src_ref=thin_ready.at[place],
            dst_ref=thin_line.at[sender],
            send_sem=thin_line_sems.at[0, place],
            recv_sem=thin_line_sems.at[1, sender],
            device_id=spot.line(place),
            device_id_type=MESH,
        )

    first_copy = remote(first_out, first_got, first_sems, 0, spot.cross)

    @pl.when(step == 0)
    def _():
        spot.greet(*[spot.flip(bit) for bit in spot.bits], spot.cross)

        def put(at):
            first_out[at, :] = first[at, :]

        by_rows(first.shape[0], STEP, put)
        first_copy.start()
        mine = spot.bit(1)
        for place in range(hi):
            for k in range(thin_sends[0].shape[1]):
                thin_sends[0][place, k] = thin[place, 2 * k + 1 - mine]
                thin_keeps[0][place, k] = thin[place, 2 * k + mine]
        thin_copy(0).start()

    for stage in range(stages):

        @pl.when(step == stage + 1)
        def _(stage=stage):
            thin_copy(stage).wait_recv()
            if stage < stages - 1:
                mine = spot.bit(spot.bits[stage + 1])
                for place in range(hi):
                    for k in range(thin_sends[stage + 1].shape[1]):
                        a, b = 2 * k + 1 - mine, 2 * k + mine
                        thin_sends[stage + 1][place, k] = (
                            thin_keeps[stage][place, a] + thin_gots[stage][place, a]
                        )
                        thin_keeps[stage + 1][place, k] = (
                            thin_keeps[stage][place, b] + thin_gots[stage][place, b]
                        )
                thin_copy(stage + 1).start()
            else:
                for place in range(hi):
                    thin_ready[place] = thin_keeps[stage][place, 0] + thin_gots[stage][place, 0]
                for distance in range(1, hi):
                    thin_line_copy(spot.away(distance), spot.z).start()

    @pl.when(step < units)
    def _():
        slot = lax.rem(step, RING)

        @pl.when(step >= RING)
        def _():
            cube_copy(0, step - RING).wait_send()

        for span, pieces in enumerate(spans):

            @pl.when(step // hi == span)
            def _(pieces=pieces):
                for name, begin, width, to in pieces:
                    if name == "gates":

                        def put(at, width=width, to=to):
                            made[at, to : to + width] = gates[0, at, :].astype(made.dtype)

                        by_rows(made.shape[0], STEP, put)
                        continue
                    left, right = sources[name]

                    def one(j, carry, left=left, right=right, begin=begin, width=width, to=to):
                        at = pl.ds(pl.multiple_of(j * LANE, LANE), LANE)
                        made[at, to : to + width] = lax.dot_general(
                            left[:, at],
                            right[:, begin : begin + width],
                            (((0,), (0,)), ((), ())),
                            preferred_element_type=F32,
                        ).astype(made.dtype)
                        return carry

                    lax.fori_loop(0, made.shape[0] // LANE, one, 0)

        mine = spot.bit(1)
        for k in range(sends[0].shape[1]):

            def put(at, k=k):
                def block(i):
                    at_made = pl.ds(pl.multiple_of(i * rows + at.start, each), each)
                    return made[at_made, :].astype(BF16)

                sends[0][slot, k, at, :] = block(2 * k + 1 - mine)
                keeps[0][slot, k, at, :] = block(2 * k + mine)

            by_rows(rows, each, put)
        cube_copy(0, step).start()

    for stage in range(stages):
        unit = step - stage - 1

        @pl.when(jnp.logical_and(unit >= 0, unit < units))
        def _(stage=stage, unit=unit):
            slot = lax.rem(unit, RING)
            cube_copy(stage, unit).wait_recv()

            def total(k, at):
                return (
                    keeps[stage][slot, k, at, :].astype(F32) + gots[stage][slot, k, at, :].astype(F32)
                ).astype(BF16)

            if stage < stages - 1:

                @pl.when(unit >= RING)
                def _():
                    cube_copy(stage + 1, unit - RING).wait_send()

                mine = spot.bit(spot.bits[stage + 1])
                for k in range(sends[stage + 1].shape[1]):

                    def put(at, k=k):
                        sends[stage + 1][slot, k, at, :] = total(2 * k + 1 - mine, at)
                        keeps[stage + 1][slot, k, at, :] = total(2 * k + mine, at)

                    by_rows(rows, each, put)
                cube_copy(stage + 1, unit).start()
            else:
                span, place = unit // hi, lax.rem(unit, hi)

                def put(at):
                    ready[unit, at, :] = total(0, at)

                by_rows(rows, each, put)

                @pl.when(place != spot.z)
                def _():
                    line_copy(span, place, spot.z).start()

    @pl.when(step == last_step)
    def _():
        for span in range(all_spans):
            for distance in range(1, hi):
                place = spot.away(distance)
                line_copy(span, place, place).wait_recv()
                line_copy(span, place, spot.z).wait_send()

            def give(at, span=span):
                own = ready[span * hi + spot.z, at, :]
                if span < kept:
                    for distance in range(hi):
                        place = spot.away(distance)
                        apart[span, place, at, :] = got_line[span, place, at, :] if distance else own
                else:
                    value = own.astype(F32)
                    for distance in range(1, hi):
                        value = value + got_line[span, spot.away(distance), at, :].astype(F32)
                    summed[span - kept, at, :] = value

            by_rows(rows, each, give)
        for stage in range(stages):
            for unit in range(units - RING, units):
                cube_copy(stage, unit).wait_send()
            thin_copy(stage).wait_send()
        value = thin_ready[spot.z]
        for distance in range(1, hi):
            place = spot.away(distance)
            thin_line_copy(place, place).wait_recv()
            thin_line_copy(place, spot.z).wait_send()
            value = value + thin_line[place]
        thin_own[...] = value
        first_copy.wait()

        def take(at):
            first_other[at, :] = first_got[at, :]

        by_rows(first.shape[0], STEP, take)


def column_spans(widths, width):
    spans, here, room = [], [], width
    for name, size in widths:
        begin = 0
        while begin < size:
            count = min(size - begin, room)
            here.append((name, begin, count, width - room))
            begin, room = begin + count, room - count
            if room == 0:
                spans, here, room = spans + [here], [], width
    assert not here
    return spans


def send_grads(grid, feed, rec, gates, first, thin):
    hi, inner = grid.hi, grid.inner_size
    second, cot, gate_low, up_low, hidden = feed
    normed, branch, gelu_low, input_low, mixed = rec
    d = second.shape[1]
    rows = d // grid.n
    slab = d // hi
    width = gate_low.shape[1]
    kept = 3
    channels = mixed.shape[1]
    spans = column_spans([(name, width) for name in ("gate", "up", "down")], width) + column_spans(
        [(name, channels) for name in ("gelu", "input", "out")] + [("gates", gates.shape[1])], width
    )
    all_spans = len(spans)
    units = all_spans * hi
    stages = inner.bit_length() - 1

    def place_of(i):
        return lax.rem(jnp.minimum(i, units - 1), hi)

    def slab_of(a):
        return pl.BlockSpec((a.shape[0], slab), lambda i: (0, place_of(i)))

    def whole(a):
        zeros = (0,) * a.ndim
        return pl.BlockSpec(a.shape, lambda i: zeros, pipeline_mode=pl.Buffered(1))

    apart = jax.ShapeDtypeStruct((kept, hi, rows, width), BF16)
    summed = jax.ShapeDtypeStruct((all_spans - kept, rows, width), F32)
    other = jax.ShapeDtypeStruct(first.shape, BF16)
    thin = thin.reshape(hi, inner, 8, thin.shape[1] // 8)
    thin_shape = thin.shape[2:]
    thin_own = jax.ShapeDtypeStruct(thin_shape, F32)
    outs = [apart, summed, other, thin_own]

    def halves(lead, tail, kind):
        return [
            pltpu.VMEM((lead, inner >> (stage + 1)) + tail, kind) for stage in range(stages)
        ]

    gates = gates.reshape(hi, slab, gates.shape[1])
    return pl.pallas_call(
        functools.partial(grads_kernel, grid.n, grid.tensor, spans, kept),
        grid=(units + stages,),
        out_shape=outs,
        in_specs=[slab_of(a) for a in (second, cot, normed, branch)]
        + [whole(a) for a in (gate_low, up_low, hidden, gelu_low, input_low, mixed)]
        + [pl.BlockSpec((1,) + gates.shape[1:], lambda i: (place_of(i), 0, 0))]
        + [whole(first), whole(thin)],
        out_specs=[whole(a) for a in outs],
        scratch_shapes=halves(RING, (rows, width), BF16) * 3
        + halves(hi, thin_shape, F32) * 3
        + [
            pltpu.VMEM((slab, width), BF16 if rows % 16 == 0 else F32),
            pltpu.VMEM((units, rows, width), BF16),
            pltpu.VMEM((all_spans, hi, rows, width), BF16),
            pltpu.VMEM(first.shape, BF16),
            pltpu.VMEM(first.shape, BF16),
            pltpu.VMEM((hi,) + thin_shape, F32),
            pltpu.VMEM((hi,) + thin_shape, F32),
            pltpu.SemaphoreType.DMA((stages, 2, RING)),
            pltpu.SemaphoreType.DMA((2, units)),
            pltpu.SemaphoreType.DMA((2, 1)),
            pltpu.SemaphoreType.DMA((2, stages)),
            pltpu.SemaphoreType.DMA((2, hi)),
        ],
        compiler_params=pltpu.CompilerParams(
            collective_id=4, has_side_effects=True, vmem_limit_bytes=GRANT
        ),
        name="send_grads",
    )(
        second, cot, normed, branch, gate_low, up_low, hidden, gelu_low, input_low, mixed, gates,
        first, thin,
    )


def rms_norm(values, gain):
    scale = lax.rsqrt(jnp.mean(values * values, axis=-1, keepdims=True) + 1e-06)
    return values * scale * gain


def causal_conv(extended, marks, weight, bias):
    margin = weight.shape[0] - 1
    tok_count = extended.shape[1] - margin
    current = marks[:, margin:]
    total = bias + weight[0] * extended[:, margin:]
    for offset in range(1, margin + 1):
        moved = extended[:, margin - offset : margin - offset + tok_count]
        same = (marks[:, margin - offset : margin - offset + tok_count] == current)[..., None]
        total = total + jnp.where(same, weight[offset] * moved, 0.0)
    return total


def lru_terms(inlet_pre, forget_pre, conv_vals, rate, starts):
    inlet = jax.nn.sigmoid(inlet_pre)
    forget = jax.nn.sigmoid(forget_pre)
    log_decay = -8.0 * forget * jax.nn.softplus(rate)
    decay = jnp.where(starts, 0.0, jnp.exp(log_decay))
    scaler = jnp.where(starts, 1.0, jnp.sqrt(-jnp.expm1(2.0 * log_decay)))
    return (decay, scaler * inlet * conv_vals)


def gelu_product(gate_pre, up_pre):
    return jax.nn.gelu(gate_pre) * up_pre


def dot(left, right):
    return jnp.dot(left, right, preferred_element_type=F32)


def dot_nt(left, right):
    return jnp.einsum("ik,jk->ij", left, right, preferred_element_type=F32)


def dot_tn(left, right):
    return jnp.einsum("ki,kj->ij", left, right, preferred_element_type=F32)


def local(
    block_in,
    segment_ids,
    cotangent,
    first_gain,
    gelu_weight,
    gelu_bias,
    input_weight,
    input_bias,
    conv_weight,
    conv_bias,
    inlet_weight,
    inlet_bias,
    forget_weight,
    forget_bias,
    decay_rate,
    out_weight,
    out_bias,
    second_gain,
    mlp_gate,
    mlp_up,
    mlp_down,
):
    grid = Grid()
    seq_count, tok_count, width = block_in.shape
    head_count, block_size = gelu_weight.shape[1:]
    channels = head_count * block_size
    margin = CONV - 1
    rows_all = seq_count * tok_count
    rows_half = rows_all // grid.tensor
    d_own = gelu_weight.shape[0]
    lane_own = gelu_bias.shape[1]
    units = mlp_gate.shape[1]
    unit_tiles = units // LANE
    window_tiles = -(-unit_tiles // grid.hi)
    window = window_tiles * LANE

    rec_own = jnp.stack(
        [
            input_weight.reshape(d_own, channels),
            gelu_weight.reshape(d_own, channels),
            out_weight.reshape(channels, d_own).T,
        ]
    )
    gates_own = jnp.stack([inlet_weight, forget_weight]).reshape(-1, block_size)
    thin_own = jnp.concatenate(
        [
            v.reshape(-1)
            for v in (
                first_gain,
                out_bias,
                second_gain,
                gelu_bias,
                input_bias,
                conv_weight,
                conv_bias,
                inlet_bias,
                forget_bias,
                decay_rate,
            )
        ]
    )
    gate_rows = gates_own.shape[0]
    thin_size = thin_own.size
    thin_rows = -(-thin_size // block_size)
    spare = -(gate_rows + thin_rows) % 16
    thin_own = jnp.pad(thin_own, (0, (thin_rows + spare) * block_size - thin_size))
    gates_own = jnp.concatenate([gates_own, thin_own.reshape(-1, block_size)])
    feed_own = jnp.stack([mlp_gate, mlp_up, mlp_down.T])
    feed_windows = jnp.stack(
        [
            feed_own[:, :, tile * LANE : tile * LANE + window]
            for tile in (
                min(place * window_tiles, unit_tiles - window_tiles) for place in range(grid.hi)
            )
        ],
        axis=1,
    )
    cot_rows = cotangent.reshape(grid.tensor, rows_half, width)
    cot_own = pick(cot_rows, grid.t)
    rec_all, gates_all, feed_all, cot_all = blank(
        (3, grid.n, d_own, channels),
        (grid.n,) + gates_own.shape,
        (3, grid.n + grid.hi, d_own, window),
        (grid.hi, grid.tensor, rows_half, width),
    )
    rec_all = lax.dynamic_update_slice(rec_all, rec_own[:, None], (0, grid.w, 0, 0))
    gates_all = lax.dynamic_update_slice(gates_all, gates_own[None], (grid.w, 0, 0))
    feed_all = lax.dynamic_update_slice(feed_all, feed_windows, (0, grid.n, 0, 0))
    feed_all = lax.dynamic_update_slice(
        feed_all, lax.dynamic_slice_in_dim(feed_windows, grid.z, 1, 1), (0, grid.w, 0, 0)
    )
    cot_all = lax.dynamic_update_slice(cot_all, cot_own[None, None], (grid.z, grid.t, 0, 0))
    rec_all, gates_all, feed_all, cot_all = bring_weights(
        grid, rec_all, gates_all, feed_all, cot_all
    )
    feed_all = feed_all[:, : grid.n]
    rec_all = rec_all.reshape(3, width, channels)
    input_full, gelu_full, out_turned = rec_all[0], rec_all[1], rec_all[2]
    thin_all = gates_all[:, gate_rows:].reshape(grid.n, -1)[:, :thin_size]
    gates_all = gates_all[:, :gate_rows]
    gates_all = (
        gates_all.reshape(grid.n, 2, head_count, lane_own, block_size)
        .transpose(1, 2, 0, 3, 4)
        .reshape(2, head_count, block_size, block_size)
    )
    inlet_full, forget_full = gates_all[0], gates_all[1]

    thin_all = thin_all.astype(F32)
    gain_first, out_shift, gain_second = (
        thin_all[:, i * d_own : (i + 1) * d_own].reshape(width) for i in range(3)
    )
    per = head_count * lane_own
    lane_rows = (
        thin_all[:, 3 * d_own :]
        .reshape(grid.n, CONV + 6, head_count, lane_own)
        .transpose(1, 2, 0, 3)
        .reshape(CONV + 6, channels)
    )
    gelu_shift, input_shift = lane_rows[0], lane_rows[1]
    conv_taps = lane_rows[2 : 2 + CONV]
    conv_offset, inlet_shift, forget_shift, rate_wide = (lane_rows[2 + CONV + i] for i in range(4))
    inlet_shift = inlet_shift.reshape(head_count, block_size)
    forget_shift = forget_shift.reshape(head_count, block_size)
    rate_wide = rate_wide.reshape(head_count, block_size)

    feed_all = feed_all.reshape(3, width, window)
    gate_full, up_full, down_turned = feed_all[0], feed_all[1], feed_all[2]
    first_tile = jnp.minimum(grid.z * window_tiles, unit_tiles - window_tiles)
    unit_place = lax.iota(jnp.int32, window) + first_tile * LANE
    valid = (unit_place >= grid.z * window)[None, :]

    inputs = block_in.astype(F32).reshape(rows_all, width)
    normed = rms_norm(inputs, gain_first).astype(BF16)
    input_pre = dot(normed, input_full) + input_shift
    input_branch = input_pre.astype(BF16).reshape(seq_count, tok_count, channels)
    marks = (segment_ids + 1).astype(BF16)
    rim_values, rim_marks = shifted(
        (input_branch[:, tok_count - margin :], marks[:, tok_count - margin :]), "wide", 1
    )
    extended = jnp.concatenate([rim_values, input_branch], axis=1).astype(F32)
    marks_ext = jnp.concatenate([rim_marks, marks], axis=1).astype(F32)
    conv_out = causal_conv(extended, marks_ext, conv_taps, conv_offset)
    blocks = conv_out.astype(BF16).reshape(seq_count, tok_count, head_count, block_size)
    inlet_pre = (
        jnp.einsum("sthc,hcd->sthd", blocks, inlet_full, preferred_element_type=F32) + inlet_shift
    )
    forget_pre = (
        jnp.einsum("sthc,hcd->sthd", blocks, forget_full, preferred_element_type=F32) + forget_shift
    )
    starts = (marks_ext[:, margin:] != marks_ext[:, margin - 1 : margin - 1 + tok_count])[
        :, :, None, None
    ]
    blocks_wide = blocks.astype(F32)
    decay, drive = lru_terms(inlet_pre, forget_pre, blocks_wide, rate_wide, starts)
    flat = (seq_count, tok_count, channels)
    decay_cum, local_state = local_scan(decay.reshape(flat), drive.reshape(flat), False)
    gelu_pre = dot(normed, gelu_full) + gelu_shift
    gelu_branch = jax.nn.gelu(gelu_pre).reshape(flat)
    state_in = prefix_wide(grid, jnp.stack([decay_cum[:, -1], local_state[:, -1]]), False)
    state = local_state + decay_cum * state_in[:, None]
    mixed = (state * gelu_branch).astype(BF16).reshape(rows_all, channels)
    branch_part = dot_nt(mixed, out_turned).reshape(grid.tensor, rows_half, width)
    own_inputs = pick(inputs.reshape(grid.tensor, rows_half, width), grid.t)
    resid, second_all = bring_second(
        grid, branch_part, own_inputs, out_shift[None], gain_second[None]
    )

    rows_feed = grid.hi * rows_all
    second_all = second_all.reshape(rows_feed, width)
    cot_all = cot_all.reshape(rows_feed, width)
    gate_pre = dot(second_all, gate_full)
    up_pre = dot(second_all, up_full)
    product, pull_feed = jax.vjp(gelu_product, gate_pre, up_pre)
    hidden = jnp.where(valid, product, 0.0).astype(BF16)
    hidden_grad = jnp.where(valid, dot(cot_all, down_turned), 0.0)
    gate_pre_grad, up_pre_grad = pull_feed(hidden_grad)
    gate_low = gate_pre_grad.astype(BF16)
    up_low = up_pre_grad.astype(BF16)
    second_part = dot_nt(gate_low, gate_full) + dot_nt(up_low, up_full)
    shape_rows = (grid.hi, grid.tensor, rows_half, width)
    branch_low, gain_two_grad = sum_rows(
        grid, True, second_part.astype(BF16).reshape(shape_rows), resid, cot_own, gain_second[None]
    )
    branch_low = branch_low.reshape(rows_all, width)
    gain_two_grad = jnp.sum(gain_two_grad, axis=0)
    feed_part = dot_nt(hidden, down_turned).astype(BF16)
    block_out, _ = sum_rows(
        grid, False, feed_part.reshape(shape_rows), resid, cot_own, gain_second[None]
    )
    block_out = block_out.reshape(block_in.shape)

    out_shift_grad = jnp.sum(branch_low.astype(F32), axis=0)
    mixed_grad = dot(branch_low, out_turned).reshape(flat)
    state_grad = mixed_grad * gelu_branch
    _, pull_gelu = jax.vjp(jax.nn.gelu, gelu_pre)
    (gelu_pre_grad,) = pull_gelu((mixed_grad * state).reshape(rows_all, channels))
    gelu_low = gelu_pre_grad.astype(BF16)
    gelu_b_grad = jnp.sum(gelu_low.astype(F32), axis=0)
    decay_flat = decay.reshape(flat)
    next_decay = jnp.concatenate([decay_flat[:, 1:], jnp.ones_like(decay_flat[:, :1])], axis=1)
    tail_decay, local_carried = local_scan(next_decay, state_grad, True)
    head_decay = decay_flat[:, 0]
    from_right = prefix_wide(
        grid,
        jnp.stack([head_decay * tail_decay[:, 0], head_decay * local_carried[:, 0]]),
        True,
    )
    carried = (local_carried + tail_decay * from_right[:, None]).reshape(blocks.shape)
    prev_state = jnp.concatenate([state_in[:, None], state[:, :-1]], axis=1).reshape(blocks.shape)

    def lru_local(inlet_arg, forget_arg, block_arg, rate_arg):
        return lru_terms(inlet_arg, forget_arg, block_arg, rate_arg, starts)

    _, pull_lru = jax.vjp(lru_local, inlet_pre, forget_pre, blocks_wide, rate_wide)
    inlet_grad, forget_grad, block_direct, rate_grad = pull_lru((carried * prev_state, carried))
    inlet_low = inlet_grad.astype(BF16)
    forget_low = forget_grad.astype(BF16)
    inlet_b_grad = jnp.sum(inlet_low.astype(F32), axis=(0, 1))
    forget_b_grad = jnp.sum(forget_low.astype(F32), axis=(0, 1))
    gate_w_grads = jnp.stack(
        [
            jnp.einsum("sthc,sthd->hcd", blocks, low, preferred_element_type=F32)
            for low in (inlet_low, forget_low)
        ]
    )
    gate_w_grads = (
        gate_w_grads.reshape(2, head_count, grid.n, lane_own, block_size)
        .transpose(2, 0, 1, 3, 4)
        .reshape(width, block_size)
        .astype(BF16)
    )
    conv_grad = (
        block_direct
        + jnp.einsum("sthd,hcd->sthc", inlet_low, inlet_full, preferred_element_type=F32)
        + jnp.einsum("sthd,hcd->sthc", forget_low, forget_full, preferred_element_type=F32)
    )

    def conv_local(ext_arg, taps_arg, offset_arg):
        return causal_conv(ext_arg, marks_ext, taps_arg, offset_arg)

    _, pull_conv = jax.vjp(conv_local, extended, conv_taps, conv_offset)
    ext_grad, taps_grad, offset_grad = pull_conv(conv_grad.reshape(flat))
    rim_grad = shifted(ext_grad[:, :margin], "wide", -1)
    branch_input_grad = ext_grad[:, margin:] + jnp.concatenate(
        [jnp.zeros((seq_count, tok_count - margin, channels), F32), rim_grad], axis=1
    )
    input_low = branch_input_grad.astype(BF16).reshape(rows_all, channels)
    input_b_grad = jnp.sum(input_low.astype(F32), axis=0)
    first_part = dot_nt(input_low, input_full) + dot_nt(gelu_low, gelu_full)
    scale_first = lax.rsqrt(jnp.mean(inputs * inputs, axis=-1, keepdims=True) + 1e-06)
    gain_one_grad = jnp.sum(first_part * inputs * scale_first, axis=0)
    first_part = first_part.astype(BF16)
    gain_grads = jnp.stack([gain_one_grad, gain_two_grad])
    gain_grads = gain_grads + grid.swap(gain_grads)

    lane_grads = jnp.stack(
        [
            v.reshape(channels)
            for v in (
                gelu_b_grad,
                input_b_grad,
                taps_grad[0],
                taps_grad[1],
                taps_grad[2],
                taps_grad[3],
                offset_grad,
                inlet_b_grad,
                forget_b_grad,
                rate_grad,
            )
        ]
    )
    lane_grads = (
        lane_grads.reshape(CONV + 6, head_count, grid.n, lane_own)
        .transpose(2, 0, 1, 3)
        .reshape(grid.n, -1)
    )
    thin_grads = jnp.concatenate(
        [v.reshape(grid.n, d_own) for v in (gain_grads[0], out_shift_grad, gain_grads[1])]
        + [lane_grads],
        axis=1,
    )
    feed_grads, rec_grads, first_other, thin = send_grads(
        grid,
        (second_all, cot_all, gate_low, up_low, hidden),
        (normed, branch_low, gelu_low, input_low, mixed),
        gate_w_grads,
        first_part,
        thin_grads,
    )
    thin = thin.reshape(-1)
    rec_grads = jnp.concatenate(list(rec_grads), axis=1)
    gelu_w_grad = rec_grads[:, :channels]
    input_w_grad = rec_grads[:, channels : 2 * channels]
    out_grad = rec_grads[:, 2 * channels : 3 * channels]
    gate_w_grads = rec_grads[:, 3 * channels :].reshape(2, head_count, lane_own, block_size)

    def feed_weight_grad(got):
        pieces = []
        for place in range(grid.hi):
            begin = min(place * window_tiles, unit_tiles - window_tiles)
            skip = min(place * window_tiles - begin, window_tiles)
            if skip < window_tiles:
                pieces.append(got[place, :, skip * LANE :])
        return jnp.concatenate(pieces, axis=1).astype(F32)

    gate_grad, up_grad, down_grad = (feed_weight_grad(got) for got in feed_grads)
    down_grad = down_grad.T
    first_grad = first_part.astype(F32) + first_other.astype(F32)
    _, pull_first = jax.vjp(rms_norm, inputs, gain_first)
    input_norm_grad, _ = pull_first(first_grad)
    block_grad = (branch_low.astype(F32) + input_norm_grad).reshape(block_in.shape)
    gain_one_own, out_shift_own, gain_two_own = (
        thin[i * d_own : (i + 1) * d_own] for i in range(3)
    )
    lanes = thin[3 * d_own :].reshape(CONV + 6, head_count, lane_own)
    weight_shape = gelu_weight.shape
    return (
        block_out,
        block_grad,
        gain_one_own,
        gelu_w_grad.reshape(weight_shape),
        lanes[0],
        input_w_grad.reshape(weight_shape),
        lanes[1],
        lanes[2 : 2 + CONV],
        lanes[2 + CONV],
        gate_w_grads[0],
        lanes[3 + CONV],
        gate_w_grads[1],
        lanes[4 + CONV],
        lanes[5 + CONV],
        out_grad.T.reshape(out_weight.shape),
        out_shift_own,
        gain_two_own,
        gate_grad,
        up_grad,
        down_grad,
    )


def solution(mesh):
    in_specs = (
        P(None, "wide", None),
        P(None, "wide"),
        P(None, "wide", None),
        P("wide"),
        P("wide", "tensor", None),
        P("tensor", "wide"),
        P("wide", "tensor", None),
        P("tensor", "wide"),
        P(None, "tensor", "wide"),
        P("tensor", "wide"),
        P("tensor", "wide", None),
        P("tensor", "wide"),
        P("tensor", "wide", None),
        P("tensor", "wide"),
        P("tensor", "wide"),
        P("tensor", None, "wide"),
        P("wide"),
        P("wide"),
        P("wide", "tensor"),
        P("wide", "tensor"),
        P("tensor", "wide"),
    )
    out_specs = (
        P(None, "wide", None),
        P(None, "wide", None),
        P("wide"),
        P("wide", "tensor", None),
        P("tensor", "wide"),
        P("wide", "tensor", None),
        P("tensor", "wide"),
        P(None, "tensor", "wide"),
        P("tensor", "wide"),
        P("tensor", "wide", None),
        P("tensor", "wide"),
        P("tensor", "wide", None),
        P("tensor", "wide"),
        P("tensor", "wide"),
        P("tensor", None, "wide"),
        P("wide"),
        P("wide"),
        P("wide", "tensor"),
        P("wide", "tensor"),
        P("tensor", "wide"),
    )
    return jax.shard_map(local, mesh=mesh, in_specs=in_specs, out_specs=out_specs, check_vma=False)
```

```python
import functools

import jax
import jax.numpy as jnp
from jax import lax
from jax.experimental import pallas as pl
from jax.experimental.pallas import tpu as pltpu
from jax.sharding import PartitionSpec as P

CONV = 4
LANE = 128
GRANT = 60 * 1024 * 1024
F32 = jnp.float32
BF16 = jnp.bfloat16

LINE = 4


class Grid:
    def __init__(self):
        self.n = lax.axis_size("wide")
        self.hi = LINE
        self.inner_size = self.n // LINE
        self.tensor = lax.axis_size("tensor")
        self.w = lax.axis_index("wide")
        self.t = lax.axis_index("tensor")
        self.z = self.w // self.inner_size
        self.inner = lax.rem(self.w, self.inner_size)

    def flip(self, value, bit):
        return lax.ppermute(value, "wide", [(i, i ^ bit) for i in range(self.n)])

    def swap(self, value):
        size = self.tensor
        pairs = [(i, (i + 1) % size) for i in range(size)]
        return lax.ppermute(value, "tensor", pairs)


def shifted(shard, axis, by):
    size = lax.axis_size(axis)
    place = lax.axis_index(axis) - by
    there = jnp.logical_and(place >= 0, place < size)
    pairs = [(i, (i + by) % size) for i in range(size)]
    moved = lax.ppermute(shard, axis, pairs)
    return jax.tree.map(lambda a: jnp.where(there, a, jnp.zeros_like(a)), moved)


def pick(values, index, axis=0):
    return lax.dynamic_index_in_dim(values, index, axis, keepdims=False)


MESH = pl.DeviceIdType.MESH


class Spot:
    def __init__(self, n, tensor):
        self.n = n
        self.hi = LINE
        self.inner_size = n // LINE
        self.bits = [1 << i for i in range(self.inner_size.bit_length() - 1)]
        self.tensor = tensor
        self.w = lax.axis_index("wide")
        self.t = lax.axis_index("tensor")
        self.z = self.w // self.inner_size
        self.inner = lax.rem(self.w, self.inner_size)
        self.cross = {"tensor": lax.rem(self.t + 1, tensor)}

    def bit(self, which):
        return lax.rem(self.inner // which, 2)

    def flip(self, which):
        return {"wide": self.w + which - 2 * which * self.bit(which)}

    def line(self, place):
        return {"wide": place * self.inner_size + self.inner}

    def away(self, distance):
        return lax.rem(self.z + distance, self.hi)

    def greet(self, *sides):
        barrier = pltpu.get_barrier_semaphore()
        for side in sides:
            pl.semaphore_signal(barrier, inc=1, device_id=side, device_id_type=MESH)
        for distance in range(1, self.hi):
            pl.semaphore_signal(
                barrier, inc=1, device_id=self.line(self.away(distance)), device_id_type=MESH
            )
        pl.semaphore_wait(barrier, len(sides) + self.hi - 1)


def remote(src, dst, sems, index, side):
    return pltpu.make_async_remote_copy(
        src_ref=src,
        dst_ref=dst,
        send_sem=sems.at[0, index],
        recv_sem=sems.at[1, index],
        device_id=side,
        device_id_type=MESH,
    )


class Fans:
    def __init__(self, spot, at, sems, base, sides):
        self.spot, self.at, self.sems, self.base, self.sides = spot, at, sems, base, sides
        self.kinds = sorted(range(1 << len(sides)), key=lambda k: (bin(k).count("1"), -k))

    def onto(self, k):
        low = (k & -k) if k else 1 << len(self.sides)
        return [i for i in reversed(range(len(self.sides))) if (1 << i) < low]

    def copy(self, place, k, i, here=False):
        spot, hi = self.spot, self.spot.hi
        landed = k if here else k | (1 << i)
        index = self.base + (landed - 1) * hi + lax.rem(place - spot.z + hi, hi)
        ref = self.at(place, k)
        return remote(ref, ref, self.sems, index, self.sides[i])

    def hand_on(self, place, k):
        for i in self.onto(k):
            self.copy(place, k, i).start()

    def arrive(self, place, k):
        low = (k & -k).bit_length() - 1
        self.copy(place, k, low, here=True).wait_recv()

    def pass_on(self, place):
        for k in self.kinds:
            if k and self.onto(k):
                self.arrive(place, k)
                self.hand_on(place, k)

    def finish(self, place):
        for k in self.kinds:
            if k and not self.onto(k):
                self.arrive(place, k)
        self.finish_sends(place)

    def finish_sends(self, place):
        for k in self.kinds:
            for i in self.onto(k):
                self.copy(place, k, i).wait_send()

    def count(sides, hi):
        return ((1 << sides) - 1) * hi


class Chain:
    def __init__(self, spot, at, sems, sides):
        self.spot, self.at, self.sems = spot, at, sems
        self.fans = Fans(spot, at, sems, 2 * (spot.hi - 1), sides)

    def line_copy(self, s, up):
        spot, hi = self.spot, self.spot.hi
        owner = spot.z - (s - 1) if up else spot.z + (s - 1)
        other = spot.z + 1 if up else spot.z - 1
        ref = self.at(owner, 0)
        return remote(ref, ref, self.sems, (s - 1) if up else hi + s - 2, spot.line(other))

    def line_here(self, s, up):
        spot, hi = self.spot, self.spot.hi
        owner = spot.z - s if up else spot.z + s
        other = spot.z - 1 if up else spot.z + 1
        ref = self.at(owner, 0)
        return remote(ref, ref, self.sems, (s - 1) if up else hi + s - 2, spot.line(other))

    def first(self):
        spot, hi = self.spot, self.spot.hi

        @pl.when(spot.z < hi - 1)
        def _():
            self.line_copy(1, True).start()

        @pl.when(spot.z > 0)
        def _():
            self.line_copy(1, False).start()

        self.fans.hand_on(spot.z, 0)

    def onward(self, s):
        spot, hi = self.spot, self.spot.hi

        @pl.when(spot.z >= s)
        def _():
            self.line_here(s, True).wait_recv()

        if s < hi - 1:

            @pl.when(jnp.logical_and(spot.z >= s, spot.z < hi - 1))
            def _():
                self.line_copy(s + 1, True).start()

        @pl.when(spot.z >= s)
        def _():
            self.fans.hand_on(spot.z - s, 0)

        @pl.when(spot.z <= hi - 1 - s)
        def _():
            self.line_here(s, False).wait_recv()

        if s < hi - 1:

            @pl.when(jnp.logical_and(spot.z <= hi - 1 - s, spot.z > 0))
            def _():
                self.line_copy(s + 1, False).start()

        @pl.when(spot.z <= hi - 1 - s)
        def _():
            self.fans.hand_on(spot.z + s, 0)

    def places(self, s, act):
        spot = self.spot
        if s == 0:
            act(spot.z)
            return

        @pl.when(spot.z >= s)
        def _():
            act(spot.z - s)

        @pl.when(spot.z <= spot.hi - 1 - s)
        def _():
            act(spot.z + s)

    def second(self, s):
        self.places(s, self.fans.pass_on)

    def finish(self):
        for s in range(self.spot.hi):
            self.places(s, self.fans.finish)
        self.finish_line()

    def finish_sends(self):
        for s in range(self.spot.hi):
            self.places(s, self.fans.finish_sends)
        self.finish_line()

    def finish_line(self):
        spot, hi = self.spot, self.spot.hi
        for s in range(1, hi):

            @pl.when(jnp.logical_and(spot.z >= s - 1, spot.z < hi - 1))
            def _():
                self.line_copy(s, True).wait_send()

            @pl.when(jnp.logical_and(spot.z <= hi - s, spot.z > 0))
            def _():
                self.line_copy(s, False).wait_send()


def chain_sems(sides):
    return pltpu.SemaphoreType.DMA((2, 2 * (LINE - 1) + ((1 << sides) - 1) * LINE))


class Turns:
    def __init__(self, spot, window_of, at, sems, sides):
        self.spot, self.window_of, self.at, self.sems = spot, window_of, at, sems
        self.fans = Fans(spot, at, sems, spot.hi, sides)

    def line_copy(self, distance):
        spot = self.spot
        place = spot.away(distance)
        return remote(self.window_of(place), self.at(spot.z, 0), self.sems, distance, spot.line(place))

    def back(self, distance):
        return lax.rem(self.spot.z - distance + self.spot.hi, self.spot.hi)

    def line_here(self, distance):
        place = self.back(distance)
        ref = self.at(place, 0)
        return remote(ref, ref, self.sems, distance, self.spot.line(place))

    def first(self):
        for distance in range(1, self.spot.hi):
            self.line_copy(distance).start()
        self.fans.hand_on(self.spot.z, 0)

    def onward(self, distance):
        self.line_here(distance).wait_recv()
        self.fans.hand_on(self.back(distance), 0)

    def second(self, distance):
        self.fans.pass_on(self.back(distance))

    def finish(self):
        for distance in range(self.spot.hi):
            self.fans.finish(self.back(distance))
            if distance:
                self.line_copy(distance).wait_send()


def weights_kernel(
    n, tensor, rec, gates, thin, feed, cot, rec_all, gates_all, thin_all, feed_all, cot_all,
    rec_sems, gates_sems, thin_sems, feed_sems, cot_sems,
):
    del rec, gates, thin, feed, cot
    spot = Spot(n, tensor)
    hi = spot.hi

    def index(place, k):
        return place * spot.inner_size + jnp.bitwise_xor(spot.inner, k)

    cube = [spot.flip(bit) for bit in spot.bits]
    moves = [
        Chain(spot, lambda place, k: thin_all.at[index(place, k)], thin_sems, cube),
        Chain(spot, lambda place, k: gates_all.at[:, index(place, k)], gates_sems, cube),
        Chain(spot, lambda place, k: rec_all.at[:, index(place, k)], rec_sems, cube),
        Turns(
            spot,
            lambda place: feed_all.at[:, n + place],
            lambda place, k: feed_all.at[:, index(place, k)],
            feed_sems,
            cube,
        ),
        Chain(
            spot,
            lambda place, k: cot_all.at[place, lax.rem(spot.t + k, tensor)],
            cot_sems,
            [spot.cross],
        ),
    ]
    spot.greet(*cube, spot.cross)
    for move in moves:
        move.first()
    for s in range(1, hi):
        for move in moves:
            move.onward(s)
        for move in moves:
            move.second(s - 1)
    for move in moves:
        move.second(hi - 1)
    for move in moves:
        move.finish()


def blank(*shapes):
    return pl.pallas_call(
        lambda *refs: None,
        out_shape=[jax.ShapeDtypeStruct(shape, BF16) for shape in shapes],
        out_specs=[pl.BlockSpec(memory_space=pl.ANY)] * len(shapes),
        compiler_params=pltpu.CompilerParams(vmem_limit_bytes=GRANT),
        name="blank",
    )()


def bring_weights(grid, rec, gates, thin, feed, cot):
    n, hi, tensor = grid.n, grid.hi, grid.tensor
    far = pl.BlockSpec(memory_space=pl.ANY)
    arrays = (rec, gates, thin, feed, cot)
    cube = grid.inner_size.bit_length() - 1
    return pl.pallas_call(
        functools.partial(weights_kernel, n, tensor),
        out_shape=[jax.ShapeDtypeStruct(a.shape, a.dtype) for a in arrays],
        in_specs=[far] * len(arrays),
        out_specs=[far] * len(arrays),
        input_output_aliases={i: i for i in range(len(arrays))},
        scratch_shapes=[
            chain_sems(cube),
            chain_sems(cube),
            chain_sems(cube),
            pltpu.SemaphoreType.DMA((2, grid.inner_size * hi)),
            chain_sems(1),
        ],
        compiler_params=pltpu.CompilerParams(
            collective_id=0, has_side_effects=True, vmem_limit_bytes=GRANT
        ),
        name="bring_weights",
    )(*arrays)


def by_rows(rows, step, act):
    def one(i, carry):
        act(pl.ds(pl.multiple_of(i * step, step), step))
        return carry

    lax.fori_loop(0, rows // step, one, 0)


STEP = 16


GELU_SLOPE = 0.7978845608028654
GELU_CUBE = 0.044715
HALO = 8
GELU_SHIFT, INPUT_SHIFT, TAPS, CONV_SHIFT, INLET_SHIFT, FORGET_SHIFT, RATE_SOFT, RATE_SIGMOID = 0, 1, 2, 6, 7, 8, 9, 10
LANE_ROWS = 16


def gelu_of(v):
    bent = jnp.tanh(GELU_SLOPE * (v + GELU_CUBE * (v * v * v)))
    half = 0.5 * (1.0 + bent)
    slope = half + 0.5 * v * (1.0 - bent * bent) * (GELU_SLOPE * (1.0 + 3.0 * GELU_CUBE * (v * v)))
    return v * half, slope


def minus_expm1(x):
    series = jnp.ones_like(x)
    for k in range(9, 1, -1):
        series = 1.0 + series * x * (1.0 / k)
    return jnp.where(x > -0.5, -x * series, 1.0 - jnp.exp(x))


def decay_of(forget, soft, starts):
    log_decay = -8.0 * forget * soft
    decay = jnp.where(starts, 0.0, jnp.exp(log_decay))
    scaler = jnp.where(starts, 1.0, jnp.sqrt(minus_expm1(2.0 * log_decay)))
    return decay, scaler


def tile_scan(a, b, state_in, decay_in, reverse):
    place = lax.broadcasted_iota(jnp.int32, a.shape, 0)
    for by in (1, 2, 4):
        turn = 8 - by if reverse else by
        ok = place < 8 - by if reverse else place >= by
        b = jnp.where(ok, a * pltpu.roll(b, turn, 0) + b, b)
        a = jnp.where(ok, a * pltpu.roll(a, turn, 0), a)
    return a * decay_in, b + a * state_in


def scan_rows(seqs, length, width, read, write, reverse):
    tiles = length // 8
    last = 0 if reverse else 7

    def one(i, carry):
        tile = tiles - 1 - i if reverse else i
        after = []
        for s in range(seqs):
            decay_in, state_in = carry[s]
            at = pl.ds(pl.multiple_of(s * length + tile * 8, 8), 8)
            a, b = tile_scan(*read(at), state_in, decay_in, reverse)
            write(at, a, b)
            after.append(
                tuple(jnp.broadcast_to(v[last : last + 1], (8, width)) for v in (a, b))
            )
        return tuple(after)

    start = (jnp.ones((8, width), F32), jnp.zeros((8, width), F32))
    lax.fori_loop(0, tiles, one, (start,) * seqs)


def enter_kernel(
    seqs, x, halo, gain, w_input, w_gelu, w_inlet, w_forget, lanes, flags,
    normed, ext, conv, gelu_pre, inlet_pre, forget_pre, cum, local, held, factor, addend,
):
    rows = x.shape[0]
    length = rows // seqs
    width = conv.shape[1]

    @pl.when(pl.program_id(0) == 0)
    def _():
        def norm(source, at, to):
            value = source[at, :].astype(F32)
            scale = lax.rsqrt(jnp.mean(value * value, axis=-1, keepdims=True) + 1e-06)
            value = (value * scale * gain[...]).astype(BF16)
            held[pl.ds(pl.multiple_of(at.start + to, STEP), STEP), :] = value
            return value

        def main(at):
            normed[at, :] = norm(x, at, 0)

        by_rows(rows, STEP, main)
        by_rows(halo.shape[0], STEP, lambda at: norm(halo, at, rows))

    table = lanes[...]

    def row(i):
        return table[i : i + 1]

    branch = (dot(held[...], w_input[0]) + row(INPUT_SHIFT)).astype(BF16)
    gelu_pre[...] = dot(held[0:rows, :], w_gelu[0]) + row(GELU_SHIFT)
    for s in range(seqs):
        here = slice(s * length, (s + 1) * length)
        front = rows + s * HALO
        longer = jnp.concatenate(
            [branch[front : front + HALO].astype(F32), branch[here].astype(F32)], axis=0
        )
        ext[s] = longer.astype(BF16)
        total = row(CONV_SHIFT) + row(TAPS) * longer[HALO:]
        for k in range(1, CONV):
            moved = pltpu.roll(longer, k, 0)[HALO:]
            total = total + jnp.where(flags[here, k : k + 1] > 0.5, row(TAPS + k) * moved, 0.0)
        conv[here, :] = total.astype(BF16)
    blocks = conv[...]
    inlet_pre[...] = dot(blocks, w_inlet[0]) + row(INLET_SHIFT)
    forget_pre[...] = dot(blocks, w_forget[0]) + row(FORGET_SHIFT)

    def terms(at):
        starts = flags[at, 0:1] > 0.5
        decay, scaler = decay_of(jax.nn.sigmoid(forget_pre[at, :]), row(RATE_SOFT), starts)
        factor[at, :] = decay
        addend[at, :] = scaler * jax.nn.sigmoid(inlet_pre[at, :]) * conv[at, :].astype(F32)

    by_rows(rows, 32, terms)

    def write(at, a, b):
        cum[at, :] = a
        local[at, :] = b

    scan_rows(seqs, length, width, lambda at: (factor[at, :], addend[at, :]), write, False)


def enter_recurrence(x, halo, gain, rec, inlet, forget, lanes, flags, seqs):
    rows, d = x.shape
    heads, width = inlet.shape[:2]
    channels = heads * width
    longer = rows // seqs + HALO

    def fixed(a):
        return pl.BlockSpec(a.shape, lambda h: (0, 0))

    def column(count):
        return pl.BlockSpec((count, width), lambda h: (0, h))

    def weight(k):
        return pl.BlockSpec((1, d, width), lambda h: (k, 0, h))

    head = pl.BlockSpec((1, width, width), lambda h: (h, 0, 0))
    wide = jax.ShapeDtypeStruct((rows, channels), F32)
    return pl.pallas_call(
        functools.partial(enter_kernel, seqs),
        grid=(heads,),
        out_shape=[
            jax.ShapeDtypeStruct((rows, d), BF16),
            jax.ShapeDtypeStruct((seqs, longer, channels), BF16),
            jax.ShapeDtypeStruct((rows, channels), BF16),
        ]
        + [wide] * 5,
        in_specs=[fixed(x), fixed(halo), fixed(gain), weight(0), weight(1), head, head]
        + [column(LANE_ROWS), fixed(flags)],
        out_specs=[
            fixed(x),
            pl.BlockSpec((seqs, longer, width), lambda h: (0, 0, h)),
            column(rows),
        ]
        + [column(rows)] * 5,
        scratch_shapes=[
            pltpu.VMEM((rows + halo.shape[0], d), BF16),
            pltpu.VMEM((rows, width), F32),
            pltpu.VMEM((rows, width), F32),
        ],
        compiler_params=pltpu.CompilerParams(vmem_limit_bytes=GRANT),
        name="enter_recurrence",
    )(x, halo, gain, rec, rec, inlet, forget, lanes, flags)


class Prefix:
    def __init__(self, spot, seqs, reverse, tots, gots, line, cube_sems, line_sems):
        self.spot, self.seqs, self.reverse = spot, seqs, reverse
        self.tots, self.gots, self.line = tots, gots, line
        self.cube_sems, self.line_sems = cube_sems, line_sems

    def line_copy(self, place, sender):
        stages = len(self.spot.bits)
        return pltpu.make_async_remote_copy(
            src_ref=self.tots.at[stages],
            dst_ref=self.line.at[sender],
            send_sem=self.line_sems.at[0, place],
            recv_sem=self.line_sems.at[1, sender],
            device_id=self.spot.line(place),
            device_id_type=MESH,
        )

    def run(self):
        spot, seqs, hi = self.spot, self.seqs, self.spot.hi
        a, b = slice(0, seqs), slice(seqs, 2 * seqs)
        width = self.tots.shape[2]
        enter_a, enter_b = jnp.ones((seqs, width), F32), jnp.zeros((seqs, width), F32)
        for stage, bit in enumerate(spot.bits):
            copy = remote(
                self.tots.at[stage], self.gots.at[stage], self.cube_sems, stage, spot.flip(bit)
            )
            copy.start()
            copy.wait()
            mine_a, mine_b = self.tots[stage, a, :], self.tots[stage, b, :]
            got_a, got_b = self.gots[stage, a, :], self.gots[stage, b, :]
            after = spot.bit(bit) == (0 if self.reverse else 1)
            enter_b = jnp.where(after, enter_a * got_b + enter_b, enter_b)
            enter_a = jnp.where(after, enter_a * got_a, enter_a)
            self.tots[stage + 1, a, :] = mine_a * got_a
            self.tots[stage + 1, b, :] = jnp.where(
                after, mine_a * got_b + mine_b, got_a * mine_b + got_b
            )
            self.tots[stage + 1, 2 * seqs :, :] = jnp.zeros((8 - 2 * seqs, width), F32)
        for distance in range(1, hi):
            self.line_copy(spot.away(distance), spot.z).start()
        for distance in range(1, hi):
            place = spot.away(distance)
            self.line_copy(place, place).wait_recv()
            self.line_copy(place, spot.z).wait_send()
        come = jnp.zeros((seqs, width), F32)
        for place in reversed(range(hi)) if self.reverse else range(hi):
            before = spot.z < place if self.reverse else spot.z > place
            come = jnp.where(before, self.line[place, a, :] * come + self.line[place, b, :], come)
        return enter_a * come + enter_b


def prefix_scratch(grid, channels):
    stages = grid.inner_size.bit_length() - 1
    return [
        pltpu.VMEM((stages + 1, 8, channels), F32),
        pltpu.VMEM((stages, 8, channels), F32),
        pltpu.VMEM((grid.hi, 8, channels), F32),
        pltpu.SemaphoreType.DMA((2, stages)),
        pltpu.SemaphoreType.DMA((2, grid.hi)),
    ]


def second_kernel(
    n, tensor, seqs, cum, local, gelu_pre, w_out, x, shift, gain,
    entered, mixed, resid, second,
    part, out, got, tots, gots, line, cube_sems, line_sems, swap_sems,
):
    spot = Spot(n, tensor)
    rows = resid.shape[0]
    every = x.shape[0]
    length = every // seqs
    spot.greet(*[spot.flip(bit) for bit in spot.bits], spot.cross)
    tots[0] = jnp.zeros_like(tots[0])
    for s in range(seqs):
        last = slice((s + 1) * length - 1, (s + 1) * length)
        tots[0, s : s + 1, :] = cum[last, :]
        tots[0, seqs + s : seqs + s + 1, :] = local[last, :]
    enter = Prefix(spot, seqs, False, tots, gots, line, cube_sems, line_sems).run()
    entered[...] = jnp.zeros_like(entered)
    entered[0:seqs, :] = enter
    for s in range(seqs):

        def mix(at, s=s):
            here = pl.ds(pl.multiple_of(s * length + at.start, STEP), STEP)
            state = local[here, :] + cum[here, :] * enter[s : s + 1]
            mixed[here, :] = (state * gelu_of(gelu_pre[here, :])[0]).astype(BF16)

        by_rows(length, STEP, mix)
    values = mixed[...]

    def branch(j, carry):
        at = pl.ds(pl.multiple_of(j * 256, 256), 256)
        value = dot_nt(values, w_out[0, at, :])
        for side in range(tensor):
            part[side, :, at] = value[side * rows : (side + 1) * rows]
        return carry

    lax.fori_loop(0, x.shape[1] // 256, branch, 0)

    def put(at):
        out[at, :] = part[1 - spot.t, at, :].astype(BF16)

    by_rows(rows, STEP, put)
    copy = remote(out, got, swap_sems, 0, spot.cross)
    copy.start()
    copy.wait()

    def norm(at):
        own = x[pl.ds(pl.multiple_of(spot.t * rows + at.start, STEP), STEP), :].astype(F32)
        value = own + (part[spot.t, at, :] + got[at, :].astype(F32) + shift[...])
        resid[at, :] = value
        scale = lax.rsqrt(jnp.mean(value * value, axis=-1, keepdims=True) + 1e-06)
        second[at, :] = (value * scale * gain[...]).astype(BF16)

    by_rows(rows, STEP, norm)


def make_second(grid, cum, local, gelu_pre, rec, x, shift, gain, seqs):
    every, d = x.shape
    channels = cum.shape[1]
    rows = every // grid.tensor
    near = pl.BlockSpec(memory_space=pltpu.VMEM)
    return pl.pallas_call(
        functools.partial(second_kernel, grid.n, grid.tensor, seqs),
        grid=(1,),
        out_shape=[
            jax.ShapeDtypeStruct((8, channels), F32),
            jax.ShapeDtypeStruct((every, channels), BF16),
            jax.ShapeDtypeStruct((rows, d), F32),
            jax.ShapeDtypeStruct((rows, d), BF16),
        ],
        in_specs=[near] * 3 + [pl.BlockSpec((1, d, channels), lambda i: (2, 0, 0))] + [near] * 3,
        out_specs=[near] * 4,
        scratch_shapes=[
            pltpu.VMEM((grid.tensor, rows, d), F32),
            pltpu.VMEM((rows, d), BF16),
            pltpu.VMEM((rows, d), BF16),
        ]
        + prefix_scratch(grid, channels)
        + [pltpu.SemaphoreType.DMA((2, 1))],
        compiler_params=pltpu.CompilerParams(
            collective_id=1, has_side_effects=True, vmem_limit_bytes=GRANT
        ),
        name="make_second",
    )(cum, local, gelu_pre, rec, x, shift, gain)


def leave_kernel(
    n, tensor, seqs, branch, w_out, gelu_pre, local, cum, inlet_pre, forget_pre, conv, ext, entered,
    w_inlet, w_forget, lanes, flags,
    gelu_low, input_low, gate_grads, lane_grads, shift_grad,
    tail, carried, factor, addend, back, rim, tots, gots, line, cube_sems, line_sems, rim_sems,
):
    spot = Spot(n, tensor)
    every, channels = conv.shape
    length = every // seqs
    heads, width = w_inlet.shape[:2]
    behind = {"wide": lax.rem(spot.w + n - 1, n)}
    ahead = {"wide": lax.rem(spot.w + 1, n)}
    spot.greet(*[spot.flip(bit) for bit in spot.bits], behind, ahead)
    tots[0] = jnp.zeros_like(tots[0])
    lane_grads[...] = jnp.zeros_like(lane_grads)
    shift_grad[...] = jnp.zeros_like(shift_grad)

    def add(at):
        shift_grad[...] += jnp.sum(branch[at, :].astype(F32).reshape(2, 8, -1), axis=0)

    by_rows(every, STEP, add)

    def decays(at, cols):
        soft = lanes[RATE_SOFT : RATE_SOFT + 1, cols]
        return decay_of(jax.nn.sigmoid(forget_pre[at, cols]), soft, flags[at, 0:1] > 0.5)

    def upward(h, none):
        cols = pl.ds(pl.multiple_of(h * width, width), width)
        grad = dot(branch[...], w_out[0, :, cols])
        gelu, slope = gelu_of(gelu_pre[:, cols])
        for s in range(seqs):
            here = slice(s * length, (s + 1) * length)
            state = local[here, cols] + cum[here, cols] * entered[s : s + 1, cols]
            low = (grad[here] * state * slope[here]).astype(BF16)
            gelu_low[here, cols] = low
            lane_grads[0:1, cols] += jnp.sum(low.astype(F32), axis=0, keepdims=True)
            decay, _ = decays(here, cols)
            place = lax.broadcasted_iota(jnp.int32, (length, width), 0)
            factor[here, :] = jnp.where(place < length - 1, pltpu.roll(decay, length - 1, 0), 1.0)
        addend[...] = grad * gelu

        def write(at, a, b):
            tail[at, cols] = a
            carried[at, cols] = b

        scan_rows(seqs, length, width, lambda at: (factor[at, :], addend[at, :]), write, True)
        for s in range(seqs):
            first = slice(s * length, s * length + 8)
            decay, _ = decays(first, cols)
            tots[0, s : s + 1, cols] = decay[0:1] * tail[first, cols][0:1]
            tots[0, seqs + s : seqs + s + 1, cols] = decay[0:1] * carried[first, cols][0:1]
        return none

    lax.fori_loop(0, heads, upward, 0)
    come = Prefix(spot, seqs, True, tots, gots, line, cube_sems, line_sems).run()
    tots[0, 0:seqs, :] = come

    def downward(h, none):
        cols = pl.ds(pl.multiple_of(h * width, width), width)

        def row(i):
            return lanes[i : i + 1, cols]

        sums = []
        for s in range(seqs):
            here = slice(s * length, (s + 1) * length)
            place = lax.broadcasted_iota(jnp.int32, (length, width), 0)
            starts = flags[here, 0:1] > 0.5
            blocks = conv[here, cols].astype(F32)
            enter = entered[s : s + 1, cols]
            state = local[here, cols] + cum[here, cols] * enter
            before = jnp.where(place > 0, pltpu.roll(state, 1, 0), enter)
            carry = carried[here, cols] + tail[here, cols] * tots[0, s : s + 1, cols]
            inlet = jax.nn.sigmoid(inlet_pre[here, cols])
            forget = jax.nn.sigmoid(forget_pre[here, cols])
            soft = row(RATE_SOFT)
            decay, scaler = decay_of(forget, soft, starts)
            log_grad = jnp.where(
                starts, 0.0, carry * before * decay - carry * inlet * blocks * (decay * decay) / scaler
            )
            rate_grad = jnp.sum(log_grad * (-8.0 * forget), axis=0, keepdims=True) * row(RATE_SIGMOID)
            inlet_low = (carry * scaler * blocks * (inlet * (1.0 - inlet))).astype(BF16)
            forget_low = (log_grad * (-8.0 * soft) * (forget * (1.0 - forget))).astype(BF16)
            conv_grad = (
                carry * scaler * inlet
                + dot_nt(inlet_low, w_inlet[h])
                + dot_nt(forget_low, w_forget[h])
            )
            longer = ext[s, :, cols].astype(F32)
            zeros = jnp.zeros((HALO, width), F32)
            total = jnp.concatenate([zeros, row(TAPS) * conv_grad], axis=0)
            taps = [jnp.sum(conv_grad * longer[HALO:], axis=0, keepdims=True)]
            for k in range(1, CONV):
                masked = jnp.where(flags[here, k : k + 1] > 0.5, conv_grad, 0.0)
                moved = pltpu.roll(longer, k, 0)[HALO:]
                taps.append(jnp.sum(masked * moved, axis=0, keepdims=True))
                sent = jnp.concatenate([zeros, row(TAPS + k) * masked], axis=0)
                total = total + pltpu.roll(sent, HALO + length - k, 0)
            back[s, :, cols] = total
            lows = [jnp.sum(v.astype(F32), axis=0, keepdims=True) for v in (inlet_low, forget_low)]
            sums.append(taps + [jnp.sum(conv_grad, axis=0, keepdims=True)] + lows + [rate_grad])
            for m, low in enumerate((inlet_low, forget_low)):
                factor[here, :] = low.astype(F32) if m == 0 else factor[here, :]
                addend[here, :] = low.astype(F32) if m == 1 else addend[here, :]
        for i in range(len(sums[0])):
            lane_grads[2 + i : 3 + i, cols] = sum(each[i] for each in sums[1:]) + sums[0][i]
        for m, low in enumerate((factor, addend)):
            gate_grads[m, h] = dot_tn(conv[:, cols], low[...].astype(BF16)).astype(BF16)
        return none

    lax.fori_loop(0, heads, downward, 0)
    copy = remote(back.at[:, 0:HALO, :], rim, rim_sems, 0, behind)
    copy.start()
    copy.wait()

    def give(h, none):
        cols = pl.ds(pl.multiple_of(h * width, width), width)
        total = jnp.zeros((1, width), F32)
        for s in range(seqs):
            edge = jnp.where(spot.w < n - 1, rim[s, :, cols], 0.0)
            value = back[s, HALO:, cols]
            value = jnp.concatenate([value[: length - HALO], value[length - HALO :] + edge], axis=0)
            low = value.astype(BF16)
            input_low[s * length : (s + 1) * length, cols] = low
            total = total + jnp.sum(low.astype(F32), axis=0, keepdims=True)
        lane_grads[1:2, cols] = total
        return none

    lax.fori_loop(0, heads, give, 0)


def leave_recurrence(
    grid, branch, rec, gelu_pre, local, cum, inlet_pre, forget_pre, conv, ext, entered, inlet, forget, lanes,
    flags, seqs,
):
    every, channels = conv.shape
    d = branch.shape[1]
    heads, width = inlet.shape[:2]
    near = pl.BlockSpec(memory_space=pltpu.VMEM)
    low = jax.ShapeDtypeStruct((every, channels), BF16)
    return pl.pallas_call(
        functools.partial(leave_kernel, grid.n, grid.tensor, seqs),
        grid=(1,),
        out_shape=[
            low,
            low,
            jax.ShapeDtypeStruct((2, heads, width, width), BF16),
            jax.ShapeDtypeStruct((LANE_ROWS, channels), F32),
            jax.ShapeDtypeStruct((8, d), F32),
        ],
        in_specs=[near, pl.BlockSpec((1, d, channels), lambda i: (2, 0, 0))] + [near] * 12,
        out_specs=[near] * 5,
        scratch_shapes=[
            pltpu.VMEM((every, channels), F32),
            pltpu.VMEM((every, channels), F32),
            pltpu.VMEM((every, width), F32),
            pltpu.VMEM((every, width), F32),
            pltpu.VMEM((seqs, every // seqs + HALO, channels), F32),
            pltpu.VMEM((seqs, HALO, channels), F32),
        ]
        + prefix_scratch(grid, channels)
        + [pltpu.SemaphoreType.DMA((2, 1))],
        compiler_params=pltpu.CompilerParams(
            collective_id=5, has_side_effects=True, vmem_limit_bytes=GRANT
        ),
        name="leave_recurrence",
    )(
        branch, rec, gelu_pre, local, cum, inlet_pre, forget_pre, conv, ext, entered, inlet, forget,
        lanes, flags,
    )


class Rows:
    def __init__(self, spot, part, got, line, cross_sems, line_sems):
        self.spot, self.part, self.got, self.line = spot, part, got, line
        self.cross_sems, self.line_sems = cross_sems, line_sems
        self.rows = got.shape[1]

    def place(self, k):
        spot, hi = self.spot, self.spot.hi
        last = hi - 1
        flipped = jnp.where(spot.z * 2 < hi, 0, 1)
        z = spot.z + flipped * (last - 2 * spot.z)
        if k == last:
            place = z
        else:
            place = jnp.where(k < last - z, last - k, k - (last - z))
        return place + flipped * (last - 2 * place)

    def cross_copy(self, place):
        spot = self.spot
        return remote(
            self.part.at[place, 1 - spot.t], self.got.at[place], self.cross_sems, place, spot.cross
        )

    def start(self):
        for k in range(self.spot.hi):
            self.cross_copy(self.place(k)).start()

    def line_copy(self, s, up, here=False):
        spot, hi = self.spot, self.spot.hi
        slot = (s - 1) if up else hi + s - 2
        step = 1 if up != here else -1
        return remote(
            self.line.at[0, slot], self.line.at[1, slot], self.line_sems, slot, spot.line(spot.z + step)
        )

    def own(self, place, at):
        return self.part[place, self.spot.t, at, :].astype(F32) + self.got[place, at, :].astype(F32)

    def send(self, s, up):
        spot, hi = self.spot, self.spot.hi
        place = spot.z + hi - s if up else spot.z - hi + s
        slot = (s - 1) if up else hi + s - 2
        self.cross_copy(place).wait_recv()
        begins = spot.z == 0 if up else spot.z == hi - 1

        @pl.when(begins)
        def _():
            def put(at):
                self.line[0, slot, at, :] = self.own(place, at).astype(BF16)

            by_rows(self.rows, STEP, put)

        if s > 1:

            @pl.when(jnp.logical_not(begins))
            def _():
                self.line_copy(s - 1, up, here=True).wait_recv()

                def put(at):
                    before = self.line[1, slot - 1, at, :].astype(F32)
                    self.line[0, slot, at, :] = (self.own(place, at) + before).astype(BF16)

                by_rows(self.rows, STEP, put)

        self.line_copy(s, up).start()

    def sends_up(self, s):
        return self.spot.z <= s - 1

    def sends_down(self, s):
        return self.spot.z >= self.spot.hi - s

    def run(self, done):
        spot, hi = self.spot, self.spot.hi
        for s in range(1, hi):

            @pl.when(jnp.logical_and(self.sends_up(s), spot.z < hi - 1))
            def _():
                self.send(s, True)

            @pl.when(jnp.logical_and(self.sends_down(s), spot.z > 0))
            def _():
                self.send(s, False)

        self.cross_copy(spot.z).wait_recv()

        @pl.when(spot.z > 0)
        def _():
            self.line_copy(hi - 1, True, here=True).wait_recv()

        @pl.when(spot.z < hi - 1)
        def _():
            self.line_copy(hi - 1, False, here=True).wait_recv()

        def total(at):
            below = self.line[1, hi - 2, at, :].astype(F32)
            above = self.line[1, 2 * hi - 3, at, :].astype(F32)
            value = self.own(spot.z, at)
            value = value + jnp.where(spot.z > 0, below, 0.0)
            done(at, value + jnp.where(spot.z < hi - 1, above, 0.0))

        by_rows(self.rows, STEP, total)

    def finish(self):
        spot, hi = self.spot, self.spot.hi
        for place in range(hi):
            self.cross_copy(place).wait_send()
        for s in range(1, hi):

            @pl.when(jnp.logical_and(self.sends_up(s), spot.z < hi - 1))
            def _():
                self.line_copy(s, True).wait_send()

            @pl.when(jnp.logical_and(self.sends_down(s), spot.z > 0))
            def _():
                self.line_copy(s, False).wait_send()


def feed_kernel(
    n, tensor, unit_tiles, own, w_gate, w_up, w_down, cot, resid, gain,
    whole, gate_low, up_low, hidden, both, gain_grad,
    part, got, line, mine, other, sems, cross_sems, line_sems, swap_sems,
):
    spot = Spot(n, tensor)
    hi = spot.hi
    rows, d = own.shape
    width = w_gate.shape[2]
    every = tensor * rows
    spot.greet(spot.cross)

    def put(at):
        whole[spot.z, spot.t, at, :] = own[at, :]

    by_rows(rows, STEP, put)
    chain = Chain(
        spot, lambda place, k: whole.at[place, lax.rem(spot.t + k, tensor)], sems, [spot.cross]
    )
    chain.first()
    gain_grad[...] = jnp.zeros_like(gain_grad)
    tiles = width // LANE
    skip = spot.z * tiles - jnp.minimum(spot.z * tiles, unit_tiles - tiles)
    chunk = 256

    def work(place):
        def ahead(j, none):
            cols = pl.ds(pl.multiple_of(j * chunk, chunk), chunk)
            rows_in = whole[place].reshape(every, d)
            gate, slope = gelu_of(dot(rows_in, w_gate[0, :, cols]))
            up = dot(rows_in, w_up[0, :, cols])
            grad = dot(cot[place].reshape(every, d), w_down[0, :, cols])
            at = lax.broadcasted_iota(jnp.int32, (1, chunk), 1) + j * chunk
            ok = at >= skip * LANE
            grad = jnp.where(ok, grad, 0.0)
            hidden[place, :, cols] = jnp.where(ok, gate * up, 0.0).astype(BF16)
            gate_low[place, :, cols] = (grad * up * slope).astype(BF16)
            up_low[place, :, cols] = (grad * gate).astype(BF16)
            return none

        lax.fori_loop(0, width // chunk, ahead, 0)

        def back(j, none):
            cols = pl.ds(pl.multiple_of(j * chunk, chunk), chunk)
            value = dot_nt(gate_low[place], w_gate[0, cols, :])
            value = (value + dot_nt(up_low[place], w_up[0, cols, :])).astype(BF16)
            for side in range(tensor):
                part[place, side, :, cols] = value[side * rows : (side + 1) * rows]
            return none

        lax.fori_loop(0, d // chunk, back, 0)

    def come_and_work(place):
        chain.fans.arrive(place, 1)
        work(place)

    for s in range(1, hi):
        chain.onward(s)
        chain.places(s - 1, come_and_work)
    chain.places(hi - 1, come_and_work)
    sums = Rows(spot, part, got, line, cross_sems, line_sems)
    sums.start()
    chain.finish_sends()

    def done(at, total):
        value = resid[at, :]
        scale = lax.rsqrt(jnp.mean(value * value, axis=-1, keepdims=True) + 1e-06)
        turned = total * gain[...]
        inner = jnp.mean(turned * value, axis=-1, keepdims=True)
        grad = cot[spot.z, spot.t, at, :].astype(F32)
        grad = grad + scale * turned - value * (scale * scale * scale * inner)
        gained = total * value * scale
        gain_grad[...] += jnp.sum(gained.reshape(2, 8, -1), axis=0)
        mine[at, :] = grad.astype(BF16)

    sums.run(done)
    copy = remote(mine, other, swap_sems, 0, spot.cross)
    copy.start()
    sums.finish()
    share(spot, copy, mine, other, both)


def share(spot, copy, mine, other, both):
    def keep(at):
        both[spot.t, at, :] = mine[at, :]

    by_rows(mine.shape[0], STEP, keep)
    copy.wait()

    def take(at):
        both[1 - spot.t, at, :] = other[at, :]

    by_rows(mine.shape[0], STEP, take)


def rows_scratch(grid, rows, width):
    hi = grid.hi
    return [
        pltpu.VMEM((hi, rows, width), BF16),
        pltpu.VMEM((2, 2 * (hi - 1), rows, width), BF16),
        pltpu.VMEM((rows, width), BF16),
        pltpu.VMEM((rows, width), BF16),
    ]


def rows_sems(grid):
    hi = grid.hi
    return [
        pltpu.SemaphoreType.DMA((2, hi)),
        pltpu.SemaphoreType.DMA((2, 2 * (hi - 1))),
        pltpu.SemaphoreType.DMA((2, 1)),
    ]


def feed_forward(grid, own, feed, cot, resid, gain, unit_tiles):
    rows, d = own.shape
    hi, tensor = grid.hi, grid.tensor
    width = feed.shape[-1]
    near = pl.BlockSpec(memory_space=pltpu.VMEM)
    whole = jax.ShapeDtypeStruct((hi, tensor, rows, d), BF16)
    low = jax.ShapeDtypeStruct((hi, tensor * rows, width), BF16)
    feed = feed.reshape(3, -1, width)

    def weight(k):
        return pl.BlockSpec((1, d, width), lambda i: (k, 0, 0))

    return pl.pallas_call(
        functools.partial(feed_kernel, grid.n, tensor, unit_tiles),
        grid=(1,),
        out_shape=[
            whole,
            low,
            low,
            low,
            jax.ShapeDtypeStruct((tensor, rows, d), BF16),
            jax.ShapeDtypeStruct((8, d), F32),
        ],
        in_specs=[near] + [weight(k) for k in range(3)] + [near] * 3,
        out_specs=[near] * 6,
        scratch_shapes=[pltpu.VMEM(whole.shape, BF16)]
        + rows_scratch(grid, rows, d)
        + [chain_sems(1)]
        + rows_sems(grid),
        compiler_params=pltpu.CompilerParams(
            collective_id=2, has_side_effects=True, vmem_limit_bytes=GRANT
        ),
        name="feed_forward",
    )(own, feed, feed, feed, cot, resid, gain)


def out_kernel(
    n, tensor, part_in, resid, both, part, got, line, mine, other, cross_sems, line_sems, swap_sems
):
    spot = Spot(n, tensor)
    spot.greet(spot.cross)
    rows = resid.shape[0]
    for place in range(spot.hi):
        for side in range(tensor):

            def put(at, place=place, side=side):
                part[place, side, at, :] = part_in[place, side, at, :]

            by_rows(rows, STEP, put)
    sums = Rows(spot, part, got, line, cross_sems, line_sems)
    sums.start()

    def done(at, total):
        mine[at, :] = (resid[at, :] + total).astype(BF16)

    sums.run(done)
    copy = remote(mine, other, swap_sems, 0, spot.cross)
    copy.start()
    sums.finish()
    share(spot, copy, mine, other, both)


def block_output(grid, part, resid):
    rows, width = resid.shape
    near = pl.BlockSpec(memory_space=pltpu.VMEM)
    return pl.pallas_call(
        functools.partial(out_kernel, grid.n, grid.tensor),
        out_shape=jax.ShapeDtypeStruct((grid.tensor, rows, width), BF16),
        in_specs=[near] * 2,
        out_specs=near,
        scratch_shapes=[pltpu.VMEM(part.shape, BF16)] + rows_scratch(grid, rows, width) + rows_sems(grid),
        compiler_params=pltpu.CompilerParams(
            collective_id=3, has_side_effects=True, vmem_limit_bytes=GRANT
        ),
        name="block_output",
    )(part, resid)


RING = 4


def tile_rows(rows):
    return 16 if rows % 16 == 0 else 8


def grads_kernel(
    n, tensor, spans, kept,
    second, cot, normed, branch, gate_low, up_low, hidden, gelu_low, input_low, mixed, gates, first, thin,
    apart, summed, first_other, thin_own, *refs,
):
    stages = (n // LINE).bit_length() - 1
    lists = [refs[i * stages : (i + 1) * stages] for i in range(6)]
    sends, keeps, gots, thin_sends, thin_keeps, thin_gots = lists
    (
        made, ready, got_line, first_out, first_got, thin_ready, thin_line,
        cube_sems, line_sems, first_sems, thin_sems, thin_line_sems,
    ) = refs[6 * stages :]
    spot = Spot(n, tensor)
    hi = spot.hi
    all_spans = len(spans)
    units = all_spans * hi
    step = pl.program_id(0)
    rows = ready.shape[1]
    each = tile_rows(rows)
    last_step = units + stages - 1
    sources = {
        "gate": (second, gate_low),
        "up": (second, up_low),
        "down": (cot, hidden),
        "gelu": (normed, gelu_low),
        "input": (normed, input_low),
        "out": (branch, mixed),
    }

    def cube_copy(stage, unit):
        slot = lax.rem(unit, RING)
        return remote(
            sends[stage].at[slot],
            gots[stage].at[slot],
            cube_sems.at[stage],
            slot,
            spot.flip(spot.bits[stage]),
        )

    def line_copy(span, place, sender):
        return pltpu.make_async_remote_copy(
            src_ref=ready.at[span * hi + place],
            dst_ref=got_line.at[span, sender],
            send_sem=line_sems.at[0, span * hi + place],
            recv_sem=line_sems.at[1, span * hi + sender],
            device_id=spot.line(place),
            device_id_type=MESH,
        )

    def thin_copy(stage):
        return remote(
            thin_sends[stage], thin_gots[stage], thin_sems, stage, spot.flip(spot.bits[stage])
        )

    def thin_line_copy(place, sender):
        return pltpu.make_async_remote_copy(
            src_ref=thin_ready.at[place],
            dst_ref=thin_line.at[sender],
            send_sem=thin_line_sems.at[0, place],
            recv_sem=thin_line_sems.at[1, sender],
            device_id=spot.line(place),
            device_id_type=MESH,
        )

    first_copy = remote(first_out, first_got, first_sems, 0, spot.cross)

    @pl.when(step == 0)
    def _():
        spot.greet(*[spot.flip(bit) for bit in spot.bits], spot.cross)

        def put(at):
            first_out[at, :] = first[at, :]

        by_rows(first.shape[0], STEP, put)
        first_copy.start()
        mine = spot.bit(1)
        for place in range(hi):
            for k in range(thin_sends[0].shape[1]):
                thin_sends[0][place, k] = thin[place, 2 * k + 1 - mine]
                thin_keeps[0][place, k] = thin[place, 2 * k + mine]
        thin_copy(0).start()

    for stage in range(stages):

        @pl.when(step == stage + 1)
        def _(stage=stage):
            thin_copy(stage).wait_recv()
            if stage < stages - 1:
                mine = spot.bit(spot.bits[stage + 1])
                for place in range(hi):
                    for k in range(thin_sends[stage + 1].shape[1]):
                        a, b = 2 * k + 1 - mine, 2 * k + mine
                        thin_sends[stage + 1][place, k] = (
                            thin_keeps[stage][place, a] + thin_gots[stage][place, a]
                        )
                        thin_keeps[stage + 1][place, k] = (
                            thin_keeps[stage][place, b] + thin_gots[stage][place, b]
                        )
                thin_copy(stage + 1).start()
            else:
                for place in range(hi):
                    thin_ready[place] = thin_keeps[stage][place, 0] + thin_gots[stage][place, 0]
                for distance in range(1, hi):
                    thin_line_copy(spot.away(distance), spot.z).start()

    @pl.when(step < units)
    def _():
        slot = lax.rem(step, RING)

        @pl.when(step >= RING)
        def _():
            cube_copy(0, step - RING).wait_send()

        for span, pieces in enumerate(spans):

            @pl.when(step // hi == span)
            def _(pieces=pieces):
                for name, begin, width, to in pieces:
                    if name == "gates":

                        def put(at, width=width, to=to):
                            made[at, to : to + width] = gates[0, at, :].astype(made.dtype)

                        by_rows(made.shape[0], STEP, put)
                        continue
                    left, right = sources[name]

                    def one(j, carry, left=left, right=right, begin=begin, width=width, to=to):
                        at = pl.ds(pl.multiple_of(j * LANE, LANE), LANE)
                        made[at, to : to + width] = lax.dot_general(
                            left[:, at],
                            right[:, begin : begin + width],
                            (((0,), (0,)), ((), ())),
                            preferred_element_type=F32,
                        ).astype(made.dtype)
                        return carry

                    lax.fori_loop(0, made.shape[0] // LANE, one, 0)

        mine = spot.bit(1)
        for k in range(sends[0].shape[1]):

            def put(at, k=k):
                def block(i):
                    at_made = pl.ds(pl.multiple_of(i * rows + at.start, each), each)
                    return made[at_made, :].astype(BF16)

                sends[0][slot, k, at, :] = block(2 * k + 1 - mine)
                keeps[0][slot, k, at, :] = block(2 * k + mine)

            by_rows(rows, each, put)
        cube_copy(0, step).start()

    for stage in range(stages):
        unit = step - stage - 1

        @pl.when(jnp.logical_and(unit >= 0, unit < units))
        def _(stage=stage, unit=unit):
            slot = lax.rem(unit, RING)
            cube_copy(stage, unit).wait_recv()

            def total(k, at):
                return (
                    keeps[stage][slot, k, at, :].astype(F32) + gots[stage][slot, k, at, :].astype(F32)
                ).astype(BF16)

            if stage < stages - 1:

                @pl.when(unit >= RING)
                def _():
                    cube_copy(stage + 1, unit - RING).wait_send()

                mine = spot.bit(spot.bits[stage + 1])
                for k in range(sends[stage + 1].shape[1]):

                    def put(at, k=k):
                        sends[stage + 1][slot, k, at, :] = total(2 * k + 1 - mine, at)
                        keeps[stage + 1][slot, k, at, :] = total(2 * k + mine, at)

                    by_rows(rows, each, put)
                cube_copy(stage + 1, unit).start()
            else:
                span, place = unit // hi, lax.rem(unit, hi)

                def put(at):
                    ready[unit, at, :] = total(0, at)

                by_rows(rows, each, put)

                @pl.when(place != spot.z)
                def _():
                    line_copy(span, place, spot.z).start()

    @pl.when(step == last_step)
    def _():
        for span in range(all_spans):
            for distance in range(1, hi):
                place = spot.away(distance)
                line_copy(span, place, place).wait_recv()
                line_copy(span, place, spot.z).wait_send()

            def give(at, span=span):
                own = ready[span * hi + spot.z, at, :]
                if span < kept:
                    for distance in range(hi):
                        place = spot.away(distance)
                        apart[span, place, at, :] = got_line[span, place, at, :] if distance else own
                else:
                    value = own.astype(F32)
                    for distance in range(1, hi):
                        value = value + got_line[span, spot.away(distance), at, :].astype(F32)
                    summed[span - kept, at, :] = value

            by_rows(rows, each, give)
        for stage in range(stages):
            for unit in range(units - RING, units):
                cube_copy(stage, unit).wait_send()
            thin_copy(stage).wait_send()
        value = thin_ready[spot.z]
        for distance in range(1, hi):
            place = spot.away(distance)
            thin_line_copy(place, place).wait_recv()
            thin_line_copy(place, spot.z).wait_send()
            value = value + thin_line[place]
        thin_own[...] = value
        first_copy.wait()

        def take(at):
            first_other[at, :] = first_got[at, :]

        by_rows(first.shape[0], STEP, take)


def column_spans(widths, width):
    spans, here, room = [], [], width
    for name, size in widths:
        begin = 0
        while begin < size:
            count = min(size - begin, room)
            here.append((name, begin, count, width - room))
            begin, room = begin + count, room - count
            if room == 0:
                spans, here, room = spans + [here], [], width
    assert not here
    return spans


def send_grads(grid, feed, rec, gates, first, thin):
    hi, inner = grid.hi, grid.inner_size
    second, cot, gate_low, up_low, hidden = feed
    normed, branch, gelu_low, input_low, mixed = rec
    d = second.shape[1]
    rows = d // grid.n
    slab = d // hi
    width = gate_low.shape[1]
    kept = 3
    channels = mixed.shape[1]
    spans = column_spans([(name, width) for name in ("gate", "up", "down")], width) + column_spans(
        [(name, channels) for name in ("gelu", "input", "out")] + [("gates", gates.shape[1])], width
    )
    all_spans = len(spans)
    units = all_spans * hi
    stages = inner.bit_length() - 1

    def place_of(i):
        return lax.rem(jnp.minimum(i, units - 1), hi)

    def slab_of(a):
        return pl.BlockSpec((a.shape[0], slab), lambda i: (0, place_of(i)))

    def whole(a):
        zeros = (0,) * a.ndim
        return pl.BlockSpec(a.shape, lambda i: zeros, pipeline_mode=pl.Buffered(1))

    apart = jax.ShapeDtypeStruct((kept, hi, rows, width), BF16)
    summed = jax.ShapeDtypeStruct((all_spans - kept, rows, width), F32)
    other = jax.ShapeDtypeStruct(first.shape, BF16)
    thin = thin.reshape(hi, inner, 8, thin.shape[1] // 8)
    thin_shape = thin.shape[2:]
    thin_own = jax.ShapeDtypeStruct(thin_shape, F32)
    outs = [apart, summed, other, thin_own]

    def halves(lead, tail, kind):
        return [
            pltpu.VMEM((lead, inner >> (stage + 1)) + tail, kind) for stage in range(stages)
        ]

    gates = gates.reshape(hi, slab, gates.shape[1])
    return pl.pallas_call(
        functools.partial(grads_kernel, grid.n, grid.tensor, spans, kept),
        grid=(units + stages,),
        out_shape=outs,
        in_specs=[slab_of(a) for a in (second, cot, normed, branch)]
        + [whole(a) for a in (gate_low, up_low, hidden, gelu_low, input_low, mixed)]
        + [pl.BlockSpec((1,) + gates.shape[1:], lambda i: (place_of(i), 0, 0))]
        + [whole(first), whole(thin)],
        out_specs=[whole(a) for a in outs],
        scratch_shapes=halves(RING, (rows, width), BF16) * 3
        + halves(hi, thin_shape, F32) * 3
        + [
            pltpu.VMEM((slab, width), BF16 if rows % 16 == 0 else F32),
            pltpu.VMEM((units, rows, width), BF16),
            pltpu.VMEM((all_spans, hi, rows, width), BF16),
            pltpu.VMEM(first.shape, BF16),
            pltpu.VMEM(first.shape, BF16),
            pltpu.VMEM((hi,) + thin_shape, F32),
            pltpu.VMEM((hi,) + thin_shape, F32),
            pltpu.SemaphoreType.DMA((stages, 2, RING)),
            pltpu.SemaphoreType.DMA((2, units)),
            pltpu.SemaphoreType.DMA((2, 1)),
            pltpu.SemaphoreType.DMA((2, stages)),
            pltpu.SemaphoreType.DMA((2, hi)),
        ],
        compiler_params=pltpu.CompilerParams(
            collective_id=4, has_side_effects=True, vmem_limit_bytes=GRANT
        ),
        name="send_grads",
    )(
        second, cot, normed, branch, gate_low, up_low, hidden, gelu_low, input_low, mixed, gates,
        first, thin,
    )


def rms_norm(values, gain):
    scale = lax.rsqrt(jnp.mean(values * values, axis=-1, keepdims=True) + 1e-06)
    return values * scale * gain


def dot(left, right):
    return jnp.dot(left, right, preferred_element_type=F32)


def dot_nt(left, right):
    return jnp.einsum("ik,jk->ij", left, right, preferred_element_type=F32)


def dot_tn(left, right):
    return jnp.einsum("ki,kj->ij", left, right, preferred_element_type=F32)


def local(
    block_in,
    segment_ids,
    cotangent,
    first_gain,
    gelu_weight,
    gelu_bias,
    input_weight,
    input_bias,
    conv_weight,
    conv_bias,
    inlet_weight,
    inlet_bias,
    forget_weight,
    forget_bias,
    decay_rate,
    out_weight,
    out_bias,
    second_gain,
    mlp_gate,
    mlp_up,
    mlp_down,
):
    grid = Grid()
    seq_count, tok_count, width = block_in.shape
    head_count, block_size = gelu_weight.shape[1:]
    channels = head_count * block_size
    margin = CONV - 1
    rows_all = seq_count * tok_count
    rows_half = rows_all // grid.tensor
    d_own = gelu_weight.shape[0]
    lane_own = gelu_bias.shape[1]
    units = mlp_gate.shape[1]
    unit_tiles = units // LANE
    window_tiles = -(-unit_tiles // grid.hi)
    window = window_tiles * LANE

    halo_rows = block_in[:, tok_count - HALO :]
    marks = (segment_ids + 1).astype(BF16)
    halo, rim_marks = shifted((halo_rows, marks[:, tok_count - margin :]), "wide", 1)
    halo = halo.reshape(seq_count * HALO, width)
    marks_ext = jnp.concatenate([rim_marks, marks], axis=1)
    earlier = [marks_ext[:, margin - k : margin - k + tok_count] == marks for k in range(1, CONV)]
    flags = jnp.stack([jnp.logical_not(earlier[0])] + earlier, axis=-1).astype(F32)
    flags = jnp.pad(flags.reshape(rows_all, CONV), ((0, 0), (0, 8 - CONV)))

    rec_own = jnp.stack(
        [
            input_weight.reshape(d_own, channels),
            gelu_weight.reshape(d_own, channels),
            out_weight.reshape(channels, d_own).T,
        ]
    )
    gates_own = jnp.stack([inlet_weight, forget_weight]).reshape(2 * head_count, lane_own, block_size)
    per_lane = jnp.stack([gelu_bias, input_bias])
    per_lane = jnp.concatenate(
        [per_lane, conv_weight, jnp.stack([conv_bias, inlet_bias, forget_bias, decay_rate])]
    )
    lane_table = lax.dynamic_update_slice(
        jnp.zeros((CONV + 6, head_count, block_size), BF16), per_lane, (0, 0, grid.w * lane_own)
    )
    per_width = jnp.stack([first_gain, out_bias, second_gain])
    width_table = lax.dynamic_update_slice(
        jnp.zeros((3, width), BF16), per_width, (0, grid.w * d_own)
    )
    thin_own = jnp.concatenate(
        [lane_table.reshape(CONV + 6, channels), width_table.reshape(-1, channels)]
    )
    thin_count = thin_own.shape[0]
    thin_own = jnp.pad(thin_own, ((0, -thin_count % 16), (0, 0)))
    feed_own = jnp.stack([mlp_gate, mlp_up, mlp_down.T])
    feed_windows = jnp.stack(
        [
            feed_own[:, :, tile * LANE : tile * LANE + window]
            for tile in (
                min(place * window_tiles, unit_tiles - window_tiles) for place in range(grid.hi)
            )
        ],
        axis=1,
    )
    cot_rows = cotangent.reshape(grid.tensor, rows_half, width)
    cot_own = pick(cot_rows, grid.t)
    rec_all, gates_all, thin_all, feed_all, cot_all = blank(
        (3, grid.n, d_own, channels),
        (2 * head_count, grid.n, lane_own, block_size),
        (grid.n,) + thin_own.shape,
        (3, grid.n + grid.hi, d_own, window),
        (grid.hi, grid.tensor, rows_half, width),
    )
    rec_all = lax.dynamic_update_slice(rec_all, rec_own[:, None], (0, grid.w, 0, 0))
    gates_all = lax.dynamic_update_slice(gates_all, gates_own[:, None], (0, grid.w, 0, 0))
    thin_all = lax.dynamic_update_slice(thin_all, thin_own[None], (grid.w, 0, 0))
    feed_all = lax.dynamic_update_slice(feed_all, feed_windows, (0, grid.n, 0, 0))
    feed_all = lax.dynamic_update_slice(
        feed_all, lax.dynamic_slice_in_dim(feed_windows, grid.z, 1, 1), (0, grid.w, 0, 0)
    )
    cot_all = lax.dynamic_update_slice(cot_all, cot_own[None, None], (grid.z, grid.t, 0, 0))
    rec_all, gates_all, thin_all, feed_all, cot_all = bring_weights(
        grid, rec_all, gates_all, thin_all, feed_all, cot_all
    )
    rec_all = rec_all.reshape(3, width, channels)
    input_full, gelu_full = rec_all[0], rec_all[1]
    gates_all = gates_all.reshape(2, head_count, block_size, block_size)
    inlet_full, forget_full = gates_all[0], gates_all[1]
    table = jnp.sum(thin_all.astype(F32), axis=0)
    lane_rows = table[: CONV + 6]
    gain_first, out_shift, gain_second = table[CONV + 6 : thin_count].reshape(3, width)
    rate = lane_rows[CONV + 5]
    lanes = jnp.concatenate([lane_rows[: CONV + 5], jnp.stack([jax.nn.softplus(rate), jax.nn.sigmoid(rate)])])
    lanes = jnp.pad(lanes, ((0, LANE_ROWS - lanes.shape[0]), (0, 0)))

    x = block_in.reshape(rows_all, width)
    normed, ext, conv, gelu_pre, inlet_pre, forget_pre, cum, local_state = enter_recurrence(
        x, halo, gain_first[None], rec_all, inlet_full, forget_full, lanes, flags, seq_count
    )
    entered, mixed, resid, second_own = make_second(
        grid, cum, local_state, gelu_pre, rec_all, x, out_shift[None], gain_second[None], seq_count
    )

    rows_feed = grid.hi * rows_all
    second_all, gate_low, up_low, hidden, branch_low, gain_two_grad = feed_forward(
        grid, second_own, feed_all, cot_all, resid, gain_second[None], unit_tiles
    )
    second_all, cot_all = (v.reshape(rows_feed, width) for v in (second_all, cot_all))
    gate_low, up_low, hidden = (v.reshape(rows_feed, window) for v in (gate_low, up_low, hidden))
    branch_low = branch_low.reshape(rows_all, width)
    gain_two_grad = jnp.sum(gain_two_grad, axis=0)
    feed_part = dot_nt(hidden, feed_all[2, : grid.n].reshape(width, window)).astype(BF16)
    feed_part = feed_part.reshape(grid.hi, grid.tensor, rows_half, width)
    block_out = block_output(grid, feed_part, resid).reshape(block_in.shape)

    gelu_low, input_low, gate_w_grads, lane_grads, out_shift_grad = leave_recurrence(
        grid, branch_low, rec_all, gelu_pre, local_state, cum, inlet_pre, forget_pre, conv, ext, entered,
        inlet_full, forget_full, lanes, flags, seq_count,
    )
    out_shift_grad = jnp.sum(out_shift_grad, axis=0)
    gate_w_grads = (
        gate_w_grads.reshape(2, head_count, grid.n, lane_own, block_size)
        .transpose(2, 0, 1, 3, 4)
        .reshape(width, block_size)
    )
    first_part = dot_nt(input_low, input_full) + dot_nt(gelu_low, gelu_full)
    inputs = x.astype(F32)
    scale_first = lax.rsqrt(jnp.mean(inputs * inputs, axis=-1, keepdims=True) + 1e-06)
    gain_one_grad = jnp.sum(first_part * inputs * scale_first, axis=0)
    first_part = first_part.astype(BF16)
    gain_grads = jnp.stack([gain_one_grad, gain_two_grad])
    gain_grads = gain_grads + grid.swap(gain_grads)

    lane_grads = (
        lane_grads[: CONV + 6]
        .reshape(CONV + 6, head_count, grid.n, lane_own)
        .transpose(2, 0, 1, 3)
        .reshape(grid.n, -1)
    )
    thin_grads = jnp.concatenate(
        [v.reshape(grid.n, d_own) for v in (gain_grads[0], out_shift_grad, gain_grads[1])]
        + [lane_grads],
        axis=1,
    )
    feed_grads, rec_grads, first_other, thin = send_grads(
        grid,
        (second_all, cot_all, gate_low, up_low, hidden),
        (normed, branch_low, gelu_low, input_low, mixed),
        gate_w_grads,
        first_part,
        thin_grads,
    )
    thin = thin.reshape(-1)
    rec_grads = jnp.concatenate(list(rec_grads), axis=1)
    gelu_w_grad = rec_grads[:, :channels]
    input_w_grad = rec_grads[:, channels : 2 * channels]
    out_grad = rec_grads[:, 2 * channels : 3 * channels]
    gate_w_grads = rec_grads[:, 3 * channels :].reshape(2, head_count, lane_own, block_size)

    def feed_weight_grad(got):
        pieces = []
        for place in range(grid.hi):
            begin = min(place * window_tiles, unit_tiles - window_tiles)
            skip = min(place * window_tiles - begin, window_tiles)
            if skip < window_tiles:
                pieces.append(got[place, :, skip * LANE :])
        return jnp.concatenate(pieces, axis=1).astype(F32)

    gate_grad, up_grad, down_grad = (feed_weight_grad(got) for got in feed_grads)
    down_grad = down_grad.T
    first_grad = first_part.astype(F32) + first_other.astype(F32)
    _, pull_first = jax.vjp(rms_norm, inputs, gain_first)
    input_norm_grad, _ = pull_first(first_grad)
    block_grad = (branch_low.astype(F32) + input_norm_grad).reshape(block_in.shape)
    gain_one_own, out_shift_own, gain_two_own = (
        thin[i * d_own : (i + 1) * d_own] for i in range(3)
    )
    lanes = thin[3 * d_own :].reshape(CONV + 6, head_count, lane_own)
    weight_shape = gelu_weight.shape
    return (
        block_out,
        block_grad,
        gain_one_own,
        gelu_w_grad.reshape(weight_shape),
        lanes[0],
        input_w_grad.reshape(weight_shape),
        lanes[1],
        lanes[2 : 2 + CONV],
        lanes[2 + CONV],
        gate_w_grads[0],
        lanes[3 + CONV],
        gate_w_grads[1],
        lanes[4 + CONV],
        lanes[5 + CONV],
        out_grad.T.reshape(out_weight.shape),
        out_shift_own,
        gain_two_own,
        gate_grad,
        up_grad,
        down_grad,
    )


def solution(mesh):
    in_specs = (
        P(None, "wide", None),
        P(None, "wide"),
        P(None, "wide", None),
        P("wide"),
        P("wide", "tensor", None),
        P("tensor", "wide"),
        P("wide", "tensor", None),
        P("tensor", "wide"),
        P(None, "tensor", "wide"),
        P("tensor", "wide"),
        P("tensor", "wide", None),
        P("tensor", "wide"),
        P("tensor", "wide", None),
        P("tensor", "wide"),
        P("tensor", "wide"),
        P("tensor", None, "wide"),
        P("wide"),
        P("wide"),
        P("wide", "tensor"),
        P("wide", "tensor"),
        P("tensor", "wide"),
    )
    out_specs = (
        P(None, "wide", None),
        P(None, "wide", None),
        P("wide"),
        P("wide", "tensor", None),
        P("tensor", "wide"),
        P("wide", "tensor", None),
        P("tensor", "wide"),
        P(None, "tensor", "wide"),
        P("tensor", "wide"),
        P("tensor", "wide", None),
        P("tensor", "wide"),
        P("tensor", "wide", None),
        P("tensor", "wide"),
        P("tensor", "wide"),
        P("tensor", None, "wide"),
        P("wide"),
        P("wide"),
        P("wide", "tensor"),
        P("wide", "tensor"),
        P("tensor", "wide"),
    )
    return jax.shard_map(local, mesh=mesh, in_specs=in_specs, out_specs=out_specs, check_vma=False)
```

```python
import functools

import jax
import jax.numpy as jnp
from jax import lax
from jax.experimental import pallas as pl
from jax.experimental.pallas import tpu as pltpu
from jax.sharding import PartitionSpec as P

CONV = 4
LANE = 128
GRANT = 60 * 1024 * 1024
F32 = jnp.float32
BF16 = jnp.bfloat16

LINE = 4


class Grid:
    def __init__(self):
        self.n = lax.axis_size("wide")
        self.hi = LINE
        self.inner_size = self.n // LINE
        self.tensor = lax.axis_size("tensor")
        self.w = lax.axis_index("wide")
        self.t = lax.axis_index("tensor")
        self.z = self.w // self.inner_size
        self.inner = lax.rem(self.w, self.inner_size)

    def flip(self, value, bit):
        return lax.ppermute(value, "wide", [(i, i ^ bit) for i in range(self.n)])

    def swap(self, value):
        size = self.tensor
        pairs = [(i, (i + 1) % size) for i in range(size)]
        return lax.ppermute(value, "tensor", pairs)


def shifted(shard, axis, by):
    size = lax.axis_size(axis)
    place = lax.axis_index(axis) - by
    there = jnp.logical_and(place >= 0, place < size)
    pairs = [(i, (i + by) % size) for i in range(size)]
    moved = lax.ppermute(shard, axis, pairs)
    return jax.tree.map(lambda a: jnp.where(there, a, jnp.zeros_like(a)), moved)


def pick(values, index, axis=0):
    return lax.dynamic_index_in_dim(values, index, axis, keepdims=False)


MESH = pl.DeviceIdType.MESH


class Spot:
    def __init__(self, n, tensor):
        self.n = n
        self.hi = LINE
        self.inner_size = n // LINE
        self.bits = [1 << i for i in range(self.inner_size.bit_length() - 1)]
        self.tensor = tensor
        self.w = lax.axis_index("wide")
        self.t = lax.axis_index("tensor")
        self.z = self.w // self.inner_size
        self.inner = lax.rem(self.w, self.inner_size)
        self.cross = {"tensor": lax.rem(self.t + 1, tensor)}

    def bit(self, which):
        return lax.rem(self.inner // which, 2)

    def flip(self, which):
        return {"wide": self.w + which - 2 * which * self.bit(which)}

    def line(self, place):
        return {"wide": place * self.inner_size + self.inner}

    def away(self, distance):
        return lax.rem(self.z + distance, self.hi)

    def greet(self, *sides):
        barrier = pltpu.get_barrier_semaphore()
        for side in sides:
            pl.semaphore_signal(barrier, inc=1, device_id=side, device_id_type=MESH)
        for distance in range(1, self.hi):
            pl.semaphore_signal(
                barrier, inc=1, device_id=self.line(self.away(distance)), device_id_type=MESH
            )
        pl.semaphore_wait(barrier, len(sides) + self.hi - 1)


def remote(src, dst, sems, index, side):
    return pltpu.make_async_remote_copy(
        src_ref=src,
        dst_ref=dst,
        send_sem=sems.at[0, index],
        recv_sem=sems.at[1, index],
        device_id=side,
        device_id_type=MESH,
    )


class Fans:
    def __init__(self, spot, at, sems, base, sides):
        self.spot, self.at, self.sems, self.base, self.sides = spot, at, sems, base, sides
        self.kinds = sorted(range(1 << len(sides)), key=lambda k: (bin(k).count("1"), -k))

    def onto(self, k):
        low = (k & -k) if k else 1 << len(self.sides)
        return [i for i in reversed(range(len(self.sides))) if (1 << i) < low]

    def copy(self, place, k, i, here=False):
        spot, hi = self.spot, self.spot.hi
        landed = k if here else k | (1 << i)
        index = self.base + (landed - 1) * hi + lax.rem(place - spot.z + hi, hi)
        ref = self.at(place, k)
        return remote(ref, ref, self.sems, index, self.sides[i])

    def hand_on(self, place, k):
        for i in self.onto(k):
            self.copy(place, k, i).start()

    def arrive(self, place, k):
        low = (k & -k).bit_length() - 1
        self.copy(place, k, low, here=True).wait_recv()

    def pass_on(self, place):
        for k in self.kinds:
            if k and self.onto(k):
                self.arrive(place, k)
                self.hand_on(place, k)

    def finish(self, place):
        for k in self.kinds:
            if k and not self.onto(k):
                self.arrive(place, k)
        self.finish_sends(place)

    def finish_sends(self, place):
        for k in self.kinds:
            for i in self.onto(k):
                self.copy(place, k, i).wait_send()

    def count(sides, hi):
        return ((1 << sides) - 1) * hi


class Chain:
    def __init__(self, spot, at, sems, sides):
        self.spot, self.at, self.sems = spot, at, sems
        self.fans = Fans(spot, at, sems, 2 * (spot.hi - 1), sides)

    def line_copy(self, s, up):
        spot, hi = self.spot, self.spot.hi
        owner = spot.z - (s - 1) if up else spot.z + (s - 1)
        other = spot.z + 1 if up else spot.z - 1
        ref = self.at(owner, 0)
        return remote(ref, ref, self.sems, (s - 1) if up else hi + s - 2, spot.line(other))

    def line_here(self, s, up):
        spot, hi = self.spot, self.spot.hi
        owner = spot.z - s if up else spot.z + s
        other = spot.z - 1 if up else spot.z + 1
        ref = self.at(owner, 0)
        return remote(ref, ref, self.sems, (s - 1) if up else hi + s - 2, spot.line(other))

    def first(self):
        self.first_line()
        self.fans.hand_on(self.spot.z, 0)

    def first_line(self):
        spot, hi = self.spot, self.spot.hi

        @pl.when(spot.z < hi - 1)
        def _():
            self.line_copy(1, True).start()

        @pl.when(spot.z > 0)
        def _():
            self.line_copy(1, False).start()

    def onward(self, s):
        spot, hi = self.spot, self.spot.hi

        @pl.when(spot.z >= s)
        def _():
            self.line_here(s, True).wait_recv()

        if s < hi - 1:

            @pl.when(jnp.logical_and(spot.z >= s, spot.z < hi - 1))
            def _():
                self.line_copy(s + 1, True).start()

        @pl.when(spot.z >= s)
        def _():
            self.fans.hand_on(spot.z - s, 0)

        @pl.when(spot.z <= hi - 1 - s)
        def _():
            self.line_here(s, False).wait_recv()

        if s < hi - 1:

            @pl.when(jnp.logical_and(spot.z <= hi - 1 - s, spot.z > 0))
            def _():
                self.line_copy(s + 1, False).start()

        @pl.when(spot.z <= hi - 1 - s)
        def _():
            self.fans.hand_on(spot.z + s, 0)

    def places(self, s, act):
        spot = self.spot
        if s == 0:
            act(spot.z)
            return

        @pl.when(spot.z >= s)
        def _():
            act(spot.z - s)

        @pl.when(spot.z <= spot.hi - 1 - s)
        def _():
            act(spot.z + s)

    def second(self, s):
        self.places(s, self.fans.pass_on)

    def finish(self):
        for s in range(self.spot.hi):
            self.places(s, self.fans.finish)
        self.finish_line()

    def finish_sends(self):
        for s in range(self.spot.hi):
            self.places(s, self.fans.finish_sends)
        self.finish_line()

    def finish_line(self):
        spot, hi = self.spot, self.spot.hi
        for s in range(1, hi):

            @pl.when(jnp.logical_and(spot.z >= s - 1, spot.z < hi - 1))
            def _():
                self.line_copy(s, True).wait_send()

            @pl.when(jnp.logical_and(spot.z <= hi - s, spot.z > 0))
            def _():
                self.line_copy(s, False).wait_send()


def chain_sems(sides):
    return pltpu.SemaphoreType.DMA((2, 2 * (LINE - 1) + ((1 << sides) - 1) * LINE))


class Turns:
    def __init__(self, spot, distances, window_of, at, sems, sides):
        self.spot, self.window_of, self.at, self.sems = spot, window_of, at, sems
        self.distances = distances
        self.fans = Fans(spot, at, sems, spot.hi, sides)

    def line_copy(self, distance):
        spot = self.spot
        place = spot.away(distance)
        return remote(self.window_of(place), self.at(spot.z, 0), self.sems, distance, spot.line(place))

    def back(self, distance):
        return lax.rem(self.spot.z - distance + self.spot.hi, self.spot.hi)

    def line_here(self, distance):
        place = self.back(distance)
        ref = self.at(place, 0)
        return remote(ref, ref, self.sems, distance, self.spot.line(place))

    def first(self):
        for distance in self.distances:
            self.start(distance)

    def start(self, distance):
        if distance:
            self.line_copy(distance).start()
        else:
            self.fans.hand_on(self.spot.z, 0)

    def onward(self, distance):
        if distance in self.distances:
            self.line_here(distance).wait_recv()
            self.fans.hand_on(self.back(distance), 0)

    def second(self, distance):
        if distance in self.distances:
            self.fans.pass_on(self.back(distance))

    def finish(self):
        for distance in self.distances:
            self.fans.finish(self.back(distance))
            if distance:
                self.line_copy(distance).wait_send()


EARLY = (2,)
LATE = (0, 1, 3)


def feed_turns(spot, distances, feed, sems, cube):
    def index(place, k):
        return place * spot.inner_size + jnp.bitwise_xor(spot.inner, k)

    return Turns(
        spot,
        distances,
        lambda place: feed.at[:, spot.n + place],
        lambda place, k: feed.at[:, index(place, k)],
        sems,
        cube,
    )


def weights_kernel(
    n, tensor, rec, gates, thin, feed, rec_all, gates_all, thin_all, feed_all,
    rec_sems, gates_sems, thin_sems, feed_sems,
):
    del rec, gates, thin, feed
    spot = Spot(n, tensor)
    hi = spot.hi

    def index(place, k):
        return place * spot.inner_size + jnp.bitwise_xor(spot.inner, k)

    cube = [spot.flip(bit) for bit in spot.bits]
    moves = [
        Chain(spot, lambda place, k: thin_all.at[index(place, k)], thin_sems, cube),
        Chain(spot, lambda place, k: gates_all.at[:, index(place, k)], gates_sems, cube),
        Chain(spot, lambda place, k: rec_all.at[:, index(place, k)], rec_sems, cube),
        feed_turns(spot, EARLY, feed_all, feed_sems, cube),
    ]
    spot.greet(*cube)
    for move in moves:
        move.first()
    for s in range(1, hi):
        for move in moves:
            move.onward(s)
        for move in moves:
            move.second(s - 1)
    for move in moves:
        move.second(hi - 1)
    for move in moves:
        move.finish()


def turn_sems(grid):
    return pltpu.SemaphoreType.DMA((2, grid.n))


def blank(*shapes):
    return pl.pallas_call(
        lambda *refs: None,
        out_shape=[jax.ShapeDtypeStruct(shape, BF16) for shape in shapes],
        out_specs=[pl.BlockSpec(memory_space=pl.ANY)] * len(shapes),
        compiler_params=pltpu.CompilerParams(vmem_limit_bytes=GRANT),
        name="blank",
    )()


def bring_weights(grid, rec, gates, thin, feed):
    n, hi, tensor = grid.n, grid.hi, grid.tensor
    far = pl.BlockSpec(memory_space=pl.ANY)
    arrays = (rec, gates, thin, feed)
    cube = grid.inner_size.bit_length() - 1
    return pl.pallas_call(
        functools.partial(weights_kernel, n, tensor),
        out_shape=[jax.ShapeDtypeStruct(a.shape, a.dtype) for a in arrays],
        in_specs=[far] * len(arrays),
        out_specs=[far] * len(arrays),
        input_output_aliases={i: i for i in range(len(arrays))},
        scratch_shapes=[
            chain_sems(cube),
            chain_sems(cube),
            chain_sems(cube),
            turn_sems(grid),
        ],
        compiler_params=pltpu.CompilerParams(
            collective_id=0, has_side_effects=True, vmem_limit_bytes=GRANT
        ),
        name="bring_weights",
    )(*arrays)


def by_rows(rows, step, act):
    def one(i, carry):
        act(pl.ds(pl.multiple_of(i * step, step), step))
        return carry

    lax.fori_loop(0, rows // step, one, 0)


STEP = 16


GELU_SLOPE = 0.7978845608028654
GELU_CUBE = 0.044715
HALO = 8
GELU_SHIFT, INPUT_SHIFT, TAPS, CONV_SHIFT, INLET_SHIFT, FORGET_SHIFT, RATE_SOFT, RATE_SIGMOID = 0, 1, 2, 6, 7, 8, 9, 10
LANE_ROWS = 16


def gelu_of(v):
    bent = jnp.tanh(GELU_SLOPE * (v + GELU_CUBE * (v * v * v)))
    half = 0.5 * (1.0 + bent)
    slope = half + 0.5 * v * (1.0 - bent * bent) * (GELU_SLOPE * (1.0 + 3.0 * GELU_CUBE * (v * v)))
    return v * half, slope


def minus_expm1(x):
    series = jnp.ones_like(x)
    for k in range(9, 1, -1):
        series = 1.0 + series * x * (1.0 / k)
    return jnp.where(x > -0.5, -x * series, 1.0 - jnp.exp(x))


def decay_of(forget, soft, starts):
    log_decay = -8.0 * forget * soft
    decay = jnp.where(starts, 0.0, jnp.exp(log_decay))
    scaler = jnp.where(starts, 1.0, jnp.sqrt(minus_expm1(2.0 * log_decay)))
    return decay, scaler


def tile_scan(a, b, state_in, decay_in, reverse):
    place = lax.broadcasted_iota(jnp.int32, a.shape, 0)
    for by in (1, 2, 4):
        turn = 8 - by if reverse else by
        ok = place < 8 - by if reverse else place >= by
        b = jnp.where(ok, a * pltpu.roll(b, turn, 0) + b, b)
        a = jnp.where(ok, a * pltpu.roll(a, turn, 0), a)
    return a * decay_in, b + a * state_in


def scan_rows(seqs, length, width, read, write, reverse):
    tiles = length // 8
    last = 0 if reverse else 7

    def one(i, carry):
        tile = tiles - 1 - i if reverse else i
        after = []
        for s in range(seqs):
            decay_in, state_in = carry[s]
            at = pl.ds(pl.multiple_of(s * length + tile * 8, 8), 8)
            a, b = tile_scan(*read(at), state_in, decay_in, reverse)
            write(at, a, b)
            after.append(
                tuple(jnp.broadcast_to(v[last : last + 1], (8, width)) for v in (a, b))
            )
        return tuple(after)

    start = (jnp.ones((8, width), F32), jnp.zeros((8, width), F32))
    lax.fori_loop(0, tiles, one, (start,) * seqs)


def first_kernel(x, input_low, gelu_low, w_input, w_gelu, scale, part, gained):
    value = dot_nt(input_low[...], w_input[0]) + dot_nt(gelu_low[...], w_gelu[0])
    part[...] = value.astype(BF16)
    gained[...] = jnp.sum(
        (value * x[...].astype(F32) * scale[:, 0:1]).reshape(-1, 8, value.shape[1]), axis=0
    )


def first_gradient(x, input_low, gelu_low, rec, scale):
    rows, d = x.shape
    channels = input_low.shape[1]
    chunk = 512

    def fixed(a):
        return pl.BlockSpec(a.shape, lambda i: (0, 0))

    def weight(k):
        return pl.BlockSpec((1, chunk, channels), lambda i: (k, i, 0))

    column = pl.BlockSpec((rows, chunk), lambda i: (0, i))
    return pl.pallas_call(
        first_kernel,
        grid=(d // chunk,),
        out_shape=[jax.ShapeDtypeStruct((rows, d), BF16), jax.ShapeDtypeStruct((8, d), F32)],
        in_specs=[column, fixed(input_low), fixed(gelu_low), weight(0), weight(1), fixed(scale)],
        out_specs=[column, pl.BlockSpec((8, chunk), lambda i: (0, i))],
        compiler_params=pltpu.CompilerParams(vmem_limit_bytes=GRANT),
        name="first_gradient",
    )(x, input_low, gelu_low, rec, rec, scale)


class Prefix:
    def __init__(self, spot, seqs, reverse, tots, gots, line, cube_sems, line_sems):
        self.spot, self.seqs, self.reverse = spot, seqs, reverse
        self.tots, self.gots, self.line = tots, gots, line
        self.cube_sems, self.line_sems = cube_sems, line_sems

    def line_copy(self, place, sender):
        stages = len(self.spot.bits)
        return pltpu.make_async_remote_copy(
            src_ref=self.tots.at[stages],
            dst_ref=self.line.at[sender],
            send_sem=self.line_sems.at[0, place],
            recv_sem=self.line_sems.at[1, sender],
            device_id=self.spot.line(place),
            device_id_type=MESH,
        )

    def run(self):
        spot, seqs, hi = self.spot, self.seqs, self.spot.hi
        a, b = slice(0, seqs), slice(seqs, 2 * seqs)
        width = self.tots.shape[2]
        enter_a, enter_b = jnp.ones((seqs, width), F32), jnp.zeros((seqs, width), F32)
        for stage, bit in enumerate(spot.bits):
            copy = remote(
                self.tots.at[stage], self.gots.at[stage], self.cube_sems, stage, spot.flip(bit)
            )
            copy.start()
            copy.wait()
            mine_a, mine_b = self.tots[stage, a, :], self.tots[stage, b, :]
            got_a, got_b = self.gots[stage, a, :], self.gots[stage, b, :]
            after = spot.bit(bit) == (0 if self.reverse else 1)
            enter_b = jnp.where(after, enter_a * got_b + enter_b, enter_b)
            enter_a = jnp.where(after, enter_a * got_a, enter_a)
            self.tots[stage + 1, a, :] = mine_a * got_a
            self.tots[stage + 1, b, :] = jnp.where(
                after, mine_a * got_b + mine_b, got_a * mine_b + got_b
            )
            self.tots[stage + 1, 2 * seqs :, :] = jnp.zeros((8 - 2 * seqs, width), F32)
        for distance in range(1, hi):
            self.line_copy(spot.away(distance), spot.z).start()
        for distance in range(1, hi):
            place = spot.away(distance)
            self.line_copy(place, place).wait_recv()
            self.line_copy(place, spot.z).wait_send()
        come = jnp.zeros((seqs, width), F32)
        for place in reversed(range(hi)) if self.reverse else range(hi):
            before = spot.z < place if self.reverse else spot.z > place
            come = jnp.where(before, self.line[place, a, :] * come + self.line[place, b, :], come)
        return enter_a * come + enter_b


def prefix_scratch(grid, channels):
    stages = grid.inner_size.bit_length() - 1
    return [
        pltpu.VMEM((stages + 1, 8, channels), F32),
        pltpu.VMEM((stages, 8, channels), F32),
        pltpu.VMEM((grid.hi, 8, channels), F32),
        pltpu.SemaphoreType.DMA((2, stages)),
        pltpu.SemaphoreType.DMA((2, grid.hi)),
    ]


def forward_kernel(
    n, tensor, seqs, heads,
    x, halo, gain, w_input, w_gelu, w_inlet, w_forget, lanes, flags, w_out, shift, gain_second, feed, cot,
    normed, ext, conv, gelu_pre, inlet_pre, forget_pre, cum, local, entered, mixed, resid, second,
    feed_all, cot_all,
    held, factor, addend, part, out, got, tots, gots, line, cube_sems, line_sems, swap_sems, feed_sems, cot_sems,
):
    del feed, cot
    spot = Spot(n, tensor)
    hi = spot.hi
    rows = x.shape[0]
    length = rows // seqs
    width = conv.shape[1]
    step = pl.program_id(0)
    cube = [spot.flip(bit) for bit in spot.bits]
    turns = feed_turns(spot, LATE, feed_all, feed_sems, cube)
    chain = Chain(
        spot,
        lambda place, k: cot_all.at[place, lax.rem(spot.t + k, tensor)],
        cot_sems,
        [spot.cross],
    )

    @pl.when(step == 0)
    def _():
        spot.greet(*cube, spot.cross)
        turns.start(1)
        turns.start(0)
        chain.fans.hand_on(spot.z, 0)

        def norm(source, at, to):
            value = source[at, :].astype(F32)
            scale = lax.rsqrt(jnp.mean(value * value, axis=-1, keepdims=True) + 1e-06)
            value = (value * scale * gain[...]).astype(BF16)
            held[pl.ds(pl.multiple_of(at.start + to, STEP), STEP), :] = value
            return value

        def main(at):
            normed[at, :] = norm(x, at, 0)

        by_rows(rows, STEP, main)
        by_rows(halo.shape[0], STEP, lambda at: norm(halo, at, rows))

    @pl.when(step < heads)
    def _():
        table = lanes[...]
        cols = pl.ds(pl.multiple_of(step * width, width), width)

        def row(i):
            return table[i : i + 1]

        branch = (dot(held[...], w_input[0]) + row(INPUT_SHIFT)).astype(BF16)
        gelu_pre[:, cols] = dot(held[0:rows, :], w_gelu[0]) + row(GELU_SHIFT)
        for s in range(seqs):
            here = slice(s * length, (s + 1) * length)
            front = rows + s * HALO
            longer = jnp.concatenate(
                [branch[front : front + HALO].astype(F32), branch[here].astype(F32)], axis=0
            )
            ext[s] = longer.astype(BF16)
            total = row(CONV_SHIFT) + row(TAPS) * longer[HALO:]
            for k in range(1, CONV):
                moved = pltpu.roll(longer, k, 0)[HALO:]
                total = total + jnp.where(flags[here, k : k + 1] > 0.5, row(TAPS + k) * moved, 0.0)
            conv[here, :] = total.astype(BF16)
        blocks = conv[...]
        inlet_pre[...] = dot(blocks, w_inlet[0]) + row(INLET_SHIFT)
        forget_pre[...] = dot(blocks, w_forget[0]) + row(FORGET_SHIFT)

        def terms(at):
            starts = flags[at, 0:1] > 0.5
            decay, scaler = decay_of(jax.nn.sigmoid(forget_pre[at, :]), row(RATE_SOFT), starts)
            factor[at, :] = decay
            addend[at, :] = scaler * jax.nn.sigmoid(inlet_pre[at, :]) * conv[at, :].astype(F32)

        by_rows(rows, 32, terms)

        def write(at, a, b):
            cum[at, cols] = a
            local[at, cols] = b

        scan_rows(seqs, length, width, lambda at: (factor[at, :], addend[at, :]), write, False)

    @pl.when(step == heads)
    def _():
        chain.first_line()
        tots[0] = jnp.zeros_like(tots[0])
        for s in range(seqs):
            tots[0, s : s + 1, :] = cum[(s + 1) * length - 8 : (s + 1) * length, :][7:8]
            tots[0, seqs + s : seqs + s + 1, :] = local[(s + 1) * length - 8 : (s + 1) * length, :][7:8]
        enter = Prefix(spot, seqs, False, tots, gots, line, cube_sems, line_sems).run()
        entered[...] = jnp.zeros_like(entered)
        entered[0:seqs, :] = enter
        for s in range(seqs):

            def mix(at, s=s):
                here = pl.ds(pl.multiple_of(s * length + at.start, STEP), STEP)
                state = local[here, :] + cum[here, :] * enter[s : s + 1]
                mixed[here, :] = (state * gelu_of(gelu_pre[here, :])[0]).astype(BF16)

            by_rows(length, STEP, mix)
        turns.onward(1)
        turns.start(3)
        values = mixed[...]
        own_rows = resid.shape[0]

        def branch(j, carry):
            at = pl.ds(pl.multiple_of(j * 256, 256), 256)
            value = dot_nt(values, w_out[0, at, :])
            for side in range(tensor):
                part[side, :, at] = value[side * own_rows : (side + 1) * own_rows]
            return carry

        lax.fori_loop(0, x.shape[1] // 256, branch, 0)

        def put(at):
            out[at, :] = part[1 - spot.t, at, :].astype(BF16)

        by_rows(own_rows, STEP, put)
        copy = remote(out, got, swap_sems, 0, spot.cross)
        copy.start()
        chain.onward(1)
        copy.wait()

        def norm(at):
            own = x[pl.ds(pl.multiple_of(spot.t * own_rows + at.start, STEP), STEP), :].astype(F32)
            value = own + (part[spot.t, at, :] + got[at, :].astype(F32) + shift[...])
            resid[at, :] = value
            scale = lax.rsqrt(jnp.mean(value * value, axis=-1, keepdims=True) + 1e-06)
            second[at, :] = (value * scale * gain_second[...]).astype(BF16)

        by_rows(own_rows, STEP, norm)
        turns.second(0)
        turns.onward(3)
        chain.onward(2)
        turns.second(1)
        chain.onward(3)
        turns.second(3)
        turns.finish()
        chain.finish()


def forward_recurrence(
    grid, x, halo, gain, rec, inlet, forget, lanes, flags, shift, gain_second, feed, cot, seqs
):
    rows, d = x.shape
    heads, width = inlet.shape[:2]
    channels = heads * width
    longer = rows // seqs + HALO
    own_rows = rows // grid.tensor

    def head_of(i):
        return jnp.minimum(i, heads - 1)

    def fixed(a):
        zeros = (0,) * len(a.shape)
        return pl.BlockSpec(a.shape, lambda i: zeros, pipeline_mode=pl.Buffered(1))

    def column(count):
        return pl.BlockSpec((count, width), lambda i: (0, head_of(i)))

    def weight(k):
        return pl.BlockSpec((1, d, width), lambda i: (k, 0, head_of(i)))

    head = pl.BlockSpec((1, width, width), lambda i: (head_of(i), 0, 0))
    far = pl.BlockSpec(memory_space=pl.ANY)
    wide = jax.ShapeDtypeStruct((rows, channels), F32)
    outs = [
        jax.ShapeDtypeStruct((rows, d), BF16),
        jax.ShapeDtypeStruct((seqs, longer, channels), BF16),
        jax.ShapeDtypeStruct((rows, channels), BF16),
        wide,
        wide,
        wide,
        wide,
        wide,
        jax.ShapeDtypeStruct((8, channels), F32),
        jax.ShapeDtypeStruct((rows, channels), BF16),
        jax.ShapeDtypeStruct((own_rows, d), F32),
        jax.ShapeDtypeStruct((own_rows, d), BF16),
        jax.ShapeDtypeStruct(feed.shape, BF16),
        jax.ShapeDtypeStruct(cot.shape, BF16),
    ]
    return pl.pallas_call(
        functools.partial(forward_kernel, grid.n, grid.tensor, seqs, heads),
        grid=(heads + 1,),
        out_shape=outs,
        in_specs=[fixed(x), fixed(halo), fixed(gain), weight(0), weight(1), head, head]
        + [column(LANE_ROWS), fixed(flags)]
        + [pl.BlockSpec((1, d, channels), lambda i: (2, 0, 0), pipeline_mode=pl.Buffered(1))]
        + [fixed(shift), fixed(gain_second), far, far],
        out_specs=[
            fixed(outs[0]),
            pl.BlockSpec((seqs, longer, width), lambda i: (0, 0, head_of(i))),
            column(rows),
            fixed(wide),
            column(rows),
            column(rows),
        ]
        + [fixed(a) for a in outs[6:12]]
        + [far, far],
        input_output_aliases={12: 12, 13: 13},
        scratch_shapes=[
            pltpu.VMEM((rows + halo.shape[0], d), BF16),
            pltpu.VMEM((rows, width), F32),
            pltpu.VMEM((rows, width), F32),
            pltpu.VMEM((grid.tensor, own_rows, d), F32),
            pltpu.VMEM((own_rows, d), BF16),
            pltpu.VMEM((own_rows, d), BF16),
        ]
        + prefix_scratch(grid, channels)
        + [pltpu.SemaphoreType.DMA((2, 1)), turn_sems(grid), chain_sems(1)],
        compiler_params=pltpu.CompilerParams(
            collective_id=1, has_side_effects=True, vmem_limit_bytes=GRANT
        ),
        name="forward_recurrence",
    )(x, halo, gain, rec, rec, inlet, forget, lanes, flags, rec, shift, gain_second, feed, cot)


def leave_kernel(
    n, tensor, seqs, branch, w_out, gelu_pre, local, cum, inlet_pre, forget_pre, conv, ext, entered,
    w_inlet, w_forget, lanes, flags, feed_part, resid,
    gelu_low, input_low, gate_grads, lane_grads, shift_grad, own_out,
    tail, carried, factor, addend, back, rim, tots, gots, line, cube_sems, line_sems, rim_sems,
    part, sums_got, sums_line, sums_cross, sums_sems,
):
    spot = Spot(n, tensor)
    every, channels = conv.shape
    length = every // seqs
    heads, width = w_inlet.shape[:2]
    behind = {"wide": lax.rem(spot.w + n - 1, n)}
    ahead = {"wide": lax.rem(spot.w + 1, n)}
    spot.greet(*[spot.flip(bit) for bit in spot.bits], behind, ahead, spot.cross)
    for place in range(spot.hi):
        for side in range(tensor):

            def put(at, place=place, side=side):
                part[place, side, at, :] = feed_part[place, side, at, :]

            by_rows(resid.shape[0], STEP, put)
    sums = Rows(spot, part, sums_got, sums_line, sums_cross, sums_sems)
    sums.start()
    tots[0] = jnp.zeros_like(tots[0])
    lane_grads[...] = jnp.zeros_like(lane_grads)
    shift_grad[...] = jnp.zeros_like(shift_grad)

    def add(at):
        shift_grad[...] += jnp.sum(branch[at, :].astype(F32).reshape(2, 8, -1), axis=0)

    by_rows(every, STEP, add)

    def decays(at, cols):
        soft = lanes[RATE_SOFT : RATE_SOFT + 1, cols]
        return decay_of(jax.nn.sigmoid(forget_pre[at, cols]), soft, flags[at, 0:1] > 0.5)

    def upward(h, none):
        cols = pl.ds(pl.multiple_of(h * width, width), width)
        grad = dot(branch[...], w_out[0, :, cols])
        gelu, slope = gelu_of(gelu_pre[:, cols])
        for s in range(seqs):
            here = slice(s * length, (s + 1) * length)
            state = local[here, cols] + cum[here, cols] * entered[s : s + 1, cols]
            low = (grad[here] * state * slope[here]).astype(BF16)
            gelu_low[here, cols] = low
            lane_grads[0:1, cols] += jnp.sum(low.astype(F32), axis=0, keepdims=True)
            decay, _ = decays(here, cols)
            place = lax.broadcasted_iota(jnp.int32, (length, width), 0)
            factor[here, :] = jnp.where(place < length - 1, pltpu.roll(decay, length - 1, 0), 1.0)
        addend[...] = grad * gelu

        def write(at, a, b):
            tail[at, cols] = a
            carried[at, cols] = b

        scan_rows(seqs, length, width, lambda at: (factor[at, :], addend[at, :]), write, True)
        for s in range(seqs):
            first = slice(s * length, s * length + 8)
            decay, _ = decays(first, cols)
            tots[0, s : s + 1, cols] = decay[0:1] * tail[first, cols][0:1]
            tots[0, seqs + s : seqs + s + 1, cols] = decay[0:1] * carried[first, cols][0:1]
        return none

    lax.fori_loop(0, heads // 2, upward, 0)
    sums.along(1)
    lax.fori_loop(heads // 2, heads, upward, 0)
    sums.along(2)
    come = Prefix(spot, seqs, True, tots, gots, line, cube_sems, line_sems).run()
    tots[0, 0:seqs, :] = come

    def downward(h, none):
        cols = pl.ds(pl.multiple_of(h * width, width), width)

        def row(i):
            return lanes[i : i + 1, cols]

        sums = []
        for s in range(seqs):
            here = slice(s * length, (s + 1) * length)
            place = lax.broadcasted_iota(jnp.int32, (length, width), 0)
            starts = flags[here, 0:1] > 0.5
            blocks = conv[here, cols].astype(F32)
            enter = entered[s : s + 1, cols]
            state = local[here, cols] + cum[here, cols] * enter
            before = jnp.where(place > 0, pltpu.roll(state, 1, 0), enter)
            carry = carried[here, cols] + tail[here, cols] * tots[0, s : s + 1, cols]
            inlet = jax.nn.sigmoid(inlet_pre[here, cols])
            forget = jax.nn.sigmoid(forget_pre[here, cols])
            soft = row(RATE_SOFT)
            decay, scaler = decay_of(forget, soft, starts)
            log_grad = jnp.where(
                starts, 0.0, carry * before * decay - carry * inlet * blocks * (decay * decay) / scaler
            )
            rate_grad = jnp.sum(log_grad * (-8.0 * forget), axis=0, keepdims=True) * row(RATE_SIGMOID)
            inlet_low = (carry * scaler * blocks * (inlet * (1.0 - inlet))).astype(BF16)
            forget_low = (log_grad * (-8.0 * soft) * (forget * (1.0 - forget))).astype(BF16)
            conv_grad = (
                carry * scaler * inlet
                + dot_nt(inlet_low, w_inlet[h])
                + dot_nt(forget_low, w_forget[h])
            )
            longer = ext[s, :, cols].astype(F32)
            zeros = jnp.zeros((HALO, width), F32)
            total = jnp.concatenate([zeros, row(TAPS) * conv_grad], axis=0)
            taps = [jnp.sum(conv_grad * longer[HALO:], axis=0, keepdims=True)]
            for k in range(1, CONV):
                masked = jnp.where(flags[here, k : k + 1] > 0.5, conv_grad, 0.0)
                moved = pltpu.roll(longer, k, 0)[HALO:]
                taps.append(jnp.sum(masked * moved, axis=0, keepdims=True))
                sent = jnp.concatenate([zeros, row(TAPS + k) * masked], axis=0)
                total = total + pltpu.roll(sent, HALO + length - k, 0)
            back[s, :, cols] = total
            lows = [jnp.sum(v.astype(F32), axis=0, keepdims=True) for v in (inlet_low, forget_low)]
            sums.append(taps + [jnp.sum(conv_grad, axis=0, keepdims=True)] + lows + [rate_grad])
            for m, low in enumerate((inlet_low, forget_low)):
                factor[here, :] = low.astype(F32) if m == 0 else factor[here, :]
                addend[here, :] = low.astype(F32) if m == 1 else addend[here, :]
        for i in range(len(sums[0])):
            lane_grads[2 + i : 3 + i, cols] = sum(each[i] for each in sums[1:]) + sums[0][i]
        for m, low in enumerate((factor, addend)):
            gate_grads[m, h] = dot_tn(conv[:, cols], low[...].astype(BF16)).astype(BF16)
        return none

    lax.fori_loop(0, heads, downward, 0)
    for s in range(3, spot.hi):
        sums.along(s)
    copy = remote(back.at[:, 0:HALO, :], rim, rim_sems, 0, behind)
    copy.start()
    copy.wait()

    def give(h, none):
        cols = pl.ds(pl.multiple_of(h * width, width), width)
        total = jnp.zeros((1, width), F32)
        for s in range(seqs):
            edge = jnp.where(spot.w < n - 1, rim[s, :, cols], 0.0)
            value = back[s, HALO:, cols]
            value = jnp.concatenate([value[: length - HALO], value[length - HALO :] + edge], axis=0)
            low = value.astype(BF16)
            input_low[s * length : (s + 1) * length, cols] = low
            total = total + jnp.sum(low.astype(F32), axis=0, keepdims=True)
        lane_grads[1:2, cols] = total
        return none

    lax.fori_loop(0, heads, give, 0)

    def done(at, total):
        own_out[at, :] = (resid[at, :] + total).astype(BF16)

    sums.end(done)
    sums.finish()


def leave_recurrence(
    grid, branch, rec, gelu_pre, local, cum, inlet_pre, forget_pre, conv, ext, entered, inlet, forget, lanes,
    flags, feed_part, resid, seqs,
):
    every, channels = conv.shape
    d = branch.shape[1]
    heads, width = inlet.shape[:2]
    near = pl.BlockSpec(memory_space=pltpu.VMEM)
    low = jax.ShapeDtypeStruct((every, channels), BF16)
    return pl.pallas_call(
        functools.partial(leave_kernel, grid.n, grid.tensor, seqs),
        grid=(1,),
        out_shape=[
            low,
            low,
            jax.ShapeDtypeStruct((2, heads, width, width), BF16),
            jax.ShapeDtypeStruct((LANE_ROWS, channels), F32),
            jax.ShapeDtypeStruct((8, d), F32),
            jax.ShapeDtypeStruct(resid.shape, BF16),
        ],
        in_specs=[near, pl.BlockSpec((1, d, channels), lambda i: (2, 0, 0))] + [near] * 14,
        out_specs=[near] * 6,
        scratch_shapes=[
            pltpu.VMEM((every, channels), F32),
            pltpu.VMEM((every, channels), F32),
            pltpu.VMEM((every, width), F32),
            pltpu.VMEM((every, width), F32),
            pltpu.VMEM((seqs, every // seqs + HALO, channels), F32),
            pltpu.VMEM((seqs, HALO, channels), F32),
        ]
        + prefix_scratch(grid, channels)
        + [pltpu.SemaphoreType.DMA((2, 1)), pltpu.VMEM(feed_part.shape, BF16)]
        + rows_scratch(grid, *resid.shape)[:2]
        + rows_sems(grid)[:2],
        compiler_params=pltpu.CompilerParams(
            collective_id=5, has_side_effects=True, vmem_limit_bytes=GRANT
        ),
        name="leave_recurrence",
    )(
        branch, rec, gelu_pre, local, cum, inlet_pre, forget_pre, conv, ext, entered, inlet, forget,
        lanes, flags, feed_part, resid,
    )


class Rows:
    def __init__(self, spot, part, got, line, cross_sems, line_sems):
        self.spot, self.part, self.got, self.line = spot, part, got, line
        self.cross_sems, self.line_sems = cross_sems, line_sems
        self.rows = got.shape[1]

    def place(self, k):
        spot, hi = self.spot, self.spot.hi
        last = hi - 1
        flipped = jnp.where(spot.z * 2 < hi, 0, 1)
        z = spot.z + flipped * (last - 2 * spot.z)
        if k == last:
            place = z
        else:
            place = jnp.where(k < last - z, last - k, k - (last - z))
        return place + flipped * (last - 2 * place)

    def cross_copy(self, place):
        spot = self.spot
        return remote(
            self.part.at[place, 1 - spot.t], self.got.at[place], self.cross_sems, place, spot.cross
        )

    def start(self):
        for k in range(self.spot.hi):
            self.cross_copy(self.place(k)).start()

    def line_copy(self, s, up, here=False):
        spot, hi = self.spot, self.spot.hi
        slot = (s - 1) if up else hi + s - 2
        step = 1 if up != here else -1
        return remote(
            self.line.at[0, slot], self.line.at[1, slot], self.line_sems, slot, spot.line(spot.z + step)
        )

    def own(self, place, at):
        return self.part[place, self.spot.t, at, :].astype(F32) + self.got[place, at, :].astype(F32)

    def send(self, s, up):
        spot, hi = self.spot, self.spot.hi
        place = spot.z + hi - s if up else spot.z - hi + s
        slot = (s - 1) if up else hi + s - 2
        self.cross_copy(place).wait_recv()
        begins = spot.z == 0 if up else spot.z == hi - 1

        @pl.when(begins)
        def _():
            def put(at):
                self.line[0, slot, at, :] = self.own(place, at).astype(BF16)

            by_rows(self.rows, STEP, put)

        if s > 1:

            @pl.when(jnp.logical_not(begins))
            def _():
                self.line_copy(s - 1, up, here=True).wait_recv()

                def put(at):
                    before = self.line[1, slot - 1, at, :].astype(F32)
                    self.line[0, slot, at, :] = (self.own(place, at) + before).astype(BF16)

                by_rows(self.rows, STEP, put)

        self.line_copy(s, up).start()

    def sends_up(self, s):
        return self.spot.z <= s - 1

    def sends_down(self, s):
        return self.spot.z >= self.spot.hi - s

    def along(self, s):
        spot, hi = self.spot, self.spot.hi

        @pl.when(jnp.logical_and(self.sends_up(s), spot.z < hi - 1))
        def _():
            self.send(s, True)

        @pl.when(jnp.logical_and(self.sends_down(s), spot.z > 0))
        def _():
            self.send(s, False)

    def end(self, done):
        spot, hi = self.spot, self.spot.hi
        self.cross_copy(spot.z).wait_recv()

        @pl.when(spot.z > 0)
        def _():
            self.line_copy(hi - 1, True, here=True).wait_recv()

        @pl.when(spot.z < hi - 1)
        def _():
            self.line_copy(hi - 1, False, here=True).wait_recv()

        def total(at):
            below = self.line[1, hi - 2, at, :].astype(F32)
            above = self.line[1, 2 * hi - 3, at, :].astype(F32)
            value = self.own(spot.z, at)
            value = value + jnp.where(spot.z > 0, below, 0.0)
            done(at, value + jnp.where(spot.z < hi - 1, above, 0.0))

        by_rows(self.rows, STEP, total)

    def finish(self):
        spot, hi = self.spot, self.spot.hi
        for place in range(hi):
            self.cross_copy(place).wait_send()
        for s in range(1, hi):

            @pl.when(jnp.logical_and(self.sends_up(s), spot.z < hi - 1))
            def _():
                self.line_copy(s, True).wait_send()

            @pl.when(jnp.logical_and(self.sends_down(s), spot.z > 0))
            def _():
                self.line_copy(s, False).wait_send()


def feed_kernel(
    n, tensor, unit_tiles, own, w_gate, w_up, w_down, cot, resid, gain,
    whole, gate_low, up_low, hidden, both, gain_grad, feed_part,
    part, got, line, mine, other, sems, cross_sems, line_sems, swap_sems,
):
    spot = Spot(n, tensor)
    hi = spot.hi
    rows, d = own.shape
    width = w_gate.shape[2]
    every = tensor * rows
    spot.greet(spot.cross)

    def put(at):
        whole[spot.z, spot.t, at, :] = own[at, :]

    by_rows(rows, STEP, put)
    chain = Chain(
        spot, lambda place, k: whole.at[place, lax.rem(spot.t + k, tensor)], sems, [spot.cross]
    )
    chain.first()
    gain_grad[...] = jnp.zeros_like(gain_grad)
    tiles = width // LANE
    skip = spot.z * tiles - jnp.minimum(spot.z * tiles, unit_tiles - tiles)
    chunk = 256

    def work(place):
        def ahead(j, none):
            cols = pl.ds(pl.multiple_of(j * chunk, chunk), chunk)
            rows_in = whole[place].reshape(every, d)
            gate, slope = gelu_of(dot(rows_in, w_gate[0, :, cols]))
            up = dot(rows_in, w_up[0, :, cols])
            grad = dot(cot[place].reshape(every, d), w_down[0, :, cols])
            at = lax.broadcasted_iota(jnp.int32, (1, chunk), 1) + j * chunk
            ok = at >= skip * LANE
            grad = jnp.where(ok, grad, 0.0)
            hidden[place, :, cols] = jnp.where(ok, gate * up, 0.0).astype(BF16)
            gate_low[place, :, cols] = (grad * up * slope).astype(BF16)
            up_low[place, :, cols] = (grad * gate).astype(BF16)
            return none

        lax.fori_loop(0, width // chunk, ahead, 0)

        def back(j, none):
            cols = pl.ds(pl.multiple_of(j * chunk, chunk), chunk)
            value = dot_nt(gate_low[place], w_gate[0, cols, :])
            value = (value + dot_nt(up_low[place], w_up[0, cols, :])).astype(BF16)
            for side in range(tensor):
                part[place, side, :, cols] = value[side * rows : (side + 1) * rows]
            return none

        lax.fori_loop(0, d // chunk, back, 0)

    def come_and_work(place):
        chain.fans.arrive(place, 1)
        work(place)

    for s in range(1, hi):
        chain.onward(s)
        chain.places(s - 1, come_and_work)
    chain.places(hi - 1, come_and_work)
    sums = Rows(spot, part, got, line, cross_sems, line_sems)
    sums.start()

    def give(i, none):
        place, j = i // (d // chunk), lax.rem(i, d // chunk)
        cols = pl.ds(pl.multiple_of(j * chunk, chunk), chunk)
        value = dot_nt(hidden[place], w_down[0, cols, :]).astype(BF16)
        for side in range(tensor):
            feed_part[place, side, :, cols] = value[side * rows : (side + 1) * rows]
        return none

    lax.fori_loop(0, hi * (d // chunk), give, 0)
    chain.finish_sends()

    def done(at, total):
        value = resid[at, :]
        scale = lax.rsqrt(jnp.mean(value * value, axis=-1, keepdims=True) + 1e-06)
        turned = total * gain[...]
        inner = jnp.mean(turned * value, axis=-1, keepdims=True)
        grad = cot[spot.z, spot.t, at, :].astype(F32)
        grad = grad + scale * turned - value * (scale * scale * scale * inner)
        gained = total * value * scale
        gain_grad[...] += jnp.sum(gained.reshape(2, 8, -1), axis=0)
        mine[at, :] = grad.astype(BF16)

    for s in range(1, hi):
        sums.along(s)
    sums.end(done)
    copy = remote(mine, other, swap_sems, 0, spot.cross)
    copy.start()
    sums.finish()
    share(spot, copy, mine, other, both)


def share(spot, copy, mine, other, both):
    def keep(at):
        both[spot.t, at, :] = mine[at, :]

    by_rows(mine.shape[0], STEP, keep)
    copy.wait()

    def take(at):
        both[1 - spot.t, at, :] = other[at, :]

    by_rows(mine.shape[0], STEP, take)


def rows_scratch(grid, rows, width):
    hi = grid.hi
    return [
        pltpu.VMEM((hi, rows, width), BF16),
        pltpu.VMEM((2, 2 * (hi - 1), rows, width), BF16),
        pltpu.VMEM((rows, width), BF16),
        pltpu.VMEM((rows, width), BF16),
    ]


def rows_sems(grid):
    hi = grid.hi
    return [
        pltpu.SemaphoreType.DMA((2, hi)),
        pltpu.SemaphoreType.DMA((2, 2 * (hi - 1))),
        pltpu.SemaphoreType.DMA((2, 1)),
    ]


def feed_forward(grid, own, feed, cot, resid, gain, unit_tiles):
    rows, d = own.shape
    hi, tensor = grid.hi, grid.tensor
    width = feed.shape[-1]
    near = pl.BlockSpec(memory_space=pltpu.VMEM)
    whole = jax.ShapeDtypeStruct((hi, tensor, rows, d), BF16)
    low = jax.ShapeDtypeStruct((hi, tensor * rows, width), BF16)
    feed = feed.reshape(3, -1, width)

    def weight(k):
        return pl.BlockSpec((1, d, width), lambda i: (k, 0, 0))

    return pl.pallas_call(
        functools.partial(feed_kernel, grid.n, tensor, unit_tiles),
        grid=(1,),
        out_shape=[
            whole,
            low,
            low,
            low,
            jax.ShapeDtypeStruct((tensor, rows, d), BF16),
            jax.ShapeDtypeStruct((8, d), F32),
            whole,
        ],
        in_specs=[near] + [weight(k) for k in range(3)] + [near] * 3,
        out_specs=[near] * 7,
        scratch_shapes=[pltpu.VMEM(whole.shape, BF16)]
        + rows_scratch(grid, rows, d)
        + [chain_sems(1)]
        + rows_sems(grid),
        compiler_params=pltpu.CompilerParams(
            collective_id=2, has_side_effects=True, vmem_limit_bytes=GRANT
        ),
        name="feed_forward",
    )(own, feed, feed, feed, cot, resid, gain)


RING = 4


def tile_rows(rows):
    return 16 if rows % 16 == 0 else 8


SENDING = 8
HELD = 2


def place_at(j, hi):
    return lax.rem(2 * j + hi // 2 + (2 * j) // hi, hi)


def grads_kernel(
    n, tensor, spans, kept,
    unit_tiles,
    second, cot, normed, branch, gate_low, up_low, hidden, gelu_low, input_low, mixed, gates, first, own_out, thin,
    apart, summed, first_other, block_out, thin_own, *refs,
):
    stages = (n // LINE).bit_length() - 1
    lists = [refs[i * stages : (i + 1) * stages] for i in range(6)]
    sends, keeps, gots, thin_sends, thin_keeps, thin_gots = lists
    (
        made, ready, got_line, first_out, first_got, thin_ready, thin_line,
        cube_sems, line_sems, first_sems, thin_sems, thin_line_sems,
    ) = refs[6 * stages :]
    spot = Spot(n, tensor)
    hi = spot.hi
    all_spans = len(spans)
    units = all_spans * hi
    step = pl.program_id(0)
    rows = ready.shape[1]
    width = ready.shape[2]
    each = tile_rows(rows)
    last_step = units + stages - 1
    first_rows, out_rows = first.shape[0], own_out.shape[0]

    def place_of(unit):
        return place_at(lax.rem(unit, hi), hi)

    sources = {
        "gate": (second, gate_low),
        "up": (second, up_low),
        "down": (cot, hidden),
        "gelu": (normed, gelu_low),
        "input": (normed, input_low),
        "out": (branch, mixed),
    }

    def cube_copy(stage, unit):
        slot = lax.rem(unit, RING)
        return remote(
            sends[stage].at[slot],
            gots[stage].at[slot],
            cube_sems.at[stage],
            slot,
            spot.flip(spot.bits[stage]),
        )

    def line_copy(unit):
        slot = lax.rem(unit, SENDING)
        span = unit // hi
        return pltpu.make_async_remote_copy(
            src_ref=ready.at[slot],
            dst_ref=got_line.at[span, spot.z],
            send_sem=line_sems.at[0, slot],
            recv_sem=line_sems.at[1, span * hi + spot.z],
            device_id=spot.line(place_of(unit)),
            device_id_type=MESH,
        )

    def line_here(span, sender):
        here = got_line.at[span, sender]
        return pltpu.make_async_remote_copy(
            src_ref=here,
            dst_ref=here,
            send_sem=line_sems.at[0, 0],
            recv_sem=line_sems.at[1, span * hi + sender],
            device_id=spot.line(sender),
            device_id_type=MESH,
        )

    def line_sent(unit):
        @pl.when(jnp.logical_and(unit >= 0, place_of(unit) != spot.z))
        def _():
            line_copy(unit).wait_send()

    def settle(span):
        for distance in range(1, hi):
            line_here(span, spot.away(distance)).wait_recv()

        def give(at):
            if span < kept:
                tiles = width // LANE
                for place in range(hi):
                    skip = place * tiles - min(place * tiles, unit_tiles - tiles)
                    if skip < tiles:
                        value = got_line[span, place, at, skip * LANE :].astype(F32)
                        apart[span, at, place * width : (place + 1) * width - skip * LANE] = value
            else:
                value = got_line[span, 0, at, :].astype(F32)
                for place in range(1, hi):
                    value = value + got_line[span, place, at, :].astype(F32)
                blocks = width // summed.shape[2]
                for j in range(blocks):
                    cols = slice(j * summed.shape[2], (j + 1) * summed.shape[2])
                    summed[(span - kept) * blocks + j, at, :] = value[:, cols]

        by_rows(rows, each, give)

    def thin_copy(stage):
        return remote(
            thin_sends[stage], thin_gots[stage], thin_sems, stage, spot.flip(spot.bits[stage])
        )

    def thin_line_copy(place, sender):
        return pltpu.make_async_remote_copy(
            src_ref=thin_ready.at[place],
            dst_ref=thin_line.at[sender],
            send_sem=thin_line_sems.at[0, place],
            recv_sem=thin_line_sems.at[1, sender],
            device_id=spot.line(place),
            device_id_type=MESH,
        )

    first_copy = remote(first_out, first_got, first_sems, 0, spot.cross)

    @pl.when(step == 0)
    def _():
        spot.greet(*[spot.flip(bit) for bit in spot.bits], spot.cross)

        def put(at):
            first_out[at, :] = first[at, :]

        by_rows(first_rows, STEP, put)

        def put_out(at):
            to = pl.ds(pl.multiple_of(first_rows + at.start, STEP), STEP)
            first_out[to, :] = own_out[at, :]

        by_rows(out_rows, STEP, put_out)
        first_copy.start()
        mine = spot.bit(1)
        for place in range(hi):
            for k in range(thin_sends[0].shape[1]):
                thin_sends[0][place, k] = thin[place, 2 * k + 1 - mine]
                thin_keeps[0][place, k] = thin[place, 2 * k + mine]
        thin_copy(0).start()

    for stage in range(stages):

        @pl.when(step == stage + 1)
        def _(stage=stage):
            thin_copy(stage).wait_recv()
            if stage < stages - 1:
                mine = spot.bit(spot.bits[stage + 1])
                for place in range(hi):
                    for k in range(thin_sends[stage + 1].shape[1]):
                        a, b = 2 * k + 1 - mine, 2 * k + mine
                        thin_sends[stage + 1][place, k] = (
                            thin_keeps[stage][place, a] + thin_gots[stage][place, a]
                        )
                        thin_keeps[stage + 1][place, k] = (
                            thin_keeps[stage][place, b] + thin_gots[stage][place, b]
                        )
                thin_copy(stage + 1).start()
            else:
                for place in range(hi):
                    thin_ready[place] = thin_keeps[stage][place, 0] + thin_gots[stage][place, 0]
                for distance in range(1, hi):
                    thin_line_copy(spot.away(distance), spot.z).start()

    @pl.when(step < units)
    def _():
        slot = lax.rem(step, RING)

        @pl.when(step >= RING)
        def _():
            cube_copy(0, step - RING).wait_send()

        for span, pieces in enumerate(spans):

            @pl.when(step // hi == span)
            def _(pieces=pieces):
                for name, begin, width, to in pieces:
                    if name == "gates":

                        def put(at, width=width, to=to):
                            made[at, to : to + width] = gates[0, at, :].astype(made.dtype)

                        by_rows(made.shape[0], STEP, put)
                        continue
                    left, right = sources[name]

                    def one(j, carry, left=left, right=right, begin=begin, width=width, to=to):
                        at = pl.ds(pl.multiple_of(j * LANE, LANE), LANE)
                        made[at, to : to + width] = lax.dot_general(
                            left[:, at],
                            right[:, begin : begin + width],
                            (((0,), (0,)), ((), ())),
                            preferred_element_type=F32,
                        ).astype(made.dtype)
                        return carry

                    lax.fori_loop(0, made.shape[0] // LANE, one, 0)

        mine = spot.bit(1)
        for k in range(sends[0].shape[1]):

            def put(at, k=k):
                def block(i):
                    at_made = pl.ds(pl.multiple_of(i * rows + at.start, each), each)
                    return made[at_made, :].astype(BF16)

                sends[0][slot, k, at, :] = block(2 * k + 1 - mine)
                keeps[0][lax.rem(step, HELD), k, at, :] = block(2 * k + mine)

            by_rows(rows, each, put)
        cube_copy(0, step).start()

    for stage in range(stages):
        unit = step - stage - 1

        @pl.when(jnp.logical_and(unit >= 0, unit < units))
        def _(stage=stage, unit=unit):
            slot = lax.rem(unit, RING)
            held = lax.rem(unit, HELD)
            cube_copy(stage, unit).wait_recv()

            def total(k, at):
                return (
                    keeps[stage][held, k, at, :].astype(F32) + gots[stage][slot, k, at, :].astype(F32)
                ).astype(BF16)

            if stage < stages - 1:

                @pl.when(unit >= RING)
                def _():
                    cube_copy(stage + 1, unit - RING).wait_send()

                mine = spot.bit(spot.bits[stage + 1])
                for k in range(sends[stage + 1].shape[1]):

                    def put(at, k=k):
                        sends[stage + 1][slot, k, at, :] = total(2 * k + 1 - mine, at)
                        keeps[stage + 1][held, k, at, :] = total(2 * k + mine, at)

                    by_rows(rows, each, put)
                cube_copy(stage + 1, unit).start()
            else:
                line_sent(unit - SENDING)
                place = place_of(unit)

                @pl.when(place != spot.z)
                def _():
                    def put(at):
                        ready[lax.rem(unit, SENDING), at, :] = total(0, at)

                    by_rows(rows, each, put)
                    line_copy(unit).start()

                @pl.when(place == spot.z)
                def _():
                    def put(at):
                        got_line[unit // hi, spot.z, at, :] = total(0, at)

                    by_rows(rows, each, put)

    late = 2 * hi + stages - 1
    for span in range(all_spans):
        when = span * hi + hi - 1 + late
        if when < last_step:

            @pl.when(step == when)
            def _(span=span):
                settle(span)

    @pl.when(step == last_step)
    def _():
        for span in range(all_spans):
            if span * hi + hi - 1 + late >= last_step:
                settle(span)
        for unit in range(units - SENDING, units):
            line_sent(unit)
        for stage in range(stages):
            for unit in range(units - RING, units):
                cube_copy(stage, unit).wait_send()
            thin_copy(stage).wait_send()
        value = thin_ready[spot.z]
        for distance in range(1, hi):
            place = spot.away(distance)
            thin_line_copy(place, place).wait_recv()
            thin_line_copy(place, spot.z).wait_send()
            value = value + thin_line[place]
        thin_own[...] = value
        first_copy.wait()

        def take(at):
            first_other[at, :] = first_got[at, :]

        by_rows(first_rows, STEP, take)

        def take_out(at):
            other = pl.ds(pl.multiple_of(first_rows + at.start, STEP), STEP)
            block_out[spot.t, at, :] = own_out[at, :]
            block_out[1 - spot.t, at, :] = first_got[other, :]

        by_rows(out_rows, STEP, take_out)


def column_spans(widths, width):
    spans, here, room = [], [], width
    for name, size in widths:
        begin = 0
        while begin < size:
            count = min(size - begin, room)
            here.append((name, begin, count, width - room))
            begin, room = begin + count, room - count
            if room == 0:
                spans, here, room = spans + [here], [], width
    assert not here
    return spans


def send_grads(grid, feed, rec, gates, first, own_out, thin, unit_tiles):
    hi, inner = grid.hi, grid.inner_size
    second, cot, gate_low, up_low, hidden = feed
    normed, branch, gelu_low, input_low, mixed = rec
    d = second.shape[1]
    rows = d // grid.n
    slab = d // hi
    width = gate_low.shape[1]
    kept = 3
    channels = mixed.shape[1]
    spans = column_spans([(name, width) for name in ("gate", "up", "down")], width) + column_spans(
        [(name, channels) for name in ("gelu", "input", "out")] + [("gates", gates.shape[1])], width
    )
    all_spans = len(spans)
    units = all_spans * hi
    stages = inner.bit_length() - 1

    def place_of(i):
        return place_at(lax.rem(jnp.minimum(i, units - 1), hi), hi)

    def slab_of(a):
        return pl.BlockSpec((a.shape[0], slab), lambda i: (0, place_of(i)))

    def whole(a):
        zeros = (0,) * a.ndim
        return pl.BlockSpec(a.shape, lambda i: zeros, pipeline_mode=pl.Buffered(1))

    block = gates.shape[1]
    apart = jax.ShapeDtypeStruct((kept, rows, unit_tiles * LANE), F32)
    summed = jax.ShapeDtypeStruct(((all_spans - kept) * (width // block), rows, block), F32)
    both = jax.ShapeDtypeStruct((grid.tensor,) + own_out.shape, BF16)
    other = jax.ShapeDtypeStruct(first.shape, BF16)
    thin = thin.reshape(hi, inner, 8, thin.shape[1] // 8)
    thin_shape = thin.shape[2:]
    thin_own = jax.ShapeDtypeStruct(thin_shape, F32)
    outs = [apart, summed, other, both, thin_own]
    swapped = (first.shape[0] + own_out.shape[0], d)

    def halves(lead, tail, kind):
        return [
            pltpu.VMEM((lead, inner >> (stage + 1)) + tail, kind) for stage in range(stages)
        ]

    gates = gates.reshape(hi, slab, gates.shape[1])
    return pl.pallas_call(
        functools.partial(grads_kernel, grid.n, grid.tensor, spans, kept, unit_tiles),
        grid=(units + stages,),
        out_shape=outs,
        in_specs=[slab_of(a) for a in (second, cot, normed, branch)]
        + [whole(a) for a in (gate_low, up_low, hidden, gelu_low, input_low, mixed)]
        + [pl.BlockSpec((1,) + gates.shape[1:], lambda i: (place_of(i), 0, 0))]
        + [whole(first), whole(own_out), whole(thin)],
        out_specs=[whole(a) for a in outs],
        scratch_shapes=halves(RING, (rows, width), BF16)
        + halves(HELD, (rows, width), BF16)
        + halves(RING, (rows, width), BF16)
        + halves(hi, thin_shape, F32) * 3
        + [
            pltpu.VMEM((slab, width), BF16 if rows % 16 == 0 else F32),
            pltpu.VMEM((SENDING, rows, width), BF16),
            pltpu.VMEM((all_spans, hi, rows, width), BF16),
            pltpu.VMEM(swapped, BF16),
            pltpu.VMEM(swapped, BF16),
            pltpu.VMEM((hi,) + thin_shape, F32),
            pltpu.VMEM((hi,) + thin_shape, F32),
            pltpu.SemaphoreType.DMA((stages, 2, RING)),
            pltpu.SemaphoreType.DMA((2, units)),
            pltpu.SemaphoreType.DMA((2, 1)),
            pltpu.SemaphoreType.DMA((2, stages)),
            pltpu.SemaphoreType.DMA((2, hi)),
        ],
        compiler_params=pltpu.CompilerParams(
            collective_id=4, has_side_effects=True, vmem_limit_bytes=GRANT
        ),
        name="send_grads",
    )(
        second, cot, normed, branch, gate_low, up_low, hidden, gelu_low, input_low, mixed, gates,
        first, own_out, thin,
    )


def rms_norm(values, gain):
    scale = lax.rsqrt(jnp.mean(values * values, axis=-1, keepdims=True) + 1e-06)
    return values * scale * gain


def dot(left, right):
    return jnp.dot(left, right, preferred_element_type=F32)


def dot_nt(left, right):
    return jnp.einsum("ik,jk->ij", left, right, preferred_element_type=F32)


def dot_tn(left, right):
    return jnp.einsum("ki,kj->ij", left, right, preferred_element_type=F32)


def local(
    block_in,
    segment_ids,
    cotangent,
    first_gain,
    gelu_weight,
    gelu_bias,
    input_weight,
    input_bias,
    conv_weight,
    conv_bias,
    inlet_weight,
    inlet_bias,
    forget_weight,
    forget_bias,
    decay_rate,
    out_weight,
    out_bias,
    second_gain,
    mlp_gate,
    mlp_up,
    mlp_down,
):
    grid = Grid()
    seq_count, tok_count, width = block_in.shape
    head_count, block_size = gelu_weight.shape[1:]
    channels = head_count * block_size
    margin = CONV - 1
    rows_all = seq_count * tok_count
    rows_half = rows_all // grid.tensor
    d_own = gelu_weight.shape[0]
    lane_own = gelu_bias.shape[1]
    units = mlp_gate.shape[1]
    unit_tiles = units // LANE
    window_tiles = -(-unit_tiles // grid.hi)
    window = window_tiles * LANE

    halo_rows = block_in[:, tok_count - HALO :]
    marks = (segment_ids + 1).astype(BF16)
    halo, rim_marks = shifted((halo_rows, marks[:, tok_count - margin :]), "wide", 1)
    halo = halo.reshape(seq_count * HALO, width)
    marks_ext = jnp.concatenate([rim_marks, marks], axis=1)
    earlier = [marks_ext[:, margin - k : margin - k + tok_count] == marks for k in range(1, CONV)]
    flags = jnp.stack([jnp.logical_not(earlier[0])] + earlier, axis=-1).astype(F32)
    flags = jnp.pad(flags.reshape(rows_all, CONV), ((0, 0), (0, 8 - CONV)))

    rec_own = jnp.stack(
        [
            input_weight.reshape(d_own, channels),
            gelu_weight.reshape(d_own, channels),
            out_weight.reshape(channels, d_own).T,
        ]
    )
    gates_own = jnp.stack([inlet_weight, forget_weight]).reshape(2 * head_count, lane_own, block_size)
    per_lane = jnp.stack([gelu_bias, input_bias])
    per_lane = jnp.concatenate(
        [per_lane, conv_weight, jnp.stack([conv_bias, inlet_bias, forget_bias, decay_rate])]
    )
    lane_table = lax.dynamic_update_slice(
        jnp.zeros((CONV + 6, head_count, block_size), BF16), per_lane, (0, 0, grid.w * lane_own)
    )
    per_width = jnp.stack([first_gain, out_bias, second_gain])
    width_table = lax.dynamic_update_slice(
        jnp.zeros((3, width), BF16), per_width, (0, grid.w * d_own)
    )
    thin_own = jnp.concatenate(
        [lane_table.reshape(CONV + 6, channels), width_table.reshape(-1, channels)]
    )
    thin_count = thin_own.shape[0]
    thin_own = jnp.pad(thin_own, ((0, -thin_count % 16), (0, 0)))
    feed_own = jnp.stack([mlp_gate, mlp_up, mlp_down.T])
    feed_windows = jnp.stack(
        [
            feed_own[:, :, tile * LANE : tile * LANE + window]
            for tile in (
                min(place * window_tiles, unit_tiles - window_tiles) for place in range(grid.hi)
            )
        ],
        axis=1,
    )
    cot_rows = cotangent.reshape(grid.tensor, rows_half, width)
    cot_own = pick(cot_rows, grid.t)
    rec_all, gates_all, thin_all, feed_all, cot_all = blank(
        (3, grid.n, d_own, channels),
        (2 * head_count, grid.n, lane_own, block_size),
        (grid.n,) + thin_own.shape,
        (3, grid.n + grid.hi, d_own, window),
        (grid.hi, grid.tensor, rows_half, width),
    )
    rec_all = lax.dynamic_update_slice(rec_all, rec_own[:, None], (0, grid.w, 0, 0))
    gates_all = lax.dynamic_update_slice(gates_all, gates_own[:, None], (0, grid.w, 0, 0))
    thin_all = lax.dynamic_update_slice(thin_all, thin_own[None], (grid.w, 0, 0))
    feed_all = lax.dynamic_update_slice(feed_all, feed_windows, (0, grid.n, 0, 0))
    feed_all = lax.dynamic_update_slice(
        feed_all, lax.dynamic_slice_in_dim(feed_windows, grid.z, 1, 1), (0, grid.w, 0, 0)
    )
    cot_all = lax.dynamic_update_slice(cot_all, cot_own[None, None], (grid.z, grid.t, 0, 0))
    rec_all, gates_all, thin_all, feed_all = bring_weights(
        grid, rec_all, gates_all, thin_all, feed_all
    )
    rec_all = rec_all.reshape(3, width, channels)
    gates_all = gates_all.reshape(2, head_count, block_size, block_size)
    inlet_full, forget_full = gates_all[0], gates_all[1]
    table = jnp.sum(thin_all.astype(F32), axis=0)
    lane_rows = table[: CONV + 6]
    gain_first, out_shift, gain_second = table[CONV + 6 : thin_count].reshape(3, width)
    rate = lane_rows[CONV + 5]
    lanes = jnp.concatenate([lane_rows[: CONV + 5], jnp.stack([jax.nn.softplus(rate), jax.nn.sigmoid(rate)])])
    lanes = jnp.pad(lanes, ((0, LANE_ROWS - lanes.shape[0]), (0, 0)))

    x = block_in.reshape(rows_all, width)
    (
        normed,
        ext,
        conv,
        gelu_pre,
        inlet_pre,
        forget_pre,
        cum,
        local_state,
        entered,
        mixed,
        resid,
        second_own,
        feed_all,
        cot_all,
    ) = forward_recurrence(
        grid, x, halo, gain_first[None], rec_all, inlet_full, forget_full, lanes, flags, out_shift[None],
        gain_second[None], feed_all, cot_all, seq_count,
    )

    rows_feed = grid.hi * rows_all
    second_all, gate_low, up_low, hidden, branch_low, gain_two_grad, feed_part = feed_forward(
        grid, second_own, feed_all, cot_all, resid, gain_second[None], unit_tiles
    )
    second_all, cot_all = (v.reshape(rows_feed, width) for v in (second_all, cot_all))
    gate_low, up_low, hidden = (v.reshape(rows_feed, window) for v in (gate_low, up_low, hidden))
    branch_low = branch_low.reshape(rows_all, width)
    gain_two_grad = jnp.sum(gain_two_grad, axis=0)

    gelu_low, input_low, gate_w_grads, lane_grads, out_shift_grad, own_out = leave_recurrence(
        grid, branch_low, rec_all, gelu_pre, local_state, cum, inlet_pre, forget_pre, conv, ext, entered,
        inlet_full, forget_full, lanes, flags, feed_part, resid, seq_count,
    )
    out_shift_grad = jnp.sum(out_shift_grad, axis=0)
    gate_w_grads = (
        gate_w_grads.reshape(2, head_count, grid.n, lane_own, block_size)
        .transpose(2, 0, 1, 3, 4)
        .reshape(width, block_size)
    )
    inputs = x.astype(F32)
    scale_first = lax.rsqrt(jnp.mean(inputs * inputs, axis=-1, keepdims=True) + 1e-06)
    first_part, gain_one_grad = first_gradient(
        x, input_low, gelu_low, rec_all, jnp.broadcast_to(scale_first, (rows_all, 8))
    )
    gain_one_grad = jnp.sum(gain_one_grad, axis=0)
    gain_grads = jnp.stack([gain_one_grad, gain_two_grad])
    gain_grads = gain_grads + grid.swap(gain_grads)

    lane_grads = (
        lane_grads[: CONV + 6]
        .reshape(CONV + 6, head_count, grid.n, lane_own)
        .transpose(2, 0, 1, 3)
        .reshape(grid.n, -1)
    )
    thin_grads = jnp.concatenate(
        [v.reshape(grid.n, d_own) for v in (gain_grads[0], out_shift_grad, gain_grads[1])]
        + [lane_grads],
        axis=1,
    )
    feed_grads, rec_grads, first_other, block_out, thin = send_grads(
        grid,
        (second_all, cot_all, gate_low, up_low, hidden),
        (normed, branch_low, gelu_low, input_low, mixed),
        gate_w_grads,
        first_part,
        own_out,
        thin_grads,
        unit_tiles,
    )
    block_out = block_out.reshape(block_in.shape)
    thin = thin.reshape(-1)
    gate_grad, up_grad, down_grad = feed_grads[0], feed_grads[1], feed_grads[2].T
    gelu_w_grad = rec_grads[:head_count].transpose(1, 0, 2)
    input_w_grad = rec_grads[head_count : 2 * head_count].transpose(1, 0, 2)
    out_grad = rec_grads[2 * head_count : 3 * head_count].transpose(0, 2, 1)
    gate_w_grads = rec_grads[3 * head_count].reshape(2, head_count, lane_own, block_size)
    first_grad = first_part.astype(F32) + first_other.astype(F32)
    _, pull_first = jax.vjp(rms_norm, inputs, gain_first)
    input_norm_grad, _ = pull_first(first_grad)
    block_grad = (branch_low.astype(F32) + input_norm_grad).reshape(block_in.shape)
    gain_one_own, out_shift_own, gain_two_own = (
        thin[i * d_own : (i + 1) * d_own] for i in range(3)
    )
    lanes = thin[3 * d_own :].reshape(CONV + 6, head_count, lane_own)
    return (
        block_out,
        block_grad,
        gain_one_own,
        gelu_w_grad,
        lanes[0],
        input_w_grad,
        lanes[1],
        lanes[2 : 2 + CONV],
        lanes[2 + CONV],
        gate_w_grads[0],
        lanes[3 + CONV],
        gate_w_grads[1],
        lanes[4 + CONV],
        lanes[5 + CONV],
        out_grad,
        out_shift_own,
        gain_two_own,
        gate_grad,
        up_grad,
        down_grad,
    )


def solution(mesh):
    in_specs = (
        P(None, "wide", None),
        P(None, "wide"),
        P(None, "wide", None),
        P("wide"),
        P("wide", "tensor", None),
        P("tensor", "wide"),
        P("wide", "tensor", None),
        P("tensor", "wide"),
        P(None, "tensor", "wide"),
        P("tensor", "wide"),
        P("tensor", "wide", None),
        P("tensor", "wide"),
        P("tensor", "wide", None),
        P("tensor", "wide"),
        P("tensor", "wide"),
        P("tensor", None, "wide"),
        P("wide"),
        P("wide"),
        P("wide", "tensor"),
        P("wide", "tensor"),
        P("tensor", "wide"),
    )
    out_specs = (
        P(None, "wide", None),
        P(None, "wide", None),
        P("wide"),
        P("wide", "tensor", None),
        P("tensor", "wide"),
        P("wide", "tensor", None),
        P("tensor", "wide"),
        P(None, "tensor", "wide"),
        P("tensor", "wide"),
        P("tensor", "wide", None),
        P("tensor", "wide"),
        P("tensor", "wide", None),
        P("tensor", "wide"),
        P("tensor", "wide"),
        P("tensor", None, "wide"),
        P("wide"),
        P("wide"),
        P("wide", "tensor"),
        P("wide", "tensor"),
        P("tensor", "wide"),
    )
    return jax.shard_map(local, mesh=mesh, in_specs=in_specs, out_specs=out_specs, check_vma=False)
```

```python
import functools

import jax
import jax.numpy as jnp
from jax import lax
from jax.experimental import pallas as pl
from jax.experimental.pallas import tpu as pltpu
from jax.sharding import PartitionSpec as P

CONV = 4
LANE = 128
GRANT = 60 * 1024 * 1024
F32 = jnp.float32
BF16 = jnp.bfloat16

LINE = 4


class Grid:
    def __init__(self):
        self.n = lax.axis_size("wide")
        self.hi = LINE
        self.inner_size = self.n // LINE
        self.tensor = lax.axis_size("tensor")
        self.w = lax.axis_index("wide")
        self.t = lax.axis_index("tensor")
        self.z = self.w // self.inner_size
        self.inner = lax.rem(self.w, self.inner_size)

    def flip(self, value, bit):
        return lax.ppermute(value, "wide", [(i, i ^ bit) for i in range(self.n)])

    def swap(self, value):
        size = self.tensor
        pairs = [(i, (i + 1) % size) for i in range(size)]
        return lax.ppermute(value, "tensor", pairs)


def shifted(shard, axis, by):
    size = lax.axis_size(axis)
    place = lax.axis_index(axis) - by
    there = jnp.logical_and(place >= 0, place < size)
    pairs = [(i, (i + by) % size) for i in range(size)]
    moved = lax.ppermute(shard, axis, pairs)
    return jax.tree.map(lambda a: jnp.where(there, a, jnp.zeros_like(a)), moved)


def pick(values, index, axis=0):
    return lax.dynamic_index_in_dim(values, index, axis, keepdims=False)


MESH = pl.DeviceIdType.MESH


class Spot:
    def __init__(self, n, tensor):
        self.n = n
        self.hi = LINE
        self.inner_size = n // LINE
        self.bits = [1 << i for i in range(self.inner_size.bit_length() - 1)]
        self.tensor = tensor
        self.w = lax.axis_index("wide")
        self.t = lax.axis_index("tensor")
        self.z = self.w // self.inner_size
        self.inner = lax.rem(self.w, self.inner_size)
        self.cross = {"tensor": lax.rem(self.t + 1, tensor)}

    def bit(self, which):
        return lax.rem(self.inner // which, 2)

    def flip(self, which):
        return {"wide": self.w + which - 2 * which * self.bit(which)}

    def line(self, place):
        return {"wide": place * self.inner_size + self.inner}

    def away(self, distance):
        return lax.rem(self.z + distance, self.hi)

    def greet(self, *sides):
        barrier = pltpu.get_barrier_semaphore()
        for side in sides:
            pl.semaphore_signal(barrier, inc=1, device_id=side, device_id_type=MESH)
        for distance in range(1, self.hi):
            pl.semaphore_signal(
                barrier, inc=1, device_id=self.line(self.away(distance)), device_id_type=MESH
            )
        pl.semaphore_wait(barrier, len(sides) + self.hi - 1)


def remote(src, dst, sems, index, side):
    return pltpu.make_async_remote_copy(
        src_ref=src,
        dst_ref=dst,
        send_sem=sems.at[0, index],
        recv_sem=sems.at[1, index],
        device_id=side,
        device_id_type=MESH,
    )


class Fans:
    def __init__(self, spot, at, sems, base, sides):
        self.spot, self.at, self.sems, self.base, self.sides = spot, at, sems, base, sides
        self.kinds = sorted(range(1 << len(sides)), key=lambda k: (bin(k).count("1"), -k))

    def onto(self, k):
        low = (k & -k) if k else 1 << len(self.sides)
        return [i for i in reversed(range(len(self.sides))) if (1 << i) < low]

    def copy(self, place, k, i, here=False):
        spot, hi = self.spot, self.spot.hi
        landed = k if here else k | (1 << i)
        index = self.base + (landed - 1) * hi + lax.rem(place - spot.z + hi, hi)
        ref = self.at(place, k)
        return remote(ref, ref, self.sems, index, self.sides[i])

    def hand_on(self, place, k):
        for i in self.onto(k):
            self.copy(place, k, i).start()

    def arrive(self, place, k):
        low = (k & -k).bit_length() - 1
        self.copy(place, k, low, here=True).wait_recv()

    def pass_on(self, place):
        for k in self.kinds:
            if k and self.onto(k):
                self.arrive(place, k)
                self.hand_on(place, k)

    def finish(self, place):
        for k in self.kinds:
            if k and not self.onto(k):
                self.arrive(place, k)
        self.finish_sends(place)

    def finish_sends(self, place):
        for k in self.kinds:
            for i in self.onto(k):
                self.copy(place, k, i).wait_send()

    def count(sides, hi):
        return ((1 << sides) - 1) * hi


class Chain:
    def __init__(self, spot, at, sems, sides):
        self.spot, self.at, self.sems = spot, at, sems
        self.fans = Fans(spot, at, sems, 2 * (spot.hi - 1), sides)

    def line_copy(self, s, up):
        spot, hi = self.spot, self.spot.hi
        owner = spot.z - (s - 1) if up else spot.z + (s - 1)
        other = spot.z + 1 if up else spot.z - 1
        ref = self.at(owner, 0)
        return remote(ref, ref, self.sems, (s - 1) if up else hi + s - 2, spot.line(other))

    def line_here(self, s, up):
        spot, hi = self.spot, self.spot.hi
        owner = spot.z - s if up else spot.z + s
        other = spot.z - 1 if up else spot.z + 1
        ref = self.at(owner, 0)
        return remote(ref, ref, self.sems, (s - 1) if up else hi + s - 2, spot.line(other))

    def first(self):
        self.first_line()
        self.fans.hand_on(self.spot.z, 0)

    def first_line(self):
        spot, hi = self.spot, self.spot.hi

        @pl.when(spot.z < hi - 1)
        def _():
            self.line_copy(1, True).start()

        @pl.when(spot.z > 0)
        def _():
            self.line_copy(1, False).start()

    def onward(self, s):
        spot, hi = self.spot, self.spot.hi

        @pl.when(spot.z >= s)
        def _():
            self.line_here(s, True).wait_recv()

        if s < hi - 1:

            @pl.when(jnp.logical_and(spot.z >= s, spot.z < hi - 1))
            def _():
                self.line_copy(s + 1, True).start()

        @pl.when(spot.z >= s)
        def _():
            self.fans.hand_on(spot.z - s, 0)

        @pl.when(spot.z <= hi - 1 - s)
        def _():
            self.line_here(s, False).wait_recv()

        if s < hi - 1:

            @pl.when(jnp.logical_and(spot.z <= hi - 1 - s, spot.z > 0))
            def _():
                self.line_copy(s + 1, False).start()

        @pl.when(spot.z <= hi - 1 - s)
        def _():
            self.fans.hand_on(spot.z + s, 0)

    def places(self, s, act):
        spot = self.spot
        if s == 0:
            act(spot.z)
            return

        @pl.when(spot.z >= s)
        def _():
            act(spot.z - s)

        @pl.when(spot.z <= spot.hi - 1 - s)
        def _():
            act(spot.z + s)

    def second(self, s):
        self.places(s, self.fans.pass_on)

    def finish(self):
        for s in range(self.spot.hi):
            self.places(s, self.fans.finish)
        self.finish_line()

    def finish_sends(self):
        for s in range(self.spot.hi):
            self.places(s, self.fans.finish_sends)
        self.finish_line()

    def finish_line(self):
        spot, hi = self.spot, self.spot.hi
        for s in range(1, hi):

            @pl.when(jnp.logical_and(spot.z >= s - 1, spot.z < hi - 1))
            def _():
                self.line_copy(s, True).wait_send()

            @pl.when(jnp.logical_and(spot.z <= hi - s, spot.z > 0))
            def _():
                self.line_copy(s, False).wait_send()


def chain_sems(sides, *lead):
    return pltpu.SemaphoreType.DMA(lead + (2, 2 * (LINE - 1) + ((1 << sides) - 1) * LINE))


class Turns:
    def __init__(self, spot, distances, window_of, at, sems, sides):
        self.spot, self.window_of, self.at, self.sems = spot, window_of, at, sems
        self.distances = distances
        self.fans = Fans(spot, at, sems, spot.hi, sides)

    def line_copy(self, distance):
        spot = self.spot
        place = spot.away(distance)
        return remote(self.window_of(place), self.at(spot.z, 0), self.sems, distance, spot.line(place))

    def back(self, distance):
        return lax.rem(self.spot.z - distance + self.spot.hi, self.spot.hi)

    def line_here(self, distance):
        place = self.back(distance)
        ref = self.at(place, 0)
        return remote(ref, ref, self.sems, distance, self.spot.line(place))

    def first(self):
        for distance in self.distances:
            self.start(distance)

    def start(self, distance):
        if distance:
            self.line_copy(distance).start()
        else:
            self.fans.hand_on(self.spot.z, 0)

    def onward(self, distance):
        if distance in self.distances:
            self.line_here(distance).wait_recv()
            self.fans.hand_on(self.back(distance), 0)

    def second(self, distance):
        if distance in self.distances:
            self.fans.pass_on(self.back(distance))

    def finish(self):
        for distance in self.distances:
            self.fans.finish(self.back(distance))
            if distance:
                self.line_copy(distance).wait_send()


LATE = (0, 1, 2, 3)


class FeedTurns:
    def __init__(self, spot, feed, sems, cube):
        def index(place, k):
            return place * spot.inner_size + jnp.bitwise_xor(spot.inner, k)

        self.each = [
            Turns(
                spot,
                LATE,
                lambda place, m=m: feed.at[m, spot.n + place],
                lambda place, k, m=m: feed.at[m, index(place, k)],
                sems.at[m],
                cube,
            )
            for m in range(feed.shape[0])
        ]

    def start(self, distance):
        for turns in self.each:
            turns.start(distance)

    def onward(self, distance):
        for turns in self.each:
            turns.onward(distance)

    def second(self, distance):
        for turns in self.each:
            turns.second(distance)

    def finish(self):
        for turns in self.each:
            turns.finish()


def weights_kernel(
    n, tensor, rec, gates, thin, cot, rec_all, gates_all, thin_all, cot_all,
    rec_sems, gates_sems, thin_sems, cot_sems,
):
    del rec, gates, thin, cot
    spot = Spot(n, tensor)
    hi = spot.hi

    def index(place, k):
        return place * spot.inner_size + jnp.bitwise_xor(spot.inner, k)

    cube = [spot.flip(bit) for bit in spot.bits]
    moves = [
        Chain(spot, lambda place, k: thin_all.at[index(place, k)], thin_sems, cube),
        Chain(spot, lambda place, k: gates_all.at[:, index(place, k)], gates_sems, cube),
        *[
            Chain(
                spot, lambda place, k, m=m: rec_all.at[m, index(place, k)], rec_sems.at[m], cube
            )
            for m in range(rec_all.shape[0])
        ],
        Chain(
            spot,
            lambda place, k: cot_all.at[place, lax.rem(spot.t + k, tensor)],
            cot_sems,
            [spot.cross],
        ),
    ]
    spot.greet(*cube, spot.cross)
    last = moves[-1]
    for move in moves[:-1]:
        move.first()
    last.fans.hand_on(spot.z, 0)
    for s in range(1, hi):
        for move in moves[:-1]:
            move.onward(s)
        if s == 1:
            last.first_line()
        else:
            last.onward(s - 1)
        for move in moves:
            move.second(s - 1)
    last.onward(hi - 1)
    for move in moves:
        move.second(hi - 1)
    for move in moves:
        move.finish()


def turn_sems(grid, count):
    return pltpu.SemaphoreType.DMA((count, 2, grid.n))


def place_kernel(
    unit_tiles, spot, wide_in, gelu_in, out_in, gate, up, down, inlet, forget, thin, cot,
    rec_all, gates_all, thin_all, feed_all, cot_all,
):
    step = pl.program_id(0)
    hi = LINE
    width = feed_all.shape[3]
    tiles = width // LANE

    @pl.when(step == 0)
    def _():
        heads, _, lanes = wide_in.shape
        for m, source in enumerate((wide_in, gelu_in, out_in)):
            for h in range(heads):
                rec_all[m, 0, :, h * lanes : (h + 1) * lanes] = source[h]
        for m, source in enumerate((inlet, forget)):
            for h in range(heads):
                gates_all[m * heads + h, 0] = source[h]
        thin_all[0] = thin[...]
        cot_all[0, 0] = cot[0]

    place = jnp.where(step < hi, step, spot[1])
    tile = jnp.minimum(place * tiles, unit_tiles - tiles)
    for m, source in enumerate((gate, up, down)):
        feed_all[m, 0] = source[:, pl.ds(pl.multiple_of(tile * LANE, LANE), width)]


def place_own(grid, rec, feed, gates, thin, cot):
    n, hi = grid.n, grid.hi
    heads, d_own, lanes = rec[0].shape
    units = feed[0].shape[1]
    unit_tiles = units // LANE
    window = -(-unit_tiles // hi) * LANE
    lane_own, block = gates[0].shape[1:]
    spot = jnp.stack([grid.w, grid.z, grid.t])

    def fixed(a):
        zeros = (0,) * a.ndim
        return pl.BlockSpec(a.shape, lambda i, spot: zeros)

    outs = [
        (3, n, d_own, heads * lanes),
        (2 * heads, n, lane_own, block),
        (n,) + thin.shape,
        (3, n + hi, d_own, window),
        (hi,) + cot.shape,
    ]
    return pl.pallas_call(
        functools.partial(place_kernel, unit_tiles),
        grid_spec=pltpu.PrefetchScalarGridSpec(
            num_scalar_prefetch=1,
            grid=(hi + 1,),
            in_specs=[fixed(a) for a in rec + feed + gates + (thin,)]
            + [pl.BlockSpec((1,) + cot.shape[1:], lambda i, spot: (spot[2], 0, 0))],
            out_specs=[
                pl.BlockSpec((3, 1, d_own, heads * lanes), lambda i, spot: (0, spot[0], 0, 0)),
                pl.BlockSpec((2 * heads, 1, lane_own, block), lambda i, spot: (0, spot[0], 0, 0)),
                pl.BlockSpec((1,) + thin.shape, lambda i, spot: (spot[0], 0, 0)),
                pl.BlockSpec(
                    (3, 1, d_own, window),
                    lambda i, spot: (0, jnp.where(i < hi, n + i, spot[0]), 0, 0),
                ),
                pl.BlockSpec((1, 1) + cot.shape[1:], lambda i, spot: (spot[1], spot[2], 0, 0)),
            ],
        ),
        out_shape=[jax.ShapeDtypeStruct(shape, BF16) for shape in outs],
        compiler_params=pltpu.CompilerParams(vmem_limit_bytes=GRANT),
        name="place",
    )(spot, *rec, *feed, *gates, thin, cot)


def bring_weights(grid, rec, gates, thin, cot):
    n, hi, tensor = grid.n, grid.hi, grid.tensor
    far = pl.BlockSpec(memory_space=pl.ANY)
    arrays = (rec, gates, thin, cot)
    cube = grid.inner_size.bit_length() - 1
    return pl.pallas_call(
        functools.partial(weights_kernel, n, tensor),
        out_shape=[jax.ShapeDtypeStruct(a.shape, a.dtype) for a in arrays],
        in_specs=[far] * len(arrays),
        out_specs=[far] * len(arrays),
        input_output_aliases={i: i for i in range(len(arrays))},
        scratch_shapes=[
            chain_sems(cube, rec.shape[0]),
            chain_sems(cube),
            chain_sems(cube),
            chain_sems(1),
        ],
        compiler_params=pltpu.CompilerParams(
            collective_id=0, has_side_effects=True, vmem_limit_bytes=GRANT
        ),
        name="bring_weights",
    )(*arrays)


def by_rows(rows, step, act):
    def one(i, carry):
        act(pl.ds(pl.multiple_of(i * step, step), step))
        return carry

    lax.fori_loop(0, rows // step, one, 0)


STEP = 16
HALVES = 2


GELU_SLOPE = 0.7978845608028654
GELU_CUBE = 0.044715
HALO = 8
GELU_SHIFT, INPUT_SHIFT, TAPS, CONV_SHIFT, INLET_SHIFT, FORGET_SHIFT, RATE_SOFT, RATE_SIGMOID = 0, 1, 2, 6, 7, 8, 9, 10
LANE_ROWS = 16


def gelu_of(v):
    bent = jnp.tanh(GELU_SLOPE * (v + GELU_CUBE * (v * v * v)))
    half = 0.5 * (1.0 + bent)
    slope = half + 0.5 * v * (1.0 - bent * bent) * (GELU_SLOPE * (1.0 + 3.0 * GELU_CUBE * (v * v)))
    return v * half, slope


def minus_expm1(x):
    series = jnp.ones_like(x)
    for k in range(9, 1, -1):
        series = 1.0 + series * x * (1.0 / k)
    return jnp.where(x > -0.5, -x * series, 1.0 - jnp.exp(x))


def decay_of(forget, soft, starts):
    log_decay = -8.0 * forget * soft
    decay = jnp.where(starts, 0.0, jnp.exp(log_decay))
    scaler = jnp.where(starts, 1.0, jnp.sqrt(minus_expm1(2.0 * log_decay)))
    return decay, scaler


def tile_scan(a, b, state_in, decay_in, reverse):
    place = lax.broadcasted_iota(jnp.int32, a.shape, 0)
    for by in (1, 2, 4):
        turn = 8 - by if reverse else by
        ok = place < 8 - by if reverse else place >= by
        b = jnp.where(ok, a * pltpu.roll(b, turn, 0) + b, b)
        a = jnp.where(ok, a * pltpu.roll(a, turn, 0), a)
    return a * decay_in, b + a * state_in


def scan_rows(seqs, length, width, read, write, reverse):
    tiles = length // 8
    last = 0 if reverse else 7

    def one(i, carry):
        tile = tiles - 1 - i if reverse else i
        after = []
        for s in range(seqs):
            decay_in, state_in = carry[s]
            at = pl.ds(pl.multiple_of(s * length + tile * 8, 8), 8)
            a, b = tile_scan(*read(at), state_in, decay_in, reverse)
            write(at, a, b)
            after.append(
                tuple(jnp.broadcast_to(v[last : last + 1], (8, width)) for v in (a, b))
            )
        return tuple(after)

    start = (jnp.ones((8, width), F32), jnp.zeros((8, width), F32))
    lax.fori_loop(0, tiles, one, (start,) * seqs)


def first_kernel(x, input_low, gelu_low, w_input, w_gelu, scale, part, gained):
    value = dot_nt(input_low[...], w_input[0]) + dot_nt(gelu_low[...], w_gelu[0])
    part[...] = value.astype(BF16)
    gained[...] = jnp.sum(
        (value * x[...].astype(F32) * scale[:, 0:1]).reshape(-1, 8, value.shape[1]), axis=0
    )


def first_gradient(x, input_low, gelu_low, rec, scale):
    rows, d = x.shape
    channels = input_low.shape[1]
    chunk = 512

    def fixed(a):
        return pl.BlockSpec(a.shape, lambda i: (0, 0))

    def weight(k):
        return pl.BlockSpec((1, chunk, channels), lambda i: (k, i, 0))

    column = pl.BlockSpec((rows, chunk), lambda i: (0, i))
    return pl.pallas_call(
        first_kernel,
        grid=(d // chunk,),
        out_shape=[jax.ShapeDtypeStruct((rows, d), BF16), jax.ShapeDtypeStruct((8, d), F32)],
        in_specs=[column, fixed(input_low), fixed(gelu_low), weight(0), weight(1), fixed(scale)],
        out_specs=[column, pl.BlockSpec((8, chunk), lambda i: (0, i))],
        compiler_params=pltpu.CompilerParams(vmem_limit_bytes=GRANT),
        name="first_gradient",
    )(x, input_low, gelu_low, rec, rec, scale)


class Prefix:
    def __init__(self, spot, seqs, reverse, tots, gots, line, cube_sems, line_sems):
        self.spot, self.seqs, self.reverse = spot, seqs, reverse
        self.tots, self.gots, self.line = tots, gots, line
        self.cube_sems, self.line_sems = cube_sems, line_sems

    def line_copy(self, place, sender):
        stages = len(self.spot.bits)
        return pltpu.make_async_remote_copy(
            src_ref=self.tots.at[stages],
            dst_ref=self.line.at[sender],
            send_sem=self.line_sems.at[0, place],
            recv_sem=self.line_sems.at[1, sender],
            device_id=self.spot.line(place),
            device_id_type=MESH,
        )

    def run(self):
        spot, seqs, hi = self.spot, self.seqs, self.spot.hi
        a, b = slice(0, seqs), slice(seqs, 2 * seqs)
        width = self.tots.shape[2]
        enter_a, enter_b = jnp.ones((seqs, width), F32), jnp.zeros((seqs, width), F32)
        for stage, bit in enumerate(spot.bits):
            copy = remote(
                self.tots.at[stage], self.gots.at[stage], self.cube_sems, stage, spot.flip(bit)
            )
            copy.start()
            copy.wait()
            mine_a, mine_b = self.tots[stage, a, :], self.tots[stage, b, :]
            got_a, got_b = self.gots[stage, a, :], self.gots[stage, b, :]
            after = spot.bit(bit) == (0 if self.reverse else 1)
            enter_b = jnp.where(after, enter_a * got_b + enter_b, enter_b)
            enter_a = jnp.where(after, enter_a * got_a, enter_a)
            self.tots[stage + 1, a, :] = mine_a * got_a
            self.tots[stage + 1, b, :] = jnp.where(
                after, mine_a * got_b + mine_b, got_a * mine_b + got_b
            )
            self.tots[stage + 1, 2 * seqs :, :] = jnp.zeros((8 - 2 * seqs, width), F32)
        for distance in range(1, hi):
            self.line_copy(spot.away(distance), spot.z).start()
        for distance in range(1, hi):
            place = spot.away(distance)
            self.line_copy(place, place).wait_recv()
            self.line_copy(place, spot.z).wait_send()
        come = jnp.zeros((seqs, width), F32)
        for place in reversed(range(hi)) if self.reverse else range(hi):
            before = spot.z < place if self.reverse else spot.z > place
            come = jnp.where(before, self.line[place, a, :] * come + self.line[place, b, :], come)
        return enter_a * come + enter_b


def prefix_scratch(grid, channels):
    stages = grid.inner_size.bit_length() - 1
    return [
        pltpu.VMEM((stages + 1, 8, channels), F32),
        pltpu.VMEM((stages, 8, channels), F32),
        pltpu.VMEM((grid.hi, 8, channels), F32),
        pltpu.SemaphoreType.DMA((2, stages)),
        pltpu.SemaphoreType.DMA((2, grid.hi)),
    ]


def forward_kernel(
    n, tensor, seqs, heads,
    x, halo, gain, w_input, w_gelu, w_inlet, w_forget, lanes, flags, w_out, shift, gain_second, feed,
    normed, ext, conv, gelu_pre, inlet_pre, forget_pre, cum, local, entered, mixed, resid, second,
    feed_all,
    held, factor, addend, part, out, got, tots, gots, line, cube_sems, line_sems, swap_sems, feed_sems,
):
    del feed
    spot = Spot(n, tensor)
    hi = spot.hi
    rows = x.shape[0]
    length = rows // seqs
    width = conv.shape[1]
    step = pl.program_id(0)
    cube = [spot.flip(bit) for bit in spot.bits]
    turns = FeedTurns(spot, feed_all, feed_sems, cube)
    @pl.when(step == 0)
    def _():
        spot.greet(*cube, spot.cross)
        turns.start(1)
        turns.start(0)

        def norm(source, at, to):
            value = source[at, :].astype(F32)
            scale = lax.rsqrt(jnp.mean(value * value, axis=-1, keepdims=True) + 1e-06)
            value = (value * scale * gain[...]).astype(BF16)
            held[pl.ds(pl.multiple_of(at.start + to, STEP), STEP), :] = value
            return value

        def main(at):
            normed[at, :] = norm(x, at, 0)

        by_rows(rows, STEP, main)
        by_rows(halo.shape[0], STEP, lambda at: norm(halo, at, rows))

    @pl.when(step < heads)
    def _():
        table = lanes[...]
        cols = pl.ds(pl.multiple_of(step * width, width), width)

        def row(i):
            return table[i : i + 1]

        branch = (dot(held[...], w_input[0]) + row(INPUT_SHIFT)).astype(BF16)
        gelu_pre[:, cols] = dot(held[0:rows, :], w_gelu[0]) + row(GELU_SHIFT)
        for s in range(seqs):
            here = slice(s * length, (s + 1) * length)
            front = rows + s * HALO
            longer = jnp.concatenate(
                [branch[front : front + HALO].astype(F32), branch[here].astype(F32)], axis=0
            )
            ext[s] = longer.astype(BF16)
            total = row(CONV_SHIFT) + row(TAPS) * longer[HALO:]
            for k in range(1, CONV):
                moved = pltpu.roll(longer, k, 0)[HALO:]
                total = total + jnp.where(flags[here, k : k + 1] > 0.5, row(TAPS + k) * moved, 0.0)
            conv[here, :] = total.astype(BF16)
        blocks = conv[...]
        inlet_pre[...] = dot(blocks, w_inlet[0]) + row(INLET_SHIFT)
        forget_pre[...] = dot(blocks, w_forget[0]) + row(FORGET_SHIFT)

        def terms(at):
            starts = flags[at, 0:1] > 0.5
            decay, scaler = decay_of(jax.nn.sigmoid(forget_pre[at, :]), row(RATE_SOFT), starts)
            factor[at, :] = decay
            addend[at, :] = scaler * jax.nn.sigmoid(inlet_pre[at, :]) * conv[at, :].astype(F32)

        by_rows(rows, 32, terms)

        def write(at, a, b):
            cum[at, cols] = a
            local[at, cols] = b

        scan_rows(seqs, length, width, lambda at: (factor[at, :], addend[at, :]), write, False)

    @pl.when(step == heads)
    def _():
        tots[0] = jnp.zeros_like(tots[0])
        for s in range(seqs):
            tots[0, s : s + 1, :] = cum[(s + 1) * length - 8 : (s + 1) * length, :][7:8]
            tots[0, seqs + s : seqs + s + 1, :] = local[(s + 1) * length - 8 : (s + 1) * length, :][7:8]
        enter = Prefix(spot, seqs, False, tots, gots, line, cube_sems, line_sems).run()
        turns.start(3)
        turns.onward(1)
        entered[...] = jnp.zeros_like(entered)
        entered[0:seqs, :] = enter
        for s in range(seqs):

            def mix(at, s=s):
                here = pl.ds(pl.multiple_of(s * length + at.start, STEP), STEP)
                state = local[here, :] + cum[here, :] * enter[s : s + 1]
                mixed[here, :] = (state * gelu_of(gelu_pre[here, :])[0]).astype(BF16)

            by_rows(length, STEP, mix)
        turns.start(2)
        values = mixed[...]
        own_rows = resid.shape[0]

        def branch(j, carry):
            at = pl.ds(pl.multiple_of(j * 256, 256), 256)
            value = dot_nt(values, w_out[0, at, :])
            for side in range(tensor):
                part[side, :, at] = value[side * own_rows : (side + 1) * own_rows]
            return carry

        lax.fori_loop(0, x.shape[1] // 256, branch, 0)

        def put(at):
            out[at, :] = part[1 - spot.t, at, :].astype(BF16)

        by_rows(own_rows, STEP, put)
        copy = remote(out, got, swap_sems, 0, spot.cross)
        copy.start()
        copy.wait()

        def norm(at):
            own = x[pl.ds(pl.multiple_of(spot.t * own_rows + at.start, STEP), STEP), :].astype(F32)
            value = own + (part[spot.t, at, :] + got[at, :].astype(F32) + shift[...])
            resid[at, :] = value
            scale = lax.rsqrt(jnp.mean(value * value, axis=-1, keepdims=True) + 1e-06)
            second[at, :] = (value * scale * gain_second[...]).astype(BF16)

        by_rows(own_rows, STEP, norm)
        turns.second(0)
        turns.onward(3)
        turns.second(1)
        turns.onward(2)
        turns.second(3)
        turns.second(2)
        turns.finish()


def forward_recurrence(
    grid, x, halo, gain, rec, inlet, forget, lanes, flags, shift, gain_second, feed, seqs
):
    rows, d = x.shape
    heads, width = inlet.shape[:2]
    channels = heads * width
    longer = rows // seqs + HALO
    own_rows = rows // grid.tensor

    def head_of(i):
        return jnp.minimum(i, heads - 1)

    def fixed(a):
        zeros = (0,) * len(a.shape)
        return pl.BlockSpec(a.shape, lambda i: zeros, pipeline_mode=pl.Buffered(1))

    def column(count):
        return pl.BlockSpec((count, width), lambda i: (0, head_of(i)))

    def weight(k):
        return pl.BlockSpec((1, d, width), lambda i: (k, 0, head_of(i)))

    head = pl.BlockSpec((1, width, width), lambda i: (head_of(i), 0, 0))
    far = pl.BlockSpec(memory_space=pl.ANY)
    wide = jax.ShapeDtypeStruct((rows, channels), F32)
    outs = [
        jax.ShapeDtypeStruct((rows, d), BF16),
        jax.ShapeDtypeStruct((seqs, longer, channels), BF16),
        jax.ShapeDtypeStruct((rows, channels), BF16),
        wide,
        wide,
        wide,
        wide,
        wide,
        jax.ShapeDtypeStruct((8, channels), F32),
        jax.ShapeDtypeStruct((rows, channels), BF16),
        jax.ShapeDtypeStruct((own_rows, d), F32),
        jax.ShapeDtypeStruct((own_rows, d), BF16),
        jax.ShapeDtypeStruct(feed.shape, BF16),
    ]
    return pl.pallas_call(
        functools.partial(forward_kernel, grid.n, grid.tensor, seqs, heads),
        grid=(heads + 1,),
        out_shape=outs,
        in_specs=[fixed(x), fixed(halo), fixed(gain), weight(0), weight(1), head, head]
        + [column(LANE_ROWS), fixed(flags)]
        + [pl.BlockSpec((1, d, channels), lambda i: (2, 0, 0), pipeline_mode=pl.Buffered(1))]
        + [fixed(shift), fixed(gain_second), far],
        out_specs=[
            fixed(outs[0]),
            pl.BlockSpec((seqs, longer, width), lambda i: (0, 0, head_of(i))),
            column(rows),
            fixed(wide),
            column(rows),
            column(rows),
        ]
        + [fixed(a) for a in outs[6:12]]
        + [far],
        input_output_aliases={12: 12},
        scratch_shapes=[
            pltpu.VMEM((rows + halo.shape[0], d), BF16),
            pltpu.VMEM((rows, width), F32),
            pltpu.VMEM((rows, width), F32),
            pltpu.VMEM((grid.tensor, own_rows, d), F32),
            pltpu.VMEM((own_rows, d), BF16),
            pltpu.VMEM((own_rows, d), BF16),
        ]
        + prefix_scratch(grid, channels)
        + [pltpu.SemaphoreType.DMA((2, 1)), turn_sems(grid, feed.shape[0])],
        compiler_params=pltpu.CompilerParams(
            collective_id=1, has_side_effects=True, vmem_limit_bytes=GRANT
        ),
        name="forward_recurrence",
    )(x, halo, gain, rec, rec, inlet, forget, lanes, flags, rec, shift, gain_second, feed)


def leave_kernel(
    n, tensor, seqs, branch, w_out, gelu_pre, local, cum, inlet_pre, forget_pre, conv, ext, entered,
    w_inlet, w_forget, lanes, flags, feed_part, resid,
    gelu_low, input_low, gate_grads, lane_grads, shift_grad, own_out,
    tail, carried, factor, addend, back, rim, tots, gots, line, cube_sems, line_sems, rim_sems,
    part, sums_got, sums_line, sums_cross, sums_sems,
):
    spot = Spot(n, tensor)
    every, channels = conv.shape
    length = every // seqs
    heads, width = w_inlet.shape[:2]
    behind = {"wide": lax.rem(spot.w + n - 1, n)}
    ahead = {"wide": lax.rem(spot.w + 1, n)}
    spot.greet(*[spot.flip(bit) for bit in spot.bits], behind, ahead, spot.cross)
    for place in range(spot.hi):
        for side in range(tensor):

            def put(at, place=place, side=side):
                part[place, side, at, :] = feed_part[place, side, at, :]

            by_rows(resid.shape[0], STEP, put)
    half = resid.shape[0] // HALVES
    sums = [
        Rows(spot, part, sums_got, sums_line, sums_cross.at[i], sums_sems.at[i], i * half, half)
        for i in range(HALVES)
    ]
    for k in range(spot.hi):
        for each in sums:
            each.start(k)
    tots[0] = jnp.zeros_like(tots[0])
    lane_grads[...] = jnp.zeros_like(lane_grads)
    shift_grad[...] = jnp.zeros_like(shift_grad)

    def add(at):
        shift_grad[...] += jnp.sum(branch[at, :].astype(F32).reshape(2, 8, -1), axis=0)

    by_rows(every, STEP, add)

    def decays(at, cols):
        soft = lanes[RATE_SOFT : RATE_SOFT + 1, cols]
        return decay_of(jax.nn.sigmoid(forget_pre[at, cols]), soft, flags[at, 0:1] > 0.5)

    def upward(h, none):
        cols = pl.ds(pl.multiple_of(h * width, width), width)
        grad = dot(branch[...], w_out[0, :, cols])
        gelu, slope = gelu_of(gelu_pre[:, cols])
        for s in range(seqs):
            here = slice(s * length, (s + 1) * length)
            state = local[here, cols] + cum[here, cols] * entered[s : s + 1, cols]
            low = (grad[here] * state * slope[here]).astype(BF16)
            gelu_low[here, cols] = low
            lane_grads[0:1, cols] += jnp.sum(low.astype(F32), axis=0, keepdims=True)
            decay, _ = decays(here, cols)
            place = lax.broadcasted_iota(jnp.int32, (length, width), 0)
            factor[here, :] = jnp.where(place < length - 1, pltpu.roll(decay, length - 1, 0), 1.0)
        addend[...] = grad * gelu

        def write(at, a, b):
            tail[at, cols] = a
            carried[at, cols] = b

        scan_rows(seqs, length, width, lambda at: (factor[at, :], addend[at, :]), write, True)
        for s in range(seqs):
            first = slice(s * length, s * length + 8)
            decay, _ = decays(first, cols)
            tots[0, s : s + 1, cols] = decay[0:1] * tail[first, cols][0:1]
            tots[0, seqs + s : seqs + s + 1, cols] = decay[0:1] * carried[first, cols][0:1]
        return none

    lax.fori_loop(0, heads // 2, upward, 0)
    for each in sums:
        each.along(1)
    lax.fori_loop(heads // 2, heads, upward, 0)
    come = Prefix(spot, seqs, True, tots, gots, line, cube_sems, line_sems).run()
    for each in sums:
        each.along(2)
    tots[0, 0:seqs, :] = come

    def downward(h, none):
        cols = pl.ds(pl.multiple_of(h * width, width), width)

        def row(i):
            return lanes[i : i + 1, cols]

        sums = []
        for s in range(seqs):
            here = slice(s * length, (s + 1) * length)
            place = lax.broadcasted_iota(jnp.int32, (length, width), 0)
            starts = flags[here, 0:1] > 0.5
            blocks = conv[here, cols].astype(F32)
            enter = entered[s : s + 1, cols]
            state = local[here, cols] + cum[here, cols] * enter
            before = jnp.where(place > 0, pltpu.roll(state, 1, 0), enter)
            carry = carried[here, cols] + tail[here, cols] * tots[0, s : s + 1, cols]
            inlet = jax.nn.sigmoid(inlet_pre[here, cols])
            forget = jax.nn.sigmoid(forget_pre[here, cols])
            soft = row(RATE_SOFT)
            decay, scaler = decay_of(forget, soft, starts)
            log_grad = jnp.where(
                starts, 0.0, carry * before * decay - carry * inlet * blocks * (decay * decay) / scaler
            )
            rate_grad = jnp.sum(log_grad * (-8.0 * forget), axis=0, keepdims=True) * row(RATE_SIGMOID)
            inlet_low = (carry * scaler * blocks * (inlet * (1.0 - inlet))).astype(BF16)
            forget_low = (log_grad * (-8.0 * soft) * (forget * (1.0 - forget))).astype(BF16)
            conv_grad = (
                carry * scaler * inlet
                + dot_nt(inlet_low, w_inlet[h])
                + dot_nt(forget_low, w_forget[h])
            )
            longer = ext[s, :, cols].astype(F32)
            zeros = jnp.zeros((HALO, width), F32)
            total = jnp.concatenate([zeros, row(TAPS) * conv_grad], axis=0)
            taps = [jnp.sum(conv_grad * longer[HALO:], axis=0, keepdims=True)]
            for k in range(1, CONV):
                masked = jnp.where(flags[here, k : k + 1] > 0.5, conv_grad, 0.0)
                moved = pltpu.roll(longer, k, 0)[HALO:]
                taps.append(jnp.sum(masked * moved, axis=0, keepdims=True))
                sent = jnp.concatenate([zeros, row(TAPS + k) * masked], axis=0)
                total = total + pltpu.roll(sent, HALO + length - k, 0)
            back[s, :, cols] = total
            lows = [jnp.sum(v.astype(F32), axis=0, keepdims=True) for v in (inlet_low, forget_low)]
            sums.append(taps + [jnp.sum(conv_grad, axis=0, keepdims=True)] + lows + [rate_grad])
            for m, low in enumerate((inlet_low, forget_low)):
                factor[here, :] = low.astype(F32) if m == 0 else factor[here, :]
                addend[here, :] = low.astype(F32) if m == 1 else addend[here, :]
        for i in range(len(sums[0])):
            lane_grads[2 + i : 3 + i, cols] = sum(each[i] for each in sums[1:]) + sums[0][i]
        for m, low in enumerate((factor, addend)):
            gate_grads[m, h] = dot_tn(conv[:, cols], low[...].astype(BF16)).astype(BF16)
        return none

    lax.fori_loop(0, heads, downward, 0)
    copy = remote(back.at[:, 0:HALO, :], rim, rim_sems, 0, behind)
    copy.start()
    for s in range(3, spot.hi):
        for each in sums:
            each.along(s)
    copy.wait()

    def give(h, none):
        cols = pl.ds(pl.multiple_of(h * width, width), width)
        total = jnp.zeros((1, width), F32)
        for s in range(seqs):
            edge = jnp.where(spot.w < n - 1, rim[s, :, cols], 0.0)
            value = back[s, HALO:, cols]
            value = jnp.concatenate([value[: length - HALO], value[length - HALO :] + edge], axis=0)
            low = value.astype(BF16)
            input_low[s * length : (s + 1) * length, cols] = low
            total = total + jnp.sum(low.astype(F32), axis=0, keepdims=True)
        lane_grads[1:2, cols] = total
        return none

    lax.fori_loop(0, heads, give, 0)

    def done(at, total):
        own_out[at, :] = (resid[at, :] + total).astype(BF16)

    for each in sums:
        each.end(done)
    for each in sums:
        each.finish()


def leave_recurrence(
    grid, branch, rec, gelu_pre, local, cum, inlet_pre, forget_pre, conv, ext, entered, inlet, forget, lanes,
    flags, feed_part, resid, seqs,
):
    every, channels = conv.shape
    d = branch.shape[1]
    heads, width = inlet.shape[:2]
    near = pl.BlockSpec(memory_space=pltpu.VMEM)
    low = jax.ShapeDtypeStruct((every, channels), BF16)
    return pl.pallas_call(
        functools.partial(leave_kernel, grid.n, grid.tensor, seqs),
        grid=(1,),
        out_shape=[
            low,
            low,
            jax.ShapeDtypeStruct((2, heads, width, width), BF16),
            jax.ShapeDtypeStruct((LANE_ROWS, channels), F32),
            jax.ShapeDtypeStruct((8, d), F32),
            jax.ShapeDtypeStruct(resid.shape, BF16),
        ],
        in_specs=[near, pl.BlockSpec((1, d, channels), lambda i: (2, 0, 0))] + [near] * 14,
        out_specs=[near] * 6,
        scratch_shapes=[
            pltpu.VMEM((every, channels), F32),
            pltpu.VMEM((every, channels), F32),
            pltpu.VMEM((every, width), F32),
            pltpu.VMEM((every, width), F32),
            pltpu.VMEM((seqs, every // seqs + HALO, channels), F32),
            pltpu.VMEM((seqs, HALO, channels), F32),
        ]
        + prefix_scratch(grid, channels)
        + [pltpu.SemaphoreType.DMA((2, 1)), pltpu.VMEM(feed_part.shape, BF16)]
        + rows_scratch(grid, *resid.shape)[:2]
        + rows_sems(grid)[:2],
        compiler_params=pltpu.CompilerParams(
            collective_id=5, has_side_effects=True, vmem_limit_bytes=GRANT
        ),
        name="leave_recurrence",
    )(
        branch, rec, gelu_pre, local, cum, inlet_pre, forget_pre, conv, ext, entered, inlet, forget,
        lanes, flags, feed_part, resid,
    )


class Rows:
    def __init__(self, spot, part, got, line, cross_sems, line_sems, first, rows):
        self.spot, self.part, self.got, self.line = spot, part, got, line
        self.cross_sems, self.line_sems = cross_sems, line_sems
        self.first, self.rows = first, rows
        self.span = pl.ds(first, rows)

    def by_rows(self, act):
        def one(at):
            act(pl.ds(pl.multiple_of(self.first + at.start, STEP), STEP))

        by_rows(self.rows, STEP, one)

    def place(self, k):
        spot, hi = self.spot, self.spot.hi
        last = hi - 1
        flipped = jnp.where(spot.z * 2 < hi, 0, 1)
        z = spot.z + flipped * (last - 2 * spot.z)
        if k == last:
            place = z
        else:
            place = jnp.where(k < last - z, last - k, k - (last - z))
        return place + flipped * (last - 2 * place)

    def cross_copy(self, place):
        spot = self.spot
        return remote(
            self.part.at[place, 1 - spot.t, self.span],
            self.got.at[place, self.span],
            self.cross_sems,
            place,
            spot.cross,
        )

    def start(self, k):
        self.cross_copy(self.place(k)).start()

    def line_copy(self, s, up, here=False):
        spot, hi = self.spot, self.spot.hi
        slot = (s - 1) if up else hi + s - 2
        step = 1 if up != here else -1
        return remote(
            self.line.at[0, slot, self.span],
            self.line.at[1, slot, self.span],
            self.line_sems,
            slot,
            spot.line(spot.z + step),
        )

    def own(self, place, at):
        return self.part[place, self.spot.t, at, :].astype(F32) + self.got[place, at, :].astype(F32)

    def send(self, s, up):
        spot, hi = self.spot, self.spot.hi
        place = spot.z + hi - s if up else spot.z - hi + s
        slot = (s - 1) if up else hi + s - 2
        self.cross_copy(place).wait_recv()
        begins = spot.z == 0 if up else spot.z == hi - 1

        @pl.when(begins)
        def _():
            def put(at):
                self.line[0, slot, at, :] = self.own(place, at).astype(BF16)

            self.by_rows(put)

        if s > 1:

            @pl.when(jnp.logical_not(begins))
            def _():
                self.line_copy(s - 1, up, here=True).wait_recv()

                def put(at):
                    before = self.line[1, slot - 1, at, :].astype(F32)
                    self.line[0, slot, at, :] = (self.own(place, at) + before).astype(BF16)

                self.by_rows(put)

        self.line_copy(s, up).start()

    def sends_up(self, s):
        return self.spot.z <= s - 1

    def sends_down(self, s):
        return self.spot.z >= self.spot.hi - s

    def along(self, s):
        spot, hi = self.spot, self.spot.hi

        @pl.when(jnp.logical_and(self.sends_up(s), spot.z < hi - 1))
        def _():
            self.send(s, True)

        @pl.when(jnp.logical_and(self.sends_down(s), spot.z > 0))
        def _():
            self.send(s, False)

    def end(self, done):
        spot, hi = self.spot, self.spot.hi
        self.cross_copy(spot.z).wait_recv()

        @pl.when(spot.z > 0)
        def _():
            self.line_copy(hi - 1, True, here=True).wait_recv()

        @pl.when(spot.z < hi - 1)
        def _():
            self.line_copy(hi - 1, False, here=True).wait_recv()

        def total(at):
            below = self.line[1, hi - 2, at, :].astype(F32)
            above = self.line[1, 2 * hi - 3, at, :].astype(F32)
            value = self.own(spot.z, at)
            value = value + jnp.where(spot.z > 0, below, 0.0)
            done(at, value + jnp.where(spot.z < hi - 1, above, 0.0))

        self.by_rows(total)

    def finish(self):
        spot, hi = self.spot, self.spot.hi
        for place in range(hi):
            self.cross_copy(place).wait_send()
        for s in range(1, hi):

            @pl.when(jnp.logical_and(self.sends_up(s), spot.z < hi - 1))
            def _():
                self.line_copy(s, True).wait_send()

            @pl.when(jnp.logical_and(self.sends_down(s), spot.z > 0))
            def _():
                self.line_copy(s, False).wait_send()


def feed_kernel(
    n, tensor, unit_tiles, own, w_gate, w_up, w_down, cot, resid, gain,
    whole, gate_low, up_low, hidden, both, gain_grad, feed_part,
    part, got, line, mine, other, sems, cross_sems, line_sems, swap_sems,
):
    spot = Spot(n, tensor)
    hi = spot.hi
    rows, d = own.shape
    width = w_gate.shape[2]
    every = tensor * rows
    spot.greet(spot.cross)

    def put(at):
        whole[spot.z, spot.t, at, :] = own[at, :]

    by_rows(rows, STEP, put)
    half = rows // HALVES
    chains = [
        Chain(
            spot,
            lambda place, k, i=i: whole.at[
                place, lax.rem(spot.t + k, tensor), pl.ds(i * half, half)
            ],
            sems.at[i],
            [spot.cross],
        )
        for i in range(HALVES)
    ]
    for chain in chains:
        chain.first()
    gain_grad[...] = jnp.zeros_like(gain_grad)
    tiles = width // LANE
    skip = spot.z * tiles - jnp.minimum(spot.z * tiles, unit_tiles - tiles)
    chunk = 256

    def work(place):
        def ahead(j, none):
            cols = pl.ds(pl.multiple_of(j * chunk, chunk), chunk)
            rows_in = whole[place].reshape(every, d)
            gate, slope = gelu_of(dot(rows_in, w_gate[0, :, cols]))
            up = dot(rows_in, w_up[0, :, cols])
            grad = dot(cot[place].reshape(every, d), w_down[0, :, cols])
            at = lax.broadcasted_iota(jnp.int32, (1, chunk), 1) + j * chunk
            ok = at >= skip * LANE
            grad = jnp.where(ok, grad, 0.0)
            hidden[place, :, cols] = jnp.where(ok, gate * up, 0.0).astype(BF16)
            gate_low[place, :, cols] = (grad * up * slope).astype(BF16)
            up_low[place, :, cols] = (grad * gate).astype(BF16)
            return none

        lax.fori_loop(0, width // chunk, ahead, 0)

        def back(j, none):
            cols = pl.ds(pl.multiple_of(j * chunk, chunk), chunk)
            value = dot_nt(gate_low[place], w_gate[0, cols, :])
            value = (value + dot_nt(up_low[place], w_up[0, cols, :])).astype(BF16)
            for side in range(tensor):
                part[place, side, :, cols] = value[side * rows : (side + 1) * rows]
            return none

        lax.fori_loop(0, d // chunk, back, 0)

    def come_and_work(place):
        for chain in chains:
            chain.fans.arrive(place, 1)
        work(place)

    for s in range(1, hi):
        for chain in chains:
            chain.onward(s)
        chains[0].places(s - 1, come_and_work)
    chains[0].places(hi - 1, come_and_work)
    sums = [
        Rows(spot, part, got, line, cross_sems.at[i], line_sems.at[i], i * half, half)
        for i in range(HALVES)
    ]
    for k in range(hi):
        for each in sums:
            each.start(k)

    def give(i, none):
        place, j = i // (d // chunk), lax.rem(i, d // chunk)
        cols = pl.ds(pl.multiple_of(j * chunk, chunk), chunk)
        value = dot_nt(hidden[place], w_down[0, cols, :]).astype(BF16)
        for side in range(tensor):
            feed_part[place, side, :, cols] = value[side * rows : (side + 1) * rows]
        return none

    lax.fori_loop(0, hi * (d // chunk), give, 0)
    for chain in chains:
        chain.finish_sends()

    def done(at, total):
        value = resid[at, :]
        scale = lax.rsqrt(jnp.mean(value * value, axis=-1, keepdims=True) + 1e-06)
        turned = total * gain[...]
        inner = jnp.mean(turned * value, axis=-1, keepdims=True)
        grad = cot[spot.z, spot.t, at, :].astype(F32)
        grad = grad + scale * turned - value * (scale * scale * scale * inner)
        gained = total * value * scale
        gain_grad[...] += jnp.sum(gained.reshape(2, 8, -1), axis=0)
        mine[at, :] = grad.astype(BF16)

    for s in range(1, hi):
        for each in sums:
            each.along(s)
    swaps = []
    for i, each in enumerate(sums):
        each.end(done)
        span = pl.ds(i * half, half)
        swaps.append(remote(mine.at[span], other.at[span], swap_sems, i, spot.cross))
        swaps[-1].start()
    for each in sums:
        each.finish()
    share(spot, swaps, mine, other, both)


def share(spot, copies, mine, other, both):
    def keep(at):
        both[spot.t, at, :] = mine[at, :]

    by_rows(mine.shape[0], STEP, keep)
    for copy in copies:
        copy.wait()

    def take(at):
        both[1 - spot.t, at, :] = other[at, :]

    by_rows(mine.shape[0], STEP, take)


def rows_scratch(grid, rows, width):
    hi = grid.hi
    return [
        pltpu.VMEM((hi, rows, width), BF16),
        pltpu.VMEM((2, 2 * (hi - 1), rows, width), BF16),
        pltpu.VMEM((rows, width), BF16),
        pltpu.VMEM((rows, width), BF16),
    ]


def rows_sems(grid):
    hi = grid.hi
    return [
        pltpu.SemaphoreType.DMA((HALVES, 2, hi)),
        pltpu.SemaphoreType.DMA((HALVES, 2, 2 * (hi - 1))),
        pltpu.SemaphoreType.DMA((2, HALVES)),
    ]


def feed_forward(grid, own, feed, cot, resid, gain, unit_tiles):
    rows, d = own.shape
    hi, tensor = grid.hi, grid.tensor
    width = feed.shape[-1]
    near = pl.BlockSpec(memory_space=pltpu.VMEM)
    whole = jax.ShapeDtypeStruct((hi, tensor, rows, d), BF16)
    low = jax.ShapeDtypeStruct((hi, tensor * rows, width), BF16)
    feed = feed.reshape(3, -1, width)

    def weight(k):
        return pl.BlockSpec((1, d, width), lambda i: (k, 0, 0))

    return pl.pallas_call(
        functools.partial(feed_kernel, grid.n, tensor, unit_tiles),
        grid=(1,),
        out_shape=[
            whole,
            low,
            low,
            low,
            jax.ShapeDtypeStruct((tensor, rows, d), BF16),
            jax.ShapeDtypeStruct((8, d), F32),
            whole,
        ],
        in_specs=[near] + [weight(k) for k in range(3)] + [near] * 3,
        out_specs=[near] * 7,
        scratch_shapes=[pltpu.VMEM(whole.shape, BF16)]
        + rows_scratch(grid, rows, d)
        + [chain_sems(1, HALVES)]
        + rows_sems(grid),
        compiler_params=pltpu.CompilerParams(
            collective_id=2, has_side_effects=True, vmem_limit_bytes=GRANT
        ),
        name="feed_forward",
    )(own, feed, feed, feed, cot, resid, gain)


RING = 4


def tile_rows(rows):
    return 16 if rows % 16 == 0 else 8


SENDING = 8
HELD = 2


def place_at(j, hi):
    return lax.rem(2 * j + hi // 2 + (2 * j) // hi, hi)


def grads_kernel(
    n, tensor, spans, kept,
    unit_tiles,
    second, cot, normed, branch, gate_low, up_low, hidden, gelu_low, input_low, mixed, gates, first, own_out, thin,
    apart, summed, first_other, block_out, thin_own, *refs,
):
    stages = (n // LINE).bit_length() - 1
    lists = [refs[i * stages : (i + 1) * stages] for i in range(6)]
    sends, keeps, gots, thin_sends, thin_keeps, thin_gots = lists
    (
        made, ready, got_line, first_out, first_got, thin_ready, thin_line,
        cube_sems, line_sems, first_sems, thin_sems, thin_line_sems,
    ) = refs[6 * stages :]
    spot = Spot(n, tensor)
    hi = spot.hi
    all_spans = len(spans)
    units = all_spans * hi
    step = pl.program_id(0)
    rows = ready.shape[1]
    width = ready.shape[2]
    each = tile_rows(rows)
    last_step = units + stages - 1
    first_rows, out_rows = first.shape[0], own_out.shape[0]

    def place_of(unit):
        return place_at(lax.rem(unit, hi), hi)

    sources = {
        "gate": (second, gate_low),
        "up": (second, up_low),
        "down": (cot, hidden),
        "gelu": (normed, gelu_low),
        "input": (normed, input_low),
        "out": (branch, mixed),
    }

    def cube_copy(stage, unit):
        slot = lax.rem(unit, RING)
        return remote(
            sends[stage].at[slot],
            gots[stage].at[slot],
            cube_sems.at[stage],
            slot,
            spot.flip(spot.bits[stage]),
        )

    def line_copy(unit):
        slot = lax.rem(unit, SENDING)
        span = unit // hi
        return pltpu.make_async_remote_copy(
            src_ref=ready.at[slot],
            dst_ref=got_line.at[span, spot.z],
            send_sem=line_sems.at[0, slot],
            recv_sem=line_sems.at[1, span * hi + spot.z],
            device_id=spot.line(place_of(unit)),
            device_id_type=MESH,
        )

    def line_here(span, sender):
        here = got_line.at[span, sender]
        return pltpu.make_async_remote_copy(
            src_ref=here,
            dst_ref=here,
            send_sem=line_sems.at[0, 0],
            recv_sem=line_sems.at[1, span * hi + sender],
            device_id=spot.line(sender),
            device_id_type=MESH,
        )

    def line_sent(unit):
        @pl.when(jnp.logical_and(unit >= 0, place_of(unit) != spot.z))
        def _():
            line_copy(unit).wait_send()

    def settle(span):
        for distance in range(1, hi):
            line_here(span, spot.away(distance)).wait_recv()

        def give(at):
            if span < kept:
                tiles = width // LANE
                for place in range(hi):
                    skip = place * tiles - min(place * tiles, unit_tiles - tiles)
                    if skip < tiles:
                        value = got_line[span, place, at, skip * LANE :]
                        apart[span, at, place * width : (place + 1) * width - skip * LANE] = value
            else:
                value = got_line[span, 0, at, :].astype(F32)
                for place in range(1, hi):
                    value = value + got_line[span, place, at, :].astype(F32)
                blocks = width // summed.shape[2]
                for j in range(blocks):
                    cols = slice(j * summed.shape[2], (j + 1) * summed.shape[2])
                    summed[(span - kept) * blocks + j, at, :] = value[:, cols]

        by_rows(rows, each, give)

    def thin_copy(stage):
        return remote(
            thin_sends[stage], thin_gots[stage], thin_sems, stage, spot.flip(spot.bits[stage])
        )

    def thin_line_copy(place, sender):
        return pltpu.make_async_remote_copy(
            src_ref=thin_ready.at[place],
            dst_ref=thin_line.at[sender],
            send_sem=thin_line_sems.at[0, place],
            recv_sem=thin_line_sems.at[1, sender],
            device_id=spot.line(place),
            device_id_type=MESH,
        )

    first_copy = remote(first_out, first_got, first_sems, 0, spot.cross)

    @pl.when(step == 0)
    def _():
        spot.greet(*[spot.flip(bit) for bit in spot.bits], spot.cross)

        def put(at):
            first_out[at, :] = first[at, :]

        by_rows(first_rows, STEP, put)

        def put_out(at):
            to = pl.ds(pl.multiple_of(first_rows + at.start, STEP), STEP)
            first_out[to, :] = own_out[at, :]

        by_rows(out_rows, STEP, put_out)
        first_copy.start()
        mine = spot.bit(1)
        for place in range(hi):
            for k in range(thin_sends[0].shape[1]):
                thin_sends[0][place, k] = thin[place, 2 * k + 1 - mine]
                thin_keeps[0][place, k] = thin[place, 2 * k + mine]
        thin_copy(0).start()

    for stage in range(stages):

        @pl.when(step == stage + 1)
        def _(stage=stage):
            thin_copy(stage).wait_recv()
            if stage < stages - 1:
                mine = spot.bit(spot.bits[stage + 1])
                for place in range(hi):
                    for k in range(thin_sends[stage + 1].shape[1]):
                        a, b = 2 * k + 1 - mine, 2 * k + mine
                        thin_sends[stage + 1][place, k] = (
                            thin_keeps[stage][place, a] + thin_gots[stage][place, a]
                        )
                        thin_keeps[stage + 1][place, k] = (
                            thin_keeps[stage][place, b] + thin_gots[stage][place, b]
                        )
                thin_copy(stage + 1).start()
            else:
                for place in range(hi):
                    thin_ready[place] = thin_keeps[stage][place, 0] + thin_gots[stage][place, 0]
                for distance in range(1, hi):
                    thin_line_copy(spot.away(distance), spot.z).start()

    @pl.when(step < units)
    def _():
        slot = lax.rem(step, RING)

        @pl.when(step >= RING)
        def _():
            cube_copy(0, step - RING).wait_send()

        for span, pieces in enumerate(spans):

            @pl.when(step // hi == span)
            def _(pieces=pieces):
                for name, begin, width, to in pieces:
                    if name == "gates":

                        def put(at, width=width, to=to):
                            made[at, to : to + width] = gates[0, at, :].astype(made.dtype)

                        by_rows(made.shape[0], STEP, put)
                        continue
                    left, right = sources[name]

                    def one(j, carry, left=left, right=right, begin=begin, width=width, to=to):
                        at = pl.ds(pl.multiple_of(j * LANE, LANE), LANE)
                        made[at, to : to + width] = lax.dot_general(
                            left[:, at],
                            right[:, begin : begin + width],
                            (((0,), (0,)), ((), ())),
                            preferred_element_type=F32,
                        ).astype(made.dtype)
                        return carry

                    lax.fori_loop(0, made.shape[0] // LANE, one, 0)

        mine = spot.bit(1)
        for k in range(sends[0].shape[1]):

            def put(at, k=k):
                def block(i):
                    at_made = pl.ds(pl.multiple_of(i * rows + at.start, each), each)
                    return made[at_made, :].astype(BF16)

                sends[0][slot, k, at, :] = block(2 * k + 1 - mine)
                keeps[0][lax.rem(step, HELD), k, at, :] = block(2 * k + mine)

            by_rows(rows, each, put)
        cube_copy(0, step).start()

    for stage in range(stages):
        unit = step - stage - 1

        @pl.when(jnp.logical_and(unit >= 0, unit < units))
        def _(stage=stage, unit=unit):
            slot = lax.rem(unit, RING)
            held = lax.rem(unit, HELD)
            cube_copy(stage, unit).wait_recv()

            def total(k, at):
                return (
                    keeps[stage][held, k, at, :].astype(F32) + gots[stage][slot, k, at, :].astype(F32)
                ).astype(BF16)

            if stage < stages - 1:

                @pl.when(unit >= RING)
                def _():
                    cube_copy(stage + 1, unit - RING).wait_send()

                mine = spot.bit(spot.bits[stage + 1])
                for k in range(sends[stage + 1].shape[1]):

                    def put(at, k=k):
                        sends[stage + 1][slot, k, at, :] = total(2 * k + 1 - mine, at)
                        keeps[stage + 1][held, k, at, :] = total(2 * k + mine, at)

                    by_rows(rows, each, put)
                cube_copy(stage + 1, unit).start()
            else:
                line_sent(unit - SENDING)
                place = place_of(unit)

                @pl.when(place != spot.z)
                def _():
                    def put(at):
                        ready[lax.rem(unit, SENDING), at, :] = total(0, at)

                    by_rows(rows, each, put)
                    line_copy(unit).start()

                @pl.when(place == spot.z)
                def _():
                    def put(at):
                        got_line[unit // hi, spot.z, at, :] = total(0, at)

                    by_rows(rows, each, put)

    late = 2 * hi + stages - 1
    for span in range(all_spans):
        when = span * hi + hi - 1 + late
        if when < last_step:

            @pl.when(step == when)
            def _(span=span):
                settle(span)

    @pl.when(step == last_step)
    def _():
        for span in range(all_spans):
            if span * hi + hi - 1 + late >= last_step:
                settle(span)
        for unit in range(units - SENDING, units):
            line_sent(unit)
        for stage in range(stages):
            for unit in range(units - RING, units):
                cube_copy(stage, unit).wait_send()
            thin_copy(stage).wait_send()
        value = thin_ready[spot.z]
        for distance in range(1, hi):
            place = spot.away(distance)
            thin_line_copy(place, place).wait_recv()
            thin_line_copy(place, spot.z).wait_send()
            value = value + thin_line[place]
        thin_own[...] = value
        first_copy.wait()

        def take(at):
            first_other[at, :] = first_got[at, :]

        by_rows(first_rows, STEP, take)

        def take_out(at):
            other = pl.ds(pl.multiple_of(first_rows + at.start, STEP), STEP)
            block_out[spot.t, at, :] = own_out[at, :]
            block_out[1 - spot.t, at, :] = first_got[other, :]

        by_rows(out_rows, STEP, take_out)


def column_spans(widths, width):
    spans, here, room = [], [], width
    for name, size in widths:
        begin = 0
        while begin < size:
            count = min(size - begin, room)
            here.append((name, begin, count, width - room))
            begin, room = begin + count, room - count
            if room == 0:
                spans, here, room = spans + [here], [], width
    assert not here
    return spans


def send_grads(grid, feed, rec, gates, first, own_out, thin, unit_tiles):
    hi, inner = grid.hi, grid.inner_size
    second, cot, gate_low, up_low, hidden = feed
    normed, branch, gelu_low, input_low, mixed = rec
    d = second.shape[1]
    rows = d // grid.n
    slab = d // hi
    width = gate_low.shape[1]
    kept = 3
    channels = mixed.shape[1]
    spans = column_spans([(name, width) for name in ("gate", "up", "down")], width) + column_spans(
        [(name, channels) for name in ("gelu", "input", "out")] + [("gates", gates.shape[1])], width
    )
    all_spans = len(spans)
    units = all_spans * hi
    stages = inner.bit_length() - 1

    def place_of(i):
        return place_at(lax.rem(jnp.minimum(i, units - 1), hi), hi)

    def slab_of(a):
        return pl.BlockSpec((a.shape[0], slab), lambda i: (0, place_of(i)))

    def whole(a):
        zeros = (0,) * a.ndim
        return pl.BlockSpec(a.shape, lambda i: zeros, pipeline_mode=pl.Buffered(1))

    block = gates.shape[1]
    apart = jax.ShapeDtypeStruct((kept, rows, unit_tiles * LANE), BF16)
    summed = jax.ShapeDtypeStruct(((all_spans - kept) * (width // block), rows, block), F32)
    both = jax.ShapeDtypeStruct((grid.tensor,) + own_out.shape, BF16)
    other = jax.ShapeDtypeStruct(first.shape, BF16)
    thin = thin.reshape(hi, inner, 8, thin.shape[1] // 8)
    thin_shape = thin.shape[2:]
    thin_own = jax.ShapeDtypeStruct(thin_shape, F32)
    outs = [apart, summed, other, both, thin_own]
    swapped = (first.shape[0] + own_out.shape[0], d)

    def halves(lead, tail, kind):
        return [
            pltpu.VMEM((lead, inner >> (stage + 1)) + tail, kind) for stage in range(stages)
        ]

    gates = gates.reshape(hi, slab, gates.shape[1])
    return pl.pallas_call(
        functools.partial(grads_kernel, grid.n, grid.tensor, spans, kept, unit_tiles),
        grid=(units + stages,),
        out_shape=outs,
        in_specs=[slab_of(a) for a in (second, cot, normed, branch)]
        + [whole(a) for a in (gate_low, up_low, hidden, gelu_low, input_low, mixed)]
        + [pl.BlockSpec((1,) + gates.shape[1:], lambda i: (place_of(i), 0, 0))]
        + [whole(first), whole(own_out), whole(thin)],
        out_specs=[whole(a) for a in outs],
        scratch_shapes=halves(RING, (rows, width), BF16)
        + halves(HELD, (rows, width), BF16)
        + halves(RING, (rows, width), BF16)
        + halves(hi, thin_shape, F32) * 3
        + [
            pltpu.VMEM((slab, width), BF16 if rows % 16 == 0 else F32),
            pltpu.VMEM((SENDING, rows, width), BF16),
            pltpu.VMEM((all_spans, hi, rows, width), BF16),
            pltpu.VMEM(swapped, BF16),
            pltpu.VMEM(swapped, BF16),
            pltpu.VMEM((hi,) + thin_shape, F32),
            pltpu.VMEM((hi,) + thin_shape, F32),
            pltpu.SemaphoreType.DMA((stages, 2, RING)),
            pltpu.SemaphoreType.DMA((2, units)),
            pltpu.SemaphoreType.DMA((2, 1)),
            pltpu.SemaphoreType.DMA((2, stages)),
            pltpu.SemaphoreType.DMA((2, hi)),
        ],
        compiler_params=pltpu.CompilerParams(
            collective_id=4, has_side_effects=True, vmem_limit_bytes=GRANT
        ),
        name="send_grads",
    )(
        second, cot, normed, branch, gate_low, up_low, hidden, gelu_low, input_low, mixed, gates,
        first, own_out, thin,
    )


def rms_norm(values, gain):
    scale = lax.rsqrt(jnp.mean(values * values, axis=-1, keepdims=True) + 1e-06)
    return values * scale * gain


def dot(left, right):
    return jnp.dot(left, right, preferred_element_type=F32)


def dot_nt(left, right):
    return jnp.einsum("ik,jk->ij", left, right, preferred_element_type=F32)


def dot_tn(left, right):
    return jnp.einsum("ki,kj->ij", left, right, preferred_element_type=F32)


def local(
    block_in,
    segment_ids,
    cotangent,
    first_gain,
    gelu_weight,
    gelu_bias,
    input_weight,
    input_bias,
    conv_weight,
    conv_bias,
    inlet_weight,
    inlet_bias,
    forget_weight,
    forget_bias,
    decay_rate,
    out_weight,
    out_bias,
    second_gain,
    mlp_gate,
    mlp_up,
    mlp_down,
):
    grid = Grid()
    seq_count, tok_count, width = block_in.shape
    head_count, block_size = gelu_weight.shape[1:]
    channels = head_count * block_size
    margin = CONV - 1
    rows_all = seq_count * tok_count
    rows_half = rows_all // grid.tensor
    d_own = gelu_weight.shape[0]
    lane_own = gelu_bias.shape[1]
    units = mlp_gate.shape[1]
    unit_tiles = units // LANE
    window_tiles = -(-unit_tiles // grid.hi)
    window = window_tiles * LANE

    halo_rows = block_in[:, tok_count - HALO :]
    marks = (segment_ids + 1).astype(BF16)
    halo, rim_marks = shifted((halo_rows, marks[:, tok_count - margin :]), "wide", 1)
    halo = halo.reshape(seq_count * HALO, width)
    marks_ext = jnp.concatenate([rim_marks, marks], axis=1)
    earlier = [marks_ext[:, margin - k : margin - k + tok_count] == marks for k in range(1, CONV)]
    flags = jnp.stack([jnp.logical_not(earlier[0])] + earlier, axis=-1).astype(F32)
    flags = jnp.pad(flags.reshape(rows_all, CONV), ((0, 0), (0, 8 - CONV)))

    per_lane = jnp.stack([gelu_bias, input_bias])
    per_lane = jnp.concatenate(
        [per_lane, conv_weight, jnp.stack([conv_bias, inlet_bias, forget_bias, decay_rate])]
    )
    lane_table = lax.dynamic_update_slice(
        jnp.zeros((CONV + 6, head_count, block_size), BF16), per_lane, (0, 0, grid.w * lane_own)
    )
    per_width = jnp.stack([first_gain, out_bias, second_gain])
    width_table = lax.dynamic_update_slice(
        jnp.zeros((3, width), BF16), per_width, (0, grid.w * d_own)
    )
    thin_own = jnp.concatenate(
        [lane_table.reshape(CONV + 6, channels), width_table.reshape(-1, channels)]
    )
    thin_count = thin_own.shape[0]
    thin_own = jnp.pad(thin_own, ((0, -thin_count % 16), (0, 0)))
    cot_rows = cotangent.reshape(grid.tensor, rows_half, width)
    rec_all, gates_all, thin_all, feed_all, cot_all = place_own(
        grid,
        (
            input_weight.transpose(1, 0, 2),
            gelu_weight.transpose(1, 0, 2),
            out_weight.transpose(0, 2, 1),
        ),
        (mlp_gate, mlp_up, mlp_down.T),
        (inlet_weight, forget_weight),
        thin_own,
        cot_rows,
    )
    rec_all, gates_all, thin_all, cot_all = bring_weights(
        grid, rec_all, gates_all, thin_all, cot_all
    )
    rec_all = rec_all.reshape(3, width, channels)
    gates_all = gates_all.reshape(2, head_count, block_size, block_size)
    inlet_full, forget_full = gates_all[0], gates_all[1]
    table = jnp.sum(thin_all.astype(F32), axis=0)
    lane_rows = table[: CONV + 6]
    gain_first, out_shift, gain_second = table[CONV + 6 : thin_count].reshape(3, width)
    rate = lane_rows[CONV + 5]
    lanes = jnp.concatenate([lane_rows[: CONV + 5], jnp.stack([jax.nn.softplus(rate), jax.nn.sigmoid(rate)])])
    lanes = jnp.pad(lanes, ((0, LANE_ROWS - lanes.shape[0]), (0, 0)))

    x = block_in.reshape(rows_all, width)
    (
        normed,
        ext,
        conv,
        gelu_pre,
        inlet_pre,
        forget_pre,
        cum,
        local_state,
        entered,
        mixed,
        resid,
        second_own,
        feed_all,
    ) = forward_recurrence(
        grid, x, halo, gain_first[None], rec_all, inlet_full, forget_full, lanes, flags, out_shift[None],
        gain_second[None], feed_all, seq_count,
    )

    rows_feed = grid.hi * rows_all
    second_all, gate_low, up_low, hidden, branch_low, gain_two_grad, feed_part = feed_forward(
        grid, second_own, feed_all, cot_all, resid, gain_second[None], unit_tiles
    )
    second_all, cot_all = (v.reshape(rows_feed, width) for v in (second_all, cot_all))
    gate_low, up_low, hidden = (v.reshape(rows_feed, window) for v in (gate_low, up_low, hidden))
    branch_low = branch_low.reshape(rows_all, width)
    gain_two_grad = jnp.sum(gain_two_grad, axis=0)

    gelu_low, input_low, gate_w_grads, lane_grads, out_shift_grad, own_out = leave_recurrence(
        grid, branch_low, rec_all, gelu_pre, local_state, cum, inlet_pre, forget_pre, conv, ext, entered,
        inlet_full, forget_full, lanes, flags, feed_part, resid, seq_count,
    )
    out_shift_grad = jnp.sum(out_shift_grad, axis=0)
    gate_w_grads = (
        gate_w_grads.reshape(2, head_count, grid.n, lane_own, block_size)
        .transpose(2, 0, 1, 3, 4)
        .reshape(width, block_size)
    )
    inputs = x.astype(F32)
    scale_first = lax.rsqrt(jnp.mean(inputs * inputs, axis=-1, keepdims=True) + 1e-06)
    first_part, gain_one_grad = first_gradient(
        x, input_low, gelu_low, rec_all, jnp.broadcast_to(scale_first, (rows_all, 8))
    )
    gain_one_grad = jnp.sum(gain_one_grad, axis=0)
    gain_grads = jnp.stack([gain_one_grad, gain_two_grad])
    gain_grads = gain_grads + grid.swap(gain_grads)

    lane_grads = (
        lane_grads[: CONV + 6]
        .reshape(CONV + 6, head_count, grid.n, lane_own)
        .transpose(2, 0, 1, 3)
        .reshape(grid.n, -1)
    )
    thin_grads = jnp.concatenate(
        [v.reshape(grid.n, d_own) for v in (gain_grads[0], out_shift_grad, gain_grads[1])]
        + [lane_grads],
        axis=1,
    )
    feed_grads, rec_grads, first_other, block_out, thin = send_grads(
        grid,
        (second_all, cot_all, gate_low, up_low, hidden),
        (normed, branch_low, gelu_low, input_low, mixed),
        gate_w_grads,
        first_part,
        own_out,
        thin_grads,
        unit_tiles,
    )
    block_out = block_out.reshape(block_in.shape)
    thin = thin.reshape(-1)
    gate_grad, up_grad, down_grad = (feed_grads[m].astype(F32) for m in range(3))
    down_grad = down_grad.T
    gelu_w_grad = rec_grads[:head_count].transpose(1, 0, 2)
    input_w_grad = rec_grads[head_count : 2 * head_count].transpose(1, 0, 2)
    out_grad = rec_grads[2 * head_count : 3 * head_count].transpose(0, 2, 1)
    gate_w_grads = rec_grads[3 * head_count].reshape(2, head_count, lane_own, block_size)
    first_grad = first_part.astype(F32) + first_other.astype(F32)
    _, pull_first = jax.vjp(rms_norm, inputs, gain_first)
    input_norm_grad, _ = pull_first(first_grad)
    block_grad = (branch_low.astype(F32) + input_norm_grad).reshape(block_in.shape)
    gain_one_own, out_shift_own, gain_two_own = (
        thin[i * d_own : (i + 1) * d_own] for i in range(3)
    )
    lanes = thin[3 * d_own :].reshape(CONV + 6, head_count, lane_own)
    return (
        block_out,
        block_grad,
        gain_one_own,
        gelu_w_grad,
        lanes[0],
        input_w_grad,
        lanes[1],
        lanes[2 : 2 + CONV],
        lanes[2 + CONV],
        gate_w_grads[0],
        lanes[3 + CONV],
        gate_w_grads[1],
        lanes[4 + CONV],
        lanes[5 + CONV],
        out_grad,
        out_shift_own,
        gain_two_own,
        gate_grad,
        up_grad,
        down_grad,
    )


def solution(mesh):
    in_specs = (
        P(None, "wide", None),
        P(None, "wide"),
        P(None, "wide", None),
        P("wide"),
        P("wide", "tensor", None),
        P("tensor", "wide"),
        P("wide", "tensor", None),
        P("tensor", "wide"),
        P(None, "tensor", "wide"),
        P("tensor", "wide"),
        P("tensor", "wide", None),
        P("tensor", "wide"),
        P("tensor", "wide", None),
        P("tensor", "wide"),
        P("tensor", "wide"),
        P("tensor", None, "wide"),
        P("wide"),
        P("wide"),
        P("wide", "tensor"),
        P("wide", "tensor"),
        P("tensor", "wide"),
    )
    out_specs = (
        P(None, "wide", None),
        P(None, "wide", None),
        P("wide"),
        P("wide", "tensor", None),
        P("tensor", "wide"),
        P("wide", "tensor", None),
        P("tensor", "wide"),
        P(None, "tensor", "wide"),
        P("tensor", "wide"),
        P("tensor", "wide", None),
        P("tensor", "wide"),
        P("tensor", "wide", None),
        P("tensor", "wide"),
        P("tensor", "wide"),
        P("tensor", None, "wide"),
        P("wide"),
        P("wide"),
        P("wide", "tensor"),
        P("wide", "tensor"),
        P("tensor", "wide"),
    )
    return jax.shard_map(local, mesh=mesh, in_specs=in_specs, out_specs=out_specs, check_vma=False)
```

```python
import functools

import jax
import jax.numpy as jnp
from jax import lax
from jax.experimental import pallas as pl
from jax.experimental.pallas import tpu as pltpu
from jax.sharding import PartitionSpec as P

CONV = 4
LANE = 128
GRANT = 60 * 1024 * 1024
F32 = jnp.float32
BF16 = jnp.bfloat16

LINE = 4


class Grid:
    def __init__(self):
        self.n = lax.axis_size("wide")
        self.hi = LINE
        self.inner_size = self.n // LINE
        self.tensor = lax.axis_size("tensor")
        self.w = lax.axis_index("wide")
        self.t = lax.axis_index("tensor")
        self.z = self.w // self.inner_size
        self.inner = lax.rem(self.w, self.inner_size)

    def flip(self, value, bit):
        return lax.ppermute(value, "wide", [(i, i ^ bit) for i in range(self.n)])

    def swap(self, value):
        size = self.tensor
        pairs = [(i, (i + 1) % size) for i in range(size)]
        return lax.ppermute(value, "tensor", pairs)


def shifted(shard, axis, by):
    size = lax.axis_size(axis)
    place = lax.axis_index(axis) - by
    there = jnp.logical_and(place >= 0, place < size)
    pairs = [(i, (i + by) % size) for i in range(size)]
    moved = lax.ppermute(shard, axis, pairs)
    return jax.tree.map(lambda a: jnp.where(there, a, jnp.zeros_like(a)), moved)


def pick(values, index, axis=0):
    return lax.dynamic_index_in_dim(values, index, axis, keepdims=False)


MESH = pl.DeviceIdType.MESH


class Spot:
    def __init__(self, n, tensor):
        self.n = n
        self.hi = LINE
        self.inner_size = n // LINE
        self.bits = [1 << i for i in range(self.inner_size.bit_length() - 1)]
        self.tensor = tensor
        self.w = lax.axis_index("wide")
        self.t = lax.axis_index("tensor")
        self.z = self.w // self.inner_size
        self.inner = lax.rem(self.w, self.inner_size)
        self.cross = {"tensor": lax.rem(self.t + 1, tensor)}

    def bit(self, which):
        return lax.rem(self.inner // which, 2)

    def flip(self, which):
        return {"wide": self.w + which - 2 * which * self.bit(which)}

    def line(self, place):
        return {"wide": place * self.inner_size + self.inner}

    def away(self, distance):
        return lax.rem(self.z + distance, self.hi)

    def greet(self, *sides):
        barrier = pltpu.get_barrier_semaphore()
        for side in sides:
            pl.semaphore_signal(barrier, inc=1, device_id=side, device_id_type=MESH)
        for distance in range(1, self.hi):
            pl.semaphore_signal(
                barrier, inc=1, device_id=self.line(self.away(distance)), device_id_type=MESH
            )
        pl.semaphore_wait(barrier, len(sides) + self.hi - 1)


def remote(src, dst, sems, index, side):
    return pltpu.make_async_remote_copy(
        src_ref=src,
        dst_ref=dst,
        send_sem=sems.at[0, index],
        recv_sem=sems.at[1, index],
        device_id=side,
        device_id_type=MESH,
    )


class Fans:
    def __init__(self, spot, at, sems, base, sides):
        self.spot, self.at, self.sems, self.base, self.sides = spot, at, sems, base, sides
        self.kinds = sorted(range(1 << len(sides)), key=lambda k: (bin(k).count("1"), -k))

    def onto(self, k):
        low = (k & -k) if k else 1 << len(self.sides)
        return [i for i in reversed(range(len(self.sides))) if (1 << i) < low]

    def copy(self, place, k, i, here=False):
        spot, hi = self.spot, self.spot.hi
        landed = k if here else k | (1 << i)
        index = self.base + (landed - 1) * hi + lax.rem(place - spot.z + hi, hi)
        ref = self.at(place, k)
        return remote(ref, ref, self.sems, index, self.sides[i])

    def hand_on(self, place, k):
        for i in self.onto(k):
            self.copy(place, k, i).start()

    def arrive(self, place, k):
        low = (k & -k).bit_length() - 1
        self.copy(place, k, low, here=True).wait_recv()

    def pass_on(self, place):
        for k in self.kinds:
            if k and self.onto(k):
                self.arrive(place, k)
                self.hand_on(place, k)

    def finish(self, place):
        for k in self.kinds:
            if k and not self.onto(k):
                self.arrive(place, k)
        self.finish_sends(place)

    def finish_sends(self, place):
        for k in self.kinds:
            for i in self.onto(k):
                self.copy(place, k, i).wait_send()

    def count(sides, hi):
        return ((1 << sides) - 1) * hi


class Chain:
    def __init__(self, spot, at, sems, sides):
        self.spot, self.at, self.sems = spot, at, sems
        self.fans = Fans(spot, at, sems, 2 * (spot.hi - 1), sides)

    def line_copy(self, s, up):
        spot, hi = self.spot, self.spot.hi
        owner = spot.z - (s - 1) if up else spot.z + (s - 1)
        other = spot.z + 1 if up else spot.z - 1
        ref = self.at(owner, 0)
        return remote(ref, ref, self.sems, (s - 1) if up else hi + s - 2, spot.line(other))

    def line_here(self, s, up):
        spot, hi = self.spot, self.spot.hi
        owner = spot.z - s if up else spot.z + s
        other = spot.z - 1 if up else spot.z + 1
        ref = self.at(owner, 0)
        return remote(ref, ref, self.sems, (s - 1) if up else hi + s - 2, spot.line(other))

    def first(self):
        self.first_line()
        self.fans.hand_on(self.spot.z, 0)

    def first_line(self):
        spot, hi = self.spot, self.spot.hi

        @pl.when(spot.z < hi - 1)
        def _():
            self.line_copy(1, True).start()

        @pl.when(spot.z > 0)
        def _():
            self.line_copy(1, False).start()

    def onward(self, s):
        spot, hi = self.spot, self.spot.hi

        @pl.when(spot.z >= s)
        def _():
            self.line_here(s, True).wait_recv()

        if s < hi - 1:

            @pl.when(jnp.logical_and(spot.z >= s, spot.z < hi - 1))
            def _():
                self.line_copy(s + 1, True).start()

        @pl.when(spot.z >= s)
        def _():
            self.fans.hand_on(spot.z - s, 0)

        @pl.when(spot.z <= hi - 1 - s)
        def _():
            self.line_here(s, False).wait_recv()

        if s < hi - 1:

            @pl.when(jnp.logical_and(spot.z <= hi - 1 - s, spot.z > 0))
            def _():
                self.line_copy(s + 1, False).start()

        @pl.when(spot.z <= hi - 1 - s)
        def _():
            self.fans.hand_on(spot.z + s, 0)

    def places(self, s, act):
        spot = self.spot
        if s == 0:
            act(spot.z)
            return

        @pl.when(spot.z >= s)
        def _():
            act(spot.z - s)

        @pl.when(spot.z <= spot.hi - 1 - s)
        def _():
            act(spot.z + s)

    def second(self, s):
        self.places(s, self.fans.pass_on)

    def finish(self):
        for s in range(self.spot.hi):
            self.places(s, self.fans.finish)
        self.finish_line()

    def finish_sends(self):
        for s in range(self.spot.hi):
            self.places(s, self.fans.finish_sends)
        self.finish_line()

    def finish_line(self):
        spot, hi = self.spot, self.spot.hi
        for s in range(1, hi):

            @pl.when(jnp.logical_and(spot.z >= s - 1, spot.z < hi - 1))
            def _():
                self.line_copy(s, True).wait_send()

            @pl.when(jnp.logical_and(spot.z <= hi - s, spot.z > 0))
            def _():
                self.line_copy(s, False).wait_send()


def chain_sems(sides, *lead):
    return pltpu.SemaphoreType.DMA(lead + (2, 2 * (LINE - 1) + ((1 << sides) - 1) * LINE))


class Turns:
    def __init__(self, spot, distances, window_of, at, sems, sides):
        self.spot, self.window_of, self.at, self.sems = spot, window_of, at, sems
        self.distances = distances
        self.fans = Fans(spot, at, sems, spot.hi, sides)

    def line_copy(self, distance):
        spot = self.spot
        place = spot.away(distance)
        return remote(self.window_of(place), self.at(spot.z, 0), self.sems, distance, spot.line(place))

    def back(self, distance):
        return lax.rem(self.spot.z - distance + self.spot.hi, self.spot.hi)

    def line_here(self, distance):
        place = self.back(distance)
        ref = self.at(place, 0)
        return remote(ref, ref, self.sems, distance, self.spot.line(place))

    def first(self):
        for distance in self.distances:
            self.start(distance)

    def start(self, distance):
        if distance:
            self.line_copy(distance).start()
        else:
            self.fans.hand_on(self.spot.z, 0)

    def onward(self, distance):
        if distance in self.distances:
            self.line_here(distance).wait_recv()
            self.fans.hand_on(self.back(distance), 0)

    def second(self, distance):
        if distance in self.distances:
            self.fans.pass_on(self.back(distance))

    def finish(self):
        for distance in self.distances:
            self.fans.finish(self.back(distance))
            if distance:
                self.line_copy(distance).wait_send()


LATE = (0, 1, 2, 3)


class FeedTurns:
    def __init__(self, spot, feed, sems, cube):
        def index(place, k):
            return place * spot.inner_size + jnp.bitwise_xor(spot.inner, k)

        self.each = [
            Turns(
                spot,
                LATE,
                lambda place, m=m: feed.at[m, spot.n + place],
                lambda place, k, m=m: feed.at[m, index(place, k)],
                sems.at[m],
                cube,
            )
            for m in range(feed.shape[0])
        ]

    def start(self, distance):
        for turns in self.each:
            turns.start(distance)

    def onward(self, distance):
        for turns in self.each:
            turns.onward(distance)

    def second(self, distance):
        for turns in self.each:
            turns.second(distance)

    def finish(self):
        for turns in self.each:
            turns.finish()


def weights_kernel(
    n, tensor, rec, gates, thin, cot, rec_all, gates_all, thin_all, cot_all,
    rec_sems, gates_sems, thin_sems, cot_sems,
):
    del rec, gates, thin, cot
    spot = Spot(n, tensor)
    hi = spot.hi

    def index(place, k):
        return place * spot.inner_size + jnp.bitwise_xor(spot.inner, k)

    cube = [spot.flip(bit) for bit in spot.bits]
    moves = [
        Chain(spot, lambda place, k: thin_all.at[index(place, k)], thin_sems, cube),
        Chain(spot, lambda place, k: gates_all.at[:, index(place, k)], gates_sems, cube),
        *[
            Chain(
                spot, lambda place, k, m=m: rec_all.at[m, index(place, k)], rec_sems.at[m], cube
            )
            for m in range(rec_all.shape[0])
        ],
        Chain(
            spot,
            lambda place, k: cot_all.at[place, lax.rem(spot.t + k, tensor)],
            cot_sems,
            [spot.cross],
        ),
    ]
    spot.greet(*cube, spot.cross)
    last = moves[-1]
    for move in moves[:-1]:
        move.first()
    last.fans.hand_on(spot.z, 0)
    for s in range(1, hi):
        for move in moves[:-1]:
            move.onward(s)
        if s == 1:
            last.first_line()
        else:
            last.onward(s - 1)
        for move in moves:
            move.second(s - 1)
    last.onward(hi - 1)
    for move in moves:
        move.second(hi - 1)
    for move in moves:
        move.finish()


def turn_sems(grid, count):
    return pltpu.SemaphoreType.DMA((count, 2, grid.n))


def place_kernel(
    unit_tiles, spot, wide_in, gelu_in, out_in, gate, up, down, inlet, forget, thin, cot,
    rec_all, gates_all, thin_all, feed_all, cot_all,
):
    step = pl.program_id(0)
    hi = LINE
    width = feed_all.shape[3]
    tiles = width // LANE

    @pl.when(step == 0)
    def _():
        heads, _, lanes = wide_in.shape
        for m, source in enumerate((wide_in, gelu_in, out_in)):
            for h in range(heads):
                rec_all[m, 0, :, h * lanes : (h + 1) * lanes] = source[h]
        for m, source in enumerate((inlet, forget)):
            for h in range(heads):
                gates_all[m * heads + h, 0] = source[h]
        thin_all[0] = thin[...]
        cot_all[0, 0] = cot[0]

    place = jnp.where(step < hi, step, spot[1])
    tile = jnp.minimum(place * tiles, unit_tiles - tiles)
    for m, source in enumerate((gate, up, down)):
        feed_all[m, 0] = source[:, pl.ds(pl.multiple_of(tile * LANE, LANE), width)]


def place_own(grid, rec, feed, gates, thin, cot):
    n, hi = grid.n, grid.hi
    heads, d_own, lanes = rec[0].shape
    units = feed[0].shape[1]
    unit_tiles = units // LANE
    window = -(-unit_tiles // hi) * LANE
    lane_own, block = gates[0].shape[1:]
    spot = jnp.stack([grid.w, grid.z, grid.t])

    def fixed(a):
        zeros = (0,) * a.ndim
        return pl.BlockSpec(a.shape, lambda i, spot: zeros)

    outs = [
        (3, n, d_own, heads * lanes),
        (2 * heads, n, lane_own, block),
        (n,) + thin.shape,
        (3, n + hi, d_own, window),
        (hi,) + cot.shape,
    ]
    return pl.pallas_call(
        functools.partial(place_kernel, unit_tiles),
        grid_spec=pltpu.PrefetchScalarGridSpec(
            num_scalar_prefetch=1,
            grid=(hi + 1,),
            in_specs=[fixed(a) for a in rec + feed + gates + (thin,)]
            + [pl.BlockSpec((1,) + cot.shape[1:], lambda i, spot: (spot[2], 0, 0))],
            out_specs=[
                pl.BlockSpec((3, 1, d_own, heads * lanes), lambda i, spot: (0, spot[0], 0, 0)),
                pl.BlockSpec((2 * heads, 1, lane_own, block), lambda i, spot: (0, spot[0], 0, 0)),
                pl.BlockSpec((1,) + thin.shape, lambda i, spot: (spot[0], 0, 0)),
                pl.BlockSpec(
                    (3, 1, d_own, window),
                    lambda i, spot: (0, jnp.where(i < hi, n + i, spot[0]), 0, 0),
                ),
                pl.BlockSpec((1, 1) + cot.shape[1:], lambda i, spot: (spot[1], spot[2], 0, 0)),
            ],
        ),
        out_shape=[jax.ShapeDtypeStruct(shape, BF16) for shape in outs],
        compiler_params=pltpu.CompilerParams(vmem_limit_bytes=GRANT),
        name="place",
    )(spot, *rec, *feed, *gates, thin, cot)


def bring_weights(grid, rec, gates, thin, cot):
    n, hi, tensor = grid.n, grid.hi, grid.tensor
    far = pl.BlockSpec(memory_space=pl.ANY)
    arrays = (rec, gates, thin, cot)
    cube = grid.inner_size.bit_length() - 1
    return pl.pallas_call(
        functools.partial(weights_kernel, n, tensor),
        out_shape=[jax.ShapeDtypeStruct(a.shape, a.dtype) for a in arrays],
        in_specs=[far] * len(arrays),
        out_specs=[far] * len(arrays),
        input_output_aliases={i: i for i in range(len(arrays))},
        scratch_shapes=[
            chain_sems(cube, rec.shape[0]),
            chain_sems(cube),
            chain_sems(cube),
            chain_sems(1),
        ],
        compiler_params=pltpu.CompilerParams(
            collective_id=0, has_side_effects=True, vmem_limit_bytes=GRANT
        ),
        name="bring_weights",
    )(*arrays)


def by_rows(rows, step, act):
    def one(i, carry):
        act(pl.ds(pl.multiple_of(i * step, step), step))
        return carry

    lax.fori_loop(0, rows // step, one, 0)


STEP = 16
HALVES = 2


GELU_SLOPE = 0.7978845608028654
GELU_CUBE = 0.044715
HALO = 8
GELU_SHIFT, INPUT_SHIFT, TAPS, CONV_SHIFT, INLET_SHIFT, FORGET_SHIFT, RATE_SOFT, RATE_SIGMOID = 0, 1, 2, 6, 7, 8, 9, 10
LANE_ROWS = 16


def gelu_of(v):
    bent = jnp.tanh(GELU_SLOPE * (v + GELU_CUBE * (v * v * v)))
    half = 0.5 * (1.0 + bent)
    slope = half + 0.5 * v * (1.0 - bent * bent) * (GELU_SLOPE * (1.0 + 3.0 * GELU_CUBE * (v * v)))
    return v * half, slope


def minus_expm1(x):
    series = jnp.ones_like(x)
    for k in range(9, 1, -1):
        series = 1.0 + series * x * (1.0 / k)
    return jnp.where(x > -0.5, -x * series, 1.0 - jnp.exp(x))


def decay_of(forget, soft, starts):
    log_decay = -8.0 * forget * soft
    decay = jnp.where(starts, 0.0, jnp.exp(log_decay))
    scaler = jnp.where(starts, 1.0, jnp.sqrt(minus_expm1(2.0 * log_decay)))
    return decay, scaler


def tile_scan(a, b, state_in, decay_in, reverse):
    place = lax.broadcasted_iota(jnp.int32, a.shape, 0)
    for by in (1, 2, 4):
        turn = 8 - by if reverse else by
        ok = place < 8 - by if reverse else place >= by
        b = jnp.where(ok, a * pltpu.roll(b, turn, 0) + b, b)
        a = jnp.where(ok, a * pltpu.roll(a, turn, 0), a)
    return a * decay_in, b + a * state_in


def scan_rows(seqs, length, width, read, write, reverse):
    tiles = length // 8
    last = 0 if reverse else 7

    def one(i, carry):
        tile = tiles - 1 - i if reverse else i
        after = []
        for s in range(seqs):
            decay_in, state_in = carry[s]
            at = pl.ds(pl.multiple_of(s * length + tile * 8, 8), 8)
            a, b = tile_scan(*read(at), state_in, decay_in, reverse)
            write(at, a, b)
            after.append(
                tuple(jnp.broadcast_to(v[last : last + 1], (8, width)) for v in (a, b))
            )
        return tuple(after)

    start = (jnp.ones((8, width), F32), jnp.zeros((8, width), F32))
    lax.fori_loop(0, tiles, one, (start,) * seqs)


def first_kernel(x, input_low, gelu_low, w_input, w_gelu, scale, part, gained):
    value = dot_nt(input_low[...], w_input[0]) + dot_nt(gelu_low[...], w_gelu[0])
    part[...] = value.astype(BF16)
    gained[...] = jnp.sum(
        (value * x[...].astype(F32) * scale[:, 0:1]).reshape(-1, 8, value.shape[1]), axis=0
    )


def first_gradient(x, input_low, gelu_low, rec, scale):
    rows, d = x.shape
    channels = input_low.shape[1]
    chunk = 512

    def fixed(a):
        return pl.BlockSpec(a.shape, lambda i: (0, 0))

    def weight(k):
        return pl.BlockSpec((1, chunk, channels), lambda i: (k, i, 0))

    column = pl.BlockSpec((rows, chunk), lambda i: (0, i))
    return pl.pallas_call(
        first_kernel,
        grid=(d // chunk,),
        out_shape=[jax.ShapeDtypeStruct((rows, d), BF16), jax.ShapeDtypeStruct((8, d), F32)],
        in_specs=[column, fixed(input_low), fixed(gelu_low), weight(0), weight(1), fixed(scale)],
        out_specs=[column, pl.BlockSpec((8, chunk), lambda i: (0, i))],
        compiler_params=pltpu.CompilerParams(vmem_limit_bytes=GRANT),
        name="first_gradient",
    )(x, input_low, gelu_low, rec, rec, scale)


class Prefix:
    def __init__(self, spot, seqs, reverse, tots, gots, line, cube_sems, line_sems):
        self.spot, self.seqs, self.reverse = spot, seqs, reverse
        self.tots, self.gots, self.line = tots, gots, line
        self.cube_sems, self.line_sems = cube_sems, line_sems

    def line_copy(self, place, sender):
        stages = len(self.spot.bits)
        return pltpu.make_async_remote_copy(
            src_ref=self.tots.at[stages],
            dst_ref=self.line.at[sender],
            send_sem=self.line_sems.at[0, place],
            recv_sem=self.line_sems.at[1, sender],
            device_id=self.spot.line(place),
            device_id_type=MESH,
        )

    def run(self):
        spot, seqs, hi = self.spot, self.seqs, self.spot.hi
        a, b = slice(0, seqs), slice(seqs, 2 * seqs)
        width = self.tots.shape[2]
        enter_a, enter_b = jnp.ones((seqs, width), F32), jnp.zeros((seqs, width), F32)
        for stage, bit in enumerate(spot.bits):
            copy = remote(
                self.tots.at[stage], self.gots.at[stage], self.cube_sems, stage, spot.flip(bit)
            )
            copy.start()
            copy.wait()
            mine_a, mine_b = self.tots[stage, a, :], self.tots[stage, b, :]
            got_a, got_b = self.gots[stage, a, :], self.gots[stage, b, :]
            after = spot.bit(bit) == (0 if self.reverse else 1)
            enter_b = jnp.where(after, enter_a * got_b + enter_b, enter_b)
            enter_a = jnp.where(after, enter_a * got_a, enter_a)
            self.tots[stage + 1, a, :] = mine_a * got_a
            self.tots[stage + 1, b, :] = jnp.where(
                after, mine_a * got_b + mine_b, got_a * mine_b + got_b
            )
            self.tots[stage + 1, 2 * seqs :, :] = jnp.zeros((8 - 2 * seqs, width), F32)
        for distance in range(1, hi):
            self.line_copy(spot.away(distance), spot.z).start()
        for distance in range(1, hi):
            place = spot.away(distance)
            self.line_copy(place, place).wait_recv()
            self.line_copy(place, spot.z).wait_send()
        come = jnp.zeros((seqs, width), F32)
        for place in reversed(range(hi)) if self.reverse else range(hi):
            before = spot.z < place if self.reverse else spot.z > place
            come = jnp.where(before, self.line[place, a, :] * come + self.line[place, b, :], come)
        return enter_a * come + enter_b


def prefix_scratch(grid, channels):
    stages = grid.inner_size.bit_length() - 1
    return [
        pltpu.VMEM((stages + 1, 8, channels), F32),
        pltpu.VMEM((stages, 8, channels), F32),
        pltpu.VMEM((grid.hi, 8, channels), F32),
        pltpu.SemaphoreType.DMA((2, stages)),
        pltpu.SemaphoreType.DMA((2, grid.hi)),
    ]


def forward_kernel(
    n, tensor, seqs, heads,
    x, halo, gain, w_input, w_gelu, w_inlet, w_forget, lanes, flags, w_out, shift, gain_second, feed,
    normed, ext, conv, gelu_pre, inlet_pre, forget_pre, cum, local, entered, mixed, resid, second,
    feed_all,
    held, factor, addend, part, out, got, tots, gots, line, cube_sems, line_sems, swap_sems, feed_sems,
):
    del feed
    spot = Spot(n, tensor)
    hi = spot.hi
    rows = x.shape[0]
    length = rows // seqs
    width = conv.shape[1]
    step = pl.program_id(0)
    cube = [spot.flip(bit) for bit in spot.bits]
    turns = FeedTurns(spot, feed_all, feed_sems, cube)
    @pl.when(step == 0)
    def _():
        spot.greet(*cube, spot.cross)
        turns.start(1)
        turns.start(0)

        def norm(source, at, to):
            value = source[at, :].astype(F32)
            scale = lax.rsqrt(jnp.mean(value * value, axis=-1, keepdims=True) + 1e-06)
            value = (value * scale * gain[...]).astype(BF16)
            held[pl.ds(pl.multiple_of(at.start + to, STEP), STEP), :] = value
            return value

        def main(at):
            normed[at, :] = norm(x, at, 0)

        by_rows(rows, STEP, main)
        by_rows(halo.shape[0], STEP, lambda at: norm(halo, at, rows))

    @pl.when(step < heads)
    def _():
        table = lanes[...]
        cols = pl.ds(pl.multiple_of(step * width, width), width)

        def row(i):
            return table[i : i + 1]

        branch = (dot(held[...], w_input[0]) + row(INPUT_SHIFT)).astype(BF16)
        gelu_pre[:, cols] = dot(held[0:rows, :], w_gelu[0]) + row(GELU_SHIFT)
        for s in range(seqs):
            here = slice(s * length, (s + 1) * length)
            front = rows + s * HALO
            longer = jnp.concatenate(
                [branch[front : front + HALO].astype(F32), branch[here].astype(F32)], axis=0
            )
            ext[s] = longer.astype(BF16)
            total = row(CONV_SHIFT) + row(TAPS) * longer[HALO:]
            for k in range(1, CONV):
                moved = pltpu.roll(longer, k, 0)[HALO:]
                total = total + jnp.where(flags[here, k : k + 1] > 0.5, row(TAPS + k) * moved, 0.0)
            conv[here, :] = total.astype(BF16)
        blocks = conv[...]
        inlet_pre[...] = dot(blocks, w_inlet[0]) + row(INLET_SHIFT)
        forget_pre[...] = dot(blocks, w_forget[0]) + row(FORGET_SHIFT)

        def terms(at):
            starts = flags[at, 0:1] > 0.5
            decay, scaler = decay_of(jax.nn.sigmoid(forget_pre[at, :]), row(RATE_SOFT), starts)
            factor[at, :] = decay
            addend[at, :] = scaler * jax.nn.sigmoid(inlet_pre[at, :]) * conv[at, :].astype(F32)

        by_rows(rows, 32, terms)

        def write(at, a, b):
            cum[at, cols] = a
            local[at, cols] = b

        scan_rows(seqs, length, width, lambda at: (factor[at, :], addend[at, :]), write, False)

    @pl.when(step == heads)
    def _():
        tots[0] = jnp.zeros_like(tots[0])
        for s in range(seqs):
            tots[0, s : s + 1, :] = cum[(s + 1) * length - 8 : (s + 1) * length, :][7:8]
            tots[0, seqs + s : seqs + s + 1, :] = local[(s + 1) * length - 8 : (s + 1) * length, :][7:8]
        enter = Prefix(spot, seqs, False, tots, gots, line, cube_sems, line_sems).run()
        turns.start(3)
        turns.onward(1)
        entered[...] = jnp.zeros_like(entered)
        entered[0:seqs, :] = enter
        for s in range(seqs):

            def mix(at, s=s):
                here = pl.ds(pl.multiple_of(s * length + at.start, STEP), STEP)
                state = local[here, :] + cum[here, :] * enter[s : s + 1]
                mixed[here, :] = (state * gelu_of(gelu_pre[here, :])[0]).astype(BF16)

            by_rows(length, STEP, mix)
        turns.start(2)
        values = mixed[...]
        own_rows = resid.shape[0]

        def branch(j, carry):
            at = pl.ds(pl.multiple_of(j * 256, 256), 256)
            value = dot_nt(values, w_out[0, at, :])
            for side in range(tensor):
                part[side, :, at] = value[side * own_rows : (side + 1) * own_rows]
            return carry

        lax.fori_loop(0, x.shape[1] // 256, branch, 0)

        def put(at):
            out[at, :] = part[1 - spot.t, at, :].astype(BF16)

        by_rows(own_rows, STEP, put)
        copy = remote(out, got, swap_sems, 0, spot.cross)
        copy.start()
        copy.wait()

        def norm(at):
            own = x[pl.ds(pl.multiple_of(spot.t * own_rows + at.start, STEP), STEP), :].astype(F32)
            value = own + (part[spot.t, at, :] + got[at, :].astype(F32) + shift[...])
            resid[at, :] = value
            scale = lax.rsqrt(jnp.mean(value * value, axis=-1, keepdims=True) + 1e-06)
            second[at, :] = (value * scale * gain_second[...]).astype(BF16)

        by_rows(own_rows, STEP, norm)
        turns.second(0)
        turns.onward(3)
        turns.second(1)
        turns.onward(2)
        turns.second(3)
        turns.second(2)
        turns.finish()


def forward_recurrence(
    grid, x, halo, gain, rec, inlet, forget, lanes, flags, shift, gain_second, feed, seqs
):
    rows, d = x.shape
    heads, width = inlet.shape[:2]
    channels = heads * width
    longer = rows // seqs + HALO
    own_rows = rows // grid.tensor

    def head_of(i):
        return jnp.minimum(i, heads - 1)

    def fixed(a):
        zeros = (0,) * len(a.shape)
        return pl.BlockSpec(a.shape, lambda i: zeros, pipeline_mode=pl.Buffered(1))

    def column(count):
        return pl.BlockSpec((count, width), lambda i: (0, head_of(i)))

    def weight(k):
        return pl.BlockSpec((1, d, width), lambda i: (k, 0, head_of(i)))

    head = pl.BlockSpec((1, width, width), lambda i: (head_of(i), 0, 0))
    far = pl.BlockSpec(memory_space=pl.ANY)
    wide = jax.ShapeDtypeStruct((rows, channels), F32)
    outs = [
        jax.ShapeDtypeStruct((rows, d), BF16),
        jax.ShapeDtypeStruct((seqs, longer, channels), BF16),
        jax.ShapeDtypeStruct((rows, channels), BF16),
        wide,
        wide,
        wide,
        wide,
        wide,
        jax.ShapeDtypeStruct((8, channels), F32),
        jax.ShapeDtypeStruct((rows, channels), BF16),
        jax.ShapeDtypeStruct((own_rows, d), F32),
        jax.ShapeDtypeStruct((own_rows, d), BF16),
        jax.ShapeDtypeStruct(feed.shape, BF16),
    ]
    return pl.pallas_call(
        functools.partial(forward_kernel, grid.n, grid.tensor, seqs, heads),
        grid=(heads + 1,),
        out_shape=outs,
        in_specs=[fixed(x), fixed(halo), fixed(gain), weight(0), weight(1), head, head]
        + [column(LANE_ROWS), fixed(flags)]
        + [pl.BlockSpec((1, d, channels), lambda i: (2, 0, 0), pipeline_mode=pl.Buffered(1))]
        + [fixed(shift), fixed(gain_second), far],
        out_specs=[
            fixed(outs[0]),
            pl.BlockSpec((seqs, longer, width), lambda i: (0, 0, head_of(i))),
            column(rows),
            fixed(wide),
            column(rows),
            column(rows),
        ]
        + [fixed(a) for a in outs[6:12]]
        + [far],
        input_output_aliases={12: 12},
        scratch_shapes=[
            pltpu.VMEM((rows + halo.shape[0], d), BF16),
            pltpu.VMEM((rows, width), F32),
            pltpu.VMEM((rows, width), F32),
            pltpu.VMEM((grid.tensor, own_rows, d), F32),
            pltpu.VMEM((own_rows, d), BF16),
            pltpu.VMEM((own_rows, d), BF16),
        ]
        + prefix_scratch(grid, channels)
        + [pltpu.SemaphoreType.DMA((2, 1)), turn_sems(grid, feed.shape[0])],
        compiler_params=pltpu.CompilerParams(
            collective_id=1, has_side_effects=True, vmem_limit_bytes=GRANT
        ),
        name="forward_recurrence",
    )(x, halo, gain, rec, rec, inlet, forget, lanes, flags, rec, shift, gain_second, feed)


def place_feed_kernel(unit_tiles, spot, gate, up, down, cot, feed_all, cot_all):
    step = pl.program_id(0)
    width = feed_all.shape[3]
    tiles = width // LANE

    @pl.when(step == 0)
    def _():
        cot_all[0, 0] = cot[0]

    place = jnp.where(step < LINE, step, spot[1])
    tile = jnp.minimum(place * tiles, unit_tiles - tiles)
    for m, source in enumerate((gate, up, down)):
        feed_all[m, 0] = source[:, pl.ds(pl.multiple_of(tile * LANE, LANE), width)]


def place_feed(grid, feed, cot):
    n, hi = grid.n, grid.hi
    d_own, units = feed[0].shape
    unit_tiles = units // LANE
    window = -(-unit_tiles // hi) * LANE
    spot = jnp.stack([grid.w, grid.z, grid.t])
    outs = [(3, n + hi, d_own, window), (hi,) + cot.shape]
    return pl.pallas_call(
        functools.partial(place_feed_kernel, unit_tiles),
        grid_spec=pltpu.PrefetchScalarGridSpec(
            num_scalar_prefetch=1,
            grid=(hi + 1,),
            in_specs=[pl.BlockSpec(a.shape, lambda i, spot: (0, 0)) for a in feed]
            + [pl.BlockSpec((1,) + cot.shape[1:], lambda i, spot: (spot[2], 0, 0))],
            out_specs=[
                pl.BlockSpec(
                    (3, 1, d_own, window),
                    lambda i, spot: (0, jnp.where(i < hi, n + i, spot[0]), 0, 0),
                ),
                pl.BlockSpec((1, 1) + cot.shape[1:], lambda i, spot: (spot[1], spot[2], 0, 0)),
            ],
        ),
        out_shape=[jax.ShapeDtypeStruct(shape, BF16) for shape in outs],
        compiler_params=pltpu.CompilerParams(vmem_limit_bytes=GRANT),
        name="place",
    )(spot, *feed, cot)


def gather_kernel(
    n, tensor, seqs, thin_lanes,
    x, halo, flags, wide_in, gelu_in, out_in, inlet_in, forget_in, thin_in, feed, cot,
    normed, ext, conv, gelu_pre, inlet_pre, forget_pre, cum, local, entered, mixed, resid, second,
    lanes, table, gates_out, rec_out, feed_all, cot_all,
    rec, gates, thin, held, factor, addend, part, out, got, tots, gots, line,
    rec_sems, gates_sems, thin_sems, feed_sems, cot_sems, cube_sems, line_sems, swap_sems, own_sem,
):
    del feed, cot
    spot = Spot(n, tensor)
    hi = spot.hi
    rows, d = x.shape
    length = rows // seqs
    heads, d_own, width = wide_in.shape
    cube = [spot.flip(bit) for bit in spot.bits]

    def index(place, k):
        return place * spot.inner_size + jnp.bitwise_xor(spot.inner, k)

    chains = [
        Chain(spot, lambda place, k: thin.at[index(place, k)], thin_sems, cube),
        Chain(spot, lambda place, k: gates.at[:, index(place, k)], gates_sems, cube),
    ] + [
        Chain(spot, lambda place, k, m=m: rec.at[m, index(place, k)], rec_sems.at[m], cube)
        for m in range(3)
    ]
    turns = FeedTurns(spot, feed_all, feed_sems, cube)
    cots = Chain(
        spot,
        lambda place, k: cot_all.at[place, lax.rem(spot.t + k, tensor)],
        cot_sems,
        [spot.cross],
    )
    for m, source in enumerate((wide_in, gelu_in, out_in)):
        for h in range(heads):
            rec[m, spot.w, :, h * width : (h + 1) * width] = source[h]
    for m, source in enumerate((inlet_in, forget_in)):
        for h in range(heads):
            gates[m * heads + h, spot.w] = source[h]
    thin[spot.w] = thin_in[...]
    spot.greet(*cube, spot.cross)
    for chain in chains:
        chain.first()
    cots.fans.hand_on(spot.z, 0)
    for s in range(1, hi):
        for chain in chains:
            chain.onward(s)
        if s == 1:
            cots.first_line()
        else:
            cots.onward(s - 1)
        for chain in chains:
            chain.second(s - 1)
    turns.start(1)
    for chain in chains:
        chain.second(hi - 1)
    for chain in chains:
        chain.finish()
    turns.start(0)
    keep = pltpu.make_async_copy(rec, rec_out, own_sem)
    keep.start()

    sums = thin[0].astype(F32)
    for i in range(1, n):
        sums = sums + thin[i].astype(F32)
    table[...] = sums
    rate = sums[RATE_SOFT : RATE_SOFT + 1]
    lanes[0:RATE_SOFT, :] = sums[0:RATE_SOFT]
    soft = jnp.maximum(rate, 0.0) + jnp.log1p(jnp.exp(-jnp.abs(rate)))
    lanes[RATE_SOFT : RATE_SOFT + 1, :] = soft
    lanes[RATE_SIGMOID : RATE_SIGMOID + 1, :] = jax.nn.sigmoid(rate)
    lanes[RATE_SIGMOID + 1 :, :] = jnp.zeros((LANE_ROWS - RATE_SIGMOID - 1, sums.shape[1]), F32)
    per = d // sums.shape[1]

    def across(i):
        first = thin_lanes + i * per
        return jnp.concatenate([sums[first + j : first + j + 1] for j in range(per)], axis=1)

    gain, shift, gain_second = across(0), across(1), across(2)

    def norm_first(source, at, to):
        value = source[at, :].astype(F32)
        scale = lax.rsqrt(jnp.mean(value * value, axis=-1, keepdims=True) + 1e-06)
        value = (value * scale * gain).astype(BF16)
        held[pl.ds(pl.multiple_of(at.start + to, STEP), STEP), :] = value
        return value

    def main(at):
        normed[at, :] = norm_first(x, at, 0)

    by_rows(rows, STEP, main)
    by_rows(halo.shape[0], STEP, lambda at: norm_first(halo, at, rows))

    def work(step, none):
        cols = pl.ds(pl.multiple_of(step * width, width), width)

        def row(i):
            return lanes[i : i + 1, cols]

        def matrix(m):
            return rec[m, :, :, cols].reshape(d, width)

        branch = (dot(held[...], matrix(0)) + row(INPUT_SHIFT)).astype(BF16)
        gelu_pre[:, cols] = dot(held[0:rows, :], matrix(1)) + row(GELU_SHIFT)
        for s in range(seqs):
            here = slice(s * length, (s + 1) * length)
            front = rows + s * HALO
            longer = jnp.concatenate(
                [branch[front : front + HALO].astype(F32), branch[here].astype(F32)], axis=0
            )
            ext[s, :, cols] = longer.astype(BF16)
            total = row(CONV_SHIFT) + row(TAPS) * longer[HALO:]
            for k in range(1, CONV):
                moved = pltpu.roll(longer, k, 0)[HALO:]
                total = total + jnp.where(flags[here, k : k + 1] > 0.5, row(TAPS + k) * moved, 0.0)
            conv[here, cols] = total.astype(BF16)
        blocks = conv[:, cols]
        for m, (to, bias) in enumerate(((inlet_pre, INLET_SHIFT), (forget_pre, FORGET_SHIFT))):
            gate = gates[m * heads + step].reshape(width, width)
            gates_out[m * heads + step] = gate
            to[:, cols] = dot(blocks, gate) + row(bias)

        def terms(at):
            starts = flags[at, 0:1] > 0.5
            decay, scaler = decay_of(jax.nn.sigmoid(forget_pre[at, cols]), row(RATE_SOFT), starts)
            factor[at, :] = decay
            addend[at, :] = scaler * jax.nn.sigmoid(inlet_pre[at, cols]) * conv[at, cols].astype(F32)

        by_rows(rows, 32, terms)

        def write(at, a, b):
            cum[at, cols] = a
            local[at, cols] = b

        scan_rows(seqs, length, width, lambda at: (factor[at, :], addend[at, :]), write, False)
        return none

    lax.fori_loop(0, heads, work, 0)
    tots[0] = jnp.zeros_like(tots[0])
    for s in range(seqs):
        tots[0, s : s + 1, :] = cum[(s + 1) * length - 8 : (s + 1) * length, :][7:8]
        tots[0, seqs + s : seqs + s + 1, :] = local[(s + 1) * length - 8 : (s + 1) * length, :][7:8]
    enter = Prefix(spot, seqs, False, tots, gots, line, cube_sems, line_sems).run()
    turns.start(3)
    turns.onward(1)
    cots.onward(3)
    turns.start(2)
    entered[...] = jnp.zeros_like(entered)
    entered[0:seqs, :] = enter
    for s in range(seqs):

        def mix(at, s=s):
            here = pl.ds(pl.multiple_of(s * length + at.start, STEP), STEP)
            state = local[here, :] + cum[here, :] * enter[s : s + 1]
            mixed[here, :] = (state * gelu_of(gelu_pre[here, :])[0]).astype(BF16)

        by_rows(length, STEP, mix)
    values = mixed[...]
    own_rows = resid.shape[0]
    each, slab = n // hi, d // hi

    def branch(j, none):
        at = pl.ds(pl.multiple_of(j * slab, LANE), slab)
        weights = rec[2, pl.ds(j * each, each)].reshape(slab, heads * width)
        value = dot_nt(values, weights)
        for side in range(tensor):
            part[side, :, at] = value[side * own_rows : (side + 1) * own_rows]
        return none

    lax.fori_loop(0, hi, branch, 0)

    def put(at):
        out[at, :] = part[1 - spot.t, at, :].astype(BF16)

    by_rows(own_rows, STEP, put)
    copy = remote(out, got, swap_sems, 0, spot.cross)
    copy.start()
    copy.wait()

    def norm(at):
        own = x[pl.ds(pl.multiple_of(spot.t * own_rows + at.start, STEP), STEP), :].astype(F32)
        value = own + (part[spot.t, at, :] + got[at, :].astype(F32) + shift)
        resid[at, :] = value
        scale = lax.rsqrt(jnp.mean(value * value, axis=-1, keepdims=True) + 1e-06)
        second[at, :] = (value * scale * gain_second).astype(BF16)

    by_rows(own_rows, STEP, norm)
    turns.onward(3)
    turns.second(0)
    turns.second(1)
    turns.onward(2)
    turns.second(3)
    turns.second(2)
    turns.finish()
    cots.finish()
    keep.wait()


def gather_recurrence(grid, x, halo, flags, rec, gates, thin, thin_lanes, feed, cot, seqs):
    rows, d = x.shape
    heads, d_own, width = rec[0].shape
    lane_own = gates[0].shape[1]
    n = grid.n
    channels = heads * width
    longer = rows // seqs + HALO
    own_rows = rows // grid.tensor
    near = pl.BlockSpec(memory_space=pltpu.VMEM)
    far = pl.BlockSpec(memory_space=pl.ANY)
    wide = jax.ShapeDtypeStruct((rows, channels), F32)
    whole = (3, n, d_own, channels)
    cube = grid.inner_size.bit_length() - 1
    outs = [
        jax.ShapeDtypeStruct((rows, d), BF16),
        jax.ShapeDtypeStruct((seqs, longer, channels), BF16),
        jax.ShapeDtypeStruct((rows, channels), BF16),
        wide,
        wide,
        wide,
        wide,
        wide,
        jax.ShapeDtypeStruct((8, channels), F32),
        jax.ShapeDtypeStruct((rows, channels), BF16),
        jax.ShapeDtypeStruct((own_rows, d), F32),
        jax.ShapeDtypeStruct((own_rows, d), BF16),
        jax.ShapeDtypeStruct((LANE_ROWS, channels), F32),
        jax.ShapeDtypeStruct(thin.shape, F32),
        jax.ShapeDtypeStruct((2 * heads, width, width), BF16),
        jax.ShapeDtypeStruct(whole, BF16),
        jax.ShapeDtypeStruct(feed.shape, BF16),
        jax.ShapeDtypeStruct(cot.shape, BF16),
    ]
    return pl.pallas_call(
        functools.partial(gather_kernel, n, grid.tensor, seqs, thin_lanes),
        out_shape=outs,
        in_specs=[near] * 9 + [far] * 2,
        out_specs=[near] * 15 + [far] * 3,
        input_output_aliases={9: 16, 10: 17},
        scratch_shapes=[
            pltpu.VMEM(whole, BF16),
            pltpu.VMEM((2 * heads, n, lane_own, width), BF16),
            pltpu.VMEM((n,) + thin.shape, BF16),
            pltpu.VMEM((rows + halo.shape[0], d), BF16),
            pltpu.VMEM((rows, width), F32),
            pltpu.VMEM((rows, width), F32),
            pltpu.VMEM((grid.tensor, own_rows, d), F32),
            pltpu.VMEM((own_rows, d), BF16),
            pltpu.VMEM((own_rows, d), BF16),
        ]
        + prefix_scratch(grid, channels)[:3]
        + [
            chain_sems(cube, 3),
            chain_sems(cube),
            chain_sems(cube),
            turn_sems(grid, feed.shape[0]),
            chain_sems(1),
        ]
        + prefix_scratch(grid, channels)[3:]
        + [pltpu.SemaphoreType.DMA((2, 1)), pltpu.SemaphoreType.DMA],
        compiler_params=pltpu.CompilerParams(
            collective_id=6, has_side_effects=True, vmem_limit_bytes=GRANT
        ),
        name="gather_recurrence",
    )(x, halo, flags, *rec, *gates, thin, feed, cot)


def leave_kernel(
    n, tensor, seqs, branch, w_out, gelu_pre, local, cum, inlet_pre, forget_pre, conv, ext, entered,
    w_inlet, w_forget, lanes, flags, feed_part, resid,
    gelu_low, input_low, gate_grads, lane_grads, shift_grad, own_out,
    tail, carried, factor, addend, back, rim, tots, gots, line, cube_sems, line_sems, rim_sems,
    part, sums_got, sums_line, sums_cross, sums_sems,
):
    spot = Spot(n, tensor)
    every, channels = conv.shape
    length = every // seqs
    heads, width = w_inlet.shape[:2]
    behind = {"wide": lax.rem(spot.w + n - 1, n)}
    ahead = {"wide": lax.rem(spot.w + 1, n)}
    spot.greet(*[spot.flip(bit) for bit in spot.bits], behind, ahead, spot.cross)
    for place in range(spot.hi):
        for side in range(tensor):

            def put(at, place=place, side=side):
                part[place, side, at, :] = feed_part[place, side, at, :]

            by_rows(resid.shape[0], STEP, put)
    half = resid.shape[0] // HALVES
    sums = [
        Rows(spot, part, sums_got, sums_line, sums_cross.at[i], sums_sems.at[i], i * half, half)
        for i in range(HALVES)
    ]
    for k in range(spot.hi):
        for each in sums:
            each.start(k)
    tots[0] = jnp.zeros_like(tots[0])
    lane_grads[...] = jnp.zeros_like(lane_grads)
    shift_grad[...] = jnp.zeros_like(shift_grad)

    def add(at):
        shift_grad[...] += jnp.sum(branch[at, :].astype(F32).reshape(2, 8, -1), axis=0)

    by_rows(every, STEP, add)

    def decays(at, cols):
        soft = lanes[RATE_SOFT : RATE_SOFT + 1, cols]
        return decay_of(jax.nn.sigmoid(forget_pre[at, cols]), soft, flags[at, 0:1] > 0.5)

    def upward(h, none):
        cols = pl.ds(pl.multiple_of(h * width, width), width)
        grad = dot(branch[...], w_out[0, :, cols])
        gelu, slope = gelu_of(gelu_pre[:, cols])
        for s in range(seqs):
            here = slice(s * length, (s + 1) * length)
            state = local[here, cols] + cum[here, cols] * entered[s : s + 1, cols]
            low = (grad[here] * state * slope[here]).astype(BF16)
            gelu_low[here, cols] = low
            lane_grads[0:1, cols] += jnp.sum(low.astype(F32), axis=0, keepdims=True)
            decay, _ = decays(here, cols)
            place = lax.broadcasted_iota(jnp.int32, (length, width), 0)
            factor[here, :] = jnp.where(place < length - 1, pltpu.roll(decay, length - 1, 0), 1.0)
        addend[...] = grad * gelu

        def write(at, a, b):
            tail[at, cols] = a
            carried[at, cols] = b

        scan_rows(seqs, length, width, lambda at: (factor[at, :], addend[at, :]), write, True)
        for s in range(seqs):
            first = slice(s * length, s * length + 8)
            decay, _ = decays(first, cols)
            tots[0, s : s + 1, cols] = decay[0:1] * tail[first, cols][0:1]
            tots[0, seqs + s : seqs + s + 1, cols] = decay[0:1] * carried[first, cols][0:1]
        return none

    lax.fori_loop(0, heads // 2, upward, 0)
    for each in sums:
        each.along(1)
    lax.fori_loop(heads // 2, heads, upward, 0)
    come = Prefix(spot, seqs, True, tots, gots, line, cube_sems, line_sems).run()
    for each in sums:
        each.along(2)
    tots[0, 0:seqs, :] = come

    def downward(h, none):
        cols = pl.ds(pl.multiple_of(h * width, width), width)

        def row(i):
            return lanes[i : i + 1, cols]

        sums = []
        for s in range(seqs):
            here = slice(s * length, (s + 1) * length)
            place = lax.broadcasted_iota(jnp.int32, (length, width), 0)
            starts = flags[here, 0:1] > 0.5
            blocks = conv[here, cols].astype(F32)
            enter = entered[s : s + 1, cols]
            state = local[here, cols] + cum[here, cols] * enter
            before = jnp.where(place > 0, pltpu.roll(state, 1, 0), enter)
            carry = carried[here, cols] + tail[here, cols] * tots[0, s : s + 1, cols]
            inlet = jax.nn.sigmoid(inlet_pre[here, cols])
            forget = jax.nn.sigmoid(forget_pre[here, cols])
            soft = row(RATE_SOFT)
            decay, scaler = decay_of(forget, soft, starts)
            log_grad = jnp.where(
                starts, 0.0, carry * before * decay - carry * inlet * blocks * (decay * decay) / scaler
            )
            rate_grad = jnp.sum(log_grad * (-8.0 * forget), axis=0, keepdims=True) * row(RATE_SIGMOID)
            inlet_low = (carry * scaler * blocks * (inlet * (1.0 - inlet))).astype(BF16)
            forget_low = (log_grad * (-8.0 * soft) * (forget * (1.0 - forget))).astype(BF16)
            conv_grad = (
                carry * scaler * inlet
                + dot_nt(inlet_low, w_inlet[h])
                + dot_nt(forget_low, w_forget[h])
            )
            longer = ext[s, :, cols].astype(F32)
            zeros = jnp.zeros((HALO, width), F32)
            total = jnp.concatenate([zeros, row(TAPS) * conv_grad], axis=0)
            taps = [jnp.sum(conv_grad * longer[HALO:], axis=0, keepdims=True)]
            for k in range(1, CONV):
                masked = jnp.where(flags[here, k : k + 1] > 0.5, conv_grad, 0.0)
                moved = pltpu.roll(longer, k, 0)[HALO:]
                taps.append(jnp.sum(masked * moved, axis=0, keepdims=True))
                sent = jnp.concatenate([zeros, row(TAPS + k) * masked], axis=0)
                total = total + pltpu.roll(sent, HALO + length - k, 0)
            back[s, :, cols] = total
            lows = [jnp.sum(v.astype(F32), axis=0, keepdims=True) for v in (inlet_low, forget_low)]
            sums.append(taps + [jnp.sum(conv_grad, axis=0, keepdims=True)] + lows + [rate_grad])
            for m, low in enumerate((inlet_low, forget_low)):
                factor[here, :] = low.astype(F32) if m == 0 else factor[here, :]
                addend[here, :] = low.astype(F32) if m == 1 else addend[here, :]
        for i in range(len(sums[0])):
            lane_grads[2 + i : 3 + i, cols] = sum(each[i] for each in sums[1:]) + sums[0][i]
        for m, low in enumerate((factor, addend)):
            gate_grads[m, h] = dot_tn(conv[:, cols], low[...].astype(BF16)).astype(BF16)
        return none

    lax.fori_loop(0, heads, downward, 0)
    copy = remote(back.at[:, 0:HALO, :], rim, rim_sems, 0, behind)
    copy.start()
    for s in range(3, spot.hi):
        for each in sums:
            each.along(s)
    copy.wait()

    def give(h, none):
        cols = pl.ds(pl.multiple_of(h * width, width), width)
        total = jnp.zeros((1, width), F32)
        for s in range(seqs):
            edge = jnp.where(spot.w < n - 1, rim[s, :, cols], 0.0)
            value = back[s, HALO:, cols]
            value = jnp.concatenate([value[: length - HALO], value[length - HALO :] + edge], axis=0)
            low = value.astype(BF16)
            input_low[s * length : (s + 1) * length, cols] = low
            total = total + jnp.sum(low.astype(F32), axis=0, keepdims=True)
        lane_grads[1:2, cols] = total
        return none

    lax.fori_loop(0, heads, give, 0)

    def done(at, total):
        own_out[at, :] = (resid[at, :] + total).astype(BF16)

    for each in sums:
        each.end(done)
    for each in sums:
        each.finish()


def leave_recurrence(
    grid, branch, rec, gelu_pre, local, cum, inlet_pre, forget_pre, conv, ext, entered, gates, lanes,
    flags, feed_part, resid, seqs,
):
    every, channels = conv.shape
    d = branch.shape[1]
    heads, width = gates.shape[0] // 2, gates.shape[1]
    near = pl.BlockSpec(memory_space=pltpu.VMEM)
    low = jax.ShapeDtypeStruct((every, channels), BF16)
    return pl.pallas_call(
        functools.partial(leave_kernel, grid.n, grid.tensor, seqs),
        grid=(1,),
        out_shape=[
            low,
            low,
            jax.ShapeDtypeStruct((2, heads, width, width), BF16),
            jax.ShapeDtypeStruct((LANE_ROWS, channels), F32),
            jax.ShapeDtypeStruct((8, d), F32),
            jax.ShapeDtypeStruct(resid.shape, BF16),
        ],
        in_specs=[near, pl.BlockSpec((1, d, channels), lambda i: (2, 0, 0))]
        + [near] * 8
        + [pl.BlockSpec((heads, width, width), lambda i, m=m: (m, 0, 0)) for m in range(2)]
        + [near] * 4,
        out_specs=[near] * 6,
        scratch_shapes=[
            pltpu.VMEM((every, channels), F32),
            pltpu.VMEM((every, channels), F32),
            pltpu.VMEM((every, width), F32),
            pltpu.VMEM((every, width), F32),
            pltpu.VMEM((seqs, every // seqs + HALO, channels), F32),
            pltpu.VMEM((seqs, HALO, channels), F32),
        ]
        + prefix_scratch(grid, channels)
        + [pltpu.SemaphoreType.DMA((2, 1)), pltpu.VMEM(feed_part.shape, BF16)]
        + rows_scratch(grid, *resid.shape)[:2]
        + rows_sems(grid)[:2],
        compiler_params=pltpu.CompilerParams(
            collective_id=5, has_side_effects=True, vmem_limit_bytes=GRANT
        ),
        name="leave_recurrence",
    )(
        branch, rec, gelu_pre, local, cum, inlet_pre, forget_pre, conv, ext, entered, gates, gates,
        lanes, flags, feed_part, resid,
    )


class Rows:
    def __init__(self, spot, part, got, line, cross_sems, line_sems, first, rows):
        self.spot, self.part, self.got, self.line = spot, part, got, line
        self.cross_sems, self.line_sems = cross_sems, line_sems
        self.first, self.rows = first, rows
        self.span = pl.ds(first, rows)

    def by_rows(self, act):
        def one(at):
            act(pl.ds(pl.multiple_of(self.first + at.start, STEP), STEP))

        by_rows(self.rows, STEP, one)

    def place(self, k):
        spot, hi = self.spot, self.spot.hi
        last = hi - 1
        flipped = jnp.where(spot.z * 2 < hi, 0, 1)
        z = spot.z + flipped * (last - 2 * spot.z)
        if k == last:
            place = z
        else:
            place = jnp.where(k < last - z, last - k, k - (last - z))
        return place + flipped * (last - 2 * place)

    def cross_copy(self, place):
        spot = self.spot
        return remote(
            self.part.at[place, 1 - spot.t, self.span],
            self.got.at[place, self.span],
            self.cross_sems,
            place,
            spot.cross,
        )

    def start(self, k):
        self.cross_copy(self.place(k)).start()

    def line_copy(self, s, up, here=False):
        spot, hi = self.spot, self.spot.hi
        slot = (s - 1) if up else hi + s - 2
        step = 1 if up != here else -1
        return remote(
            self.line.at[0, slot, self.span],
            self.line.at[1, slot, self.span],
            self.line_sems,
            slot,
            spot.line(spot.z + step),
        )

    def own(self, place, at):
        return self.part[place, self.spot.t, at, :].astype(F32) + self.got[place, at, :].astype(F32)

    def send(self, s, up):
        spot, hi = self.spot, self.spot.hi
        place = spot.z + hi - s if up else spot.z - hi + s
        slot = (s - 1) if up else hi + s - 2
        self.cross_copy(place).wait_recv()
        begins = spot.z == 0 if up else spot.z == hi - 1

        @pl.when(begins)
        def _():
            def put(at):
                self.line[0, slot, at, :] = self.own(place, at).astype(BF16)

            self.by_rows(put)

        if s > 1:

            @pl.when(jnp.logical_not(begins))
            def _():
                self.line_copy(s - 1, up, here=True).wait_recv()

                def put(at):
                    before = self.line[1, slot - 1, at, :].astype(F32)
                    self.line[0, slot, at, :] = (self.own(place, at) + before).astype(BF16)

                self.by_rows(put)

        self.line_copy(s, up).start()

    def sends_up(self, s):
        return self.spot.z <= s - 1

    def sends_down(self, s):
        return self.spot.z >= self.spot.hi - s

    def along(self, s):
        spot, hi = self.spot, self.spot.hi

        @pl.when(jnp.logical_and(self.sends_up(s), spot.z < hi - 1))
        def _():
            self.send(s, True)

        @pl.when(jnp.logical_and(self.sends_down(s), spot.z > 0))
        def _():
            self.send(s, False)

    def end(self, done):
        spot, hi = self.spot, self.spot.hi
        self.cross_copy(spot.z).wait_recv()

        @pl.when(spot.z > 0)
        def _():
            self.line_copy(hi - 1, True, here=True).wait_recv()

        @pl.when(spot.z < hi - 1)
        def _():
            self.line_copy(hi - 1, False, here=True).wait_recv()

        def total(at):
            below = self.line[1, hi - 2, at, :].astype(F32)
            above = self.line[1, 2 * hi - 3, at, :].astype(F32)
            value = self.own(spot.z, at)
            value = value + jnp.where(spot.z > 0, below, 0.0)
            done(at, value + jnp.where(spot.z < hi - 1, above, 0.0))

        self.by_rows(total)

    def finish(self):
        spot, hi = self.spot, self.spot.hi
        for place in range(hi):
            self.cross_copy(place).wait_send()
        for s in range(1, hi):

            @pl.when(jnp.logical_and(self.sends_up(s), spot.z < hi - 1))
            def _():
                self.line_copy(s, True).wait_send()

            @pl.when(jnp.logical_and(self.sends_down(s), spot.z > 0))
            def _():
                self.line_copy(s, False).wait_send()


def feed_kernel(
    n, tensor, unit_tiles, own, w_gate, w_up, w_down, cot, resid, gain,
    whole, gate_low, up_low, hidden, both, gain_grad, feed_part,
    part, got, line, mine, other, sems, cross_sems, line_sems, swap_sems,
):
    spot = Spot(n, tensor)
    hi = spot.hi
    rows, d = own.shape
    width = w_gate.shape[2]
    every = tensor * rows
    spot.greet(spot.cross)

    def put(at):
        whole[spot.z, spot.t, at, :] = own[at, :]

    by_rows(rows, STEP, put)
    half = rows // HALVES
    chains = [
        Chain(
            spot,
            lambda place, k, i=i: whole.at[
                place, lax.rem(spot.t + k, tensor), pl.ds(i * half, half)
            ],
            sems.at[i],
            [spot.cross],
        )
        for i in range(HALVES)
    ]
    for chain in chains:
        chain.first()
    gain_grad[...] = jnp.zeros_like(gain_grad)
    tiles = width // LANE
    skip = spot.z * tiles - jnp.minimum(spot.z * tiles, unit_tiles - tiles)
    chunk = 256

    def work(place):
        def ahead(j, none):
            cols = pl.ds(pl.multiple_of(j * chunk, chunk), chunk)
            rows_in = whole[place].reshape(every, d)
            gate, slope = gelu_of(dot(rows_in, w_gate[0, :, cols]))
            up = dot(rows_in, w_up[0, :, cols])
            grad = dot(cot[place].reshape(every, d), w_down[0, :, cols])
            at = lax.broadcasted_iota(jnp.int32, (1, chunk), 1) + j * chunk
            ok = at >= skip * LANE
            grad = jnp.where(ok, grad, 0.0)
            hidden[place, :, cols] = jnp.where(ok, gate * up, 0.0).astype(BF16)
            gate_low[place, :, cols] = (grad * up * slope).astype(BF16)
            up_low[place, :, cols] = (grad * gate).astype(BF16)
            return none

        lax.fori_loop(0, width // chunk, ahead, 0)

        def back(j, none):
            cols = pl.ds(pl.multiple_of(j * chunk, chunk), chunk)
            value = dot_nt(gate_low[place], w_gate[0, cols, :])
            value = (value + dot_nt(up_low[place], w_up[0, cols, :])).astype(BF16)
            for side in range(tensor):
                part[place, side, :, cols] = value[side * rows : (side + 1) * rows]
            return none

        lax.fori_loop(0, d // chunk, back, 0)

    def come_and_work(place):
        for chain in chains:
            chain.fans.arrive(place, 1)
        work(place)

    for s in range(1, hi):
        for chain in chains:
            chain.onward(s)
        chains[0].places(s - 1, come_and_work)
    chains[0].places(hi - 1, come_and_work)
    sums = [
        Rows(spot, part, got, line, cross_sems.at[i], line_sems.at[i], i * half, half)
        for i in range(HALVES)
    ]
    for k in range(hi):
        for each in sums:
            each.start(k)

    def give(i, none):
        place, j = i // (d // chunk), lax.rem(i, d // chunk)
        cols = pl.ds(pl.multiple_of(j * chunk, chunk), chunk)
        value = dot_nt(hidden[place], w_down[0, cols, :]).astype(BF16)
        for side in range(tensor):
            feed_part[place, side, :, cols] = value[side * rows : (side + 1) * rows]
        return none

    lax.fori_loop(0, hi * (d // chunk), give, 0)
    for chain in chains:
        chain.finish_sends()

    def done(at, total):
        value = resid[at, :]
        scale = lax.rsqrt(jnp.mean(value * value, axis=-1, keepdims=True) + 1e-06)
        turned = total * gain[...]
        inner = jnp.mean(turned * value, axis=-1, keepdims=True)
        grad = cot[spot.z, spot.t, at, :].astype(F32)
        grad = grad + scale * turned - value * (scale * scale * scale * inner)
        gained = total * value * scale
        gain_grad[...] += jnp.sum(gained.reshape(2, 8, -1), axis=0)
        mine[at, :] = grad.astype(BF16)

    for s in range(1, hi):
        for each in sums:
            each.along(s)
    swaps = []
    for i, each in enumerate(sums):
        each.end(done)
        span = pl.ds(i * half, half)
        swaps.append(remote(mine.at[span], other.at[span], swap_sems, i, spot.cross))
        swaps[-1].start()
    for each in sums:
        each.finish()
    share(spot, swaps, mine, other, both)


def share(spot, copies, mine, other, both):
    def keep(at):
        both[spot.t, at, :] = mine[at, :]

    by_rows(mine.shape[0], STEP, keep)
    for copy in copies:
        copy.wait()

    def take(at):
        both[1 - spot.t, at, :] = other[at, :]

    by_rows(mine.shape[0], STEP, take)


def rows_scratch(grid, rows, width):
    hi = grid.hi
    return [
        pltpu.VMEM((hi, rows, width), BF16),
        pltpu.VMEM((2, 2 * (hi - 1), rows, width), BF16),
        pltpu.VMEM((rows, width), BF16),
        pltpu.VMEM((rows, width), BF16),
    ]


def rows_sems(grid):
    hi = grid.hi
    return [
        pltpu.SemaphoreType.DMA((HALVES, 2, hi)),
        pltpu.SemaphoreType.DMA((HALVES, 2, 2 * (hi - 1))),
        pltpu.SemaphoreType.DMA((2, HALVES)),
    ]


def feed_forward(grid, own, feed, cot, resid, gain, unit_tiles):
    rows, d = own.shape
    hi, tensor = grid.hi, grid.tensor
    width = feed.shape[-1]
    near = pl.BlockSpec(memory_space=pltpu.VMEM)
    whole = jax.ShapeDtypeStruct((hi, tensor, rows, d), BF16)
    low = jax.ShapeDtypeStruct((hi, tensor * rows, width), BF16)
    feed = feed.reshape(3, -1, width)

    def weight(k):
        return pl.BlockSpec((1, d, width), lambda i: (k, 0, 0))

    return pl.pallas_call(
        functools.partial(feed_kernel, grid.n, tensor, unit_tiles),
        grid=(1,),
        out_shape=[
            whole,
            low,
            low,
            low,
            jax.ShapeDtypeStruct((tensor, rows, d), BF16),
            jax.ShapeDtypeStruct((8, d), F32),
            whole,
        ],
        in_specs=[near] + [weight(k) for k in range(3)] + [near] * 3,
        out_specs=[near] * 7,
        scratch_shapes=[pltpu.VMEM(whole.shape, BF16)]
        + rows_scratch(grid, rows, d)
        + [chain_sems(1, HALVES)]
        + rows_sems(grid),
        compiler_params=pltpu.CompilerParams(
            collective_id=2, has_side_effects=True, vmem_limit_bytes=GRANT
        ),
        name="feed_forward",
    )(own, feed, feed, feed, cot, resid, gain)


RING = 4


def tile_rows(rows):
    return 16 if rows % 16 == 0 else 8


SENDING = 8
HELD = 2


def place_at(j, hi):
    return lax.rem(2 * j + hi // 2 + (2 * j) // hi, hi)


def grads_kernel(
    n, tensor, spans, kept,
    unit_tiles,
    second, cot, normed, branch, gate_low, up_low, hidden, gelu_low, input_low, mixed, gates, first, own_out, thin,
    apart, summed, first_other, block_out, thin_own, *refs,
):
    stages = (n // LINE).bit_length() - 1
    lists = [refs[i * stages : (i + 1) * stages] for i in range(6)]
    sends, keeps, gots, thin_sends, thin_keeps, thin_gots = lists
    (
        made, ready, got_line, first_out, first_got, thin_ready, thin_line,
        cube_sems, line_sems, first_sems, thin_sems, thin_line_sems,
    ) = refs[6 * stages :]
    spot = Spot(n, tensor)
    hi = spot.hi
    all_spans = len(spans)
    units = all_spans * hi
    step = pl.program_id(0)
    rows = ready.shape[1]
    width = ready.shape[2]
    each = tile_rows(rows)
    last_step = units + stages - 1
    first_rows, out_rows = first.shape[0], own_out.shape[0]

    def place_of(unit):
        return place_at(lax.rem(unit, hi), hi)

    sources = {
        "gate": (second, gate_low),
        "up": (second, up_low),
        "down": (cot, hidden),
        "gelu": (normed, gelu_low),
        "input": (normed, input_low),
        "out": (branch, mixed),
    }

    def cube_copy(stage, unit):
        slot = lax.rem(unit, RING)
        return remote(
            sends[stage].at[slot],
            gots[stage].at[slot],
            cube_sems.at[stage],
            slot,
            spot.flip(spot.bits[stage]),
        )

    def line_copy(unit):
        slot = lax.rem(unit, SENDING)
        span = unit // hi
        return pltpu.make_async_remote_copy(
            src_ref=ready.at[slot],
            dst_ref=got_line.at[span, spot.z],
            send_sem=line_sems.at[0, slot],
            recv_sem=line_sems.at[1, span * hi + spot.z],
            device_id=spot.line(place_of(unit)),
            device_id_type=MESH,
        )

    def line_here(span, sender):
        here = got_line.at[span, sender]
        return pltpu.make_async_remote_copy(
            src_ref=here,
            dst_ref=here,
            send_sem=line_sems.at[0, 0],
            recv_sem=line_sems.at[1, span * hi + sender],
            device_id=spot.line(sender),
            device_id_type=MESH,
        )

    def line_sent(unit):
        @pl.when(jnp.logical_and(unit >= 0, place_of(unit) != spot.z))
        def _():
            line_copy(unit).wait_send()

    def settle(span):
        for distance in range(1, hi):
            line_here(span, spot.away(distance)).wait_recv()

        def give(at):
            if span < kept:
                tiles = width // LANE
                for place in range(hi):
                    skip = place * tiles - min(place * tiles, unit_tiles - tiles)
                    if skip < tiles:
                        value = got_line[span, place, at, skip * LANE :]
                        apart[span, at, place * width : (place + 1) * width - skip * LANE] = value
            else:
                value = got_line[span, 0, at, :].astype(F32)
                for place in range(1, hi):
                    value = value + got_line[span, place, at, :].astype(F32)
                blocks = width // summed.shape[2]
                for j in range(blocks):
                    cols = slice(j * summed.shape[2], (j + 1) * summed.shape[2])
                    summed[(span - kept) * blocks + j, at, :] = value[:, cols]

        by_rows(rows, each, give)

    def thin_copy(stage):
        return remote(
            thin_sends[stage], thin_gots[stage], thin_sems, stage, spot.flip(spot.bits[stage])
        )

    def thin_line_copy(place, sender):
        return pltpu.make_async_remote_copy(
            src_ref=thin_ready.at[place],
            dst_ref=thin_line.at[sender],
            send_sem=thin_line_sems.at[0, place],
            recv_sem=thin_line_sems.at[1, sender],
            device_id=spot.line(place),
            device_id_type=MESH,
        )

    first_copy = remote(first_out, first_got, first_sems, 0, spot.cross)

    @pl.when(step == 0)
    def _():
        spot.greet(*[spot.flip(bit) for bit in spot.bits], spot.cross)

        def put(at):
            first_out[at, :] = first[at, :]

        by_rows(first_rows, STEP, put)

        def put_out(at):
            to = pl.ds(pl.multiple_of(first_rows + at.start, STEP), STEP)
            first_out[to, :] = own_out[at, :]

        by_rows(out_rows, STEP, put_out)
        first_copy.start()
        mine = spot.bit(1)
        for place in range(hi):
            for k in range(thin_sends[0].shape[1]):
                thin_sends[0][place, k] = thin[place, 2 * k + 1 - mine]
                thin_keeps[0][place, k] = thin[place, 2 * k + mine]
        thin_copy(0).start()

    for stage in range(stages):

        @pl.when(step == stage + 1)
        def _(stage=stage):
            thin_copy(stage).wait_recv()
            if stage < stages - 1:
                mine = spot.bit(spot.bits[stage + 1])
                for place in range(hi):
                    for k in range(thin_sends[stage + 1].shape[1]):
                        a, b = 2 * k + 1 - mine, 2 * k + mine
                        thin_sends[stage + 1][place, k] = (
                            thin_keeps[stage][place, a] + thin_gots[stage][place, a]
                        )
                        thin_keeps[stage + 1][place, k] = (
                            thin_keeps[stage][place, b] + thin_gots[stage][place, b]
                        )
                thin_copy(stage + 1).start()
            else:
                for place in range(hi):
                    thin_ready[place] = thin_keeps[stage][place, 0] + thin_gots[stage][place, 0]
                for distance in range(1, hi):
                    thin_line_copy(spot.away(distance), spot.z).start()

    @pl.when(step < units)
    def _():
        slot = lax.rem(step, RING)

        @pl.when(step >= RING)
        def _():
            cube_copy(0, step - RING).wait_send()

        for span, pieces in enumerate(spans):

            @pl.when(step // hi == span)
            def _(pieces=pieces):
                for name, begin, width, to in pieces:
                    if name == "gates":

                        def put(at, width=width, to=to):
                            made[at, to : to + width] = gates[0, at, :].astype(made.dtype)

                        by_rows(made.shape[0], STEP, put)
                        continue
                    left, right = sources[name]

                    def one(j, carry, left=left, right=right, begin=begin, width=width, to=to):
                        at = pl.ds(pl.multiple_of(j * LANE, LANE), LANE)
                        made[at, to : to + width] = lax.dot_general(
                            left[:, at],
                            right[:, begin : begin + width],
                            (((0,), (0,)), ((), ())),
                            preferred_element_type=F32,
                        ).astype(made.dtype)
                        return carry

                    lax.fori_loop(0, made.shape[0] // LANE, one, 0)

        mine = spot.bit(1)
        for k in range(sends[0].shape[1]):

            def put(at, k=k):
                def block(i):
                    at_made = pl.ds(pl.multiple_of(i * rows + at.start, each), each)
                    return made[at_made, :].astype(BF16)

                sends[0][slot, k, at, :] = block(2 * k + 1 - mine)
                keeps[0][lax.rem(step, HELD), k, at, :] = block(2 * k + mine)

            by_rows(rows, each, put)
        cube_copy(0, step).start()

    for stage in range(stages):
        unit = step - stage - 1

        @pl.when(jnp.logical_and(unit >= 0, unit < units))
        def _(stage=stage, unit=unit):
            slot = lax.rem(unit, RING)
            held = lax.rem(unit, HELD)
            cube_copy(stage, unit).wait_recv()

            def total(k, at):
                return (
                    keeps[stage][held, k, at, :].astype(F32) + gots[stage][slot, k, at, :].astype(F32)
                ).astype(BF16)

            if stage < stages - 1:

                @pl.when(unit >= RING)
                def _():
                    cube_copy(stage + 1, unit - RING).wait_send()

                mine = spot.bit(spot.bits[stage + 1])
                for k in range(sends[stage + 1].shape[1]):

                    def put(at, k=k):
                        sends[stage + 1][slot, k, at, :] = total(2 * k + 1 - mine, at)
                        keeps[stage + 1][held, k, at, :] = total(2 * k + mine, at)

                    by_rows(rows, each, put)
                cube_copy(stage + 1, unit).start()
            else:
                line_sent(unit - SENDING)
                place = place_of(unit)

                @pl.when(place != spot.z)
                def _():
                    def put(at):
                        ready[lax.rem(unit, SENDING), at, :] = total(0, at)

                    by_rows(rows, each, put)
                    line_copy(unit).start()

                @pl.when(place == spot.z)
                def _():
                    def put(at):
                        got_line[unit // hi, spot.z, at, :] = total(0, at)

                    by_rows(rows, each, put)

    late = 2 * hi + stages - 1
    for span in range(all_spans):
        when = span * hi + hi - 1 + late
        if when < last_step:

            @pl.when(step == when)
            def _(span=span):
                settle(span)

    @pl.when(step == last_step)
    def _():
        for span in range(all_spans):
            if span * hi + hi - 1 + late >= last_step:
                settle(span)
        for unit in range(units - SENDING, units):
            line_sent(unit)
        for stage in range(stages):
            for unit in range(units - RING, units):
                cube_copy(stage, unit).wait_send()
            thin_copy(stage).wait_send()
        value = thin_ready[spot.z]
        for distance in range(1, hi):
            place = spot.away(distance)
            thin_line_copy(place, place).wait_recv()
            thin_line_copy(place, spot.z).wait_send()
            value = value + thin_line[place]
        thin_own[...] = value
        first_copy.wait()

        def take(at):
            first_other[at, :] = first_got[at, :]

        by_rows(first_rows, STEP, take)

        def take_out(at):
            other = pl.ds(pl.multiple_of(first_rows + at.start, STEP), STEP)
            block_out[spot.t, at, :] = own_out[at, :]
            block_out[1 - spot.t, at, :] = first_got[other, :]

        by_rows(out_rows, STEP, take_out)


def column_spans(widths, width):
    spans, here, room = [], [], width
    for name, size in widths:
        begin = 0
        while begin < size:
            count = min(size - begin, room)
            here.append((name, begin, count, width - room))
            begin, room = begin + count, room - count
            if room == 0:
                spans, here, room = spans + [here], [], width
    assert not here
    return spans


def send_grads(grid, feed, rec, gates, first, own_out, thin, unit_tiles):
    hi, inner = grid.hi, grid.inner_size
    second, cot, gate_low, up_low, hidden = feed
    normed, branch, gelu_low, input_low, mixed = rec
    d = second.shape[1]
    rows = d // grid.n
    slab = d // hi
    width = gate_low.shape[1]
    kept = 3
    channels = mixed.shape[1]
    spans = column_spans([(name, width) for name in ("gate", "up", "down")], width) + column_spans(
        [(name, channels) for name in ("gelu", "input", "out")] + [("gates", gates.shape[1])], width
    )
    all_spans = len(spans)
    units = all_spans * hi
    stages = inner.bit_length() - 1

    def place_of(i):
        return place_at(lax.rem(jnp.minimum(i, units - 1), hi), hi)

    def slab_of(a):
        return pl.BlockSpec((a.shape[0], slab), lambda i: (0, place_of(i)))

    def whole(a):
        zeros = (0,) * a.ndim
        return pl.BlockSpec(a.shape, lambda i: zeros, pipeline_mode=pl.Buffered(1))

    block = gates.shape[1]
    apart = jax.ShapeDtypeStruct((kept, rows, unit_tiles * LANE), BF16)
    summed = jax.ShapeDtypeStruct(((all_spans - kept) * (width // block), rows, block), F32)
    both = jax.ShapeDtypeStruct((grid.tensor,) + own_out.shape, BF16)
    other = jax.ShapeDtypeStruct(first.shape, BF16)
    thin = thin.reshape(hi, inner, 8, thin.shape[1] // 8)
    thin_shape = thin.shape[2:]
    thin_own = jax.ShapeDtypeStruct(thin_shape, F32)
    outs = [apart, summed, other, both, thin_own]
    swapped = (first.shape[0] + own_out.shape[0], d)

    def halves(lead, tail, kind):
        return [
            pltpu.VMEM((lead, inner >> (stage + 1)) + tail, kind) for stage in range(stages)
        ]

    gates = gates.reshape(hi, slab, gates.shape[1])
    return pl.pallas_call(
        functools.partial(grads_kernel, grid.n, grid.tensor, spans, kept, unit_tiles),
        grid=(units + stages,),
        out_shape=outs,
        in_specs=[slab_of(a) for a in (second, cot, normed, branch)]
        + [whole(a) for a in (gate_low, up_low, hidden, gelu_low, input_low, mixed)]
        + [pl.BlockSpec((1,) + gates.shape[1:], lambda i: (place_of(i), 0, 0))]
        + [whole(first), whole(own_out), whole(thin)],
        out_specs=[whole(a) for a in outs],
        scratch_shapes=halves(RING, (rows, width), BF16)
        + halves(HELD, (rows, width), BF16)
        + halves(RING, (rows, width), BF16)
        + halves(hi, thin_shape, F32) * 3
        + [
            pltpu.VMEM((slab, width), BF16 if rows % 16 == 0 else F32),
            pltpu.VMEM((SENDING, rows, width), BF16),
            pltpu.VMEM((all_spans, hi, rows, width), BF16),
            pltpu.VMEM(swapped, BF16),
            pltpu.VMEM(swapped, BF16),
            pltpu.VMEM((hi,) + thin_shape, F32),
            pltpu.VMEM((hi,) + thin_shape, F32),
            pltpu.SemaphoreType.DMA((stages, 2, RING)),
            pltpu.SemaphoreType.DMA((2, units)),
            pltpu.SemaphoreType.DMA((2, 1)),
            pltpu.SemaphoreType.DMA((2, stages)),
            pltpu.SemaphoreType.DMA((2, hi)),
        ],
        compiler_params=pltpu.CompilerParams(
            collective_id=4, has_side_effects=True, vmem_limit_bytes=GRANT
        ),
        name="send_grads",
    )(
        second, cot, normed, branch, gate_low, up_low, hidden, gelu_low, input_low, mixed, gates,
        first, own_out, thin,
    )


def rms_norm(values, gain):
    scale = lax.rsqrt(jnp.mean(values * values, axis=-1, keepdims=True) + 1e-06)
    return values * scale * gain


def dot(left, right):
    return jnp.dot(left, right, preferred_element_type=F32)


def dot_nt(left, right):
    return jnp.einsum("ik,jk->ij", left, right, preferred_element_type=F32)


def dot_tn(left, right):
    return jnp.einsum("ki,kj->ij", left, right, preferred_element_type=F32)


def local(
    block_in,
    segment_ids,
    cotangent,
    first_gain,
    gelu_weight,
    gelu_bias,
    input_weight,
    input_bias,
    conv_weight,
    conv_bias,
    inlet_weight,
    inlet_bias,
    forget_weight,
    forget_bias,
    decay_rate,
    out_weight,
    out_bias,
    second_gain,
    mlp_gate,
    mlp_up,
    mlp_down,
):
    grid = Grid()
    seq_count, tok_count, width = block_in.shape
    head_count, block_size = gelu_weight.shape[1:]
    channels = head_count * block_size
    margin = CONV - 1
    rows_all = seq_count * tok_count
    rows_half = rows_all // grid.tensor
    d_own = gelu_weight.shape[0]
    lane_own = gelu_bias.shape[1]
    units = mlp_gate.shape[1]
    unit_tiles = units // LANE
    window_tiles = -(-unit_tiles // grid.hi)
    window = window_tiles * LANE

    halo_rows = block_in[:, tok_count - HALO :]
    marks = (segment_ids + 1).astype(BF16)
    halo, rim_marks = shifted((halo_rows, marks[:, tok_count - margin :]), "wide", 1)
    halo = halo.reshape(seq_count * HALO, width)
    marks_ext = jnp.concatenate([rim_marks, marks], axis=1)
    earlier = [marks_ext[:, margin - k : margin - k + tok_count] == marks for k in range(1, CONV)]
    flags = jnp.stack([jnp.logical_not(earlier[0])] + earlier, axis=-1).astype(F32)
    flags = jnp.pad(flags.reshape(rows_all, CONV), ((0, 0), (0, 8 - CONV)))

    per_lane = jnp.stack([gelu_bias, input_bias])
    per_lane = jnp.concatenate(
        [per_lane, conv_weight, jnp.stack([conv_bias, inlet_bias, forget_bias, decay_rate])]
    )
    lane_table = lax.dynamic_update_slice(
        jnp.zeros((CONV + 6, head_count, block_size), BF16), per_lane, (0, 0, grid.w * lane_own)
    )
    per_width = jnp.stack([first_gain, out_bias, second_gain])
    width_table = lax.dynamic_update_slice(
        jnp.zeros((3, width), BF16), per_width, (0, grid.w * d_own)
    )
    thin_own = jnp.concatenate(
        [lane_table.reshape(CONV + 6, channels), width_table.reshape(-1, channels)]
    )
    thin_count = thin_own.shape[0]
    thin_own = jnp.pad(thin_own, ((0, -thin_count % 16), (0, 0)))
    cot_rows = cotangent.reshape(grid.tensor, rows_half, width)
    rec_own = (
        input_weight.transpose(1, 0, 2),
        gelu_weight.transpose(1, 0, 2),
        out_weight.transpose(0, 2, 1),
    )
    feed_own = (mlp_gate, mlp_up, mlp_down.T)
    gates_own = (inlet_weight, forget_weight)
    x = block_in.reshape(rows_all, width)

    if d_own % STEP == 0 and lane_own % STEP == 0:
        feed_all, cot_all = place_feed(grid, feed_own, cot_rows)
        (
            normed,
            ext,
            conv,
            gelu_pre,
            inlet_pre,
            forget_pre,
            cum,
            local_state,
            entered,
            mixed,
            resid,
            second_own,
            lanes,
            table,
            gates_all,
            rec_all,
            feed_all,
            cot_all,
        ) = gather_recurrence(
            grid, x, halo, flags, rec_own, gates_own, thin_own, CONV + 6, feed_all, cot_all, seq_count
        )
        rec_all = rec_all.reshape(3, width, channels)
        gain_first, _, gain_second = table[CONV + 6 : thin_count].reshape(3, width)
    else:
        rec_all, gates_all, thin_all, feed_all, cot_all = place_own(
            grid, rec_own, feed_own, gates_own, thin_own, cot_rows
        )
        rec_all, gates_all, thin_all, cot_all = bring_weights(
            grid, rec_all, gates_all, thin_all, cot_all
        )
        rec_all = rec_all.reshape(3, width, channels)
        gates_all = gates_all.reshape(2 * head_count, block_size, block_size)
        table = jnp.sum(thin_all.astype(F32), axis=0)
        gain_first, out_shift, gain_second = table[CONV + 6 : thin_count].reshape(3, width)
        rate = table[CONV + 5]
        lanes = jnp.concatenate(
            [table[: CONV + 5], jnp.stack([jax.nn.softplus(rate), jax.nn.sigmoid(rate)])]
        )
        lanes = jnp.pad(lanes, ((0, LANE_ROWS - lanes.shape[0]), (0, 0)))
        (
            normed,
            ext,
            conv,
            gelu_pre,
            inlet_pre,
            forget_pre,
            cum,
            local_state,
            entered,
            mixed,
            resid,
            second_own,
            feed_all,
        ) = forward_recurrence(
            grid, x, halo, gain_first[None], rec_all, gates_all[:head_count], gates_all[head_count:],
            lanes, flags, out_shift[None], gain_second[None], feed_all, seq_count,
        )

    rows_feed = grid.hi * rows_all
    second_all, gate_low, up_low, hidden, branch_low, gain_two_grad, feed_part = feed_forward(
        grid, second_own, feed_all, cot_all, resid, gain_second[None], unit_tiles
    )
    second_all, cot_all = (v.reshape(rows_feed, width) for v in (second_all, cot_all))
    gate_low, up_low, hidden = (v.reshape(rows_feed, window) for v in (gate_low, up_low, hidden))
    branch_low = branch_low.reshape(rows_all, width)
    gain_two_grad = jnp.sum(gain_two_grad, axis=0)

    gelu_low, input_low, gate_w_grads, lane_grads, out_shift_grad, own_out = leave_recurrence(
        grid, branch_low, rec_all, gelu_pre, local_state, cum, inlet_pre, forget_pre, conv, ext, entered,
        gates_all, lanes, flags, feed_part, resid, seq_count,
    )
    out_shift_grad = jnp.sum(out_shift_grad, axis=0)
    gate_w_grads = (
        gate_w_grads.reshape(2, head_count, grid.n, lane_own, block_size)
        .transpose(2, 0, 1, 3, 4)
        .reshape(width, block_size)
    )
    inputs = x.astype(F32)
    scale_first = lax.rsqrt(jnp.mean(inputs * inputs, axis=-1, keepdims=True) + 1e-06)
    first_part, gain_one_grad = first_gradient(
        x, input_low, gelu_low, rec_all, jnp.broadcast_to(scale_first, (rows_all, 8))
    )
    gain_one_grad = jnp.sum(gain_one_grad, axis=0)
    gain_grads = jnp.stack([gain_one_grad, gain_two_grad])
    gain_grads = gain_grads + grid.swap(gain_grads)

    lane_grads = (
        lane_grads[: CONV + 6]
        .reshape(CONV + 6, head_count, grid.n, lane_own)
        .transpose(2, 0, 1, 3)
        .reshape(grid.n, -1)
    )
    thin_grads = jnp.concatenate(
        [v.reshape(grid.n, d_own) for v in (gain_grads[0], out_shift_grad, gain_grads[1])]
        + [lane_grads],
        axis=1,
    )
    feed_grads, rec_grads, first_other, block_out, thin = send_grads(
        grid,
        (second_all, cot_all, gate_low, up_low, hidden),
        (normed, branch_low, gelu_low, input_low, mixed),
        gate_w_grads,
        first_part,
        own_out,
        thin_grads,
        unit_tiles,
    )
    block_out = block_out.reshape(block_in.shape)
    thin = thin.reshape(-1)
    gate_grad, up_grad, down_grad = (feed_grads[m].astype(F32) for m in range(3))
    down_grad = down_grad.T
    gelu_w_grad = rec_grads[:head_count].transpose(1, 0, 2)
    input_w_grad = rec_grads[head_count : 2 * head_count].transpose(1, 0, 2)
    out_grad = rec_grads[2 * head_count : 3 * head_count].transpose(0, 2, 1)
    gate_w_grads = rec_grads[3 * head_count].reshape(2, head_count, lane_own, block_size)
    first_grad = first_part.astype(F32) + first_other.astype(F32)
    _, pull_first = jax.vjp(rms_norm, inputs, gain_first)
    input_norm_grad, _ = pull_first(first_grad)
    block_grad = (branch_low.astype(F32) + input_norm_grad).reshape(block_in.shape)
    gain_one_own, out_shift_own, gain_two_own = (
        thin[i * d_own : (i + 1) * d_own] for i in range(3)
    )
    lanes = thin[3 * d_own :].reshape(CONV + 6, head_count, lane_own)
    return (
        block_out,
        block_grad,
        gain_one_own,
        gelu_w_grad,
        lanes[0],
        input_w_grad,
        lanes[1],
        lanes[2 : 2 + CONV],
        lanes[2 + CONV],
        gate_w_grads[0],
        lanes[3 + CONV],
        gate_w_grads[1],
        lanes[4 + CONV],
        lanes[5 + CONV],
        out_grad,
        out_shift_own,
        gain_two_own,
        gate_grad,
        up_grad,
        down_grad,
    )


def solution(mesh):
    in_specs = (
        P(None, "wide", None),
        P(None, "wide"),
        P(None, "wide", None),
        P("wide"),
        P("wide", "tensor", None),
        P("tensor", "wide"),
        P("wide", "tensor", None),
        P("tensor", "wide"),
        P(None, "tensor", "wide"),
        P("tensor", "wide"),
        P("tensor", "wide", None),
        P("tensor", "wide"),
        P("tensor", "wide", None),
        P("tensor", "wide"),
        P("tensor", "wide"),
        P("tensor", None, "wide"),
        P("wide"),
        P("wide"),
        P("wide", "tensor"),
        P("wide", "tensor"),
        P("tensor", "wide"),
    )
    out_specs = (
        P(None, "wide", None),
        P(None, "wide", None),
        P("wide"),
        P("wide", "tensor", None),
        P("tensor", "wide"),
        P("wide", "tensor", None),
        P("tensor", "wide"),
        P(None, "tensor", "wide"),
        P("tensor", "wide"),
        P("tensor", "wide", None),
        P("tensor", "wide"),
        P("tensor", "wide", None),
        P("tensor", "wide"),
        P("tensor", "wide"),
        P("tensor", None, "wide"),
        P("wide"),
        P("wide"),
        P("wide", "tensor"),
        P("wide", "tensor"),
        P("tensor", "wide"),
    )
    return jax.shard_map(local, mesh=mesh, in_specs=in_specs, out_specs=out_specs, check_vma=False)
```

```python
import functools

import jax
import jax.numpy as jnp
from jax import lax
from jax.experimental import pallas as pl
from jax.experimental.pallas import tpu as pltpu
from jax.sharding import PartitionSpec as P

CONV = 4
LANE = 128
GRANT = 60 * 1024 * 1024
F32 = jnp.float32
BF16 = jnp.bfloat16

LINE = 4


class Grid:
    def __init__(self):
        self.n = lax.axis_size("wide")
        self.hi = LINE
        self.inner_size = self.n // LINE
        self.tensor = lax.axis_size("tensor")
        self.w = lax.axis_index("wide")
        self.t = lax.axis_index("tensor")
        self.z = self.w // self.inner_size
        self.inner = lax.rem(self.w, self.inner_size)

    def flip(self, value, bit):
        return lax.ppermute(value, "wide", [(i, i ^ bit) for i in range(self.n)])

    def swap(self, value):
        size = self.tensor
        pairs = [(i, (i + 1) % size) for i in range(size)]
        return lax.ppermute(value, "tensor", pairs)


def shifted(shard, axis, by):
    size = lax.axis_size(axis)
    place = lax.axis_index(axis) - by
    there = jnp.logical_and(place >= 0, place < size)
    pairs = [(i, (i + by) % size) for i in range(size)]
    moved = lax.ppermute(shard, axis, pairs)
    return jax.tree.map(lambda a: jnp.where(there, a, jnp.zeros_like(a)), moved)


def pick(values, index, axis=0):
    return lax.dynamic_index_in_dim(values, index, axis, keepdims=False)


MESH = pl.DeviceIdType.MESH


class Spot:
    def __init__(self, n, tensor):
        self.n = n
        self.hi = LINE
        self.inner_size = n // LINE
        self.bits = [1 << i for i in range(self.inner_size.bit_length() - 1)]
        self.tensor = tensor
        self.w = lax.axis_index("wide")
        self.t = lax.axis_index("tensor")
        self.z = self.w // self.inner_size
        self.inner = lax.rem(self.w, self.inner_size)
        self.cross = {"tensor": lax.rem(self.t + 1, tensor)}

    def bit(self, which):
        return lax.rem(self.inner // which, 2)

    def flip(self, which):
        return {"wide": self.w + which - 2 * which * self.bit(which)}

    def line(self, place):
        return {"wide": place * self.inner_size + self.inner}

    def away(self, distance):
        return lax.rem(self.z + distance, self.hi)

    def greet(self, *sides):
        barrier = pltpu.get_barrier_semaphore()
        for side in sides:
            pl.semaphore_signal(barrier, inc=1, device_id=side, device_id_type=MESH)
        for distance in range(1, self.hi):
            pl.semaphore_signal(
                barrier, inc=1, device_id=self.line(self.away(distance)), device_id_type=MESH
            )
        pl.semaphore_wait(barrier, len(sides) + self.hi - 1)


def remote(src, dst, sems, index, side):
    return pltpu.make_async_remote_copy(
        src_ref=src,
        dst_ref=dst,
        send_sem=sems.at[0, index],
        recv_sem=sems.at[1, index],
        device_id=side,
        device_id_type=MESH,
    )


class Fans:
    def __init__(self, spot, at, sems, base, sides):
        self.spot, self.at, self.sems, self.base, self.sides = spot, at, sems, base, sides
        self.kinds = sorted(range(1 << len(sides)), key=lambda k: (bin(k).count("1"), -k))

    def onto(self, k):
        low = (k & -k) if k else 1 << len(self.sides)
        return [i for i in reversed(range(len(self.sides))) if (1 << i) < low]

    def copy(self, place, k, i, here=False):
        spot, hi = self.spot, self.spot.hi
        landed = k if here else k | (1 << i)
        index = self.base + (landed - 1) * hi + lax.rem(place - spot.z + hi, hi)
        ref = self.at(place, k)
        return remote(ref, ref, self.sems, index, self.sides[i])

    def hand_on(self, place, k):
        for i in self.onto(k):
            self.copy(place, k, i).start()

    def arrive(self, place, k):
        low = (k & -k).bit_length() - 1
        self.copy(place, k, low, here=True).wait_recv()

    def pass_on(self, place):
        for k in self.kinds:
            if k and self.onto(k):
                self.arrive(place, k)
                self.hand_on(place, k)

    def finish(self, place):
        for k in self.kinds:
            if k and not self.onto(k):
                self.arrive(place, k)
        self.finish_sends(place)

    def finish_sends(self, place):
        for k in self.kinds:
            for i in self.onto(k):
                self.copy(place, k, i).wait_send()

    def count(sides, hi):
        return ((1 << sides) - 1) * hi


class Chain:
    def __init__(self, spot, at, sems, sides):
        self.spot, self.at, self.sems = spot, at, sems
        self.fans = Fans(spot, at, sems, 2 * (spot.hi - 1), sides)

    def line_copy(self, s, up):
        spot, hi = self.spot, self.spot.hi
        owner = spot.z - (s - 1) if up else spot.z + (s - 1)
        other = spot.z + 1 if up else spot.z - 1
        ref = self.at(owner, 0)
        return remote(ref, ref, self.sems, (s - 1) if up else hi + s - 2, spot.line(other))

    def line_here(self, s, up):
        spot, hi = self.spot, self.spot.hi
        owner = spot.z - s if up else spot.z + s
        other = spot.z - 1 if up else spot.z + 1
        ref = self.at(owner, 0)
        return remote(ref, ref, self.sems, (s - 1) if up else hi + s - 2, spot.line(other))

    def first(self):
        self.first_line()
        self.fans.hand_on(self.spot.z, 0)

    def first_line(self):
        spot, hi = self.spot, self.spot.hi

        @pl.when(spot.z < hi - 1)
        def _():
            self.line_copy(1, True).start()

        @pl.when(spot.z > 0)
        def _():
            self.line_copy(1, False).start()

    def onward(self, s):
        spot, hi = self.spot, self.spot.hi

        @pl.when(spot.z >= s)
        def _():
            self.line_here(s, True).wait_recv()

        if s < hi - 1:

            @pl.when(jnp.logical_and(spot.z >= s, spot.z < hi - 1))
            def _():
                self.line_copy(s + 1, True).start()

        @pl.when(spot.z >= s)
        def _():
            self.fans.hand_on(spot.z - s, 0)

        @pl.when(spot.z <= hi - 1 - s)
        def _():
            self.line_here(s, False).wait_recv()

        if s < hi - 1:

            @pl.when(jnp.logical_and(spot.z <= hi - 1 - s, spot.z > 0))
            def _():
                self.line_copy(s + 1, False).start()

        @pl.when(spot.z <= hi - 1 - s)
        def _():
            self.fans.hand_on(spot.z + s, 0)

    def places(self, s, act):
        spot = self.spot
        if s == 0:
            act(spot.z)
            return

        @pl.when(spot.z >= s)
        def _():
            act(spot.z - s)

        @pl.when(spot.z <= spot.hi - 1 - s)
        def _():
            act(spot.z + s)

    def second(self, s):
        self.places(s, self.fans.pass_on)

    def finish(self):
        for s in range(self.spot.hi):
            self.places(s, self.fans.finish)
        self.finish_line()

    def finish_sends(self):
        for s in range(self.spot.hi):
            self.places(s, self.fans.finish_sends)
        self.finish_line()

    def finish_line(self):
        spot, hi = self.spot, self.spot.hi
        for s in range(1, hi):

            @pl.when(jnp.logical_and(spot.z >= s - 1, spot.z < hi - 1))
            def _():
                self.line_copy(s, True).wait_send()

            @pl.when(jnp.logical_and(spot.z <= hi - s, spot.z > 0))
            def _():
                self.line_copy(s, False).wait_send()


def chain_sems(sides, *lead):
    return pltpu.SemaphoreType.DMA(lead + (2, 2 * (LINE - 1) + ((1 << sides) - 1) * LINE))


class Turns:
    def __init__(self, spot, distances, window_of, at, sems, sides):
        self.spot, self.window_of, self.at, self.sems = spot, window_of, at, sems
        self.distances = distances
        self.fans = Fans(spot, at, sems, spot.hi, sides)

    def line_copy(self, distance):
        spot = self.spot
        place = spot.away(distance)
        return remote(self.window_of(place), self.at(spot.z, 0), self.sems, distance, spot.line(place))

    def back(self, distance):
        return lax.rem(self.spot.z - distance + self.spot.hi, self.spot.hi)

    def line_here(self, distance):
        place = self.back(distance)
        ref = self.at(place, 0)
        return remote(ref, ref, self.sems, distance, self.spot.line(place))

    def first(self):
        for distance in self.distances:
            self.start(distance)

    def start(self, distance):
        if distance:
            self.line_copy(distance).start()
        else:
            self.fans.hand_on(self.spot.z, 0)

    def onward(self, distance):
        if distance in self.distances:
            self.line_here(distance).wait_recv()
            self.fans.hand_on(self.back(distance), 0)

    def second(self, distance):
        if distance in self.distances:
            self.fans.pass_on(self.back(distance))

    def finish(self):
        for distance in self.distances:
            self.fans.finish(self.back(distance))
            if distance:
                self.line_copy(distance).wait_send()


LATE = (0, 1, 2, 3)


class FeedTurns:
    def __init__(self, spot, feed, sems, cube):
        def index(place, k):
            return place * spot.inner_size + jnp.bitwise_xor(spot.inner, k)

        self.each = [
            Turns(
                spot,
                LATE,
                lambda place, m=m: feed.at[m, spot.n + place],
                lambda place, k, m=m: feed.at[m, index(place, k)],
                sems.at[m],
                cube,
            )
            for m in range(feed.shape[0])
        ]

    def start(self, distance):
        for turns in self.each:
            turns.start(distance)

    def onward(self, distance):
        for turns in self.each:
            turns.onward(distance)

    def second(self, distance):
        for turns in self.each:
            turns.second(distance)

    def finish(self):
        for turns in self.each:
            turns.finish()


def weights_kernel(
    n, tensor, rec, gates, thin, cot, rec_all, gates_all, thin_all, cot_all,
    rec_sems, gates_sems, thin_sems, cot_sems,
):
    del rec, gates, thin, cot
    spot = Spot(n, tensor)
    hi = spot.hi

    def index(place, k):
        return place * spot.inner_size + jnp.bitwise_xor(spot.inner, k)

    cube = [spot.flip(bit) for bit in spot.bits]
    moves = [
        Chain(spot, lambda place, k: thin_all.at[index(place, k)], thin_sems, cube),
        Chain(spot, lambda place, k: gates_all.at[:, index(place, k)], gates_sems, cube),
        *[
            Chain(
                spot, lambda place, k, m=m: rec_all.at[m, index(place, k)], rec_sems.at[m], cube
            )
            for m in range(rec_all.shape[0])
        ],
        Chain(
            spot,
            lambda place, k: cot_all.at[place, lax.rem(spot.t + k, tensor)],
            cot_sems,
            [spot.cross],
        ),
    ]
    spot.greet(*cube, spot.cross)
    last = moves[-1]
    for move in moves[:-1]:
        move.first()
    last.fans.hand_on(spot.z, 0)
    for s in range(1, hi):
        for move in moves[:-1]:
            move.onward(s)
        if s == 1:
            last.first_line()
        else:
            last.onward(s - 1)
        for move in moves:
            move.second(s - 1)
    last.onward(hi - 1)
    for move in moves:
        move.second(hi - 1)
    for move in moves:
        move.finish()


def turn_sems(grid, count):
    return pltpu.SemaphoreType.DMA((count, 2, grid.n))


def place_kernel(
    unit_tiles, spot, wide_in, gelu_in, out_in, gate, up, down, inlet, forget, thin, cot,
    rec_all, gates_all, thin_all, feed_all, cot_all,
):
    step = pl.program_id(0)
    hi = LINE
    width = feed_all.shape[3]
    tiles = width // LANE

    @pl.when(step == 0)
    def _():
        heads, _, lanes = wide_in.shape
        for m, source in enumerate((wide_in, gelu_in, out_in)):
            for h in range(heads):
                rec_all[m, 0, :, h * lanes : (h + 1) * lanes] = source[h]
        for m, source in enumerate((inlet, forget)):
            for h in range(heads):
                gates_all[m * heads + h, 0] = source[h]
        thin_all[0] = thin[...]
        cot_all[0, 0] = cot[0]

    place = jnp.where(step < hi, step, spot[1])
    tile = jnp.minimum(place * tiles, unit_tiles - tiles)
    for m, source in enumerate((gate, up, down)):
        feed_all[m, 0] = source[:, pl.ds(pl.multiple_of(tile * LANE, LANE), width)]


def place_own(grid, rec, feed, gates, thin, cot):
    n, hi = grid.n, grid.hi
    heads, d_own, lanes = rec[0].shape
    units = feed[0].shape[1]
    unit_tiles = units // LANE
    window = -(-unit_tiles // hi) * LANE
    lane_own, block = gates[0].shape[1:]
    spot = jnp.stack([grid.w, grid.z, grid.t])

    def fixed(a):
        zeros = (0,) * a.ndim
        return pl.BlockSpec(a.shape, lambda i, spot: zeros)

    outs = [
        (3, n, d_own, heads * lanes),
        (2 * heads, n, lane_own, block),
        (n,) + thin.shape,
        (3, n + hi, d_own, window),
        (hi,) + cot.shape,
    ]
    return pl.pallas_call(
        functools.partial(place_kernel, unit_tiles),
        grid_spec=pltpu.PrefetchScalarGridSpec(
            num_scalar_prefetch=1,
            grid=(hi + 1,),
            in_specs=[fixed(a) for a in rec + feed + gates + (thin,)]
            + [pl.BlockSpec((1,) + cot.shape[1:], lambda i, spot: (spot[2], 0, 0))],
            out_specs=[
                pl.BlockSpec((3, 1, d_own, heads * lanes), lambda i, spot: (0, spot[0], 0, 0)),
                pl.BlockSpec((2 * heads, 1, lane_own, block), lambda i, spot: (0, spot[0], 0, 0)),
                pl.BlockSpec((1,) + thin.shape, lambda i, spot: (spot[0], 0, 0)),
                pl.BlockSpec(
                    (3, 1, d_own, window),
                    lambda i, spot: (0, jnp.where(i < hi, n + i, spot[0]), 0, 0),
                ),
                pl.BlockSpec((1, 1) + cot.shape[1:], lambda i, spot: (spot[1], spot[2], 0, 0)),
            ],
        ),
        out_shape=[jax.ShapeDtypeStruct(shape, BF16) for shape in outs],
        compiler_params=pltpu.CompilerParams(vmem_limit_bytes=GRANT),
        name="place",
    )(spot, *rec, *feed, *gates, thin, cot)


def bring_weights(grid, rec, gates, thin, cot):
    n, hi, tensor = grid.n, grid.hi, grid.tensor
    far = pl.BlockSpec(memory_space=pl.ANY)
    arrays = (rec, gates, thin, cot)
    cube = grid.inner_size.bit_length() - 1
    return pl.pallas_call(
        functools.partial(weights_kernel, n, tensor),
        out_shape=[jax.ShapeDtypeStruct(a.shape, a.dtype) for a in arrays],
        in_specs=[far] * len(arrays),
        out_specs=[far] * len(arrays),
        input_output_aliases={i: i for i in range(len(arrays))},
        scratch_shapes=[
            chain_sems(cube, rec.shape[0]),
            chain_sems(cube),
            chain_sems(cube),
            chain_sems(1),
        ],
        compiler_params=pltpu.CompilerParams(
            collective_id=0, has_side_effects=True, vmem_limit_bytes=GRANT
        ),
        name="bring_weights",
    )(*arrays)


def by_rows(rows, step, act):
    def one(i, carry):
        act(pl.ds(pl.multiple_of(i * step, step), step))
        return carry

    lax.fori_loop(0, rows // step, one, 0)


STEP = 16
HALVES = 2


GELU_SLOPE = 0.7978845608028654
GELU_CUBE = 0.044715
HALO = 8
GELU_SHIFT, INPUT_SHIFT, TAPS, CONV_SHIFT, INLET_SHIFT, FORGET_SHIFT, RATE_SOFT, RATE_SIGMOID = 0, 1, 2, 6, 7, 8, 9, 10
LANE_ROWS = 16


def gelu_of(v):
    bent = jnp.tanh(GELU_SLOPE * (v + GELU_CUBE * (v * v * v)))
    half = 0.5 * (1.0 + bent)
    slope = half + 0.5 * v * (1.0 - bent * bent) * (GELU_SLOPE * (1.0 + 3.0 * GELU_CUBE * (v * v)))
    return v * half, slope


def minus_expm1(x):
    series = jnp.ones_like(x)
    for k in range(9, 1, -1):
        series = 1.0 + series * x * (1.0 / k)
    return jnp.where(x > -0.5, -x * series, 1.0 - jnp.exp(x))


def decay_of(forget, soft, starts):
    log_decay = -8.0 * forget * soft
    decay = jnp.where(starts, 0.0, jnp.exp(log_decay))
    scaler = jnp.where(starts, 1.0, jnp.sqrt(minus_expm1(2.0 * log_decay)))
    return decay, scaler


def tile_scan(a, b, state_in, decay_in, reverse):
    place = lax.broadcasted_iota(jnp.int32, a.shape, 0)
    for by in (1, 2, 4):
        turn = 8 - by if reverse else by
        ok = place < 8 - by if reverse else place >= by
        b = jnp.where(ok, a * pltpu.roll(b, turn, 0) + b, b)
        a = jnp.where(ok, a * pltpu.roll(a, turn, 0), a)
    return a * decay_in, b + a * state_in


def scan_rows(seqs, length, width, read, write, reverse):
    tiles = length // 8
    last = 0 if reverse else 7

    def one(i, carry):
        tile = tiles - 1 - i if reverse else i
        after = []
        for s in range(seqs):
            decay_in, state_in = carry[s]
            at = pl.ds(pl.multiple_of(s * length + tile * 8, 8), 8)
            a, b = tile_scan(*read(at), state_in, decay_in, reverse)
            write(at, a, b)
            after.append(
                tuple(jnp.broadcast_to(v[last : last + 1], (8, width)) for v in (a, b))
            )
        return tuple(after)

    start = (jnp.ones((8, width), F32), jnp.zeros((8, width), F32))
    lax.fori_loop(0, tiles, one, (start,) * seqs)


class Prefix:
    def __init__(self, spot, seqs, reverse, tots, gots, line, cube_sems, line_sems):
        self.spot, self.seqs, self.reverse = spot, seqs, reverse
        self.tots, self.gots, self.line = tots, gots, line
        self.cube_sems, self.line_sems = cube_sems, line_sems

    def line_copy(self, place, sender):
        stages = len(self.spot.bits)
        return pltpu.make_async_remote_copy(
            src_ref=self.tots.at[stages],
            dst_ref=self.line.at[sender],
            send_sem=self.line_sems.at[0, place],
            recv_sem=self.line_sems.at[1, sender],
            device_id=self.spot.line(place),
            device_id_type=MESH,
        )

    def run(self):
        spot, seqs, hi = self.spot, self.seqs, self.spot.hi
        a, b = slice(0, seqs), slice(seqs, 2 * seqs)
        width = self.tots.shape[2]
        enter_a, enter_b = jnp.ones((seqs, width), F32), jnp.zeros((seqs, width), F32)
        for stage, bit in enumerate(spot.bits):
            copy = remote(
                self.tots.at[stage], self.gots.at[stage], self.cube_sems, stage, spot.flip(bit)
            )
            copy.start()
            copy.wait()
            mine_a, mine_b = self.tots[stage, a, :], self.tots[stage, b, :]
            got_a, got_b = self.gots[stage, a, :], self.gots[stage, b, :]
            after = spot.bit(bit) == (0 if self.reverse else 1)
            enter_b = jnp.where(after, enter_a * got_b + enter_b, enter_b)
            enter_a = jnp.where(after, enter_a * got_a, enter_a)
            self.tots[stage + 1, a, :] = mine_a * got_a
            self.tots[stage + 1, b, :] = jnp.where(
                after, mine_a * got_b + mine_b, got_a * mine_b + got_b
            )
            self.tots[stage + 1, 2 * seqs :, :] = jnp.zeros((8 - 2 * seqs, width), F32)
        for distance in range(1, hi):
            self.line_copy(spot.away(distance), spot.z).start()
        for distance in range(1, hi):
            place = spot.away(distance)
            self.line_copy(place, place).wait_recv()
            self.line_copy(place, spot.z).wait_send()
        come = jnp.zeros((seqs, width), F32)
        for place in reversed(range(hi)) if self.reverse else range(hi):
            before = spot.z < place if self.reverse else spot.z > place
            come = jnp.where(before, self.line[place, a, :] * come + self.line[place, b, :], come)
        return enter_a * come + enter_b


def prefix_scratch(grid, channels):
    stages = grid.inner_size.bit_length() - 1
    return [
        pltpu.VMEM((stages + 1, 8, channels), F32),
        pltpu.VMEM((stages, 8, channels), F32),
        pltpu.VMEM((grid.hi, 8, channels), F32),
        pltpu.SemaphoreType.DMA((2, stages)),
        pltpu.SemaphoreType.DMA((2, grid.hi)),
    ]


def forward_kernel(
    n, tensor, seqs, heads,
    x, halo, gain, w_input, w_gelu, w_inlet, w_forget, lanes, flags, w_out, shift, gain_second, feed,
    normed, ext, conv, gelu_pre, inlet_pre, forget_pre, cum, local, entered, mixed, resid, second,
    feed_all,
    held, factor, addend, part, out, got, tots, gots, line, cube_sems, line_sems, swap_sems, feed_sems,
):
    del feed
    spot = Spot(n, tensor)
    hi = spot.hi
    rows = x.shape[0]
    length = rows // seqs
    width = conv.shape[1]
    step = pl.program_id(0)
    cube = [spot.flip(bit) for bit in spot.bits]
    turns = FeedTurns(spot, feed_all, feed_sems, cube)
    @pl.when(step == 0)
    def _():
        spot.greet(*cube, spot.cross)
        turns.start(1)
        turns.start(0)

        def norm(source, at, to):
            value = source[at, :].astype(F32)
            scale = lax.rsqrt(jnp.mean(value * value, axis=-1, keepdims=True) + 1e-06)
            value = (value * scale * gain[...]).astype(BF16)
            held[pl.ds(pl.multiple_of(at.start + to, STEP), STEP), :] = value
            return value

        def main(at):
            normed[at, :] = norm(x, at, 0)

        by_rows(rows, STEP, main)
        by_rows(halo.shape[0], STEP, lambda at: norm(halo, at, rows))

    @pl.when(step < heads)
    def _():
        table = lanes[...]
        cols = pl.ds(pl.multiple_of(step * width, width), width)

        def row(i):
            return table[i : i + 1]

        branch = (dot(held[...], w_input[0]) + row(INPUT_SHIFT)).astype(BF16)
        gelu_pre[:, cols] = dot(held[0:rows, :], w_gelu[0]) + row(GELU_SHIFT)
        for s in range(seqs):
            here = slice(s * length, (s + 1) * length)
            front = rows + s * HALO
            longer = jnp.concatenate(
                [branch[front : front + HALO].astype(F32), branch[here].astype(F32)], axis=0
            )
            ext[s] = longer.astype(BF16)
            total = row(CONV_SHIFT) + row(TAPS) * longer[HALO:]
            for k in range(1, CONV):
                moved = pltpu.roll(longer, k, 0)[HALO:]
                total = total + jnp.where(flags[here, k : k + 1] > 0.5, row(TAPS + k) * moved, 0.0)
            conv[here, :] = total.astype(BF16)
        blocks = conv[...]
        inlet_pre[...] = dot(blocks, w_inlet[0]) + row(INLET_SHIFT)
        forget_pre[...] = dot(blocks, w_forget[0]) + row(FORGET_SHIFT)

        def terms(at):
            starts = flags[at, 0:1] > 0.5
            decay, scaler = decay_of(jax.nn.sigmoid(forget_pre[at, :]), row(RATE_SOFT), starts)
            factor[at, :] = decay
            addend[at, :] = scaler * jax.nn.sigmoid(inlet_pre[at, :]) * conv[at, :].astype(F32)

        by_rows(rows, 32, terms)

        def write(at, a, b):
            cum[at, cols] = a
            local[at, cols] = b

        scan_rows(seqs, length, width, lambda at: (factor[at, :], addend[at, :]), write, False)

    @pl.when(step == heads)
    def _():
        tots[0] = jnp.zeros_like(tots[0])
        for s in range(seqs):
            tots[0, s : s + 1, :] = cum[(s + 1) * length - 8 : (s + 1) * length, :][7:8]
            tots[0, seqs + s : seqs + s + 1, :] = local[(s + 1) * length - 8 : (s + 1) * length, :][7:8]
        enter = Prefix(spot, seqs, False, tots, gots, line, cube_sems, line_sems).run()
        turns.start(3)
        turns.onward(1)
        entered[...] = jnp.zeros_like(entered)
        entered[0:seqs, :] = enter
        for s in range(seqs):

            def mix(at, s=s):
                here = pl.ds(pl.multiple_of(s * length + at.start, STEP), STEP)
                state = local[here, :] + cum[here, :] * enter[s : s + 1]
                mixed[here, :] = (state * gelu_of(gelu_pre[here, :])[0]).astype(BF16)

            by_rows(length, STEP, mix)
        turns.start(2)
        values = mixed[...]
        own_rows = resid.shape[0]

        def branch(j, carry):
            at = pl.ds(pl.multiple_of(j * 256, 256), 256)
            value = dot_nt(values, w_out[0, at, :])
            for side in range(tensor):
                part[side, :, at] = value[side * own_rows : (side + 1) * own_rows]
            return carry

        lax.fori_loop(0, x.shape[1] // 256, branch, 0)

        def put(at):
            out[at, :] = part[1 - spot.t, at, :].astype(BF16)

        by_rows(own_rows, STEP, put)
        copy = remote(out, got, swap_sems, 0, spot.cross)
        copy.start()
        copy.wait()

        def norm(at):
            own = x[pl.ds(pl.multiple_of(spot.t * own_rows + at.start, STEP), STEP), :].astype(F32)
            value = own + (part[spot.t, at, :] + got[at, :].astype(F32) + shift[...])
            resid[at, :] = value
            scale = lax.rsqrt(jnp.mean(value * value, axis=-1, keepdims=True) + 1e-06)
            second[at, :] = (value * scale * gain_second[...]).astype(BF16)

        by_rows(own_rows, STEP, norm)
        turns.second(0)
        turns.onward(3)
        turns.second(1)
        turns.onward(2)
        turns.second(3)
        turns.second(2)
        turns.finish()


def forward_recurrence(
    grid, x, halo, gain, rec, inlet, forget, lanes, flags, shift, gain_second, feed, seqs
):
    rows, d = x.shape
    heads, width = inlet.shape[:2]
    channels = heads * width
    longer = rows // seqs + HALO
    own_rows = rows // grid.tensor

    def head_of(i):
        return jnp.minimum(i, heads - 1)

    def fixed(a):
        zeros = (0,) * len(a.shape)
        return pl.BlockSpec(a.shape, lambda i: zeros, pipeline_mode=pl.Buffered(1))

    def column(count):
        return pl.BlockSpec((count, width), lambda i: (0, head_of(i)))

    def weight(k):
        return pl.BlockSpec((1, d, width), lambda i: (k, 0, head_of(i)))

    head = pl.BlockSpec((1, width, width), lambda i: (head_of(i), 0, 0))
    far = pl.BlockSpec(memory_space=pl.ANY)
    wide = jax.ShapeDtypeStruct((rows, channels), F32)
    outs = [
        jax.ShapeDtypeStruct((rows, d), BF16),
        jax.ShapeDtypeStruct((seqs, longer, channels), BF16),
        jax.ShapeDtypeStruct((rows, channels), BF16),
        wide,
        wide,
        wide,
        wide,
        wide,
        jax.ShapeDtypeStruct((8, channels), F32),
        jax.ShapeDtypeStruct((rows, channels), BF16),
        jax.ShapeDtypeStruct((own_rows, d), F32),
        jax.ShapeDtypeStruct((own_rows, d), BF16),
        jax.ShapeDtypeStruct(feed.shape, BF16),
    ]
    return pl.pallas_call(
        functools.partial(forward_kernel, grid.n, grid.tensor, seqs, heads),
        grid=(heads + 1,),
        out_shape=outs,
        in_specs=[fixed(x), fixed(halo), fixed(gain), weight(0), weight(1), head, head]
        + [column(LANE_ROWS), fixed(flags)]
        + [pl.BlockSpec((1, d, channels), lambda i: (2, 0, 0), pipeline_mode=pl.Buffered(1))]
        + [fixed(shift), fixed(gain_second), far],
        out_specs=[
            fixed(outs[0]),
            pl.BlockSpec((seqs, longer, width), lambda i: (0, 0, head_of(i))),
            column(rows),
            fixed(wide),
            column(rows),
            column(rows),
        ]
        + [fixed(a) for a in outs[6:12]]
        + [far],
        input_output_aliases={12: 12},
        scratch_shapes=[
            pltpu.VMEM((rows + halo.shape[0], d), BF16),
            pltpu.VMEM((rows, width), F32),
            pltpu.VMEM((rows, width), F32),
            pltpu.VMEM((grid.tensor, own_rows, d), F32),
            pltpu.VMEM((own_rows, d), BF16),
            pltpu.VMEM((own_rows, d), BF16),
        ]
        + prefix_scratch(grid, channels)
        + [pltpu.SemaphoreType.DMA((2, 1)), turn_sems(grid, feed.shape[0])],
        compiler_params=pltpu.CompilerParams(
            collective_id=1, has_side_effects=True, vmem_limit_bytes=GRANT
        ),
        name="forward_recurrence",
    )(x, halo, gain, rec, rec, inlet, forget, lanes, flags, rec, shift, gain_second, feed)


def place_feed_kernel(unit_tiles, spot, gate, up, down, cot, feed_all, cot_all):
    step = pl.program_id(0)
    width = feed_all.shape[3]
    tiles = width // LANE

    @pl.when(step == 0)
    def _():
        cot_all[0, 0] = cot[0]

    place = jnp.where(step < LINE, step, spot[1])
    tile = jnp.minimum(place * tiles, unit_tiles - tiles)
    for m, source in enumerate((gate, up, down)):
        feed_all[m, 0] = source[:, pl.ds(pl.multiple_of(tile * LANE, LANE), width)]


def place_feed(grid, feed, cot):
    n, hi = grid.n, grid.hi
    d_own, units = feed[0].shape
    unit_tiles = units // LANE
    window = -(-unit_tiles // hi) * LANE
    spot = jnp.stack([grid.w, grid.z, grid.t])
    outs = [(3, n + hi, d_own, window), (hi,) + cot.shape]
    return pl.pallas_call(
        functools.partial(place_feed_kernel, unit_tiles),
        grid_spec=pltpu.PrefetchScalarGridSpec(
            num_scalar_prefetch=1,
            grid=(hi + 1,),
            in_specs=[pl.BlockSpec(a.shape, lambda i, spot: (0, 0)) for a in feed]
            + [pl.BlockSpec((1,) + cot.shape[1:], lambda i, spot: (spot[2], 0, 0))],
            out_specs=[
                pl.BlockSpec(
                    (3, 1, d_own, window),
                    lambda i, spot: (0, jnp.where(i < hi, n + i, spot[0]), 0, 0),
                ),
                pl.BlockSpec((1, 1) + cot.shape[1:], lambda i, spot: (spot[1], spot[2], 0, 0)),
            ],
        ),
        out_shape=[jax.ShapeDtypeStruct(shape, BF16) for shape in outs],
        compiler_params=pltpu.CompilerParams(vmem_limit_bytes=GRANT),
        name="place",
    )(spot, *feed, cot)


def gather_kernel(
    n, tensor, seqs, thin_lanes,
    x, halo, flags, wide_in, gelu_in, out_in, inlet_in, forget_in, thin_in, feed, cot,
    entered, mixed, resid, second, lanes, table, gates_out,
    normed_out, ext_out, conv_out, gelu_out, inlet_out, forget_out, cum_out, local_out, rec_out, feed_all, cot_all,
    normed, ext, conv, gelu_pre, inlet_pre, forget_pre, cum, local, out_sems,
    rec, gates, thin, held, factor, addend, part, out, got, tots, gots, line,
    rec_sems, gates_sems, thin_sems, feed_sems, cot_sems, cube_sems, line_sems, swap_sems, own_sem,
):
    del feed, cot
    spot = Spot(n, tensor)
    hi = spot.hi
    rows, d = x.shape
    length = rows // seqs
    heads, d_own, width = wide_in.shape
    cube = [spot.flip(bit) for bit in spot.bits]

    def index(place, k):
        return place * spot.inner_size + jnp.bitwise_xor(spot.inner, k)

    chains = [
        Chain(spot, lambda place, k: thin.at[index(place, k)], thin_sems, cube),
        Chain(spot, lambda place, k: gates.at[:, index(place, k)], gates_sems, cube),
    ] + [
        Chain(spot, lambda place, k, m=m: rec.at[m, index(place, k)], rec_sems.at[m], cube)
        for m in range(3)
    ]
    turns = FeedTurns(spot, feed_all, feed_sems, cube)
    cots = Chain(
        spot,
        lambda place, k: cot_all.at[place, lax.rem(spot.t + k, tensor)],
        cot_sems,
        [spot.cross],
    )
    for m, source in enumerate((wide_in, gelu_in, out_in)):
        for h in range(heads):
            rec[m, spot.w, :, h * width : (h + 1) * width] = source[h]
    for m, source in enumerate((inlet_in, forget_in)):
        for h in range(heads):
            gates[m * heads + h, spot.w] = source[h]
    thin[spot.w] = thin_in[...]
    spot.greet(*cube, spot.cross)
    for chain in chains:
        chain.first()
    cots.fans.hand_on(spot.z, 0)
    for s in range(1, hi):
        for chain in chains:
            chain.onward(s)
        if s == 1:
            cots.first_line()
        else:
            cots.onward(s - 1)
        for chain in chains:
            chain.second(s - 1)
    turns.start(1)
    for chain in chains:
        chain.second(hi - 1)
    for chain in chains:
        chain.finish()
    turns.start(0)
    keep = pltpu.make_async_copy(rec, rec_out, own_sem)
    keep.start()

    sums = thin[0].astype(F32)
    for i in range(1, n):
        sums = sums + thin[i].astype(F32)
    table[...] = sums
    rate = sums[RATE_SOFT : RATE_SOFT + 1]
    lanes[0:RATE_SOFT, :] = sums[0:RATE_SOFT]
    soft = jnp.maximum(rate, 0.0) + jnp.log1p(jnp.exp(-jnp.abs(rate)))
    lanes[RATE_SOFT : RATE_SOFT + 1, :] = soft
    lanes[RATE_SIGMOID : RATE_SIGMOID + 1, :] = jax.nn.sigmoid(rate)
    lanes[RATE_SIGMOID + 1 :, :] = jnp.zeros((LANE_ROWS - RATE_SIGMOID - 1, sums.shape[1]), F32)
    per = d // sums.shape[1]

    def across(i):
        first = thin_lanes + i * per
        return jnp.concatenate([sums[first + j : first + j + 1] for j in range(per)], axis=1)

    gain, shift, gain_second = across(0), across(1), across(2)

    def norm_first(source, at, to):
        value = source[at, :].astype(F32)
        scale = lax.rsqrt(jnp.mean(value * value, axis=-1, keepdims=True) + 1e-06)
        value = (value * scale * gain).astype(BF16)
        held[pl.ds(pl.multiple_of(at.start + to, STEP), STEP), :] = value
        return value

    def main(at):
        normed[at, :] = norm_first(x, at, 0)

    by_rows(rows, STEP, main)
    by_rows(halo.shape[0], STEP, lambda at: norm_first(halo, at, rows))

    def work(step, none):
        cols = pl.ds(pl.multiple_of(step * width, width), width)

        def row(i):
            return lanes[i : i + 1, cols]

        def matrix(m):
            return rec[m, :, :, cols].reshape(d, width)

        branch = (dot(held[...], matrix(0)) + row(INPUT_SHIFT)).astype(BF16)
        gelu_pre[:, cols] = dot(held[0:rows, :], matrix(1)) + row(GELU_SHIFT)
        for s in range(seqs):
            here = slice(s * length, (s + 1) * length)
            front = rows + s * HALO
            longer = jnp.concatenate(
                [branch[front : front + HALO].astype(F32), branch[here].astype(F32)], axis=0
            )
            ext[s, :, cols] = longer.astype(BF16)
            total = row(CONV_SHIFT) + row(TAPS) * longer[HALO:]
            for k in range(1, CONV):
                moved = pltpu.roll(longer, k, 0)[HALO:]
                total = total + jnp.where(flags[here, k : k + 1] > 0.5, row(TAPS + k) * moved, 0.0)
            conv[here, cols] = total.astype(BF16)
        blocks = conv[:, cols]
        for m, (to, bias) in enumerate(((inlet_pre, INLET_SHIFT), (forget_pre, FORGET_SHIFT))):
            gate = gates[m * heads + step].reshape(width, width)
            gates_out[m * heads + step] = gate
            to[:, cols] = dot(blocks, gate) + row(bias)

        def terms(at):
            starts = flags[at, 0:1] > 0.5
            decay, scaler = decay_of(jax.nn.sigmoid(forget_pre[at, cols]), row(RATE_SOFT), starts)
            factor[at, :] = decay
            addend[at, :] = scaler * jax.nn.sigmoid(inlet_pre[at, cols]) * conv[at, cols].astype(F32)

        by_rows(rows, 32, terms)

        def write(at, a, b):
            cum[at, cols] = a
            local[at, cols] = b

        scan_rows(seqs, length, width, lambda at: (factor[at, :], addend[at, :]), write, False)
        return none

    lax.fori_loop(0, heads, work, 0)
    tots[0] = jnp.zeros_like(tots[0])
    for s in range(seqs):
        tots[0, s : s + 1, :] = cum[(s + 1) * length - 8 : (s + 1) * length, :][7:8]
        tots[0, seqs + s : seqs + s + 1, :] = local[(s + 1) * length - 8 : (s + 1) * length, :][7:8]
    outs = [
        pltpu.make_async_copy(held_here, to, out_sems.at[i])
        for i, (held_here, to) in enumerate(
            (
                (normed, normed_out),
                (ext, ext_out),
                (conv, conv_out),
                (gelu_pre, gelu_out),
                (inlet_pre, inlet_out),
                (forget_pre, forget_out),
                (cum, cum_out),
                (local, local_out),
            )
        )
    ]
    for copy in outs:
        copy.start()
    enter = Prefix(spot, seqs, False, tots, gots, line, cube_sems, line_sems).run()
    turns.start(3)
    turns.onward(1)
    cots.onward(3)
    turns.start(2)
    entered[...] = jnp.zeros_like(entered)
    entered[0:seqs, :] = enter
    for s in range(seqs):

        def mix(at, s=s):
            here = pl.ds(pl.multiple_of(s * length + at.start, STEP), STEP)
            state = local[here, :] + cum[here, :] * enter[s : s + 1]
            mixed[here, :] = (state * gelu_of(gelu_pre[here, :])[0]).astype(BF16)

        by_rows(length, STEP, mix)
    values = mixed[...]
    own_rows = resid.shape[0]
    each, slab = n // hi, d // hi

    def branch(j, none):
        at = pl.ds(pl.multiple_of(j * slab, LANE), slab)
        weights = rec[2, pl.ds(j * each, each)].reshape(slab, heads * width)
        value = dot_nt(values, weights)
        for side in range(tensor):
            part[side, :, at] = value[side * own_rows : (side + 1) * own_rows]
        return none

    lax.fori_loop(0, hi, branch, 0)

    def put(at):
        out[at, :] = part[1 - spot.t, at, :].astype(BF16)

    by_rows(own_rows, STEP, put)
    copy = remote(out, got, swap_sems, 0, spot.cross)
    copy.start()
    copy.wait()

    def norm(at):
        own = x[pl.ds(pl.multiple_of(spot.t * own_rows + at.start, STEP), STEP), :].astype(F32)
        value = own + (part[spot.t, at, :] + got[at, :].astype(F32) + shift)
        resid[at, :] = value
        scale = lax.rsqrt(jnp.mean(value * value, axis=-1, keepdims=True) + 1e-06)
        second[at, :] = (value * scale * gain_second).astype(BF16)

    by_rows(own_rows, STEP, norm)
    turns.onward(3)
    turns.second(0)
    turns.second(1)
    turns.onward(2)
    turns.second(3)
    turns.second(2)
    turns.finish()
    cots.finish()
    keep.wait()
    for copy in outs:
        copy.wait()


def gather_recurrence(grid, x, halo, flags, rec, gates, thin, thin_lanes, feed, cot, seqs):
    rows, d = x.shape
    heads, d_own, width = rec[0].shape
    lane_own = gates[0].shape[1]
    n = grid.n
    channels = heads * width
    longer = rows // seqs + HALO
    own_rows = rows // grid.tensor
    near = pl.BlockSpec(memory_space=pltpu.VMEM)
    far = pl.BlockSpec(memory_space=pl.ANY)
    wide = jax.ShapeDtypeStruct((rows, channels), F32)
    whole = (3, n, d_own, channels)
    cube = grid.inner_size.bit_length() - 1
    saved = [
        jax.ShapeDtypeStruct((rows, d), BF16),
        jax.ShapeDtypeStruct((seqs, longer, channels), BF16),
        jax.ShapeDtypeStruct((rows, channels), BF16),
    ] + [wide] * 5
    outs = [
        jax.ShapeDtypeStruct((8, channels), F32),
        jax.ShapeDtypeStruct((rows, channels), BF16),
        jax.ShapeDtypeStruct((own_rows, d), F32),
        jax.ShapeDtypeStruct((own_rows, d), BF16),
        jax.ShapeDtypeStruct((LANE_ROWS, channels), F32),
        jax.ShapeDtypeStruct(thin.shape, F32),
        jax.ShapeDtypeStruct((2 * heads, width, width), BF16),
    ]
    moved = [
        jax.ShapeDtypeStruct(whole, BF16),
        jax.ShapeDtypeStruct(feed.shape, BF16),
        jax.ShapeDtypeStruct(cot.shape, BF16),
    ]
    return pl.pallas_call(
        functools.partial(gather_kernel, n, grid.tensor, seqs, thin_lanes),
        out_shape=outs + saved + moved,
        in_specs=[near] * 9 + [far] * 2,
        out_specs=[near] * len(outs) + [far] * (len(saved) + len(moved)),
        input_output_aliases={9: 16, 10: 17},
        scratch_shapes=[pltpu.VMEM(a.shape, a.dtype) for a in saved]
        + [pltpu.SemaphoreType.DMA((len(saved),))]
        + [
            pltpu.VMEM(whole, BF16),
            pltpu.VMEM((2 * heads, n, lane_own, width), BF16),
            pltpu.VMEM((n,) + thin.shape, BF16),
            pltpu.VMEM((rows + halo.shape[0], d), BF16),
            pltpu.VMEM((rows, width), F32),
            pltpu.VMEM((rows, width), F32),
            pltpu.VMEM((grid.tensor, own_rows, d), F32),
            pltpu.VMEM((own_rows, d), BF16),
            pltpu.VMEM((own_rows, d), BF16),
        ]
        + prefix_scratch(grid, channels)[:3]
        + [
            chain_sems(cube, 3),
            chain_sems(cube),
            chain_sems(cube),
            turn_sems(grid, feed.shape[0]),
            chain_sems(1),
        ]
        + prefix_scratch(grid, channels)[3:]
        + [pltpu.SemaphoreType.DMA((2, 1)), pltpu.SemaphoreType.DMA],
        compiler_params=pltpu.CompilerParams(
            collective_id=6, has_side_effects=True, vmem_limit_bytes=GRANT
        ),
        name="gather_recurrence",
    )(x, halo, flags, *rec, *gates, thin, feed, cot)


def leave_kernel(
    n, tensor, seqs, branch, w_out, gelu_pre, local, cum, inlet_pre, forget_pre, conv, ext, entered,
    w_inlet, w_forget, lanes, flags, feed_part, resid,
    gelu_low, input_low, gate_grads, lane_grads, shift_grad, own_out,
    tail, carried, factor, addend, back, rim, tots, gots, line, cube_sems, line_sems, rim_sems,
    part, sums_got, sums_line, sums_cross, sums_sems,
):
    spot = Spot(n, tensor)
    every, channels = conv.shape
    length = every // seqs
    heads, width = w_inlet.shape[:2]
    behind = {"wide": lax.rem(spot.w + n - 1, n)}
    ahead = {"wide": lax.rem(spot.w + 1, n)}
    spot.greet(*[spot.flip(bit) for bit in spot.bits], behind, ahead, spot.cross)
    for place in range(spot.hi):
        for side in range(tensor):

            def put(at, place=place, side=side):
                part[place, side, at, :] = feed_part[place, side, at, :]

            by_rows(resid.shape[0], STEP, put)
    half = resid.shape[0] // HALVES
    sums = [
        Rows(spot, part, sums_got, sums_line, sums_cross.at[i], sums_sems.at[i], i * half, half)
        for i in range(HALVES)
    ]
    for k in range(spot.hi):
        for each in sums:
            each.start(k)
    tots[0] = jnp.zeros_like(tots[0])
    lane_grads[...] = jnp.zeros_like(lane_grads)
    shift_grad[...] = jnp.zeros_like(shift_grad)

    def add(at):
        shift_grad[...] += jnp.sum(branch[at, :].astype(F32).reshape(2, 8, -1), axis=0)

    by_rows(every, STEP, add)

    def decays(at, cols):
        soft = lanes[RATE_SOFT : RATE_SOFT + 1, cols]
        return decay_of(jax.nn.sigmoid(forget_pre[at, cols]), soft, flags[at, 0:1] > 0.5)

    def upward(h, none):
        cols = pl.ds(pl.multiple_of(h * width, width), width)
        grad = dot(branch[...], w_out[0, :, cols])
        gelu, slope = gelu_of(gelu_pre[:, cols])
        for s in range(seqs):
            here = slice(s * length, (s + 1) * length)
            state = local[here, cols] + cum[here, cols] * entered[s : s + 1, cols]
            low = (grad[here] * state * slope[here]).astype(BF16)
            gelu_low[here, cols] = low
            lane_grads[0:1, cols] += jnp.sum(low.astype(F32), axis=0, keepdims=True)
            decay, _ = decays(here, cols)
            place = lax.broadcasted_iota(jnp.int32, (length, width), 0)
            factor[here, :] = jnp.where(place < length - 1, pltpu.roll(decay, length - 1, 0), 1.0)
        addend[...] = grad * gelu

        def write(at, a, b):
            tail[at, cols] = a
            carried[at, cols] = b

        scan_rows(seqs, length, width, lambda at: (factor[at, :], addend[at, :]), write, True)
        for s in range(seqs):
            first = slice(s * length, s * length + 8)
            decay, _ = decays(first, cols)
            tots[0, s : s + 1, cols] = decay[0:1] * tail[first, cols][0:1]
            tots[0, seqs + s : seqs + s + 1, cols] = decay[0:1] * carried[first, cols][0:1]
        return none

    lax.fori_loop(0, heads // 2, upward, 0)
    for each in sums:
        each.along(1)
    lax.fori_loop(heads // 2, heads, upward, 0)
    come = Prefix(spot, seqs, True, tots, gots, line, cube_sems, line_sems).run()
    for each in sums:
        each.along(2)
    tots[0, 0:seqs, :] = come

    def downward(h, none):
        cols = pl.ds(pl.multiple_of(h * width, width), width)

        def row(i):
            return lanes[i : i + 1, cols]

        sums = []
        for s in range(seqs):
            here = slice(s * length, (s + 1) * length)
            place = lax.broadcasted_iota(jnp.int32, (length, width), 0)
            starts = flags[here, 0:1] > 0.5
            blocks = conv[here, cols].astype(F32)
            enter = entered[s : s + 1, cols]
            state = local[here, cols] + cum[here, cols] * enter
            before = jnp.where(place > 0, pltpu.roll(state, 1, 0), enter)
            carry = carried[here, cols] + tail[here, cols] * tots[0, s : s + 1, cols]
            inlet = jax.nn.sigmoid(inlet_pre[here, cols])
            forget = jax.nn.sigmoid(forget_pre[here, cols])
            soft = row(RATE_SOFT)
            decay, scaler = decay_of(forget, soft, starts)
            log_grad = jnp.where(
                starts, 0.0, carry * before * decay - carry * inlet * blocks * (decay * decay) / scaler
            )
            rate_grad = jnp.sum(log_grad * (-8.0 * forget), axis=0, keepdims=True) * row(RATE_SIGMOID)
            inlet_low = (carry * scaler * blocks * (inlet * (1.0 - inlet))).astype(BF16)
            forget_low = (log_grad * (-8.0 * soft) * (forget * (1.0 - forget))).astype(BF16)
            conv_grad = (
                carry * scaler * inlet
                + dot_nt(inlet_low, w_inlet[h])
                + dot_nt(forget_low, w_forget[h])
            )
            longer = ext[s, :, cols].astype(F32)
            zeros = jnp.zeros((HALO, width), F32)
            total = jnp.concatenate([zeros, row(TAPS) * conv_grad], axis=0)
            taps = [jnp.sum(conv_grad * longer[HALO:], axis=0, keepdims=True)]
            for k in range(1, CONV):
                masked = jnp.where(flags[here, k : k + 1] > 0.5, conv_grad, 0.0)
                moved = pltpu.roll(longer, k, 0)[HALO:]
                taps.append(jnp.sum(masked * moved, axis=0, keepdims=True))
                sent = jnp.concatenate([zeros, row(TAPS + k) * masked], axis=0)
                total = total + pltpu.roll(sent, HALO + length - k, 0)
            back[s, :, cols] = total
            lows = [jnp.sum(v.astype(F32), axis=0, keepdims=True) for v in (inlet_low, forget_low)]
            sums.append(taps + [jnp.sum(conv_grad, axis=0, keepdims=True)] + lows + [rate_grad])
            for m, low in enumerate((inlet_low, forget_low)):
                factor[here, :] = low.astype(F32) if m == 0 else factor[here, :]
                addend[here, :] = low.astype(F32) if m == 1 else addend[here, :]
        for i in range(len(sums[0])):
            lane_grads[2 + i : 3 + i, cols] = sum(each[i] for each in sums[1:]) + sums[0][i]
        for m, low in enumerate((factor, addend)):
            gate_grads[m, h] = dot_tn(conv[:, cols], low[...].astype(BF16)).astype(BF16)
        return none

    lax.fori_loop(0, heads, downward, 0)
    copy = remote(back.at[:, 0:HALO, :], rim, rim_sems, 0, behind)
    copy.start()
    for s in range(3, spot.hi):
        for each in sums:
            each.along(s)
    copy.wait()

    def give(h, none):
        cols = pl.ds(pl.multiple_of(h * width, width), width)
        total = jnp.zeros((1, width), F32)
        for s in range(seqs):
            edge = jnp.where(spot.w < n - 1, rim[s, :, cols], 0.0)
            value = back[s, HALO:, cols]
            value = jnp.concatenate([value[: length - HALO], value[length - HALO :] + edge], axis=0)
            low = value.astype(BF16)
            input_low[s * length : (s + 1) * length, cols] = low
            total = total + jnp.sum(low.astype(F32), axis=0, keepdims=True)
        lane_grads[1:2, cols] = total
        return none

    lax.fori_loop(0, heads, give, 0)

    def done(at, total):
        own_out[at, :] = (resid[at, :] + total).astype(BF16)

    for each in sums:
        each.end(done)
    for each in sums:
        each.finish()


def leave_recurrence(
    grid, branch, rec, gelu_pre, local, cum, inlet_pre, forget_pre, conv, ext, entered, gates, lanes,
    flags, feed_part, resid, seqs,
):
    every, channels = conv.shape
    d = branch.shape[1]
    heads, width = gates.shape[0] // 2, gates.shape[1]
    near = pl.BlockSpec(memory_space=pltpu.VMEM)
    low = jax.ShapeDtypeStruct((every, channels), BF16)
    return pl.pallas_call(
        functools.partial(leave_kernel, grid.n, grid.tensor, seqs),
        grid=(1,),
        out_shape=[
            low,
            low,
            jax.ShapeDtypeStruct((2, heads, width, width), BF16),
            jax.ShapeDtypeStruct((LANE_ROWS, channels), F32),
            jax.ShapeDtypeStruct((8, d), F32),
            jax.ShapeDtypeStruct(resid.shape, BF16),
        ],
        in_specs=[near, pl.BlockSpec((1, d, channels), lambda i: (2, 0, 0))]
        + [near] * 8
        + [pl.BlockSpec((heads, width, width), lambda i, m=m: (m, 0, 0)) for m in range(2)]
        + [near] * 4,
        out_specs=[near] * 6,
        scratch_shapes=[
            pltpu.VMEM((every, channels), F32),
            pltpu.VMEM((every, channels), F32),
            pltpu.VMEM((every, width), F32),
            pltpu.VMEM((every, width), F32),
            pltpu.VMEM((seqs, every // seqs + HALO, channels), F32),
            pltpu.VMEM((seqs, HALO, channels), F32),
        ]
        + prefix_scratch(grid, channels)
        + [pltpu.SemaphoreType.DMA((2, 1)), pltpu.VMEM(feed_part.shape, BF16)]
        + rows_scratch(grid, *resid.shape)[:2]
        + rows_sems(grid)[:2],
        compiler_params=pltpu.CompilerParams(
            collective_id=5, has_side_effects=True, vmem_limit_bytes=GRANT
        ),
        name="leave_recurrence",
    )(
        branch, rec, gelu_pre, local, cum, inlet_pre, forget_pre, conv, ext, entered, gates, gates,
        lanes, flags, feed_part, resid,
    )


class Rows:
    def __init__(self, spot, part, got, line, cross_sems, line_sems, first, rows):
        self.spot, self.part, self.got, self.line = spot, part, got, line
        self.cross_sems, self.line_sems = cross_sems, line_sems
        self.first, self.rows = first, rows
        self.span = pl.ds(first, rows)

    def by_rows(self, act):
        def one(at):
            act(pl.ds(pl.multiple_of(self.first + at.start, STEP), STEP))

        by_rows(self.rows, STEP, one)

    def place(self, k):
        spot, hi = self.spot, self.spot.hi
        last = hi - 1
        flipped = jnp.where(spot.z * 2 < hi, 0, 1)
        z = spot.z + flipped * (last - 2 * spot.z)
        if k == last:
            place = z
        else:
            place = jnp.where(k < last - z, last - k, k - (last - z))
        return place + flipped * (last - 2 * place)

    def cross_copy(self, place):
        spot = self.spot
        return remote(
            self.part.at[place, 1 - spot.t, self.span],
            self.got.at[place, self.span],
            self.cross_sems,
            place,
            spot.cross,
        )

    def start(self, k):
        self.cross_copy(self.place(k)).start()

    def line_copy(self, s, up, here=False):
        spot, hi = self.spot, self.spot.hi
        slot = (s - 1) if up else hi + s - 2
        step = 1 if up != here else -1
        return remote(
            self.line.at[0, slot, self.span],
            self.line.at[1, slot, self.span],
            self.line_sems,
            slot,
            spot.line(spot.z + step),
        )

    def own(self, place, at):
        return self.part[place, self.spot.t, at, :].astype(F32) + self.got[place, at, :].astype(F32)

    def send(self, s, up):
        spot, hi = self.spot, self.spot.hi
        place = spot.z + hi - s if up else spot.z - hi + s
        slot = (s - 1) if up else hi + s - 2
        self.cross_copy(place).wait_recv()
        begins = spot.z == 0 if up else spot.z == hi - 1

        @pl.when(begins)
        def _():
            def put(at):
                self.line[0, slot, at, :] = self.own(place, at).astype(BF16)

            self.by_rows(put)

        if s > 1:

            @pl.when(jnp.logical_not(begins))
            def _():
                self.line_copy(s - 1, up, here=True).wait_recv()

                def put(at):
                    before = self.line[1, slot - 1, at, :].astype(F32)
                    self.line[0, slot, at, :] = (self.own(place, at) + before).astype(BF16)

                self.by_rows(put)

        self.line_copy(s, up).start()

    def sends_up(self, s):
        return self.spot.z <= s - 1

    def sends_down(self, s):
        return self.spot.z >= self.spot.hi - s

    def along(self, s):
        spot, hi = self.spot, self.spot.hi

        @pl.when(jnp.logical_and(self.sends_up(s), spot.z < hi - 1))
        def _():
            self.send(s, True)

        @pl.when(jnp.logical_and(self.sends_down(s), spot.z > 0))
        def _():
            self.send(s, False)

    def end(self, done):
        spot, hi = self.spot, self.spot.hi
        self.cross_copy(spot.z).wait_recv()

        @pl.when(spot.z > 0)
        def _():
            self.line_copy(hi - 1, True, here=True).wait_recv()

        @pl.when(spot.z < hi - 1)
        def _():
            self.line_copy(hi - 1, False, here=True).wait_recv()

        def total(at):
            below = self.line[1, hi - 2, at, :].astype(F32)
            above = self.line[1, 2 * hi - 3, at, :].astype(F32)
            value = self.own(spot.z, at)
            value = value + jnp.where(spot.z > 0, below, 0.0)
            done(at, value + jnp.where(spot.z < hi - 1, above, 0.0))

        self.by_rows(total)

    def finish(self):
        spot, hi = self.spot, self.spot.hi
        for place in range(hi):
            self.cross_copy(place).wait_send()
        for s in range(1, hi):

            @pl.when(jnp.logical_and(self.sends_up(s), spot.z < hi - 1))
            def _():
                self.line_copy(s, True).wait_send()

            @pl.when(jnp.logical_and(self.sends_down(s), spot.z > 0))
            def _():
                self.line_copy(s, False).wait_send()


def feed_kernel(
    n, tensor, unit_tiles, own, w_gate, w_up, w_down, cot, resid, gain,
    whole_out, gate_out, up_out, hidden_out, feed_out, both, gain_grad,
    whole, gate_low, up_low, hidden, feed_part, out_sems,
    part, got, line, mine, other, sems, cross_sems, line_sems, swap_sems,
):
    spot = Spot(n, tensor)
    hi = spot.hi
    rows, d = own.shape
    width = w_gate.shape[2]
    every = tensor * rows
    spot.greet(spot.cross)

    def put(at):
        whole[spot.z, spot.t, at, :] = own[at, :]

    by_rows(rows, STEP, put)
    half = rows // HALVES
    chains = [
        Chain(
            spot,
            lambda place, k, i=i: whole.at[
                place, lax.rem(spot.t + k, tensor), pl.ds(i * half, half)
            ],
            sems.at[i],
            [spot.cross],
        )
        for i in range(HALVES)
    ]
    for chain in chains:
        chain.first()
    gain_grad[...] = jnp.zeros_like(gain_grad)
    tiles = width // LANE
    skip = spot.z * tiles - jnp.minimum(spot.z * tiles, unit_tiles - tiles)
    chunk = 256

    def work(place):
        def ahead(j, none):
            cols = pl.ds(pl.multiple_of(j * chunk, chunk), chunk)
            rows_in = whole[place].reshape(every, d)
            gate, slope = gelu_of(dot(rows_in, w_gate[0, :, cols]))
            up = dot(rows_in, w_up[0, :, cols])
            grad = dot(cot[place].reshape(every, d), w_down[0, :, cols])
            at = lax.broadcasted_iota(jnp.int32, (1, chunk), 1) + j * chunk
            ok = at >= skip * LANE
            grad = jnp.where(ok, grad, 0.0)
            hidden[place, :, cols] = jnp.where(ok, gate * up, 0.0).astype(BF16)
            gate_low[place, :, cols] = (grad * up * slope).astype(BF16)
            up_low[place, :, cols] = (grad * gate).astype(BF16)
            return none

        lax.fori_loop(0, width // chunk, ahead, 0)

        def back(j, none):
            cols = pl.ds(pl.multiple_of(j * chunk, chunk), chunk)
            value = dot_nt(gate_low[place], w_gate[0, cols, :])
            value = (value + dot_nt(up_low[place], w_up[0, cols, :])).astype(BF16)
            for side in range(tensor):
                part[place, side, :, cols] = value[side * rows : (side + 1) * rows]
            return none

        lax.fori_loop(0, d // chunk, back, 0)

    def come_and_work(place):
        for chain in chains:
            chain.fans.arrive(place, 1)
        work(place)

    for s in range(1, hi):
        for chain in chains:
            chain.onward(s)
        chains[0].places(s - 1, come_and_work)
    chains[0].places(hi - 1, come_and_work)
    sums = [
        Rows(spot, part, got, line, cross_sems.at[i], line_sems.at[i], i * half, half)
        for i in range(HALVES)
    ]
    for k in range(hi):
        for each in sums:
            each.start(k)
    outs = [
        pltpu.make_async_copy(held, to, out_sems.at[i])
        for i, (held, to) in enumerate(
            (
                (gate_low, gate_out),
                (up_low, up_out),
                (hidden, hidden_out),
                (whole, whole_out),
                (feed_part, feed_out),
            )
        )
    ]
    for copy in outs[:3]:
        copy.start()

    def give(i, none):
        place, j = i // (d // chunk), lax.rem(i, d // chunk)
        cols = pl.ds(pl.multiple_of(j * chunk, chunk), chunk)
        value = dot_nt(hidden[place], w_down[0, cols, :]).astype(BF16)
        for side in range(tensor):
            feed_part[place, side, :, cols] = value[side * rows : (side + 1) * rows]
        return none

    lax.fori_loop(0, hi * (d // chunk), give, 0)
    for chain in chains:
        chain.finish_sends()
    for copy in outs[3:]:
        copy.start()

    def done(at, total):
        value = resid[at, :]
        scale = lax.rsqrt(jnp.mean(value * value, axis=-1, keepdims=True) + 1e-06)
        turned = total * gain[...]
        inner = jnp.mean(turned * value, axis=-1, keepdims=True)
        grad = cot[spot.z, spot.t, at, :].astype(F32)
        grad = grad + scale * turned - value * (scale * scale * scale * inner)
        gained = total * value * scale
        gain_grad[...] += jnp.sum(gained.reshape(2, 8, -1), axis=0)
        mine[at, :] = grad.astype(BF16)

    for s in range(1, hi):
        for each in sums:
            each.along(s)
    swaps = []
    for i, each in enumerate(sums):
        each.end(done)
        span = pl.ds(i * half, half)
        swaps.append(remote(mine.at[span], other.at[span], swap_sems, i, spot.cross))
        swaps[-1].start()
    for each in sums:
        each.finish()
    share(spot, swaps, mine, other, both)
    for copy in outs:
        copy.wait()


def share(spot, copies, mine, other, both):
    def keep(at):
        both[spot.t, at, :] = mine[at, :]

    by_rows(mine.shape[0], STEP, keep)
    for copy in copies:
        copy.wait()

    def take(at):
        both[1 - spot.t, at, :] = other[at, :]

    by_rows(mine.shape[0], STEP, take)


def rows_scratch(grid, rows, width):
    hi = grid.hi
    return [
        pltpu.VMEM((hi, rows, width), BF16),
        pltpu.VMEM((2, 2 * (hi - 1), rows, width), BF16),
        pltpu.VMEM((rows, width), BF16),
        pltpu.VMEM((rows, width), BF16),
    ]


def rows_sems(grid):
    hi = grid.hi
    return [
        pltpu.SemaphoreType.DMA((HALVES, 2, hi)),
        pltpu.SemaphoreType.DMA((HALVES, 2, 2 * (hi - 1))),
        pltpu.SemaphoreType.DMA((2, HALVES)),
    ]


def feed_forward(grid, own, feed, cot, resid, gain, unit_tiles):
    rows, d = own.shape
    hi, tensor = grid.hi, grid.tensor
    width = feed.shape[-1]
    near = pl.BlockSpec(memory_space=pltpu.VMEM)
    whole = jax.ShapeDtypeStruct((hi, tensor, rows, d), BF16)
    low = jax.ShapeDtypeStruct((hi, tensor * rows, width), BF16)
    feed = feed.reshape(3, -1, width)

    def weight(k):
        return pl.BlockSpec((1, d, width), lambda i: (k, 0, 0))

    return pl.pallas_call(
        functools.partial(feed_kernel, grid.n, tensor, unit_tiles),
        grid=(1,),
        out_shape=[
            whole,
            low,
            low,
            low,
            whole,
            jax.ShapeDtypeStruct((tensor, rows, d), BF16),
            jax.ShapeDtypeStruct((8, d), F32),
        ],
        in_specs=[near] + [weight(k) for k in range(3)] + [near] * 3,
        out_specs=[pl.BlockSpec(memory_space=pl.ANY)] * 5 + [near] * 2,
        scratch_shapes=[pltpu.VMEM(a.shape, BF16) for a in (whole, low, low, low, whole)]
        + [pltpu.SemaphoreType.DMA((5,)), pltpu.VMEM(whole.shape, BF16)]
        + rows_scratch(grid, rows, d)
        + [chain_sems(1, HALVES)]
        + rows_sems(grid),
        compiler_params=pltpu.CompilerParams(
            collective_id=2, has_side_effects=True, vmem_limit_bytes=GRANT
        ),
        name="feed_forward",
    )(own, feed, feed, feed, cot, resid, gain)


RING = 4


def tile_rows(rows):
    return 16 if rows % 16 == 0 else 8


SENDING = 8
HELD = 2


def place_at(j, hi):
    return lax.rem(2 * j + hi // 2 + (2 * j) // hi, hi)


def grads_kernel(
    n, tensor, spans, kept,
    unit_tiles,
    second, cot, normed, branch, gate_low, up_low, hidden, gelu_low, input_low, mixed, gates,
    w_input, w_gelu, x, scale, own_out, thin,
    gate_rows, up_rows, down_rows, summed, first_grad, block_out, thin_own, *refs,
):
    stages = (n // LINE).bit_length() - 1
    lists = [refs[i * stages : (i + 1) * stages] for i in range(6)]
    sends, keeps, gots, thin_sends, thin_keeps, thin_gots = lists
    (
        made, ready, got_line, first_out, first_got, thin_ready, thin_line, gained, thin_all, thin_send, thin_got,
        cube_sems, line_sems, first_sems, thin_sems, thin_line_sems, gain_sems,
    ) = refs[6 * stages :]
    spot = Spot(n, tensor)
    hi = spot.hi
    all_spans = len(spans)
    units = all_spans * hi
    step = pl.program_id(0)
    rows = ready.shape[1]
    width = ready.shape[2]
    each = tile_rows(rows)
    last_step = units + stages - 1
    first_rows, out_rows = first_grad.shape[0], own_out.shape[0]
    chunk = w_input.shape[1]
    begin_thin = first_grad.shape[1] // chunk

    def place_of(unit):
        return place_at(lax.rem(unit, hi), hi)

    sources = {
        "gate": (second, gate_low),
        "up": (second, up_low),
        "down": (cot, hidden),
        "gelu": (normed, gelu_low),
        "input": (normed, input_low),
        "out": (branch, mixed),
    }

    def cube_copy(stage, unit):
        slot = lax.rem(unit, RING)
        return remote(
            sends[stage].at[slot],
            gots[stage].at[slot],
            cube_sems.at[stage],
            slot,
            spot.flip(spot.bits[stage]),
        )

    def line_copy(unit):
        slot = lax.rem(unit, SENDING)
        span = unit // hi
        return pltpu.make_async_remote_copy(
            src_ref=ready.at[slot],
            dst_ref=got_line.at[span, spot.z],
            send_sem=line_sems.at[0, slot],
            recv_sem=line_sems.at[1, span * hi + spot.z],
            device_id=spot.line(place_of(unit)),
            device_id_type=MESH,
        )

    def line_here(span, sender):
        here = got_line.at[span, sender]
        return pltpu.make_async_remote_copy(
            src_ref=here,
            dst_ref=here,
            send_sem=line_sems.at[0, 0],
            recv_sem=line_sems.at[1, span * hi + sender],
            device_id=spot.line(sender),
            device_id_type=MESH,
        )

    def line_sent(unit):
        @pl.when(jnp.logical_and(unit >= 0, place_of(unit) != spot.z))
        def _():
            line_copy(unit).wait_send()

    def settle(span):
        for distance in range(1, hi):
            line_here(span, spot.away(distance)).wait_recv()

        def give(at):
            if span < kept:
                tiles = width // LANE
                for place in range(hi):
                    skip = place * tiles - min(place * tiles, unit_tiles - tiles)
                    if skip < tiles:
                        value = got_line[span, place, at, skip * LANE :]
                        cols = slice(place * width, (place + 1) * width - skip * LANE)
                        (gate_rows, up_rows, down_rows)[span][at, cols] = value
            else:
                value = got_line[span, 0, at, :].astype(F32)
                for place in range(1, hi):
                    value = value + got_line[span, place, at, :].astype(F32)
                blocks = width // summed.shape[2]
                for j in range(blocks):
                    cols = slice(j * summed.shape[2], (j + 1) * summed.shape[2])
                    summed[(span - kept) * blocks + j, at, :] = value[:, cols]

        by_rows(rows, each, give)

    def thin_copy(stage):
        return remote(
            thin_sends[stage], thin_gots[stage], thin_sems, stage, spot.flip(spot.bits[stage])
        )

    def thin_line_copy(place, sender):
        return pltpu.make_async_remote_copy(
            src_ref=thin_ready.at[place],
            dst_ref=thin_line.at[sender],
            send_sem=thin_line_sems.at[0, place],
            recv_sem=thin_line_sems.at[1, sender],
            device_id=spot.line(place),
            device_id_type=MESH,
        )

    first_copy = remote(first_out, first_got, first_sems, 0, spot.cross)

    @pl.when(step == 0)
    def _():
        spot.greet(*[spot.flip(bit) for bit in spot.bits], spot.cross)

        def put_out(at):
            to = pl.ds(pl.multiple_of(first_rows + at.start, STEP), STEP)
            first_out[to, :] = own_out[at, :]

        by_rows(out_rows, STEP, put_out)

    @pl.when(step < begin_thin)
    def _():
        cols = pl.ds(pl.multiple_of(step * chunk, chunk), chunk)
        value = dot_nt(input_low[...], w_input[0]) + dot_nt(gelu_low[...], w_gelu[0])
        first_out[0:first_rows, cols] = value.astype(BF16)
        gained[:, cols] = jnp.sum(
            (value * x[...].astype(F32) * scale[:, 0:1]).reshape(-1, 8, chunk), axis=0
        )

    @pl.when(step == begin_thin)
    def _():
        first_copy.start()
        gain = jnp.sum(gained[...], axis=0, keepdims=True)
        size = thin.shape[3]
        for place in range(hi):
            for inner in range(spot.inner_size):
                at = (place * spot.inner_size + inner) * size
                thin_all[place, inner] = thin[place, inner]
                thin_all[place, inner, 0:1, :] = gain[:, at : at + size]
        mine = spot.bit(1)
        for place in range(hi):
            for k in range(thin_sends[0].shape[1]):
                thin_sends[0][place, k] = thin_all[place, 2 * k + 1 - mine]
                thin_keeps[0][place, k] = thin_all[place, 2 * k + mine]
        thin_copy(0).start()

    for stage in range(stages):

        @pl.when(step == begin_thin + stage + 1)
        def _(stage=stage):
            thin_copy(stage).wait_recv()
            if stage < stages - 1:
                mine = spot.bit(spot.bits[stage + 1])
                for place in range(hi):
                    for k in range(thin_sends[stage + 1].shape[1]):
                        a, b = 2 * k + 1 - mine, 2 * k + mine
                        thin_sends[stage + 1][place, k] = (
                            thin_keeps[stage][place, a] + thin_gots[stage][place, a]
                        )
                        thin_keeps[stage + 1][place, k] = (
                            thin_keeps[stage][place, b] + thin_gots[stage][place, b]
                        )
                thin_copy(stage + 1).start()
            else:
                for place in range(hi):
                    thin_ready[place] = thin_keeps[stage][place, 0] + thin_gots[stage][place, 0]
                for distance in range(1, hi):
                    thin_line_copy(spot.away(distance), spot.z).start()

    @pl.when(step < units)
    def _():
        slot = lax.rem(step, RING)

        @pl.when(step >= RING)
        def _():
            cube_copy(0, step - RING).wait_send()

        for span, pieces in enumerate(spans):

            @pl.when(step // hi == span)
            def _(pieces=pieces):
                for name, begin, width, to in pieces:
                    if name == "gates":

                        def put(at, width=width, to=to):
                            made[at, to : to + width] = gates[0, at, :].astype(made.dtype)

                        by_rows(made.shape[0], STEP, put)
                        continue
                    left, right = sources[name]

                    def one(j, carry, left=left, right=right, begin=begin, width=width, to=to):
                        at = pl.ds(pl.multiple_of(j * LANE, LANE), LANE)
                        made[at, to : to + width] = lax.dot_general(
                            left[:, at],
                            right[:, begin : begin + width],
                            (((0,), (0,)), ((), ())),
                            preferred_element_type=F32,
                        ).astype(made.dtype)
                        return carry

                    lax.fori_loop(0, made.shape[0] // LANE, one, 0)

        mine = spot.bit(1)
        for k in range(sends[0].shape[1]):

            def put(at, k=k):
                def block(i):
                    at_made = pl.ds(pl.multiple_of(i * rows + at.start, each), each)
                    return made[at_made, :].astype(BF16)

                sends[0][slot, k, at, :] = block(2 * k + 1 - mine)
                keeps[0][lax.rem(step, HELD), k, at, :] = block(2 * k + mine)

            by_rows(rows, each, put)
        cube_copy(0, step).start()

    for stage in range(stages):
        unit = step - stage - 1

        @pl.when(jnp.logical_and(unit >= 0, unit < units))
        def _(stage=stage, unit=unit):
            slot = lax.rem(unit, RING)
            held = lax.rem(unit, HELD)
            cube_copy(stage, unit).wait_recv()

            def total(k, at):
                return (
                    keeps[stage][held, k, at, :].astype(F32) + gots[stage][slot, k, at, :].astype(F32)
                ).astype(BF16)

            if stage < stages - 1:

                @pl.when(unit >= RING)
                def _():
                    cube_copy(stage + 1, unit - RING).wait_send()

                mine = spot.bit(spot.bits[stage + 1])
                for k in range(sends[stage + 1].shape[1]):

                    def put(at, k=k):
                        sends[stage + 1][slot, k, at, :] = total(2 * k + 1 - mine, at)
                        keeps[stage + 1][held, k, at, :] = total(2 * k + mine, at)

                    by_rows(rows, each, put)
                cube_copy(stage + 1, unit).start()
            else:
                line_sent(unit - SENDING)
                place = place_of(unit)

                @pl.when(place != spot.z)
                def _():
                    def put(at):
                        ready[lax.rem(unit, SENDING), at, :] = total(0, at)

                    by_rows(rows, each, put)
                    line_copy(unit).start()

                @pl.when(place == spot.z)
                def _():
                    def put(at):
                        got_line[unit // hi, spot.z, at, :] = total(0, at)

                    by_rows(rows, each, put)

    late = 2 * hi + stages - 1
    for span in range(all_spans):
        when = span * hi + hi - 1 + late
        if when < last_step:

            @pl.when(step == when)
            def _(span=span):
                settle(span)

    @pl.when(step == last_step)
    def _():
        for span in range(all_spans):
            if span * hi + hi - 1 + late >= last_step:
                settle(span)
        for unit in range(units - SENDING, units):
            line_sent(unit)
        for stage in range(stages):
            for unit in range(units - RING, units):
                cube_copy(stage, unit).wait_send()
            thin_copy(stage).wait_send()
        value = thin_ready[spot.z]
        for distance in range(1, hi):
            place = spot.away(distance)
            thin_line_copy(place, place).wait_recv()
            thin_line_copy(place, spot.z).wait_send()
            value = value + thin_line[place]
        thin_send[...] = value
        copy = remote(thin_send, thin_got, gain_sems, 0, spot.cross)
        copy.start()
        first_copy.wait()

        def take(at):
            first_grad[at, :] = first_out[at, :].astype(F32) + first_got[at, :].astype(F32)

        by_rows(first_rows, STEP, take)

        def take_out(at):
            other = pl.ds(pl.multiple_of(first_rows + at.start, STEP), STEP)
            block_out[spot.t, at, :] = own_out[at, :]
            block_out[1 - spot.t, at, :] = first_got[other, :]

        by_rows(out_rows, STEP, take_out)
        copy.wait()
        row = lax.broadcasted_iota(jnp.int32, thin_own.shape, 0)
        part = jnp.logical_or(row == 0, row == 2)
        thin_own[...] = thin_send[...] + jnp.where(part, thin_got[...], 0.0)


def column_spans(widths, width):
    spans, here, room = [], [], width
    for name, size in widths:
        begin = 0
        while begin < size:
            count = min(size - begin, room)
            here.append((name, begin, count, width - room))
            begin, room = begin + count, room - count
            if room == 0:
                spans, here, room = spans + [here], [], width
    assert not here
    return spans


def send_grads(grid, feed, rec, gates, weights, x, scale, own_out, thin, unit_tiles):
    hi, inner = grid.hi, grid.inner_size
    second, cot, gate_low, up_low, hidden = feed
    normed, branch, gelu_low, input_low, mixed = rec
    d = second.shape[1]
    rows = d // grid.n
    slab = d // hi
    width = gate_low.shape[1]
    kept = 3
    channels = mixed.shape[1]
    spans = column_spans([(name, width) for name in ("gate", "up", "down")], width) + column_spans(
        [(name, channels) for name in ("gelu", "input", "out")] + [("gates", gates.shape[1])], width
    )
    all_spans = len(spans)
    units = all_spans * hi
    stages = inner.bit_length() - 1

    def place_of(i):
        return place_at(lax.rem(jnp.minimum(i, units - 1), hi), hi)

    def slab_of(a):
        return pl.BlockSpec((a.shape[0], slab), lambda i: (0, place_of(i)))

    def whole(a):
        zeros = (0,) * a.ndim
        return pl.BlockSpec(a.shape, lambda i: zeros, pipeline_mode=pl.Buffered(1))

    block = gates.shape[1]
    apart = [jax.ShapeDtypeStruct((rows, unit_tiles * LANE), BF16)] * kept
    summed = jax.ShapeDtypeStruct(((all_spans - kept) * (width // block), rows, block), F32)
    both = jax.ShapeDtypeStruct((grid.tensor,) + own_out.shape, BF16)
    first = jax.ShapeDtypeStruct(x.shape, F32)
    chunk = 256
    chunks = d // chunk
    thin = thin.reshape(hi, inner, 8, thin.shape[1] // 8)
    thin_shape = thin.shape[2:]
    thin_own = jax.ShapeDtypeStruct(thin_shape, F32)
    outs = apart + [summed, first, both, thin_own]
    swapped = (first.shape[0] + own_out.shape[0], d)

    def halves(lead, tail, kind):
        return [
            pltpu.VMEM((lead, inner >> (stage + 1)) + tail, kind) for stage in range(stages)
        ]

    gates = gates.reshape(hi, slab, gates.shape[1])
    return pl.pallas_call(
        functools.partial(grads_kernel, grid.n, grid.tensor, spans, kept, unit_tiles),
        grid=(units + stages,),
        out_shape=outs,
        in_specs=[slab_of(a) for a in (second, cot, normed, branch)]
        + [whole(a) for a in (gate_low, up_low, hidden, gelu_low, input_low, mixed)]
        + [pl.BlockSpec((1,) + gates.shape[1:], lambda i: (place_of(i), 0, 0))]
        + [
            pl.BlockSpec((1, chunk, channels), lambda i, m=m: (m, jnp.minimum(i, chunks - 1), 0))
            for m in range(2)
        ]
        + [pl.BlockSpec((x.shape[0], chunk), lambda i: (0, jnp.minimum(i, chunks - 1)))]
        + [whole(scale), whole(own_out), whole(thin)],
        out_specs=[whole(a) for a in outs],
        scratch_shapes=halves(RING, (rows, width), BF16)
        + halves(HELD, (rows, width), BF16)
        + halves(RING, (rows, width), BF16)
        + halves(hi, thin_shape, F32) * 3
        + [
            pltpu.VMEM((slab, width), BF16 if rows % 16 == 0 else F32),
            pltpu.VMEM((SENDING, rows, width), BF16),
            pltpu.VMEM((all_spans, hi, rows, width), BF16),
            pltpu.VMEM(swapped, BF16),
            pltpu.VMEM(swapped, BF16),
            pltpu.VMEM((hi,) + thin_shape, F32),
            pltpu.VMEM((hi,) + thin_shape, F32),
            pltpu.VMEM((8, d), F32),
            pltpu.VMEM((hi, inner) + thin_shape, F32),
            pltpu.VMEM(thin_shape, F32),
            pltpu.VMEM(thin_shape, F32),
            pltpu.SemaphoreType.DMA((stages, 2, RING)),
            pltpu.SemaphoreType.DMA((2, units)),
            pltpu.SemaphoreType.DMA((2, 1)),
            pltpu.SemaphoreType.DMA((2, stages)),
            pltpu.SemaphoreType.DMA((2, hi)),
            pltpu.SemaphoreType.DMA((2, 1)),
        ],
        compiler_params=pltpu.CompilerParams(
            collective_id=4, has_side_effects=True, vmem_limit_bytes=GRANT
        ),
        name="send_grads",
    )(
        second, cot, normed, branch, gate_low, up_low, hidden, gelu_low, input_low, mixed, gates,
        weights, weights, x, scale, own_out, thin,
    )


def rms_norm(values, gain):
    scale = lax.rsqrt(jnp.mean(values * values, axis=-1, keepdims=True) + 1e-06)
    return values * scale * gain


def dot(left, right):
    return jnp.dot(left, right, preferred_element_type=F32)


def dot_nt(left, right):
    return jnp.einsum("ik,jk->ij", left, right, preferred_element_type=F32)


def dot_tn(left, right):
    return jnp.einsum("ki,kj->ij", left, right, preferred_element_type=F32)


def local(
    block_in,
    segment_ids,
    cotangent,
    first_gain,
    gelu_weight,
    gelu_bias,
    input_weight,
    input_bias,
    conv_weight,
    conv_bias,
    inlet_weight,
    inlet_bias,
    forget_weight,
    forget_bias,
    decay_rate,
    out_weight,
    out_bias,
    second_gain,
    mlp_gate,
    mlp_up,
    mlp_down,
):
    grid = Grid()
    seq_count, tok_count, width = block_in.shape
    head_count, block_size = gelu_weight.shape[1:]
    channels = head_count * block_size
    margin = CONV - 1
    rows_all = seq_count * tok_count
    rows_half = rows_all // grid.tensor
    d_own = gelu_weight.shape[0]
    lane_own = gelu_bias.shape[1]
    units = mlp_gate.shape[1]
    unit_tiles = units // LANE
    window_tiles = -(-unit_tiles // grid.hi)
    window = window_tiles * LANE

    halo_rows = block_in[:, tok_count - HALO :]
    marks = (segment_ids + 1).astype(BF16)
    halo, rim_marks = shifted((halo_rows, marks[:, tok_count - margin :]), "wide", 1)
    halo = halo.reshape(seq_count * HALO, width)
    marks_ext = jnp.concatenate([rim_marks, marks], axis=1)
    earlier = [marks_ext[:, margin - k : margin - k + tok_count] == marks for k in range(1, CONV)]
    flags = jnp.stack([jnp.logical_not(earlier[0])] + earlier, axis=-1).astype(F32)
    flags = jnp.pad(flags.reshape(rows_all, CONV), ((0, 0), (0, 8 - CONV)))

    per_lane = jnp.concatenate(
        [gelu_bias, input_bias]
        + [conv_weight[k] for k in range(CONV)]
        + [conv_bias, inlet_bias, forget_bias, decay_rate]
    )
    lane_table = lax.dynamic_update_slice(
        jnp.zeros(((CONV + 6) * head_count, block_size), BF16), per_lane, (0, grid.w * lane_own)
    )
    per_width = jnp.stack([first_gain, out_bias, second_gain])
    width_table = lax.dynamic_update_slice(
        jnp.zeros((3, width), BF16), per_width, (0, grid.w * d_own)
    )
    thin_own = jnp.concatenate(
        [lane_table.reshape(CONV + 6, channels), width_table.reshape(-1, channels)]
    )
    thin_count = thin_own.shape[0]
    thin_own = jnp.pad(thin_own, ((0, -thin_count % 16), (0, 0)))
    cot_rows = cotangent.reshape(grid.tensor, rows_half, width)
    rec_own = (
        input_weight.transpose(1, 0, 2),
        gelu_weight.transpose(1, 0, 2),
        out_weight.transpose(0, 2, 1),
    )
    feed_own = (mlp_gate, mlp_up, mlp_down.T)
    gates_own = (inlet_weight, forget_weight)
    x = block_in.reshape(rows_all, width)

    if d_own % STEP == 0 and lane_own % STEP == 0:
        feed_all, cot_all = place_feed(grid, feed_own, cot_rows)
        (
            entered,
            mixed,
            resid,
            second_own,
            lanes,
            table,
            gates_all,
            normed,
            ext,
            conv,
            gelu_pre,
            inlet_pre,
            forget_pre,
            cum,
            local_state,
            rec_all,
            feed_all,
            cot_all,
        ) = gather_recurrence(
            grid, x, halo, flags, rec_own, gates_own, thin_own, CONV + 6, feed_all, cot_all, seq_count
        )
        rec_all = rec_all.reshape(3, width, channels)
        gain_first, _, gain_second = table[CONV + 6 : thin_count].reshape(3, width)
    else:
        rec_all, gates_all, thin_all, feed_all, cot_all = place_own(
            grid, rec_own, feed_own, gates_own, thin_own, cot_rows
        )
        rec_all, gates_all, thin_all, cot_all = bring_weights(
            grid, rec_all, gates_all, thin_all, cot_all
        )
        rec_all = rec_all.reshape(3, width, channels)
        gates_all = gates_all.reshape(2 * head_count, block_size, block_size)
        table = jnp.sum(thin_all.astype(F32), axis=0)
        gain_first, out_shift, gain_second = table[CONV + 6 : thin_count].reshape(3, width)
        rate = table[CONV + 5]
        lanes = jnp.concatenate(
            [table[: CONV + 5], jnp.stack([jax.nn.softplus(rate), jax.nn.sigmoid(rate)])]
        )
        lanes = jnp.pad(lanes, ((0, LANE_ROWS - lanes.shape[0]), (0, 0)))
        (
            normed,
            ext,
            conv,
            gelu_pre,
            inlet_pre,
            forget_pre,
            cum,
            local_state,
            entered,
            mixed,
            resid,
            second_own,
            feed_all,
        ) = forward_recurrence(
            grid, x, halo, gain_first[None], rec_all, gates_all[:head_count], gates_all[head_count:],
            lanes, flags, out_shift[None], gain_second[None], feed_all, seq_count,
        )

    rows_feed = grid.hi * rows_all
    second_all, gate_low, up_low, hidden, feed_part, branch_low, gain_two_grad = feed_forward(
        grid, second_own, feed_all, cot_all, resid, gain_second[None], unit_tiles
    )
    second_all, cot_all = (v.reshape(rows_feed, width) for v in (second_all, cot_all))
    gate_low, up_low, hidden = (v.reshape(rows_feed, window) for v in (gate_low, up_low, hidden))
    branch_low = branch_low.reshape(rows_all, width)
    gain_two_grad = jnp.sum(gain_two_grad, axis=0)

    gelu_low, input_low, gate_w_grads, lane_grads, out_shift_grad, own_out = leave_recurrence(
        grid, branch_low, rec_all, gelu_pre, local_state, cum, inlet_pre, forget_pre, conv, ext, entered,
        gates_all, lanes, flags, feed_part, resid, seq_count,
    )
    out_shift_grad = jnp.sum(out_shift_grad, axis=0)
    gate_w_grads = (
        gate_w_grads.reshape(2, head_count, grid.n, lane_own, block_size)
        .transpose(2, 0, 1, 3, 4)
        .reshape(width, block_size)
    )
    inputs = x.astype(F32)
    scale_first = lax.rsqrt(jnp.mean(inputs * inputs, axis=-1, keepdims=True) + 1e-06)
    lane_grads = (
        lane_grads[: CONV + 6]
        .reshape(CONV + 6, head_count, grid.n, lane_own)
        .transpose(2, 0, 1, 3)
        .reshape(grid.n, -1)
    )
    thin_grads = jnp.concatenate(
        [v.reshape(grid.n, d_own) for v in (jnp.zeros_like(gain_two_grad), out_shift_grad, gain_two_grad)]
        + [lane_grads],
        axis=1,
    )
    gate_grad, up_grad, down_grad, rec_grads, first_grad, block_out, thin = send_grads(
        grid,
        (second_all, cot_all, gate_low, up_low, hidden),
        (normed, branch_low, gelu_low, input_low, mixed),
        gate_w_grads,
        rec_all,
        x,
        jnp.broadcast_to(scale_first, (rows_all, 8)),
        own_out,
        thin_grads,
        unit_tiles,
    )
    block_out = block_out.reshape(block_in.shape)
    thin = thin.reshape(-1)
    gate_grad, up_grad = gate_grad.astype(F32), up_grad.astype(F32)
    down_grad = down_grad.astype(F32).T
    gelu_w_grad = rec_grads[:head_count].transpose(1, 0, 2)
    input_w_grad = rec_grads[head_count : 2 * head_count].transpose(1, 0, 2)
    out_grad = rec_grads[2 * head_count : 3 * head_count].transpose(0, 2, 1)
    gate_w_grads = rec_grads[3 * head_count].reshape(2, head_count, lane_own, block_size)
    _, pull_first = jax.vjp(rms_norm, inputs, gain_first)
    input_norm_grad, _ = pull_first(first_grad)
    block_grad = (branch_low.astype(F32) + input_norm_grad).reshape(block_in.shape)
    gain_one_own, out_shift_own, gain_two_own = (
        thin[i * d_own : (i + 1) * d_own] for i in range(3)
    )
    lanes = thin[3 * d_own :].reshape(CONV + 6, head_count, lane_own)
    return (
        block_out,
        block_grad,
        gain_one_own,
        gelu_w_grad,
        lanes[0],
        input_w_grad,
        lanes[1],
        lanes[2 : 2 + CONV],
        lanes[2 + CONV],
        gate_w_grads[0],
        lanes[3 + CONV],
        gate_w_grads[1],
        lanes[4 + CONV],
        lanes[5 + CONV],
        out_grad,
        out_shift_own,
        gain_two_own,
        gate_grad,
        up_grad,
        down_grad,
    )


def solution(mesh):
    in_specs = (
        P(None, "wide", None),
        P(None, "wide"),
        P(None, "wide", None),
        P("wide"),
        P("wide", "tensor", None),
        P("tensor", "wide"),
        P("wide", "tensor", None),
        P("tensor", "wide"),
        P(None, "tensor", "wide"),
        P("tensor", "wide"),
        P("tensor", "wide", None),
        P("tensor", "wide"),
        P("tensor", "wide", None),
        P("tensor", "wide"),
        P("tensor", "wide"),
        P("tensor", None, "wide"),
        P("wide"),
        P("wide"),
        P("wide", "tensor"),
        P("wide", "tensor"),
        P("tensor", "wide"),
    )
    out_specs = (
        P(None, "wide", None),
        P(None, "wide", None),
        P("wide"),
        P("wide", "tensor", None),
        P("tensor", "wide"),
        P("wide", "tensor", None),
        P("tensor", "wide"),
        P(None, "tensor", "wide"),
        P("tensor", "wide"),
        P("tensor", "wide", None),
        P("tensor", "wide"),
        P("tensor", "wide", None),
        P("tensor", "wide"),
        P("tensor", "wide"),
        P("tensor", None, "wide"),
        P("wide"),
        P("wide"),
        P("wide", "tensor"),
        P("wide", "tensor"),
        P("tensor", "wide"),
    )
    return jax.shard_map(local, mesh=mesh, in_specs=in_specs, out_specs=out_specs, check_vma=False)
```

```python
import functools

import jax
import jax.numpy as jnp
from jax import lax
from jax.experimental import pallas as pl
from jax.experimental.pallas import tpu as pltpu
from jax.sharding import PartitionSpec as P

CONV = 4
LANE = 128
GRANT = 60 * 1024 * 1024
F32 = jnp.float32
BF16 = jnp.bfloat16

LINE = 4


class Grid:
    def __init__(self):
        self.n = lax.axis_size("wide")
        self.hi = LINE
        self.inner_size = self.n // LINE
        self.tensor = lax.axis_size("tensor")
        self.w = lax.axis_index("wide")
        self.t = lax.axis_index("tensor")
        self.z = self.w // self.inner_size
        self.inner = lax.rem(self.w, self.inner_size)

    def flip(self, value, bit):
        return lax.ppermute(value, "wide", [(i, i ^ bit) for i in range(self.n)])

    def swap(self, value):
        size = self.tensor
        pairs = [(i, (i + 1) % size) for i in range(size)]
        return lax.ppermute(value, "tensor", pairs)


def shifted(shard, axis, by):
    size = lax.axis_size(axis)
    place = lax.axis_index(axis) - by
    there = jnp.logical_and(place >= 0, place < size)
    pairs = [(i, (i + by) % size) for i in range(size)]
    moved = lax.ppermute(shard, axis, pairs)
    return jax.tree.map(lambda a: jnp.where(there, a, jnp.zeros_like(a)), moved)


def pick(values, index, axis=0):
    return lax.dynamic_index_in_dim(values, index, axis, keepdims=False)


MESH = pl.DeviceIdType.MESH


class Spot:
    def __init__(self, n, tensor):
        self.n = n
        self.hi = LINE
        self.inner_size = n // LINE
        self.bits = [1 << i for i in range(self.inner_size.bit_length() - 1)]
        self.tensor = tensor
        self.w = lax.axis_index("wide")
        self.t = lax.axis_index("tensor")
        self.z = self.w // self.inner_size
        self.inner = lax.rem(self.w, self.inner_size)
        self.cross = {"tensor": lax.rem(self.t + 1, tensor)}

    def bit(self, which):
        return lax.rem(self.inner // which, 2)

    def flip(self, which):
        return {"wide": self.w + which - 2 * which * self.bit(which)}

    def line(self, place):
        return {"wide": place * self.inner_size + self.inner}

    def away(self, distance):
        return lax.rem(self.z + distance, self.hi)

    def greet(self, *sides):
        barrier = pltpu.get_barrier_semaphore()
        for side in sides:
            pl.semaphore_signal(barrier, inc=1, device_id=side, device_id_type=MESH)
        for distance in range(1, self.hi):
            pl.semaphore_signal(
                barrier, inc=1, device_id=self.line(self.away(distance)), device_id_type=MESH
            )
        pl.semaphore_wait(barrier, len(sides) + self.hi - 1)


def remote(src, dst, sems, index, side):
    return pltpu.make_async_remote_copy(
        src_ref=src,
        dst_ref=dst,
        send_sem=sems.at[0, index],
        recv_sem=sems.at[1, index],
        device_id=side,
        device_id_type=MESH,
    )


class Fans:
    def __init__(self, spot, at, sems, base, sides):
        self.spot, self.at, self.sems, self.base, self.sides = spot, at, sems, base, sides
        self.kinds = sorted(range(1 << len(sides)), key=lambda k: (bin(k).count("1"), -k))

    def onto(self, k):
        low = (k & -k) if k else 1 << len(self.sides)
        return [i for i in reversed(range(len(self.sides))) if (1 << i) < low]

    def copy(self, place, k, i, here=False):
        spot, hi = self.spot, self.spot.hi
        landed = k if here else k | (1 << i)
        index = self.base + (landed - 1) * hi + lax.rem(place - spot.z + hi, hi)
        ref = self.at(place, k)
        return remote(ref, ref, self.sems, index, self.sides[i])

    def hand_on(self, place, k):
        for i in self.onto(k):
            self.copy(place, k, i).start()

    def arrive(self, place, k):
        low = (k & -k).bit_length() - 1
        self.copy(place, k, low, here=True).wait_recv()

    def pass_on(self, place):
        for k in self.kinds:
            if k and self.onto(k):
                self.arrive(place, k)
                self.hand_on(place, k)

    def finish(self, place):
        for k in self.kinds:
            if k and not self.onto(k):
                self.arrive(place, k)
        self.finish_sends(place)

    def finish_sends(self, place):
        for k in self.kinds:
            for i in self.onto(k):
                self.copy(place, k, i).wait_send()

    def count(sides, hi):
        return ((1 << sides) - 1) * hi


class Chain:
    def __init__(self, spot, at, sems, sides):
        self.spot, self.at, self.sems = spot, at, sems
        self.fans = Fans(spot, at, sems, 2 * (spot.hi - 1), sides)

    def line_copy(self, s, up):
        spot, hi = self.spot, self.spot.hi
        owner = spot.z - (s - 1) if up else spot.z + (s - 1)
        other = spot.z + 1 if up else spot.z - 1
        ref = self.at(owner, 0)
        return remote(ref, ref, self.sems, (s - 1) if up else hi + s - 2, spot.line(other))

    def line_here(self, s, up):
        spot, hi = self.spot, self.spot.hi
        owner = spot.z - s if up else spot.z + s
        other = spot.z - 1 if up else spot.z + 1
        ref = self.at(owner, 0)
        return remote(ref, ref, self.sems, (s - 1) if up else hi + s - 2, spot.line(other))

    def first(self):
        self.first_line()
        self.fans.hand_on(self.spot.z, 0)

    def first_line(self):
        spot, hi = self.spot, self.spot.hi

        @pl.when(spot.z < hi - 1)
        def _():
            self.line_copy(1, True).start()

        @pl.when(spot.z > 0)
        def _():
            self.line_copy(1, False).start()

    def onward(self, s):
        spot, hi = self.spot, self.spot.hi

        @pl.when(spot.z >= s)
        def _():
            self.line_here(s, True).wait_recv()

        if s < hi - 1:

            @pl.when(jnp.logical_and(spot.z >= s, spot.z < hi - 1))
            def _():
                self.line_copy(s + 1, True).start()

        @pl.when(spot.z >= s)
        def _():
            self.fans.hand_on(spot.z - s, 0)

        @pl.when(spot.z <= hi - 1 - s)
        def _():
            self.line_here(s, False).wait_recv()

        if s < hi - 1:

            @pl.when(jnp.logical_and(spot.z <= hi - 1 - s, spot.z > 0))
            def _():
                self.line_copy(s + 1, False).start()

        @pl.when(spot.z <= hi - 1 - s)
        def _():
            self.fans.hand_on(spot.z + s, 0)

    def places(self, s, act):
        spot = self.spot
        if s == 0:
            act(spot.z)
            return

        @pl.when(spot.z >= s)
        def _():
            act(spot.z - s)

        @pl.when(spot.z <= spot.hi - 1 - s)
        def _():
            act(spot.z + s)

    def second(self, s):
        self.places(s, self.fans.pass_on)

    def finish(self):
        for s in range(self.spot.hi):
            self.places(s, self.fans.finish)
        self.finish_line()

    def finish_sends(self):
        for s in range(self.spot.hi):
            self.places(s, self.fans.finish_sends)
        self.finish_line()

    def finish_line(self):
        spot, hi = self.spot, self.spot.hi
        for s in range(1, hi):

            @pl.when(jnp.logical_and(spot.z >= s - 1, spot.z < hi - 1))
            def _():
                self.line_copy(s, True).wait_send()

            @pl.when(jnp.logical_and(spot.z <= hi - s, spot.z > 0))
            def _():
                self.line_copy(s, False).wait_send()


def chain_sems(sides, *lead):
    return pltpu.SemaphoreType.DMA(lead + (2, 2 * (LINE - 1) + ((1 << sides) - 1) * LINE))


class Turns:
    def __init__(self, spot, distances, window_of, at, sems, sides):
        self.spot, self.window_of, self.at, self.sems = spot, window_of, at, sems
        self.distances = distances
        self.fans = Fans(spot, at, sems, spot.hi, sides)

    def line_copy(self, distance):
        spot = self.spot
        place = spot.away(distance)
        return remote(self.window_of(place), self.at(spot.z, 0), self.sems, distance, spot.line(place))

    def back(self, distance):
        return lax.rem(self.spot.z - distance + self.spot.hi, self.spot.hi)

    def line_here(self, distance):
        place = self.back(distance)
        ref = self.at(place, 0)
        return remote(ref, ref, self.sems, distance, self.spot.line(place))

    def first(self):
        for distance in self.distances:
            self.start(distance)

    def start(self, distance):
        if distance:
            self.line_copy(distance).start()
        else:
            self.fans.hand_on(self.spot.z, 0)

    def onward(self, distance):
        if distance in self.distances:
            self.line_here(distance).wait_recv()
            self.fans.hand_on(self.back(distance), 0)

    def second(self, distance):
        if distance in self.distances:
            self.fans.pass_on(self.back(distance))

    def finish(self):
        for distance in self.distances:
            self.fans.finish(self.back(distance))
            if distance:
                self.line_copy(distance).wait_send()


LATE = (0, 1, 2, 3)


class FeedTurns:
    def __init__(self, spot, feed, sems, cube):
        def index(place, k):
            return place * spot.inner_size + jnp.bitwise_xor(spot.inner, k)

        self.each = [
            Turns(
                spot,
                LATE,
                lambda place, m=m: feed.at[m, spot.n + place],
                lambda place, k, m=m: feed.at[m, index(place, k)],
                sems.at[m],
                cube,
            )
            for m in range(feed.shape[0])
        ]

    def start(self, distance):
        for turns in self.each:
            turns.start(distance)

    def onward(self, distance):
        for turns in self.each:
            turns.onward(distance)

    def second(self, distance):
        for turns in self.each:
            turns.second(distance)

    def finish(self):
        for turns in self.each:
            turns.finish()


def weights_kernel(
    n, tensor, rec, gates, thin, cot, rec_all, gates_all, thin_all, cot_all,
    rec_sems, gates_sems, thin_sems, cot_sems,
):
    del rec, gates, thin, cot
    spot = Spot(n, tensor)
    hi = spot.hi

    def index(place, k):
        return place * spot.inner_size + jnp.bitwise_xor(spot.inner, k)

    cube = [spot.flip(bit) for bit in spot.bits]
    moves = [
        Chain(spot, lambda place, k: thin_all.at[index(place, k)], thin_sems, cube),
        Chain(spot, lambda place, k: gates_all.at[:, index(place, k)], gates_sems, cube),
        *[
            Chain(
                spot, lambda place, k, m=m: rec_all.at[m, index(place, k)], rec_sems.at[m], cube
            )
            for m in range(rec_all.shape[0])
        ],
        Chain(
            spot,
            lambda place, k: cot_all.at[place, lax.rem(spot.t + k, tensor)],
            cot_sems,
            [spot.cross],
        ),
    ]
    spot.greet(*cube, spot.cross)
    last = moves[-1]
    for move in moves[:-1]:
        move.first()
    last.fans.hand_on(spot.z, 0)
    for s in range(1, hi):
        for move in moves[:-1]:
            move.onward(s)
        if s == 1:
            last.first_line()
        else:
            last.onward(s - 1)
        for move in moves:
            move.second(s - 1)
    last.onward(hi - 1)
    for move in moves:
        move.second(hi - 1)
    for move in moves:
        move.finish()


def turn_sems(grid, count):
    return pltpu.SemaphoreType.DMA((count, 2, grid.n))


def place_kernel(
    unit_tiles, spot, wide_in, gelu_in, out_in, gate, up, down, inlet, forget, thin, cot,
    rec_all, gates_all, thin_all, feed_all, cot_all,
):
    step = pl.program_id(0)
    hi = LINE
    width = feed_all.shape[3]
    tiles = width // LANE

    @pl.when(step == 0)
    def _():
        heads, _, lanes = wide_in.shape
        for m, source in enumerate((wide_in, gelu_in, out_in)):
            for h in range(heads):
                rec_all[m, 0, :, h * lanes : (h + 1) * lanes] = source[h]
        for m, source in enumerate((inlet, forget)):
            for h in range(heads):
                gates_all[m * heads + h, 0] = source[h]
        thin_all[0] = thin[...]
        cot_all[0, 0] = cot[0]

    place = jnp.where(step < hi, step, spot[1])
    tile = jnp.minimum(place * tiles, unit_tiles - tiles)
    for m, source in enumerate((gate, up, down)):
        feed_all[m, 0] = source[:, pl.ds(pl.multiple_of(tile * LANE, LANE), width)]


def place_own(grid, rec, feed, gates, thin, cot):
    n, hi = grid.n, grid.hi
    heads, d_own, lanes = rec[0].shape
    units = feed[0].shape[1]
    unit_tiles = units // LANE
    window = -(-unit_tiles // hi) * LANE
    lane_own, block = gates[0].shape[1:]
    spot = jnp.stack([grid.w, grid.z, grid.t])

    def fixed(a):
        zeros = (0,) * a.ndim
        return pl.BlockSpec(a.shape, lambda i, spot: zeros)

    outs = [
        (3, n, d_own, heads * lanes),
        (2 * heads, n, lane_own, block),
        (n,) + thin.shape,
        (3, n + hi, d_own, window),
        (hi,) + cot.shape,
    ]
    return pl.pallas_call(
        functools.partial(place_kernel, unit_tiles),
        grid_spec=pltpu.PrefetchScalarGridSpec(
            num_scalar_prefetch=1,
            grid=(hi + 1,),
            in_specs=[fixed(a) for a in rec + feed + gates + (thin,)]
            + [pl.BlockSpec((1,) + cot.shape[1:], lambda i, spot: (spot[2], 0, 0))],
            out_specs=[
                pl.BlockSpec((3, 1, d_own, heads * lanes), lambda i, spot: (0, spot[0], 0, 0)),
                pl.BlockSpec((2 * heads, 1, lane_own, block), lambda i, spot: (0, spot[0], 0, 0)),
                pl.BlockSpec((1,) + thin.shape, lambda i, spot: (spot[0], 0, 0)),
                pl.BlockSpec(
                    (3, 1, d_own, window),
                    lambda i, spot: (0, jnp.where(i < hi, n + i, spot[0]), 0, 0),
                ),
                pl.BlockSpec((1, 1) + cot.shape[1:], lambda i, spot: (spot[1], spot[2], 0, 0)),
            ],
        ),
        out_shape=[jax.ShapeDtypeStruct(shape, BF16) for shape in outs],
        compiler_params=pltpu.CompilerParams(vmem_limit_bytes=GRANT),
        name="place",
    )(spot, *rec, *feed, *gates, thin, cot)


def bring_weights(grid, rec, gates, thin, cot):
    n, hi, tensor = grid.n, grid.hi, grid.tensor
    far = pl.BlockSpec(memory_space=pl.ANY)
    arrays = (rec, gates, thin, cot)
    cube = grid.inner_size.bit_length() - 1
    return pl.pallas_call(
        functools.partial(weights_kernel, n, tensor),
        out_shape=[jax.ShapeDtypeStruct(a.shape, a.dtype) for a in arrays],
        in_specs=[far] * len(arrays),
        out_specs=[far] * len(arrays),
        input_output_aliases={i: i for i in range(len(arrays))},
        scratch_shapes=[
            chain_sems(cube, rec.shape[0]),
            chain_sems(cube),
            chain_sems(cube),
            chain_sems(1),
        ],
        compiler_params=pltpu.CompilerParams(
            collective_id=0, has_side_effects=True, vmem_limit_bytes=GRANT
        ),
        name="bring_weights",
    )(*arrays)


def by_rows(rows, step, act):
    def one(i, carry):
        act(pl.ds(pl.multiple_of(i * step, step), step))
        return carry

    lax.fori_loop(0, rows // step, one, 0)


STEP = 16
HALVES = 2


GELU_SLOPE = 0.7978845608028654
GELU_CUBE = 0.044715
HALO = 8
GELU_SHIFT, INPUT_SHIFT, TAPS, CONV_SHIFT, INLET_SHIFT, FORGET_SHIFT, RATE_SOFT, RATE_SIGMOID = 0, 1, 2, 6, 7, 8, 9, 10
LANE_ROWS = 16


def gelu_of(v):
    bent = jnp.tanh(GELU_SLOPE * (v + GELU_CUBE * (v * v * v)))
    half = 0.5 * (1.0 + bent)
    slope = half + 0.5 * v * (1.0 - bent * bent) * (GELU_SLOPE * (1.0 + 3.0 * GELU_CUBE * (v * v)))
    return v * half, slope


def minus_expm1(x):
    series = jnp.ones_like(x)
    for k in range(9, 1, -1):
        series = 1.0 + series * x * (1.0 / k)
    return jnp.where(x > -0.5, -x * series, 1.0 - jnp.exp(x))


def decay_of(forget, soft, starts):
    log_decay = -8.0 * forget * soft
    decay = jnp.where(starts, 0.0, jnp.exp(log_decay))
    scaler = jnp.where(starts, 1.0, jnp.sqrt(minus_expm1(2.0 * log_decay)))
    return decay, scaler


def tile_scan(a, b, state_in, decay_in, reverse):
    place = lax.broadcasted_iota(jnp.int32, a.shape, 0)
    for by in (1, 2, 4):
        turn = 8 - by if reverse else by
        ok = place < 8 - by if reverse else place >= by
        b = jnp.where(ok, a * pltpu.roll(b, turn, 0) + b, b)
        a = jnp.where(ok, a * pltpu.roll(a, turn, 0), a)
    return a * decay_in, b + a * state_in


def scan_rows(seqs, length, width, read, write, reverse):
    tiles = length // 8
    last = 0 if reverse else 7

    def one(i, carry):
        tile = tiles - 1 - i if reverse else i
        after = []
        for s in range(seqs):
            decay_in, state_in = carry[s]
            at = pl.ds(pl.multiple_of(s * length + tile * 8, 8), 8)
            a, b = tile_scan(*read(at), state_in, decay_in, reverse)
            write(at, a, b)
            after.append(
                tuple(jnp.broadcast_to(v[last : last + 1], (8, width)) for v in (a, b))
            )
        return tuple(after)

    start = (jnp.ones((8, width), F32), jnp.zeros((8, width), F32))
    lax.fori_loop(0, tiles, one, (start,) * seqs)


class Prefix:
    def __init__(self, spot, seqs, reverse, tots, gots, line, cube_sems, line_sems):
        self.spot, self.seqs, self.reverse = spot, seqs, reverse
        self.tots, self.gots, self.line = tots, gots, line
        self.cube_sems, self.line_sems = cube_sems, line_sems

    def line_copy(self, place, sender):
        stages = len(self.spot.bits)
        return pltpu.make_async_remote_copy(
            src_ref=self.tots.at[stages],
            dst_ref=self.line.at[sender],
            send_sem=self.line_sems.at[0, place],
            recv_sem=self.line_sems.at[1, sender],
            device_id=self.spot.line(place),
            device_id_type=MESH,
        )

    def run(self):
        spot, seqs, hi = self.spot, self.seqs, self.spot.hi
        a, b = slice(0, seqs), slice(seqs, 2 * seqs)
        width = self.tots.shape[2]
        enter_a, enter_b = jnp.ones((seqs, width), F32), jnp.zeros((seqs, width), F32)
        for stage, bit in enumerate(spot.bits):
            copy = remote(
                self.tots.at[stage], self.gots.at[stage], self.cube_sems, stage, spot.flip(bit)
            )
            copy.start()
            copy.wait()
            mine_a, mine_b = self.tots[stage, a, :], self.tots[stage, b, :]
            got_a, got_b = self.gots[stage, a, :], self.gots[stage, b, :]
            after = spot.bit(bit) == (0 if self.reverse else 1)
            enter_b = jnp.where(after, enter_a * got_b + enter_b, enter_b)
            enter_a = jnp.where(after, enter_a * got_a, enter_a)
            self.tots[stage + 1, a, :] = mine_a * got_a
            self.tots[stage + 1, b, :] = jnp.where(
                after, mine_a * got_b + mine_b, got_a * mine_b + got_b
            )
            self.tots[stage + 1, 2 * seqs :, :] = jnp.zeros((8 - 2 * seqs, width), F32)
        for distance in range(1, hi):
            self.line_copy(spot.away(distance), spot.z).start()
        for distance in range(1, hi):
            place = spot.away(distance)
            self.line_copy(place, place).wait_recv()
            self.line_copy(place, spot.z).wait_send()
        come = jnp.zeros((seqs, width), F32)
        for place in reversed(range(hi)) if self.reverse else range(hi):
            before = spot.z < place if self.reverse else spot.z > place
            come = jnp.where(before, self.line[place, a, :] * come + self.line[place, b, :], come)
        return enter_a * come + enter_b


def prefix_scratch(grid, channels):
    stages = grid.inner_size.bit_length() - 1
    return [
        pltpu.VMEM((stages + 1, 8, channels), F32),
        pltpu.VMEM((stages, 8, channels), F32),
        pltpu.VMEM((grid.hi, 8, channels), F32),
        pltpu.SemaphoreType.DMA((2, stages)),
        pltpu.SemaphoreType.DMA((2, grid.hi)),
    ]


def forward_kernel(
    n, tensor, seqs, heads,
    x, halo, gain, w_input, w_gelu, w_inlet, w_forget, lanes, flags, w_out, shift, gain_second, feed,
    normed, ext, conv, gelu_pre, inlet_pre, forget_pre, cum, local, entered, mixed, resid, second,
    feed_all,
    held, factor, addend, part, out, got, tots, gots, line, cube_sems, line_sems, swap_sems, feed_sems,
):
    del feed
    spot = Spot(n, tensor)
    hi = spot.hi
    rows = x.shape[0]
    length = rows // seqs
    width = conv.shape[1]
    step = pl.program_id(0)
    cube = [spot.flip(bit) for bit in spot.bits]
    turns = FeedTurns(spot, feed_all, feed_sems, cube)
    @pl.when(step == 0)
    def _():
        spot.greet(*cube, spot.cross)
        turns.start(1)
        turns.start(0)

        def norm(source, at, to):
            value = source[at, :].astype(F32)
            scale = lax.rsqrt(jnp.mean(value * value, axis=-1, keepdims=True) + 1e-06)
            value = (value * scale * gain[...]).astype(BF16)
            held[pl.ds(pl.multiple_of(at.start + to, STEP), STEP), :] = value
            return value

        def main(at):
            normed[at, :] = norm(x, at, 0)

        by_rows(rows, STEP, main)
        by_rows(halo.shape[0], STEP, lambda at: norm(halo, at, rows))

    @pl.when(step < heads)
    def _():
        table = lanes[...]
        cols = pl.ds(pl.multiple_of(step * width, width), width)

        def row(i):
            return table[i : i + 1]

        branch = (dot(held[...], w_input[0]) + row(INPUT_SHIFT)).astype(BF16)
        gelu_pre[:, cols] = dot(held[0:rows, :], w_gelu[0]) + row(GELU_SHIFT)
        for s in range(seqs):
            here = slice(s * length, (s + 1) * length)
            front = rows + s * HALO
            longer = jnp.concatenate(
                [branch[front : front + HALO].astype(F32), branch[here].astype(F32)], axis=0
            )
            ext[s] = longer.astype(BF16)
            total = row(CONV_SHIFT) + row(TAPS) * longer[HALO:]
            for k in range(1, CONV):
                moved = pltpu.roll(longer, k, 0)[HALO:]
                total = total + jnp.where(flags[here, k : k + 1] > 0.5, row(TAPS + k) * moved, 0.0)
            conv[here, :] = total.astype(BF16)
        blocks = conv[...]
        inlet_pre[...] = dot(blocks, w_inlet[0]) + row(INLET_SHIFT)
        forget_pre[...] = dot(blocks, w_forget[0]) + row(FORGET_SHIFT)

        def terms(at):
            starts = flags[at, 0:1] > 0.5
            decay, scaler = decay_of(jax.nn.sigmoid(forget_pre[at, :]), row(RATE_SOFT), starts)
            factor[at, :] = decay
            addend[at, :] = scaler * jax.nn.sigmoid(inlet_pre[at, :]) * conv[at, :].astype(F32)

        by_rows(rows, 32, terms)

        def write(at, a, b):
            cum[at, cols] = a
            local[at, cols] = b

        scan_rows(seqs, length, width, lambda at: (factor[at, :], addend[at, :]), write, False)

    @pl.when(step == heads)
    def _():
        tots[0] = jnp.zeros_like(tots[0])
        for s in range(seqs):
            tots[0, s : s + 1, :] = cum[(s + 1) * length - 8 : (s + 1) * length, :][7:8]
            tots[0, seqs + s : seqs + s + 1, :] = local[(s + 1) * length - 8 : (s + 1) * length, :][7:8]
        enter = Prefix(spot, seqs, False, tots, gots, line, cube_sems, line_sems).run()
        turns.start(3)
        turns.onward(1)
        entered[...] = jnp.zeros_like(entered)
        entered[0:seqs, :] = enter
        for s in range(seqs):

            def mix(at, s=s):
                here = pl.ds(pl.multiple_of(s * length + at.start, STEP), STEP)
                state = local[here, :] + cum[here, :] * enter[s : s + 1]
                mixed[here, :] = (state * gelu_of(gelu_pre[here, :])[0]).astype(BF16)

            by_rows(length, STEP, mix)
        turns.start(2)
        values = mixed[...]
        own_rows = resid.shape[0]

        def branch(j, carry):
            at = pl.ds(pl.multiple_of(j * 256, 256), 256)
            value = dot_nt(values, w_out[0, at, :])
            for side in range(tensor):
                part[side, :, at] = value[side * own_rows : (side + 1) * own_rows]
            return carry

        lax.fori_loop(0, x.shape[1] // 256, branch, 0)

        def put(at):
            out[at, :] = part[1 - spot.t, at, :].astype(BF16)

        by_rows(own_rows, STEP, put)
        copy = remote(out, got, swap_sems, 0, spot.cross)
        copy.start()
        copy.wait()

        def norm(at):
            own = x[pl.ds(pl.multiple_of(spot.t * own_rows + at.start, STEP), STEP), :].astype(F32)
            value = own + (part[spot.t, at, :] + got[at, :].astype(F32) + shift[...])
            resid[at, :] = value
            scale = lax.rsqrt(jnp.mean(value * value, axis=-1, keepdims=True) + 1e-06)
            second[at, :] = (value * scale * gain_second[...]).astype(BF16)

        by_rows(own_rows, STEP, norm)
        turns.second(0)
        turns.onward(3)
        turns.second(1)
        turns.onward(2)
        turns.second(3)
        turns.second(2)
        turns.finish()


def forward_recurrence(
    grid, x, halo, gain, rec, inlet, forget, lanes, flags, shift, gain_second, feed, seqs
):
    rows, d = x.shape
    heads, width = inlet.shape[:2]
    channels = heads * width
    longer = rows // seqs + HALO
    own_rows = rows // grid.tensor

    def head_of(i):
        return jnp.minimum(i, heads - 1)

    def fixed(a):
        zeros = (0,) * len(a.shape)
        return pl.BlockSpec(a.shape, lambda i: zeros, pipeline_mode=pl.Buffered(1))

    def column(count):
        return pl.BlockSpec((count, width), lambda i: (0, head_of(i)))

    def weight(k):
        return pl.BlockSpec((1, d, width), lambda i: (k, 0, head_of(i)))

    head = pl.BlockSpec((1, width, width), lambda i: (head_of(i), 0, 0))
    far = pl.BlockSpec(memory_space=pl.ANY)
    wide = jax.ShapeDtypeStruct((rows, channels), F32)
    outs = [
        jax.ShapeDtypeStruct((rows, d), BF16),
        jax.ShapeDtypeStruct((seqs, longer, channels), BF16),
        jax.ShapeDtypeStruct((rows, channels), BF16),
        wide,
        wide,
        wide,
        wide,
        wide,
        jax.ShapeDtypeStruct((8, channels), F32),
        jax.ShapeDtypeStruct((rows, channels), BF16),
        jax.ShapeDtypeStruct((own_rows, d), F32),
        jax.ShapeDtypeStruct((own_rows, d), BF16),
        jax.ShapeDtypeStruct(feed.shape, BF16),
    ]
    return pl.pallas_call(
        functools.partial(forward_kernel, grid.n, grid.tensor, seqs, heads),
        grid=(heads + 1,),
        out_shape=outs,
        in_specs=[fixed(x), fixed(halo), fixed(gain), weight(0), weight(1), head, head]
        + [column(LANE_ROWS), fixed(flags)]
        + [pl.BlockSpec((1, d, channels), lambda i: (2, 0, 0), pipeline_mode=pl.Buffered(1))]
        + [fixed(shift), fixed(gain_second), far],
        out_specs=[
            fixed(outs[0]),
            pl.BlockSpec((seqs, longer, width), lambda i: (0, 0, head_of(i))),
            column(rows),
            fixed(wide),
            column(rows),
            column(rows),
        ]
        + [fixed(a) for a in outs[6:12]]
        + [far],
        input_output_aliases={12: 12},
        scratch_shapes=[
            pltpu.VMEM((rows + halo.shape[0], d), BF16),
            pltpu.VMEM((rows, width), F32),
            pltpu.VMEM((rows, width), F32),
            pltpu.VMEM((grid.tensor, own_rows, d), F32),
            pltpu.VMEM((own_rows, d), BF16),
            pltpu.VMEM((own_rows, d), BF16),
        ]
        + prefix_scratch(grid, channels)
        + [pltpu.SemaphoreType.DMA((2, 1)), turn_sems(grid, feed.shape[0])],
        compiler_params=pltpu.CompilerParams(
            collective_id=1, has_side_effects=True, vmem_limit_bytes=GRANT
        ),
        name="forward_recurrence",
    )(x, halo, gain, rec, rec, inlet, forget, lanes, flags, rec, shift, gain_second, feed)


def place_feed_kernel(unit_tiles, spot, gate, up, down, cot, feed_all, cot_all):
    step = pl.program_id(0)
    width = feed_all.shape[3]
    tiles = width // LANE

    @pl.when(step == 0)
    def _():
        cot_all[0, 0] = cot[0]

    place = jnp.where(step < LINE, step, spot[1])
    tile = jnp.minimum(place * tiles, unit_tiles - tiles)
    for m, source in enumerate((gate, up, down)):
        feed_all[m, 0] = source[:, pl.ds(pl.multiple_of(tile * LANE, LANE), width)]


def place_feed(grid, feed, cot):
    n, hi = grid.n, grid.hi
    d_own, units = feed[0].shape
    unit_tiles = units // LANE
    window = -(-unit_tiles // hi) * LANE
    spot = jnp.stack([grid.w, grid.z, grid.t])
    outs = [(3, n + hi, d_own, window), (hi,) + cot.shape]
    return pl.pallas_call(
        functools.partial(place_feed_kernel, unit_tiles),
        grid_spec=pltpu.PrefetchScalarGridSpec(
            num_scalar_prefetch=1,
            grid=(hi + 1,),
            in_specs=[pl.BlockSpec(a.shape, lambda i, spot: (0, 0)) for a in feed]
            + [pl.BlockSpec((1,) + cot.shape[1:], lambda i, spot: (spot[2], 0, 0))],
            out_specs=[
                pl.BlockSpec(
                    (3, 1, d_own, window),
                    lambda i, spot: (0, jnp.where(i < hi, n + i, spot[0]), 0, 0),
                ),
                pl.BlockSpec((1, 1) + cot.shape[1:], lambda i, spot: (spot[1], spot[2], 0, 0)),
            ],
        ),
        out_shape=[jax.ShapeDtypeStruct(shape, BF16) for shape in outs],
        compiler_params=pltpu.CompilerParams(vmem_limit_bytes=GRANT),
        name="place",
    )(spot, *feed, cot)


def gather_kernel(
    n, tensor, seqs, thin_lanes,
    x, halo, flags, wide_in, gelu_in, out_in, inlet_in, forget_in, thin_in, feed, cot,
    entered, mixed, resid, second, lanes, table, gates_out,
    normed_out, ext_out, conv_out, gelu_out, inlet_out, forget_out, cum_out, local_out, rec_out, feed_all, cot_all,
    normed, ext, conv, gelu_pre, inlet_pre, forget_pre, cum, local, out_sems,
    rec, gates, thin, held, factor, addend, part, out, got, tots, gots, line,
    rec_sems, gates_sems, thin_sems, feed_sems, cot_sems, cube_sems, line_sems, swap_sems, own_sem,
):
    del feed, cot
    spot = Spot(n, tensor)
    hi = spot.hi
    rows, d = x.shape
    length = rows // seqs
    heads, d_own, width = wide_in.shape
    cube = [spot.flip(bit) for bit in spot.bits]

    def index(place, k):
        return place * spot.inner_size + jnp.bitwise_xor(spot.inner, k)

    chains = [
        Chain(spot, lambda place, k: thin.at[index(place, k)], thin_sems, cube),
        Chain(spot, lambda place, k: gates.at[:, index(place, k)], gates_sems, cube),
    ] + [
        Chain(spot, lambda place, k, m=m: rec.at[m, index(place, k)], rec_sems.at[m], cube)
        for m in range(3)
    ]
    turns = FeedTurns(spot, feed_all, feed_sems, cube)
    cots = Chain(
        spot,
        lambda place, k: cot_all.at[place, lax.rem(spot.t + k, tensor)],
        cot_sems,
        [spot.cross],
    )
    for m, source in enumerate((wide_in, gelu_in, out_in)):
        for h in range(heads):
            rec[m, spot.w, :, h * width : (h + 1) * width] = source[h]
    for m, source in enumerate((inlet_in, forget_in)):
        for h in range(heads):
            gates[m * heads + h, spot.w] = source[h]
    thin[spot.w] = thin_in[...]
    spot.greet(*cube, spot.cross)
    for chain in chains:
        chain.first()
    cots.fans.hand_on(spot.z, 0)
    for s in range(1, hi):
        for chain in chains:
            chain.onward(s)
        if s == 1:
            cots.first_line()
        else:
            cots.onward(s - 1)
        for chain in chains:
            chain.second(s - 1)
    turns.start(1)
    for chain in chains:
        chain.second(hi - 1)
    for chain in chains:
        chain.finish()
    turns.start(0)
    keep = pltpu.make_async_copy(rec, rec_out, own_sem)

    sums = thin[0].astype(F32)
    for i in range(1, n):
        sums = sums + thin[i].astype(F32)
    table[...] = sums
    rate = sums[RATE_SOFT : RATE_SOFT + 1]
    lanes[0:RATE_SOFT, :] = sums[0:RATE_SOFT]
    soft = jnp.maximum(rate, 0.0) + jnp.log1p(jnp.exp(-jnp.abs(rate)))
    lanes[RATE_SOFT : RATE_SOFT + 1, :] = soft
    lanes[RATE_SIGMOID : RATE_SIGMOID + 1, :] = jax.nn.sigmoid(rate)
    lanes[RATE_SIGMOID + 1 :, :] = jnp.zeros((LANE_ROWS - RATE_SIGMOID - 1, sums.shape[1]), F32)
    per = d // sums.shape[1]

    def across(i):
        first = thin_lanes + i * per
        return jnp.concatenate([sums[first + j : first + j + 1] for j in range(per)], axis=1)

    gain, shift, gain_second = across(0), across(1), across(2)

    def norm_first(source, at, to):
        value = source[at, :].astype(F32)
        scale = lax.rsqrt(jnp.mean(value * value, axis=-1, keepdims=True) + 1e-06)
        value = (value * scale * gain).astype(BF16)
        held[pl.ds(pl.multiple_of(at.start + to, STEP), STEP), :] = value
        return value

    def main(at):
        normed[at, :] = norm_first(x, at, 0)

    by_rows(rows, STEP, main)
    by_rows(halo.shape[0], STEP, lambda at: norm_first(halo, at, rows))

    def work(step, none):
        cols = pl.ds(pl.multiple_of(step * width, width), width)

        def row(i):
            return lanes[i : i + 1, cols]

        def matrix(m):
            return rec[m, :, :, cols].reshape(d, width)

        branch = (dot(held[...], matrix(0)) + row(INPUT_SHIFT)).astype(BF16)
        gelu_pre[:, cols] = dot(held[0:rows, :], matrix(1)) + row(GELU_SHIFT)
        for s in range(seqs):
            here = slice(s * length, (s + 1) * length)
            front = rows + s * HALO
            longer = jnp.concatenate(
                [branch[front : front + HALO].astype(F32), branch[here].astype(F32)], axis=0
            )
            ext[s, :, cols] = longer.astype(BF16)
            total = row(CONV_SHIFT) + row(TAPS) * longer[HALO:]
            for k in range(1, CONV):
                moved = pltpu.roll(longer, k, 0)[HALO:]
                total = total + jnp.where(flags[here, k : k + 1] > 0.5, row(TAPS + k) * moved, 0.0)
            conv[here, cols] = total.astype(BF16)
        blocks = conv[:, cols]
        for m, (to, bias) in enumerate(((inlet_pre, INLET_SHIFT), (forget_pre, FORGET_SHIFT))):
            gate = gates[m * heads + step].reshape(width, width)
            gates_out[m * heads + step] = gate
            to[:, cols] = dot(blocks, gate) + row(bias)

        def terms(at):
            starts = flags[at, 0:1] > 0.5
            decay, scaler = decay_of(jax.nn.sigmoid(forget_pre[at, cols]), row(RATE_SOFT), starts)
            factor[at, :] = decay
            addend[at, :] = scaler * jax.nn.sigmoid(inlet_pre[at, cols]) * conv[at, cols].astype(F32)

        by_rows(rows, 32, terms)

        def write(at, a, b):
            cum[at, cols] = a
            local[at, cols] = b

        scan_rows(seqs, length, width, lambda at: (factor[at, :], addend[at, :]), write, False)
        return none

    lax.fori_loop(0, heads, work, 0)
    tots[0] = jnp.zeros_like(tots[0])
    for s in range(seqs):
        tots[0, s : s + 1, :] = cum[(s + 1) * length - 8 : (s + 1) * length, :][7:8]
        tots[0, seqs + s : seqs + s + 1, :] = local[(s + 1) * length - 8 : (s + 1) * length, :][7:8]
    outs = [
        pltpu.make_async_copy(held_here, to, out_sems.at[i])
        for i, (held_here, to) in enumerate(
            (
                (normed, normed_out),
                (ext, ext_out),
                (conv, conv_out),
                (gelu_pre, gelu_out),
                (inlet_pre, inlet_out),
                (forget_pre, forget_out),
                (cum, cum_out),
                (local, local_out),
            )
        )
    ]
    enter = Prefix(spot, seqs, False, tots, gots, line, cube_sems, line_sems).run()
    turns.start(3)
    turns.onward(1)
    cots.onward(3)
    turns.start(2)
    for copy in [keep] + outs:
        copy.start()
    entered[...] = jnp.zeros_like(entered)
    entered[0:seqs, :] = enter
    for s in range(seqs):

        def mix(at, s=s):
            here = pl.ds(pl.multiple_of(s * length + at.start, STEP), STEP)
            state = local[here, :] + cum[here, :] * enter[s : s + 1]
            mixed[here, :] = (state * gelu_of(gelu_pre[here, :])[0]).astype(BF16)

        by_rows(length, STEP, mix)
    values = mixed[...]
    own_rows = resid.shape[0]
    each, slab = n // hi, d // hi

    def branch(j, none):
        at = pl.ds(pl.multiple_of(j * slab, LANE), slab)
        weights = rec[2, pl.ds(j * each, each)].reshape(slab, heads * width)
        value = dot_nt(values, weights)
        for side in range(tensor):
            part[side, :, at] = value[side * own_rows : (side + 1) * own_rows]
        return none

    lax.fori_loop(0, hi, branch, 0)

    def put(at):
        out[at, :] = part[1 - spot.t, at, :].astype(BF16)

    by_rows(own_rows, STEP, put)
    copy = remote(out, got, swap_sems, 0, spot.cross)
    copy.start()
    copy.wait()

    def norm(at):
        own = x[pl.ds(pl.multiple_of(spot.t * own_rows + at.start, STEP), STEP), :].astype(F32)
        value = own + (part[spot.t, at, :] + got[at, :].astype(F32) + shift)
        resid[at, :] = value
        scale = lax.rsqrt(jnp.mean(value * value, axis=-1, keepdims=True) + 1e-06)
        second[at, :] = (value * scale * gain_second).astype(BF16)

    by_rows(own_rows, STEP, norm)
    turns.onward(3)
    turns.second(0)
    turns.second(1)
    turns.onward(2)
    turns.second(3)
    turns.second(2)
    turns.finish()
    cots.finish()
    keep.wait()
    for copy in outs:
        copy.wait()


def gather_recurrence(grid, x, halo, flags, rec, gates, thin, thin_lanes, feed, cot, seqs):
    rows, d = x.shape
    heads, d_own, width = rec[0].shape
    lane_own = gates[0].shape[1]
    n = grid.n
    channels = heads * width
    longer = rows // seqs + HALO
    own_rows = rows // grid.tensor
    near = pl.BlockSpec(memory_space=pltpu.VMEM)
    far = pl.BlockSpec(memory_space=pl.ANY)
    wide = jax.ShapeDtypeStruct((rows, channels), F32)
    whole = (3, n, d_own, channels)
    cube = grid.inner_size.bit_length() - 1
    saved = [
        jax.ShapeDtypeStruct((rows, d), BF16),
        jax.ShapeDtypeStruct((seqs, longer, channels), BF16),
        jax.ShapeDtypeStruct((rows, channels), BF16),
    ] + [wide] * 5
    outs = [
        jax.ShapeDtypeStruct((8, channels), F32),
        jax.ShapeDtypeStruct((rows, channels), BF16),
        jax.ShapeDtypeStruct((own_rows, d), F32),
        jax.ShapeDtypeStruct((own_rows, d), BF16),
        jax.ShapeDtypeStruct((LANE_ROWS, channels), F32),
        jax.ShapeDtypeStruct(thin.shape, F32),
        jax.ShapeDtypeStruct((2 * heads, width, width), BF16),
    ]
    moved = [
        jax.ShapeDtypeStruct(whole, BF16),
        jax.ShapeDtypeStruct(feed.shape, BF16),
        jax.ShapeDtypeStruct(cot.shape, BF16),
    ]
    return pl.pallas_call(
        functools.partial(gather_kernel, n, grid.tensor, seqs, thin_lanes),
        out_shape=outs + saved + moved,
        in_specs=[near] * 9 + [far] * 2,
        out_specs=[near] * len(outs) + [far] * (len(saved) + len(moved)),
        input_output_aliases={9: 16, 10: 17},
        scratch_shapes=[pltpu.VMEM(a.shape, a.dtype) for a in saved]
        + [pltpu.SemaphoreType.DMA((len(saved),))]
        + [
            pltpu.VMEM(whole, BF16),
            pltpu.VMEM((2 * heads, n, lane_own, width), BF16),
            pltpu.VMEM((n,) + thin.shape, BF16),
            pltpu.VMEM((rows + halo.shape[0], d), BF16),
            pltpu.VMEM((rows, width), F32),
            pltpu.VMEM((rows, width), F32),
            pltpu.VMEM((grid.tensor, own_rows, d), F32),
            pltpu.VMEM((own_rows, d), BF16),
            pltpu.VMEM((own_rows, d), BF16),
        ]
        + prefix_scratch(grid, channels)[:3]
        + [
            chain_sems(cube, 3),
            chain_sems(cube),
            chain_sems(cube),
            turn_sems(grid, feed.shape[0]),
            chain_sems(1),
        ]
        + prefix_scratch(grid, channels)[3:]
        + [pltpu.SemaphoreType.DMA((2, 1)), pltpu.SemaphoreType.DMA],
        compiler_params=pltpu.CompilerParams(
            collective_id=6, has_side_effects=True, vmem_limit_bytes=GRANT
        ),
        name="gather_recurrence",
    )(x, halo, flags, *rec, *gates, thin, feed, cot)


def leave_kernel(
    n, tensor, seqs, branch, w_out, gelu_pre, local, cum, inlet_pre, forget_pre, conv, ext, entered,
    w_inlet, w_forget, lanes, flags, feed_part, resid,
    gelu_low, input_low, gate_grads, lane_grads, shift_grad, own_out,
    tail, carried, factor, addend, back, rim, tots, gots, line, cube_sems, line_sems, rim_sems,
    part, sums_got, sums_line, sums_cross, sums_sems,
):
    spot = Spot(n, tensor)
    every, channels = conv.shape
    length = every // seqs
    heads, width = w_inlet.shape[:2]
    behind = {"wide": lax.rem(spot.w + n - 1, n)}
    ahead = {"wide": lax.rem(spot.w + 1, n)}
    spot.greet(*[spot.flip(bit) for bit in spot.bits], behind, ahead, spot.cross)
    for place in range(spot.hi):
        for side in range(tensor):

            def put(at, place=place, side=side):
                part[place, side, at, :] = feed_part[place, side, at, :]

            by_rows(resid.shape[0], STEP, put)
    half = resid.shape[0] // HALVES
    sums = [
        Rows(spot, part, sums_got, sums_line, sums_cross.at[i], sums_sems.at[i], i * half, half)
        for i in range(HALVES)
    ]
    for k in range(spot.hi):
        for each in sums:
            each.start(k)
    tots[0] = jnp.zeros_like(tots[0])
    lane_grads[...] = jnp.zeros_like(lane_grads)
    shift_grad[...] = jnp.zeros_like(shift_grad)

    def add(at):
        shift_grad[...] += jnp.sum(branch[at, :].astype(F32).reshape(2, 8, -1), axis=0)

    by_rows(every, STEP, add)

    def decays(at, cols):
        soft = lanes[RATE_SOFT : RATE_SOFT + 1, cols]
        return decay_of(jax.nn.sigmoid(forget_pre[at, cols]), soft, flags[at, 0:1] > 0.5)

    def upward(h, none):
        cols = pl.ds(pl.multiple_of(h * width, width), width)
        grad = dot(branch[...], w_out[0, :, cols])
        gelu, slope = gelu_of(gelu_pre[:, cols])
        for s in range(seqs):
            here = slice(s * length, (s + 1) * length)
            state = local[here, cols] + cum[here, cols] * entered[s : s + 1, cols]
            low = (grad[here] * state * slope[here]).astype(BF16)
            gelu_low[here, cols] = low
            lane_grads[0:1, cols] += jnp.sum(low.astype(F32), axis=0, keepdims=True)
            decay, _ = decays(here, cols)
            place = lax.broadcasted_iota(jnp.int32, (length, width), 0)
            factor[here, :] = jnp.where(place < length - 1, pltpu.roll(decay, length - 1, 0), 1.0)
        addend[...] = grad * gelu

        def write(at, a, b):
            tail[at, cols] = a
            carried[at, cols] = b

        scan_rows(seqs, length, width, lambda at: (factor[at, :], addend[at, :]), write, True)
        for s in range(seqs):
            first = slice(s * length, s * length + 8)
            decay, _ = decays(first, cols)
            tots[0, s : s + 1, cols] = decay[0:1] * tail[first, cols][0:1]
            tots[0, seqs + s : seqs + s + 1, cols] = decay[0:1] * carried[first, cols][0:1]
        return none

    lax.fori_loop(0, heads // 2, upward, 0)
    for each in sums:
        each.along(1)
    lax.fori_loop(heads // 2, heads, upward, 0)
    come = Prefix(spot, seqs, True, tots, gots, line, cube_sems, line_sems).run()
    for each in sums:
        each.along(2)
    tots[0, 0:seqs, :] = come

    def downward(h, none):
        cols = pl.ds(pl.multiple_of(h * width, width), width)

        def row(i):
            return lanes[i : i + 1, cols]

        sums = []
        for s in range(seqs):
            here = slice(s * length, (s + 1) * length)
            place = lax.broadcasted_iota(jnp.int32, (length, width), 0)
            starts = flags[here, 0:1] > 0.5
            blocks = conv[here, cols].astype(F32)
            enter = entered[s : s + 1, cols]
            state = local[here, cols] + cum[here, cols] * enter
            before = jnp.where(place > 0, pltpu.roll(state, 1, 0), enter)
            carry = carried[here, cols] + tail[here, cols] * tots[0, s : s + 1, cols]
            inlet = jax.nn.sigmoid(inlet_pre[here, cols])
            forget = jax.nn.sigmoid(forget_pre[here, cols])
            soft = row(RATE_SOFT)
            decay, scaler = decay_of(forget, soft, starts)
            log_grad = jnp.where(
                starts, 0.0, carry * before * decay - carry * inlet * blocks * (decay * decay) / scaler
            )
            rate_grad = jnp.sum(log_grad * (-8.0 * forget), axis=0, keepdims=True) * row(RATE_SIGMOID)
            inlet_low = (carry * scaler * blocks * (inlet * (1.0 - inlet))).astype(BF16)
            forget_low = (log_grad * (-8.0 * soft) * (forget * (1.0 - forget))).astype(BF16)
            conv_grad = (
                carry * scaler * inlet
                + dot_nt(inlet_low, w_inlet[h])
                + dot_nt(forget_low, w_forget[h])
            )
            longer = ext[s, :, cols].astype(F32)
            zeros = jnp.zeros((HALO, width), F32)
            total = jnp.concatenate([zeros, row(TAPS) * conv_grad], axis=0)
            taps = [jnp.sum(conv_grad * longer[HALO:], axis=0, keepdims=True)]
            for k in range(1, CONV):
                masked = jnp.where(flags[here, k : k + 1] > 0.5, conv_grad, 0.0)
                moved = pltpu.roll(longer, k, 0)[HALO:]
                taps.append(jnp.sum(masked * moved, axis=0, keepdims=True))
                sent = jnp.concatenate([zeros, row(TAPS + k) * masked], axis=0)
                total = total + pltpu.roll(sent, HALO + length - k, 0)
            back[s, :, cols] = total
            lows = [jnp.sum(v.astype(F32), axis=0, keepdims=True) for v in (inlet_low, forget_low)]
            sums.append(taps + [jnp.sum(conv_grad, axis=0, keepdims=True)] + lows + [rate_grad])
            for m, low in enumerate((inlet_low, forget_low)):
                factor[here, :] = low.astype(F32) if m == 0 else factor[here, :]
                addend[here, :] = low.astype(F32) if m == 1 else addend[here, :]
        for i in range(len(sums[0])):
            lane_grads[2 + i : 3 + i, cols] = sum(each[i] for each in sums[1:]) + sums[0][i]
        for m, low in enumerate((factor, addend)):
            gate_grads[m, h] = dot_tn(conv[:, cols], low[...].astype(BF16)).astype(BF16)
        return none

    lax.fori_loop(0, heads, downward, 0)
    copy = remote(back.at[:, 0:HALO, :], rim, rim_sems, 0, behind)
    copy.start()
    for s in range(3, spot.hi):
        for each in sums:
            each.along(s)
    copy.wait()

    def give(h, none):
        cols = pl.ds(pl.multiple_of(h * width, width), width)
        total = jnp.zeros((1, width), F32)
        for s in range(seqs):
            edge = jnp.where(spot.w < n - 1, rim[s, :, cols], 0.0)
            value = back[s, HALO:, cols]
            value = jnp.concatenate([value[: length - HALO], value[length - HALO :] + edge], axis=0)
            low = value.astype(BF16)
            input_low[s * length : (s + 1) * length, cols] = low
            total = total + jnp.sum(low.astype(F32), axis=0, keepdims=True)
        lane_grads[1:2, cols] = total
        return none

    lax.fori_loop(0, heads, give, 0)

    def done(at, total):
        own_out[at, :] = (resid[at, :] + total).astype(BF16)

    for each in sums:
        each.end(done)
    for each in sums:
        each.finish()


def leave_recurrence(
    grid, branch, rec, gelu_pre, local, cum, inlet_pre, forget_pre, conv, ext, entered, gates, lanes,
    flags, feed_part, resid, seqs,
):
    every, channels = conv.shape
    d = branch.shape[1]
    heads, width = gates.shape[0] // 2, gates.shape[1]
    near = pl.BlockSpec(memory_space=pltpu.VMEM)
    low = jax.ShapeDtypeStruct((every, channels), BF16)
    return pl.pallas_call(
        functools.partial(leave_kernel, grid.n, grid.tensor, seqs),
        grid=(1,),
        out_shape=[
            low,
            low,
            jax.ShapeDtypeStruct((2, heads, width, width), BF16),
            jax.ShapeDtypeStruct((LANE_ROWS, channels), F32),
            jax.ShapeDtypeStruct((8, d), F32),
            jax.ShapeDtypeStruct(resid.shape, BF16),
        ],
        in_specs=[near, pl.BlockSpec((1, d, channels), lambda i: (2, 0, 0))]
        + [near] * 8
        + [pl.BlockSpec((heads, width, width), lambda i, m=m: (m, 0, 0)) for m in range(2)]
        + [near] * 4,
        out_specs=[near] * 6,
        scratch_shapes=[
            pltpu.VMEM((every, channels), F32),
            pltpu.VMEM((every, channels), F32),
            pltpu.VMEM((every, width), F32),
            pltpu.VMEM((every, width), F32),
            pltpu.VMEM((seqs, every // seqs + HALO, channels), F32),
            pltpu.VMEM((seqs, HALO, channels), F32),
        ]
        + prefix_scratch(grid, channels)
        + [pltpu.SemaphoreType.DMA((2, 1)), pltpu.VMEM(feed_part.shape, BF16)]
        + rows_scratch(grid, *resid.shape)[:2]
        + rows_sems(grid)[:2],
        compiler_params=pltpu.CompilerParams(
            collective_id=5, has_side_effects=True, vmem_limit_bytes=GRANT
        ),
        name="leave_recurrence",
    )(
        branch, rec, gelu_pre, local, cum, inlet_pre, forget_pre, conv, ext, entered, gates, gates,
        lanes, flags, feed_part, resid,
    )


class Rows:
    def __init__(self, spot, part, got, line, cross_sems, line_sems, first, rows):
        self.spot, self.part, self.got, self.line = spot, part, got, line
        self.cross_sems, self.line_sems = cross_sems, line_sems
        self.first, self.rows = first, rows
        self.span = pl.ds(first, rows)

    def by_rows(self, act):
        def one(at):
            act(pl.ds(pl.multiple_of(self.first + at.start, STEP), STEP))

        by_rows(self.rows, STEP, one)

    def place(self, k):
        spot, hi = self.spot, self.spot.hi
        last = hi - 1
        flipped = jnp.where(spot.z * 2 < hi, 0, 1)
        z = spot.z + flipped * (last - 2 * spot.z)
        if k == last:
            place = z
        else:
            place = jnp.where(k < last - z, last - k, k - (last - z))
        return place + flipped * (last - 2 * place)

    def cross_copy(self, place):
        spot = self.spot
        return remote(
            self.part.at[place, 1 - spot.t, self.span],
            self.got.at[place, self.span],
            self.cross_sems,
            place,
            spot.cross,
        )

    def start(self, k):
        self.cross_copy(self.place(k)).start()

    def line_copy(self, s, up, here=False):
        spot, hi = self.spot, self.spot.hi
        slot = (s - 1) if up else hi + s - 2
        step = 1 if up != here else -1
        return remote(
            self.line.at[0, slot, self.span],
            self.line.at[1, slot, self.span],
            self.line_sems,
            slot,
            spot.line(spot.z + step),
        )

    def own(self, place, at):
        return self.part[place, self.spot.t, at, :].astype(F32) + self.got[place, at, :].astype(F32)

    def send(self, s, up):
        spot, hi = self.spot, self.spot.hi
        place = spot.z + hi - s if up else spot.z - hi + s
        slot = (s - 1) if up else hi + s - 2
        self.cross_copy(place).wait_recv()
        begins = spot.z == 0 if up else spot.z == hi - 1

        @pl.when(begins)
        def _():
            def put(at):
                self.line[0, slot, at, :] = self.own(place, at).astype(BF16)

            self.by_rows(put)

        if s > 1:

            @pl.when(jnp.logical_not(begins))
            def _():
                self.line_copy(s - 1, up, here=True).wait_recv()

                def put(at):
                    before = self.line[1, slot - 1, at, :].astype(F32)
                    self.line[0, slot, at, :] = (self.own(place, at) + before).astype(BF16)

                self.by_rows(put)

        self.line_copy(s, up).start()

    def sends_up(self, s):
        return self.spot.z <= s - 1

    def sends_down(self, s):
        return self.spot.z >= self.spot.hi - s

    def along(self, s):
        spot, hi = self.spot, self.spot.hi

        @pl.when(jnp.logical_and(self.sends_up(s), spot.z < hi - 1))
        def _():
            self.send(s, True)

        @pl.when(jnp.logical_and(self.sends_down(s), spot.z > 0))
        def _():
            self.send(s, False)

    def end(self, done):
        spot, hi = self.spot, self.spot.hi
        self.cross_copy(spot.z).wait_recv()

        @pl.when(spot.z > 0)
        def _():
            self.line_copy(hi - 1, True, here=True).wait_recv()

        @pl.when(spot.z < hi - 1)
        def _():
            self.line_copy(hi - 1, False, here=True).wait_recv()

        def total(at):
            below = self.line[1, hi - 2, at, :].astype(F32)
            above = self.line[1, 2 * hi - 3, at, :].astype(F32)
            value = self.own(spot.z, at)
            value = value + jnp.where(spot.z > 0, below, 0.0)
            done(at, value + jnp.where(spot.z < hi - 1, above, 0.0))

        self.by_rows(total)

    def finish(self):
        spot, hi = self.spot, self.spot.hi
        for place in range(hi):
            self.cross_copy(place).wait_send()
        for s in range(1, hi):

            @pl.when(jnp.logical_and(self.sends_up(s), spot.z < hi - 1))
            def _():
                self.line_copy(s, True).wait_send()

            @pl.when(jnp.logical_and(self.sends_down(s), spot.z > 0))
            def _():
                self.line_copy(s, False).wait_send()


def feed_kernel(
    n, tensor, unit_tiles, own, w_gate, w_up, w_down, cot, resid, gain,
    whole_out, gate_out, up_out, hidden_out, feed_out, both, gain_grad,
    whole, gate_low, up_low, hidden, feed_part, out_sems,
    part, got, line, mine, other, sems, cross_sems, line_sems, swap_sems,
):
    spot = Spot(n, tensor)
    hi = spot.hi
    rows, d = own.shape
    width = w_gate.shape[2]
    every = tensor * rows
    spot.greet(spot.cross)

    def put(at):
        whole[spot.z, spot.t, at, :] = own[at, :]

    by_rows(rows, STEP, put)
    half = rows // HALVES
    chains = [
        Chain(
            spot,
            lambda place, k, i=i: whole.at[
                place, lax.rem(spot.t + k, tensor), pl.ds(i * half, half)
            ],
            sems.at[i],
            [spot.cross],
        )
        for i in range(HALVES)
    ]
    for chain in chains:
        chain.first()
    gain_grad[...] = jnp.zeros_like(gain_grad)
    tiles = width // LANE
    skip = spot.z * tiles - jnp.minimum(spot.z * tiles, unit_tiles - tiles)
    chunk = 256

    def work(place):
        def ahead(j, none):
            cols = pl.ds(pl.multiple_of(j * chunk, chunk), chunk)
            rows_in = whole[place].reshape(every, d)
            gate, slope = gelu_of(dot(rows_in, w_gate[0, :, cols]))
            up = dot(rows_in, w_up[0, :, cols])
            grad = dot(cot[place].reshape(every, d), w_down[0, :, cols])
            at = lax.broadcasted_iota(jnp.int32, (1, chunk), 1) + j * chunk
            ok = at >= skip * LANE
            grad = jnp.where(ok, grad, 0.0)
            hidden[place, :, cols] = jnp.where(ok, gate * up, 0.0).astype(BF16)
            gate_low[place, :, cols] = (grad * up * slope).astype(BF16)
            up_low[place, :, cols] = (grad * gate).astype(BF16)
            return none

        lax.fori_loop(0, width // chunk, ahead, 0)

        def back(j, none):
            cols = pl.ds(pl.multiple_of(j * chunk, chunk), chunk)
            value = dot_nt(gate_low[place], w_gate[0, cols, :])
            value = (value + dot_nt(up_low[place], w_up[0, cols, :])).astype(BF16)
            for side in range(tensor):
                part[place, side, :, cols] = value[side * rows : (side + 1) * rows]
            return none

        lax.fori_loop(0, d // chunk, back, 0)

    def come_and_work(place):
        for chain in chains:
            chain.fans.arrive(place, 1)
        work(place)

    for s in range(1, hi):
        for chain in chains:
            chain.onward(s)
        chains[0].places(s - 1, come_and_work)
    chains[0].places(hi - 1, come_and_work)
    sums = [
        Rows(spot, part, got, line, cross_sems.at[i], line_sems.at[i], i * half, half)
        for i in range(HALVES)
    ]
    for k in range(hi):
        for each in sums:
            each.start(k)
    outs = [
        pltpu.make_async_copy(held, to, out_sems.at[i])
        for i, (held, to) in enumerate(
            (
                (gate_low, gate_out),
                (up_low, up_out),
                (hidden, hidden_out),
                (whole, whole_out),
                (feed_part, feed_out),
            )
        )
    ]
    for copy in outs[:3]:
        copy.start()

    def give(i, none):
        place, j = i // (d // chunk), lax.rem(i, d // chunk)
        cols = pl.ds(pl.multiple_of(j * chunk, chunk), chunk)
        value = dot_nt(hidden[place], w_down[0, cols, :]).astype(BF16)
        for side in range(tensor):
            feed_part[place, side, :, cols] = value[side * rows : (side + 1) * rows]
        return none

    lax.fori_loop(0, hi * (d // chunk), give, 0)
    for chain in chains:
        chain.finish_sends()
    for copy in outs[3:]:
        copy.start()

    def done(at, total):
        value = resid[at, :]
        scale = lax.rsqrt(jnp.mean(value * value, axis=-1, keepdims=True) + 1e-06)
        turned = total * gain[...]
        inner = jnp.mean(turned * value, axis=-1, keepdims=True)
        grad = cot[spot.z, spot.t, at, :].astype(F32)
        grad = grad + scale * turned - value * (scale * scale * scale * inner)
        gained = total * value * scale
        gain_grad[...] += jnp.sum(gained.reshape(2, 8, -1), axis=0)
        mine[at, :] = grad.astype(BF16)

    for s in range(1, hi):
        for each in sums:
            each.along(s)
    swaps = []
    for i, each in enumerate(sums):
        each.end(done)
        span = pl.ds(i * half, half)
        swaps.append(remote(mine.at[span], other.at[span], swap_sems, i, spot.cross))
        swaps[-1].start()
    for each in sums:
        each.finish()
    share(spot, swaps, mine, other, both)
    for copy in outs:
        copy.wait()


def share(spot, copies, mine, other, both):
    def keep(at):
        both[spot.t, at, :] = mine[at, :]

    by_rows(mine.shape[0], STEP, keep)
    for copy in copies:
        copy.wait()

    def take(at):
        both[1 - spot.t, at, :] = other[at, :]

    by_rows(mine.shape[0], STEP, take)


def rows_scratch(grid, rows, width):
    hi = grid.hi
    return [
        pltpu.VMEM((hi, rows, width), BF16),
        pltpu.VMEM((2, 2 * (hi - 1), rows, width), BF16),
        pltpu.VMEM((rows, width), BF16),
        pltpu.VMEM((rows, width), BF16),
    ]


def rows_sems(grid):
    hi = grid.hi
    return [
        pltpu.SemaphoreType.DMA((HALVES, 2, hi)),
        pltpu.SemaphoreType.DMA((HALVES, 2, 2 * (hi - 1))),
        pltpu.SemaphoreType.DMA((2, HALVES)),
    ]


def feed_forward(grid, own, feed, cot, resid, gain, unit_tiles):
    rows, d = own.shape
    hi, tensor = grid.hi, grid.tensor
    width = feed.shape[-1]
    near = pl.BlockSpec(memory_space=pltpu.VMEM)
    whole = jax.ShapeDtypeStruct((hi, tensor, rows, d), BF16)
    low = jax.ShapeDtypeStruct((hi, tensor * rows, width), BF16)
    feed = feed.reshape(3, -1, width)

    def weight(k):
        return pl.BlockSpec((1, d, width), lambda i: (k, 0, 0))

    return pl.pallas_call(
        functools.partial(feed_kernel, grid.n, tensor, unit_tiles),
        grid=(1,),
        out_shape=[
            whole,
            low,
            low,
            low,
            whole,
            jax.ShapeDtypeStruct((tensor, rows, d), BF16),
            jax.ShapeDtypeStruct((8, d), F32),
        ],
        in_specs=[near] + [weight(k) for k in range(3)] + [near] * 3,
        out_specs=[pl.BlockSpec(memory_space=pl.ANY)] * 5 + [near] * 2,
        scratch_shapes=[pltpu.VMEM(a.shape, BF16) for a in (whole, low, low, low, whole)]
        + [pltpu.SemaphoreType.DMA((5,)), pltpu.VMEM(whole.shape, BF16)]
        + rows_scratch(grid, rows, d)
        + [chain_sems(1, HALVES)]
        + rows_sems(grid),
        compiler_params=pltpu.CompilerParams(
            collective_id=2, has_side_effects=True, vmem_limit_bytes=GRANT
        ),
        name="feed_forward",
    )(own, feed, feed, feed, cot, resid, gain)


RING = 4


def tile_rows(rows):
    return 16 if rows % 16 == 0 else 8


SENDING = 8
HELD = 2


def place_at(j, hi):
    return lax.rem(2 * j + hi // 2 + (2 * j) // hi, hi)


def grads_kernel(
    n, tensor, spans, kept,
    unit_tiles,
    second, cot, normed, branch, gate_low, up_low, hidden, gelu_low, input_low, mixed, gates,
    w_input, w_gelu, x, scale, own_out, thin,
    gate_rows, up_rows, down_rows, summed, first_grad, block_out, thin_own, *refs,
):
    stages = (n // LINE).bit_length() - 1
    lists = [refs[i * stages : (i + 1) * stages] for i in range(6)]
    sends, keeps, gots, thin_sends, thin_keeps, thin_gots = lists
    (
        made, ready, got_line, first_out, first_got, thin_ready, thin_line, gained, thin_all, thin_send, thin_got,
        cube_sems, line_sems, first_sems, thin_sems, thin_line_sems, gain_sems,
    ) = refs[6 * stages :]
    spot = Spot(n, tensor)
    hi = spot.hi
    all_spans = len(spans)
    units = all_spans * hi
    step = pl.program_id(0)
    rows = ready.shape[1]
    width = ready.shape[2]
    each = tile_rows(rows)
    last_step = units + stages - 1
    first_rows, out_rows = first_grad.shape[0], own_out.shape[0]
    chunk = w_input.shape[1]
    begin_first = kept * hi
    begin_thin = begin_first + first_grad.shape[1] // chunk

    def place_of(unit):
        return place_at(lax.rem(unit, hi), hi)

    sources = {
        "gate": (second, gate_low),
        "up": (second, up_low),
        "down": (cot, hidden),
        "gelu": (normed, gelu_low),
        "input": (normed, input_low),
        "out": (branch, mixed),
    }

    def cube_copy(stage, unit):
        slot = lax.rem(unit, RING)
        return remote(
            sends[stage].at[slot],
            gots[stage].at[slot],
            cube_sems.at[stage],
            slot,
            spot.flip(spot.bits[stage]),
        )

    def line_copy(unit):
        slot = lax.rem(unit, SENDING)
        span = unit // hi
        return pltpu.make_async_remote_copy(
            src_ref=ready.at[slot],
            dst_ref=got_line.at[span, spot.z],
            send_sem=line_sems.at[0, slot],
            recv_sem=line_sems.at[1, span * hi + spot.z],
            device_id=spot.line(place_of(unit)),
            device_id_type=MESH,
        )

    def line_here(span, sender):
        here = got_line.at[span, sender]
        return pltpu.make_async_remote_copy(
            src_ref=here,
            dst_ref=here,
            send_sem=line_sems.at[0, 0],
            recv_sem=line_sems.at[1, span * hi + sender],
            device_id=spot.line(sender),
            device_id_type=MESH,
        )

    def line_sent(unit):
        @pl.when(jnp.logical_and(unit >= 0, place_of(unit) != spot.z))
        def _():
            line_copy(unit).wait_send()

    def settle(span):
        for distance in range(1, hi):
            line_here(span, spot.away(distance)).wait_recv()

        def give(at):
            if span < kept:
                tiles = width // LANE
                for place in range(hi):
                    skip = place * tiles - min(place * tiles, unit_tiles - tiles)
                    if skip < tiles:
                        value = got_line[span, place, at, skip * LANE :]
                        cols = slice(place * width, (place + 1) * width - skip * LANE)
                        (gate_rows, up_rows, down_rows)[span][at, cols] = value
            else:
                value = got_line[span, 0, at, :].astype(F32)
                for place in range(1, hi):
                    value = value + got_line[span, place, at, :].astype(F32)
                blocks = width // summed.shape[2]
                for j in range(blocks):
                    cols = slice(j * summed.shape[2], (j + 1) * summed.shape[2])
                    summed[(span - kept) * blocks + j, at, :] = value[:, cols]

        by_rows(rows, each, give)

    def thin_copy(stage):
        return remote(
            thin_sends[stage], thin_gots[stage], thin_sems, stage, spot.flip(spot.bits[stage])
        )

    def thin_line_copy(place, sender):
        return pltpu.make_async_remote_copy(
            src_ref=thin_ready.at[place],
            dst_ref=thin_line.at[sender],
            send_sem=thin_line_sems.at[0, place],
            recv_sem=thin_line_sems.at[1, sender],
            device_id=spot.line(place),
            device_id_type=MESH,
        )

    first_copy = remote(first_out, first_got, first_sems, 0, spot.cross)

    @pl.when(step == 0)
    def _():
        spot.greet(*[spot.flip(bit) for bit in spot.bits], spot.cross)

        def put_out(at):
            to = pl.ds(pl.multiple_of(first_rows + at.start, STEP), STEP)
            first_out[to, :] = own_out[at, :]

        by_rows(out_rows, STEP, put_out)

    @pl.when(jnp.logical_and(step >= begin_first, step < begin_thin))
    def _():
        cols = pl.ds(pl.multiple_of((step - begin_first) * chunk, chunk), chunk)
        value = dot_nt(input_low[...], w_input[0]) + dot_nt(gelu_low[...], w_gelu[0])
        first_out[0:first_rows, cols] = value.astype(BF16)
        gained[:, cols] = jnp.sum(
            (value * x[...].astype(F32) * scale[:, 0:1]).reshape(-1, 8, chunk), axis=0
        )

    @pl.when(step == begin_thin)
    def _():
        first_copy.start()
        gain = jnp.sum(gained[...], axis=0, keepdims=True)
        size = thin.shape[3]
        for place in range(hi):
            for inner in range(spot.inner_size):
                at = (place * spot.inner_size + inner) * size
                thin_all[place, inner] = thin[place, inner]
                thin_all[place, inner, 0:1, :] = gain[:, at : at + size]
        mine = spot.bit(1)
        for place in range(hi):
            for k in range(thin_sends[0].shape[1]):
                thin_sends[0][place, k] = thin_all[place, 2 * k + 1 - mine]
                thin_keeps[0][place, k] = thin_all[place, 2 * k + mine]
        thin_copy(0).start()

    for stage in range(stages):

        @pl.when(step == begin_thin + stage + 1)
        def _(stage=stage):
            thin_copy(stage).wait_recv()
            if stage < stages - 1:
                mine = spot.bit(spot.bits[stage + 1])
                for place in range(hi):
                    for k in range(thin_sends[stage + 1].shape[1]):
                        a, b = 2 * k + 1 - mine, 2 * k + mine
                        thin_sends[stage + 1][place, k] = (
                            thin_keeps[stage][place, a] + thin_gots[stage][place, a]
                        )
                        thin_keeps[stage + 1][place, k] = (
                            thin_keeps[stage][place, b] + thin_gots[stage][place, b]
                        )
                thin_copy(stage + 1).start()
            else:
                for place in range(hi):
                    thin_ready[place] = thin_keeps[stage][place, 0] + thin_gots[stage][place, 0]
                for distance in range(1, hi):
                    thin_line_copy(spot.away(distance), spot.z).start()

    @pl.when(step < units)
    def _():
        slot = lax.rem(step, RING)

        @pl.when(step >= RING)
        def _():
            cube_copy(0, step - RING).wait_send()

        for span, pieces in enumerate(spans):

            @pl.when(step // hi == span)
            def _(pieces=pieces):
                for name, begin, width, to in pieces:
                    if name == "gates":

                        def put(at, width=width, to=to):
                            made[at, to : to + width] = gates[0, at, :].astype(made.dtype)

                        by_rows(made.shape[0], STEP, put)
                        continue
                    left, right = sources[name]

                    def one(j, carry, left=left, right=right, begin=begin, width=width, to=to):
                        at = pl.ds(pl.multiple_of(j * LANE, LANE), LANE)
                        made[at, to : to + width] = lax.dot_general(
                            left[:, at],
                            right[:, begin : begin + width],
                            (((0,), (0,)), ((), ())),
                            preferred_element_type=F32,
                        ).astype(made.dtype)
                        return carry

                    lax.fori_loop(0, made.shape[0] // LANE, one, 0)

        mine = spot.bit(1)
        for k in range(sends[0].shape[1]):

            def put(at, k=k):
                def block(i):
                    at_made = pl.ds(pl.multiple_of(i * rows + at.start, each), each)
                    return made[at_made, :].astype(BF16)

                sends[0][slot, k, at, :] = block(2 * k + 1 - mine)
                keeps[0][lax.rem(step, HELD), k, at, :] = block(2 * k + mine)

            by_rows(rows, each, put)
        cube_copy(0, step).start()

    for stage in range(stages):
        unit = step - stage - 1

        @pl.when(jnp.logical_and(unit >= 0, unit < units))
        def _(stage=stage, unit=unit):
            slot = lax.rem(unit, RING)
            held = lax.rem(unit, HELD)
            cube_copy(stage, unit).wait_recv()

            def total(k, at):
                return (
                    keeps[stage][held, k, at, :].astype(F32) + gots[stage][slot, k, at, :].astype(F32)
                ).astype(BF16)

            if stage < stages - 1:

                @pl.when(unit >= RING)
                def _():
                    cube_copy(stage + 1, unit - RING).wait_send()

                mine = spot.bit(spot.bits[stage + 1])
                for k in range(sends[stage + 1].shape[1]):

                    def put(at, k=k):
                        sends[stage + 1][slot, k, at, :] = total(2 * k + 1 - mine, at)
                        keeps[stage + 1][held, k, at, :] = total(2 * k + mine, at)

                    by_rows(rows, each, put)
                cube_copy(stage + 1, unit).start()
            else:
                line_sent(unit - SENDING)
                place = place_of(unit)

                @pl.when(place != spot.z)
                def _():
                    def put(at):
                        ready[lax.rem(unit, SENDING), at, :] = total(0, at)

                    by_rows(rows, each, put)
                    line_copy(unit).start()

                @pl.when(place == spot.z)
                def _():
                    def put(at):
                        got_line[unit // hi, spot.z, at, :] = total(0, at)

                    by_rows(rows, each, put)

    late = 2 * hi + stages - 1
    for span in range(all_spans):
        when = span * hi + hi - 1 + late
        if when < last_step:

            @pl.when(step == when)
            def _(span=span):
                settle(span)

    @pl.when(step == last_step)
    def _():
        for span in range(all_spans):
            if span * hi + hi - 1 + late >= last_step:
                settle(span)
        for unit in range(units - SENDING, units):
            line_sent(unit)
        for stage in range(stages):
            for unit in range(units - RING, units):
                cube_copy(stage, unit).wait_send()
            thin_copy(stage).wait_send()
        value = thin_ready[spot.z]
        for distance in range(1, hi):
            place = spot.away(distance)
            thin_line_copy(place, place).wait_recv()
            thin_line_copy(place, spot.z).wait_send()
            value = value + thin_line[place]
        thin_send[...] = value
        copy = remote(thin_send, thin_got, gain_sems, 0, spot.cross)
        copy.start()
        first_copy.wait()

        def take(at):
            first_grad[at, :] = first_out[at, :].astype(F32) + first_got[at, :].astype(F32)

        by_rows(first_rows, STEP, take)

        def take_out(at):
            other = pl.ds(pl.multiple_of(first_rows + at.start, STEP), STEP)
            block_out[spot.t, at, :] = own_out[at, :]
            block_out[1 - spot.t, at, :] = first_got[other, :]

        by_rows(out_rows, STEP, take_out)
        copy.wait()
        row = lax.broadcasted_iota(jnp.int32, thin_own.shape, 0)
        part = jnp.logical_or(row == 0, row == 2)
        thin_own[...] = thin_send[...] + jnp.where(part, thin_got[...], 0.0)


def column_spans(widths, width):
    spans, here, room = [], [], width
    for name, size in widths:
        begin = 0
        while begin < size:
            count = min(size - begin, room)
            here.append((name, begin, count, width - room))
            begin, room = begin + count, room - count
            if room == 0:
                spans, here, room = spans + [here], [], width
    assert not here
    return spans


def send_grads(grid, feed, rec, gates, weights, x, scale, own_out, thin, unit_tiles):
    hi, inner = grid.hi, grid.inner_size
    second, cot, gate_low, up_low, hidden = feed
    normed, branch, gelu_low, input_low, mixed = rec
    d = second.shape[1]
    rows = d // grid.n
    slab = d // hi
    width = gate_low.shape[1]
    kept = 3
    channels = mixed.shape[1]
    spans = column_spans([(name, width) for name in ("gate", "up", "down")], width) + column_spans(
        [(name, channels) for name in ("gelu", "input", "out")] + [("gates", gates.shape[1])], width
    )
    all_spans = len(spans)
    units = all_spans * hi
    stages = inner.bit_length() - 1

    def place_of(i):
        return place_at(lax.rem(jnp.minimum(i, units - 1), hi), hi)

    def slab_of(a):
        return pl.BlockSpec((a.shape[0], slab), lambda i: (0, place_of(i)))

    def whole(a):
        zeros = (0,) * a.ndim
        return pl.BlockSpec(a.shape, lambda i: zeros, pipeline_mode=pl.Buffered(1))

    block = gates.shape[1]
    apart = [jax.ShapeDtypeStruct((rows, unit_tiles * LANE), BF16)] * kept
    summed = jax.ShapeDtypeStruct(((all_spans - kept) * (width // block), rows, block), F32)
    both = jax.ShapeDtypeStruct((grid.tensor,) + own_out.shape, BF16)
    first = jax.ShapeDtypeStruct(x.shape, F32)
    chunk = 256
    chunks = d // chunk

    def chunk_of(i):
        return jnp.clip(i - kept * hi, 0, chunks - 1)

    thin = thin.reshape(hi, inner, 8, thin.shape[1] // 8)
    thin_shape = thin.shape[2:]
    thin_own = jax.ShapeDtypeStruct(thin_shape, F32)
    outs = apart + [summed, first, both, thin_own]
    swapped = (first.shape[0] + own_out.shape[0], d)

    def halves(lead, tail, kind):
        return [
            pltpu.VMEM((lead, inner >> (stage + 1)) + tail, kind) for stage in range(stages)
        ]

    gates = gates.reshape(hi, slab, gates.shape[1])
    return pl.pallas_call(
        functools.partial(grads_kernel, grid.n, grid.tensor, spans, kept, unit_tiles),
        grid=(units + stages,),
        out_shape=outs,
        in_specs=[slab_of(a) for a in (second, cot, normed, branch)]
        + [whole(a) for a in (gate_low, up_low, hidden, gelu_low, input_low, mixed)]
        + [pl.BlockSpec((1,) + gates.shape[1:], lambda i: (place_of(i), 0, 0))]
        + [
            pl.BlockSpec((1, chunk, channels), lambda i, m=m: (m, chunk_of(i), 0))
            for m in range(2)
        ]
        + [pl.BlockSpec((x.shape[0], chunk), lambda i: (0, chunk_of(i)))]
        + [whole(scale), whole(own_out), whole(thin)],
        out_specs=[whole(a) for a in outs],
        scratch_shapes=halves(RING, (rows, width), BF16)
        + halves(HELD, (rows, width), BF16)
        + halves(RING, (rows, width), BF16)
        + halves(hi, thin_shape, F32) * 3
        + [
            pltpu.VMEM((slab, width), BF16 if rows % 16 == 0 else F32),
            pltpu.VMEM((SENDING, rows, width), BF16),
            pltpu.VMEM((all_spans, hi, rows, width), BF16),
            pltpu.VMEM(swapped, BF16),
            pltpu.VMEM(swapped, BF16),
            pltpu.VMEM((hi,) + thin_shape, F32),
            pltpu.VMEM((hi,) + thin_shape, F32),
            pltpu.VMEM((8, d), F32),
            pltpu.VMEM((hi, inner) + thin_shape, F32),
            pltpu.VMEM(thin_shape, F32),
            pltpu.VMEM(thin_shape, F32),
            pltpu.SemaphoreType.DMA((stages, 2, RING)),
            pltpu.SemaphoreType.DMA((2, units)),
            pltpu.SemaphoreType.DMA((2, 1)),
            pltpu.SemaphoreType.DMA((2, stages)),
            pltpu.SemaphoreType.DMA((2, hi)),
            pltpu.SemaphoreType.DMA((2, 1)),
        ],
        compiler_params=pltpu.CompilerParams(
            collective_id=4, has_side_effects=True, vmem_limit_bytes=GRANT
        ),
        name="send_grads",
    )(
        second, cot, normed, branch, gate_low, up_low, hidden, gelu_low, input_low, mixed, gates,
        weights, weights, x, scale, own_out, thin,
    )


def rms_norm(values, gain):
    scale = lax.rsqrt(jnp.mean(values * values, axis=-1, keepdims=True) + 1e-06)
    return values * scale * gain


def dot(left, right):
    return jnp.dot(left, right, preferred_element_type=F32)


def dot_nt(left, right):
    return jnp.einsum("ik,jk->ij", left, right, preferred_element_type=F32)


def dot_tn(left, right):
    return jnp.einsum("ki,kj->ij", left, right, preferred_element_type=F32)


def local(
    block_in,
    segment_ids,
    cotangent,
    first_gain,
    gelu_weight,
    gelu_bias,
    input_weight,
    input_bias,
    conv_weight,
    conv_bias,
    inlet_weight,
    inlet_bias,
    forget_weight,
    forget_bias,
    decay_rate,
    out_weight,
    out_bias,
    second_gain,
    mlp_gate,
    mlp_up,
    mlp_down,
):
    grid = Grid()
    seq_count, tok_count, width = block_in.shape
    head_count, block_size = gelu_weight.shape[1:]
    channels = head_count * block_size
    margin = CONV - 1
    rows_all = seq_count * tok_count
    rows_half = rows_all // grid.tensor
    d_own = gelu_weight.shape[0]
    lane_own = gelu_bias.shape[1]
    units = mlp_gate.shape[1]
    unit_tiles = units // LANE
    window_tiles = -(-unit_tiles // grid.hi)
    window = window_tiles * LANE

    halo_rows = block_in[:, tok_count - HALO :]
    marks = (segment_ids + 1).astype(BF16)
    halo, rim_marks = shifted((halo_rows, marks[:, tok_count - margin :]), "wide", 1)
    halo = halo.reshape(seq_count * HALO, width)
    marks_ext = jnp.concatenate([rim_marks, marks], axis=1)
    earlier = [marks_ext[:, margin - k : margin - k + tok_count] == marks for k in range(1, CONV)]
    flags = jnp.stack([jnp.logical_not(earlier[0])] + earlier, axis=-1).astype(F32)
    flags = jnp.pad(flags.reshape(rows_all, CONV), ((0, 0), (0, 8 - CONV)))

    per_lane = jnp.concatenate(
        [gelu_bias, input_bias]
        + [conv_weight[k] for k in range(CONV)]
        + [conv_bias, inlet_bias, forget_bias, decay_rate]
    )
    lane_table = lax.dynamic_update_slice(
        jnp.zeros(((CONV + 6) * head_count, block_size), BF16), per_lane, (0, grid.w * lane_own)
    )
    per_width = jnp.stack([first_gain, out_bias, second_gain])
    width_table = lax.dynamic_update_slice(
        jnp.zeros((3, width), BF16), per_width, (0, grid.w * d_own)
    )
    thin_own = jnp.concatenate(
        [lane_table.reshape(CONV + 6, channels), width_table.reshape(-1, channels)]
    )
    thin_count = thin_own.shape[0]
    thin_own = jnp.pad(thin_own, ((0, -thin_count % 16), (0, 0)))
    cot_rows = cotangent.reshape(grid.tensor, rows_half, width)
    rec_own = (
        input_weight.transpose(1, 0, 2),
        gelu_weight.transpose(1, 0, 2),
        out_weight.transpose(0, 2, 1),
    )
    feed_own = (mlp_gate, mlp_up, mlp_down.T)
    gates_own = (inlet_weight, forget_weight)
    x = block_in.reshape(rows_all, width)

    if d_own % STEP == 0 and lane_own % STEP == 0:
        feed_all, cot_all = place_feed(grid, feed_own, cot_rows)
        (
            entered,
            mixed,
            resid,
            second_own,
            lanes,
            table,
            gates_all,
            normed,
            ext,
            conv,
            gelu_pre,
            inlet_pre,
            forget_pre,
            cum,
            local_state,
            rec_all,
            feed_all,
            cot_all,
        ) = gather_recurrence(
            grid, x, halo, flags, rec_own, gates_own, thin_own, CONV + 6, feed_all, cot_all, seq_count
        )
        rec_all = rec_all.reshape(3, width, channels)
        gain_first, _, gain_second = table[CONV + 6 : thin_count].reshape(3, width)
    else:
        rec_all, gates_all, thin_all, feed_all, cot_all = place_own(
            grid, rec_own, feed_own, gates_own, thin_own, cot_rows
        )
        rec_all, gates_all, thin_all, cot_all = bring_weights(
            grid, rec_all, gates_all, thin_all, cot_all
        )
        rec_all = rec_all.reshape(3, width, channels)
        gates_all = gates_all.reshape(2 * head_count, block_size, block_size)
        table = jnp.sum(thin_all.astype(F32), axis=0)
        gain_first, out_shift, gain_second = table[CONV + 6 : thin_count].reshape(3, width)
        rate = table[CONV + 5]
        lanes = jnp.concatenate(
            [table[: CONV + 5], jnp.stack([jax.nn.softplus(rate), jax.nn.sigmoid(rate)])]
        )
        lanes = jnp.pad(lanes, ((0, LANE_ROWS - lanes.shape[0]), (0, 0)))
        (
            normed,
            ext,
            conv,
            gelu_pre,
            inlet_pre,
            forget_pre,
            cum,
            local_state,
            entered,
            mixed,
            resid,
            second_own,
            feed_all,
        ) = forward_recurrence(
            grid, x, halo, gain_first[None], rec_all, gates_all[:head_count], gates_all[head_count:],
            lanes, flags, out_shift[None], gain_second[None], feed_all, seq_count,
        )

    rows_feed = grid.hi * rows_all
    second_all, gate_low, up_low, hidden, feed_part, branch_low, gain_two_grad = feed_forward(
        grid, second_own, feed_all, cot_all, resid, gain_second[None], unit_tiles
    )
    second_all, cot_all = (v.reshape(rows_feed, width) for v in (second_all, cot_all))
    gate_low, up_low, hidden = (v.reshape(rows_feed, window) for v in (gate_low, up_low, hidden))
    branch_low = branch_low.reshape(rows_all, width)
    gain_two_grad = jnp.sum(gain_two_grad, axis=0)

    gelu_low, input_low, gate_w_grads, lane_grads, out_shift_grad, own_out = leave_recurrence(
        grid, branch_low, rec_all, gelu_pre, local_state, cum, inlet_pre, forget_pre, conv, ext, entered,
        gates_all, lanes, flags, feed_part, resid, seq_count,
    )
    out_shift_grad = jnp.sum(out_shift_grad, axis=0)
    gate_w_grads = (
        gate_w_grads.reshape(2, head_count, grid.n, lane_own, block_size)
        .transpose(2, 0, 1, 3, 4)
        .reshape(width, block_size)
    )
    inputs = x.astype(F32)
    scale_first = lax.rsqrt(jnp.mean(inputs * inputs, axis=-1, keepdims=True) + 1e-06)
    lane_grads = (
        lane_grads[: CONV + 6]
        .reshape(CONV + 6, head_count, grid.n, lane_own)
        .transpose(2, 0, 1, 3)
        .reshape(grid.n, -1)
    )
    thin_grads = jnp.concatenate(
        [v.reshape(grid.n, d_own) for v in (jnp.zeros_like(gain_two_grad), out_shift_grad, gain_two_grad)]
        + [lane_grads],
        axis=1,
    )
    gate_grad, up_grad, down_grad, rec_grads, first_grad, block_out, thin = send_grads(
        grid,
        (second_all, cot_all, gate_low, up_low, hidden),
        (normed, branch_low, gelu_low, input_low, mixed),
        gate_w_grads,
        rec_all,
        x,
        jnp.broadcast_to(scale_first, (rows_all, 8)),
        own_out,
        thin_grads,
        unit_tiles,
    )
    block_out = block_out.reshape(block_in.shape)
    thin = thin.reshape(-1)
    gate_grad, up_grad = gate_grad.astype(F32), up_grad.astype(F32)
    down_grad = down_grad.astype(F32).T
    gelu_w_grad = rec_grads[:head_count].transpose(1, 0, 2)
    input_w_grad = rec_grads[head_count : 2 * head_count].transpose(1, 0, 2)
    out_grad = rec_grads[2 * head_count : 3 * head_count].transpose(0, 2, 1)
    gate_w_grads = rec_grads[3 * head_count].reshape(2, head_count, lane_own, block_size)
    _, pull_first = jax.vjp(rms_norm, inputs, gain_first)
    input_norm_grad, _ = pull_first(first_grad)
    block_grad = (branch_low.astype(F32) + input_norm_grad).reshape(block_in.shape)
    gain_one_own, out_shift_own, gain_two_own = (
        thin[i * d_own : (i + 1) * d_own] for i in range(3)
    )
    lanes = thin[3 * d_own :].reshape(CONV + 6, head_count, lane_own)
    return (
        block_out,
        block_grad,
        gain_one_own,
        gelu_w_grad,
        lanes[0],
        input_w_grad,
        lanes[1],
        lanes[2 : 2 + CONV],
        lanes[2 + CONV],
        gate_w_grads[0],
        lanes[3 + CONV],
        gate_w_grads[1],
        lanes[4 + CONV],
        lanes[5 + CONV],
        out_grad,
        out_shift_own,
        gain_two_own,
        gate_grad,
        up_grad,
        down_grad,
    )


def solution(mesh):
    in_specs = (
        P(None, "wide", None),
        P(None, "wide"),
        P(None, "wide", None),
        P("wide"),
        P("wide", "tensor", None),
        P("tensor", "wide"),
        P("wide", "tensor", None),
        P("tensor", "wide"),
        P(None, "tensor", "wide"),
        P("tensor", "wide"),
        P("tensor", "wide", None),
        P("tensor", "wide"),
        P("tensor", "wide", None),
        P("tensor", "wide"),
        P("tensor", "wide"),
        P("tensor", None, "wide"),
        P("wide"),
        P("wide"),
        P("wide", "tensor"),
        P("wide", "tensor"),
        P("tensor", "wide"),
    )
    out_specs = (
        P(None, "wide", None),
        P(None, "wide", None),
        P("wide"),
        P("wide", "tensor", None),
        P("tensor", "wide"),
        P("wide", "tensor", None),
        P("tensor", "wide"),
        P(None, "tensor", "wide"),
        P("tensor", "wide"),
        P("tensor", "wide", None),
        P("tensor", "wide"),
        P("tensor", "wide", None),
        P("tensor", "wide"),
        P("tensor", "wide"),
        P("tensor", None, "wide"),
        P("wide"),
        P("wide"),
        P("wide", "tensor"),
        P("wide", "tensor"),
        P("tensor", "wide"),
    )
    return jax.shard_map(local, mesh=mesh, in_specs=in_specs, out_specs=out_specs, check_vma=False)
```
